32 devices in a mesh: row: 4 (over x, core), seq: 8 (over z, y).
Axes of the slice: x: 2, y: 2, z: 4, core: 2. Of those that a mesh axis runs over, the one named last changes fastest.
Arguments:
- tokens: bfloat16 [4, 4096, 768], P('row', 'seq'), may hold values from -6 to 6
- cotangent: bfloat16 [4, 4096, 768], P('row', 'seq'), may hold values from -6 to 6
- w_qkv: bfloat16 [768, 2304], replicated, may hold values from -0.21875 to 0.21875
- b_qkv: bfloat16 [2304], replicated, may hold values from -3 to 3
- w_out: bfloat16 [768, 768], replicated, may hold values from -4 to 4
- b_out: bfloat16 [768], replicated, may hold values from -3 to 3
- gain_one: float32 [768], replicated, may hold values from 0.1 to 1.9
- shift_one: float32 [768], replicated, may hold values from -3 to 3
- w_up: bfloat16 [768, 3072], P(None, 'seq'), may hold values from -0.21875 to 0.21875
- b_up: bfloat16 [3072], P('seq'), may hold values from -3 to 3
- w_down: bfloat16 [3072, 768], P('seq'), may hold values from -0.109375 to 0.109375
- b_down: bfloat16 [768], replicated, may hold values from -3 to 3
- gain_two: float32 [768], replicated, may hold values from 0.1 to 1.9
- shift_two: float32 [768], replicated, may hold values from -3 to 3
- feature_codes: int32 [12, 64, 64], replicated, may hold values from 0 to 15
- bias_table: float32 [12, 32], replicated, may hold values from -3 to 3
- offset_bucket: int32 [8191], replicated, may hold values from 0 to 31, as said below
Outputs:
- layer_out: bfloat16 [4, 4096, 768], P('row', 'seq')
- grad_tokens: float32 [4, 4096, 768], P('row', 'seq')
- grad_w_qkv: float32 [768, 2304], replicated
- grad_b_qkv: float32 [2304], replicated
- grad_w_out: float32 [768, 768], replicated
- grad_b_out: float32 [768], replicated
- grad_gain_one: float32 [768], replicated
- grad_shift_one: float32 [768], replicated
- grad_w_up: float32 [768, 3072], P(None, 'seq')
- grad_b_up: float32 [3072], P('seq')
- grad_w_down: float32 [3072, 768], P('seq')
- grad_b_down: float32 [768], replicated
- grad_gain_two: float32 [768], replicated
- grad_shift_two: float32 [768], replicated
- grad_bias_table: float32 [12, 32], replicated
The draws below stay inside these ranges and needn't reach their ends.
Inputs may be any that keep to these rules, and one draw needn't show every extreme that they name: `offset_bucket`: entry j stands for the key offset j - (4095) from its query. Offsets below -128 all have bucket 32 - 2, offsets above 128 all have bucket 32 - 1, offset 0 has bucket 0, and every other offset has a bucket under 32 - 2.
All inputs are finite; a program needn't handle non-finite values.
Results may differ from the reference program's by a relative error of at most 0.025.
Values may be sent and summed in bfloat16 or wider, within the bound.
A program may use at most 384 MiB of HBM per device.

```python
import math
import jax
import jax.numpy as jnp
from jax import lax

D = 768
HEADS = 12
HEAD_DIM = 64
FF = 3072
FEATURES = 64
BUCKETS = 32
WINDOW = 128
LENGTH = 4096
ROWS = 4


def draw_offset_bucket(key, part):
    key = jax.random.fold_in(key, 11)
    offsets = jnp.arange(2 * LENGTH - 1, dtype=jnp.int32) - (LENGTH - 1)
    inner = jax.random.randint(key, (2 * LENGTH - 1,), 0, BUCKETS - 2, dtype=jnp.int32)
    inner = jnp.where(offsets == 0, 0, inner)
    outer = jnp.where(offsets > WINDOW, BUCKETS - 1, inner)
    return jnp.where(offsets < -WINDOW, BUCKETS - 2, outer).astype(jnp.int32)


def with_ends(array, stream_key, low, high):
    index_at = [jax.random.randint(jax.random.fold_in(stream_key, axis), (), 0, length) for axis, length in enumerate(array.shape)]
    widest = array.shape.index(max(array.shape))
    neighbour = index_at[:widest] + [(index_at[widest] + 1) % array.shape[widest]] + index_at[widest + 1:]
    return array.at[tuple(index_at)].set(low).at[tuple(neighbour)].set(high)


def level_of(own_key, extent, split, low, high):
    gain = 1.0
    for position, blocks in split:
        draws = jax.random.uniform(jax.random.fold_in(jax.random.fold_in(own_key, 6), position), (blocks,), jnp.float32, low / len(split), high / len(split))
        gain = gain * jnp.repeat(jnp.exp(draws), extent[position] // blocks).reshape((-1,) + (1,) * (len(extent) - 1 - position))
    return gain


def noise(stream_key, dims, spread, limit, shards=(), kind=jnp.bfloat16):
    entries = jax.random.normal(stream_key, dims, jnp.float32) * spread
    if len(shards) > 0:
        entries = level_of(stream_key, dims, shards, -0.22, 0.18) * entries
    return jnp.clip(entries, min=-limit, max=limit).astype(kind)


def setup_inputs(seed: int = 0) -> dict:
    keys = jax.random.split(jax.random.key(seed), 18)
    tokens = noise(keys[0], (ROWS, LENGTH, D), 1.0, 6.0, ((0, 4), (1, 8)))
    cotangent = noise(keys[1], (ROWS, LENGTH, D), 1.0, 6.0, ((0, 4), (1, 8)))
    w_qkv = noise(keys[2], (D, 3 * D), D ** -0.5, 0.21875)
    b_qkv = noise(keys[3], (3 * D,), 0.3, 3.0)
    w_out = noise(keys[4], (D, D), 2 ** -0.5, 4.0)
    b_out = noise(keys[5], (D,), 0.3, 3.0)
    gain_one = jnp.clip(1.0 + 0.18 * jax.random.normal(keys[6], (D,), jnp.float32), 0.1, 1.9)
    shift_one = noise(keys[7], (D,), 0.3, 3.0, (), jnp.float32)
    w_up = noise(keys[8], (D, FF), D ** -0.5, 0.21875, ((1, 8),))
    b_up = noise(keys[9], (FF,), 0.3, 3.0, ((0, 8),))
    w_down = noise(keys[10], (FF, D), FF ** -0.5, 0.109375, ((0, 8),))
    b_down = noise(keys[11], (D,), 0.3, 3.0)
    gain_two = jnp.clip(1.0 + 0.18 * jax.random.normal(keys[12], (D,), jnp.float32), 0.1, 1.9)
    shift_two = noise(keys[13], (D,), 0.3, 3.0, (), jnp.float32)
    feature_codes = with_ends(jax.random.randint(keys[14], (HEADS, HEAD_DIM, FEATURES), 0, 16), jax.random.fold_in(keys[14], 1), 0, 15).astype(jnp.int32)
    bias_table = noise(keys[15], (HEADS, BUCKETS), 1.0, 3.0, (), jnp.float32)
    offset_bucket = draw_offset_bucket(jax.random.fold_in(keys[17], 71), 0)
    return {"tokens": tokens, "cotangent": cotangent, "w_qkv": w_qkv, "b_qkv": b_qkv, "w_out": w_out, "b_out": b_out, "gain_one": gain_one, "shift_one": shift_one, "w_up": w_up, "b_up": b_up, "w_down": w_down, "b_down": b_down, "gain_two": gain_two, "shift_two": shift_two, "feature_codes": feature_codes, "bias_table": bias_table, "offset_bucket": offset_bucket}


@jax.custom_vjp
def low(v):
    return lax.optimization_barrier(v.astype(jnp.bfloat16)).astype(jnp.float32)

@jax.custom_vjp
def low_back(v):
    return v

def low_keep(v):
    return (low(v), None)

def low_pass(kept, grad):
    return (grad,)

def back_keep(v):
    return (v, None)

def back_low(kept, grad):
    return (low(grad),)
low.defvjp(low_keep, low_pass)
low_back.defvjp(back_keep, back_low)
norm_eps = 1e-06
code_center = 7.5
code_spread = math.sqrt(21.25)
highest_precision_mode = lax.Precision.HIGHEST

def layer_norm(values, gain_vec, shift_vec):
    center = values - lax.optimization_barrier(jnp.mean(values, -1, keepdims=True))
    variance = lax.optimization_barrier(jnp.mean(center * center, -1, keepdims=True))
    return center * lax.rsqrt(variance + norm_eps) * gain_vec + shift_vec

def feature_map(rounded, omega_int):
    head_dim = rounded.shape[-1]
    feat_count = omega_int.shape[-1]
    factor = head_dim ** (-0.25) / code_spread
    projected = jnp.einsum('lhd,hdm->lhm', rounded, omega_int, precision=highest_precision_mode) * factor
    half_norm = lax.optimization_barrier(jnp.sum(rounded * rounded, -1, keepdims=True)) * (0.5 * head_dim ** (-0.5))
    return low(jnp.exp(projected - half_norm) * feat_count ** (-0.5))

def attention(query_features, k_feat, v_low, bias_table, offset_bucket):
    seq_len, head_count, head_dim = v_low.shape
    block_len = min(512, seq_len)
    coef_all = jnp.exp(bias_table)

    def one_block(block_start):
        q_block = lax.dynamic_slice_in_dim(query_features, block_start, block_len, 0)
        positions = block_start + jnp.arange(block_len, dtype=jnp.int32)
        offsets = jnp.arange(seq_len, dtype=jnp.int32)[None, :] - positions[:, None] + (seq_len - 1)
        buckets = jnp.take(offset_bucket, offsets, axis=0)
        coef_block = jnp.take(coef_all, buckets, axis=1)
        scores = jnp.einsum('qhm,khm->hqk', q_block, k_feat, precision=highest_precision_mode)
        weights = coef_block * scores
        attention_numerator = jnp.einsum('hqk,khd->qhd', weights, v_low, precision=highest_precision_mode)
        denominator = lax.optimization_barrier(jnp.sum(weights, -1))
        return attention_numerator / jnp.transpose(denominator)[:, :, None]
    starts = jnp.arange(seq_len // block_len, dtype=jnp.int32) * block_len
    blocks = lax.map(jax.checkpoint(one_block), starts)
    return blocks.reshape(seq_len, head_count, head_dim)

def layer_one(seq_in, params, omega_int, offset_bucket):
    w_qkv, b_qkv, w_out, b_out, gain_one, shift_one, w_up, b_up, w_down, b_down, gain_two, shift_two, bias_table = params
    seq_len, model_width = seq_in.shape
    head_count, head_dim, feat_count = omega_int.shape
    qkv_proj = low_back(jnp.dot(seq_in, w_qkv, precision=highest_precision_mode) + b_qkv)
    q_low = low(qkv_proj[:, :model_width].reshape(seq_len, head_count, head_dim))
    k_low = low(qkv_proj[:, model_width:2 * model_width].reshape(seq_len, head_count, head_dim))
    v_low = low(qkv_proj[:, 2 * model_width:].reshape(seq_len, head_count, head_dim))
    attn_out = attention(feature_map(q_low, omega_int), feature_map(k_low, omega_int), v_low, bias_table, offset_bucket)
    attn_low = low(attn_out.reshape(seq_len, model_width))
    first_sum = seq_in + low_back(jnp.dot(attn_low, w_out, precision=highest_precision_mode) + b_out)
    hidden_one = layer_norm(first_sum, gain_one, shift_one)
    hidden_low = low(hidden_one)
    pre_up = low_back(jnp.dot(hidden_low, w_up, precision=highest_precision_mode) + b_up)
    act_low = low(jax.nn.gelu(pre_up, approximate=False))
    ffn_out = low_back(jnp.dot(act_low, w_down, precision=highest_precision_mode) + b_down)
    return layer_norm(hidden_one + ffn_out, gain_two, shift_two)

def reference(tokens, cotangent, w_qkv, b_qkv, w_out, b_out, gain_one, shift_one, w_up, b_up, w_down, b_down, gain_two, shift_two, feature_codes, bias_table, offset_bucket):
    omega_int = feature_codes.astype(jnp.float32) - code_center
    primals = (tokens.astype(jnp.float32), w_qkv.astype(jnp.float32), b_qkv.astype(jnp.float32), w_out.astype(jnp.float32), b_out.astype(jnp.float32), gain_one, shift_one, w_up.astype(jnp.float32), b_up.astype(jnp.float32), w_down.astype(jnp.float32), b_down.astype(jnp.float32), gain_two, shift_two, bias_table)

    def forward(inputs, *params):

        def per_sequence(seq_in):
            return layer_one(seq_in, params, omega_int, offset_bucket)
        return lax.map(per_sequence, inputs)
    result, pullback = jax.vjp(forward, *primals)
    gradients = pullback(cotangent.astype(jnp.float32))
    return (result.astype(jnp.bfloat16), gradients[0], gradients[1], gradients[2], gradients[3], gradients[4], gradients[5], gradients[6], gradients[7], gradients[8], gradients[9], gradients[10], gradients[11], gradients[12], gradients[13])
```

```python
import functools
import math

import jax
import jax.numpy as jnp
from jax import lax
from jax.experimental import pallas as pl
from jax.experimental.pallas import tpu as pltpu
from jax.sharding import PartitionSpec as P

WINDOW = 128
LANES = 128
LINE = 512
CHUNK = 256
EPS = 1e-06
CENTER = 7.5
SPREAD = math.sqrt(21.25)
ROOT_HALF = 0.7071067811865476
INV_ROOT_TAU = 0.3989422804014327
MIB = 1 << 20
F32 = jnp.float32
BF16 = jnp.bfloat16


def nn(a, b):
    return lax.dot_general(a, b, (((1,), (0,)), ((), ())), preferred_element_type=F32)


def nt(a, b):
    return lax.dot_general(a, b, (((1,), (1,)), ((), ())), preferred_element_type=F32)


def tn(a, b):
    return lax.dot_general(a, b, (((0,), (0,)), ((), ())), preferred_element_type=F32)


def halves(values):
    upper = values.astype(BF16)
    return upper, (values - upper.astype(F32)).astype(BF16)


def block_ones(size, head_dim):
    rows = lax.broadcasted_iota(jnp.int32, (size, size), 0) // head_dim
    cols = lax.broadcasted_iota(jnp.int32, (size, size), 1) // head_dim
    return jnp.where(rows == cols, 1.0, 0.0)


def head_sums(values, ones):
    upper, lower = halves(values)
    return nn(upper, ones) + nn(lower, ones)


def first_half(shape):
    return lax.broadcasted_iota(jnp.int32, shape, len(shape) - 1) < LANES // 2


def both_heads(pair):
    first = first_half((1, LANES))
    mask_a = jnp.where(first, 1.0, 0.0).astype(pair.dtype)
    mask_b = jnp.where(first, 0.0, 1.0).astype(pair.dtype)
    return jnp.concatenate([pair * mask_a, pair * mask_b], 0)


def per_head(stacked):
    rows = stacked.shape[0] // 2
    return jnp.where(first_half((rows, LANES)), stacked[:rows], stacked[rows:])


def compact(full):
    half = LANES // 2
    return jnp.where(first_half((half, LANES)), full[:half], full[half:])


def expand(small, ones):
    return jnp.concatenate([small, small], 0) * ones


def block_state(keys, values):
    return compact(tn(keys, values)), jnp.sum(keys.astype(F32), 0, keepdims=True)


def coef_tile(line_ref, pair):
    tiles = []
    for head in range(2):
        row = line_ref[pl.ds(2 * pair + head, 1), :]
        wide = pltpu.roll(
            jnp.broadcast_to(row, (WINDOW, LINE)), LINE - WINDOW + 1, 1, stride=1, stride_axis=0
        )
        tiles.append(wide[:, : 3 * WINDOW])
    return jnp.concatenate(tiles, 0)


def far_coefs(line_ref, pair):
    first = first_half((1, LANES))
    row_a = line_ref[pl.ds(2 * pair, 1), :]
    row_b = line_ref[pl.ds(2 * pair + 1, 1), :]
    left = jnp.where(first, row_a[:, 0:1], row_b[:, 0:1])
    right = jnp.where(first, row_a[:, LINE - 2 : LINE - 1], row_b[:, LINE - 2 : LINE - 1])
    return left, right


def unskew_sum(tile):
    rows = tile.shape[0]
    padded = jnp.concatenate([tile, jnp.zeros((rows, LINE - tile.shape[1]), F32)], 1)
    while rows > 8:
        rows = rows // 2
        padded = pltpu.roll(padded[:rows], rows, 1) + padded[rows:]
    while rows > 1:
        rows = rows // 2
        padded = pltpu.roll(padded[:rows], rows, 1) + padded[rows:]
    return padded


def lanes(pair):
    return pl.ds(pl.multiple_of(pair * LANES, LANES), LANES)


def qkv_phase(x_ref, w_ref, b_ref, omega_ref, q_ref, k_ref, v_ref, qf_ref, kf_ref, head_dim):
    width = x_ref.shape[1]
    x = x_ref[...]
    ones = block_ones(CHUNK, head_dim).astype(BF16)
    factor = head_dim ** (-0.25) / SPREAD
    for part, low_ref, feat_ref in ((1, k_ref, kf_ref), (2, v_ref, None), (0, q_ref, qf_ref)):
        for chunk in range(width // CHUNK):
            cols = slice(chunk * CHUNK, (chunk + 1) * CHUNK)
            wide = slice(part * width + chunk * CHUNK, part * width + (chunk + 1) * CHUNK)
            low = (nn(x, w_ref[:, wide]) + b_ref[:, wide].astype(F32)).astype(BF16)
            low_ref[:, cols] = low
            if feat_ref is not None:
                projected = nn(low, omega_ref[chunk]) * factor
                widened = low.astype(F32)
                half_norm = head_sums(widened * widened, ones) * (0.5 * head_dim ** (-0.5))
                feat_ref[:, cols] = (
                    jnp.exp(projected - half_norm) * head_dim ** (-0.5)
                ).astype(BF16)


def line_phase(bucket_ref, table_ref, line_ref):
    buckets = table_ref.shape[1]
    one_hot = jnp.where(
        lax.broadcasted_iota(jnp.int32, (buckets, LINE), 0) == bucket_ref[...], 1.0, 0.0
    )
    logs = lax.dot_general(
        table_ref[...],
        one_hot,
        (((1,), (0,)), ((), ())),
        precision=lax.Precision.HIGHEST,
        preferred_element_type=F32,
    )
    line_ref[...] = jnp.exp(logs)


def state_phase(kf_ref, v_ref, num_ref, den_ref, total_ref, pairs):
    blocks = kf_ref.shape[0] // WINDOW
    half = LANES // 2

    @pl.loop(0, pairs)
    def _(pair):
        total = jnp.zeros((half, LANES), F32)
        total_den = jnp.zeros((1, LANES), F32)
        for block in range(blocks):
            rows = slice(block * WINDOW, (block + 1) * WINDOW)
            num, den = block_state(kf_ref[rows, lanes(pair)], v_ref[rows, lanes(pair)])
            num_ref[pair * blocks + block] = num
            den_ref[pl.ds(pair * blocks + block, 1), :] = den
            total = total + num
            total_den = total_den + den
        total_ref[pl.ds(pl.multiple_of(pair * half, half), half), :] = total
        total_ref[pl.ds(pairs * half + pair, 1), :] = total_den


def band_forward_phase(
    qf_ref, ke_ref, ve_ref, line_ref, num_ref, den_ref, before_ref, after_ref,
    out_ref, low_ref, denom_ref, left_ref, right_ref, left_den_ref, right_den_ref, pairs, head_dim,
):
    blocks = qf_ref.shape[0] // WINDOW
    half = LANES // 2

    @pl.loop(0, pairs)
    def _(pair):
        ones_f32 = block_ones(LANES, head_dim)
        ones = ones_f32.astype(BF16)
        cols = lanes(pair)
        coef = coef_tile(line_ref, pair)
        left_coef, right_coef = far_coefs(line_ref, pair)
        state_rows = pl.ds(pl.multiple_of(pair * half, half), half)
        den_row = pl.ds(pairs * half + pair, 1)
        edge_low = block_state(ke_ref[:WINDOW, cols], ve_ref[:WINDOW, cols])
        edge_high = block_state(
            ke_ref[(blocks + 1) * WINDOW :, cols], ve_ref[(blocks + 1) * WINDOW :, cols]
        )
        past = (before_ref[state_rows, :], before_ref[den_row, :])
        future = (after_ref[state_rows, :], after_ref[den_row, :])

        def block_of(block):
            index = pair * blocks + block
            return num_ref[index], den_ref[pl.ds(index, 1), :]

        def add(one, two, sign=1.0):
            return tuple(a + sign * b for a, b in zip(one, two))

        lefts = [add(past, edge_low, -1.0), past]
        for block in range(2, blocks):
            lefts.append(add(lefts[-1], block_of(block - 2)))
        rights = [add(future, edge_high, -1.0), future]
        for block in range(2, blocks):
            rights.append(add(rights[-1], block_of(blocks + 1 - block)))
        rights = rights[::-1]
        for block in range(blocks):
            rows = slice(block * WINDOW, (block + 1) * WINDOW)
            window = slice(block * WINDOW, (block + 3) * WINDOW)
            index = pair * blocks + block
            query = qf_ref[rows, cols]
            scores = nt(both_heads(query), ke_ref[window, cols])
            weights = (coef * scores).astype(BF16)
            values = ve_ref[window, cols]
            summed = nn(weights, jnp.concatenate([values, jnp.ones_like(values)], 1))
            numer = per_head(summed[:, :LANES])
            denom = per_head(summed[:, LANES:])
            left, left_den = lefts[block]
            right, right_den = rights[block]
            left_ref[index] = left
            right_ref[index] = right
            left_den_ref[pl.ds(index, 1), :] = left_den
            right_den_ref[pl.ds(index, 1), :] = right_den
            upper, lower = halves(expand(left_coef * left + right_coef * right, ones_f32))
            numer = numer + nn(query, upper) + nn(query, lower)
            den_far = left_coef * left_den + right_coef * right_den
            denom = denom + head_sums(query.astype(F32) * den_far, ones)
            out = numer / denom
            out_ref[rows, cols] = out
            low_ref[rows, cols] = out.astype(BF16)
            denom_ref[rows, cols] = denom


def norm_parts(values):
    center = values - jnp.mean(values, -1, keepdims=True)
    inv_scale = lax.rsqrt(jnp.mean(center * center, -1, keepdims=True) + EPS)
    return center * inv_scale, inv_scale


def out_phase(x_ref, low_ref, w_ref, b_ref, normed_ref, scale_ref):
    first_sum = x_ref[...].astype(F32) + nn(low_ref[...], w_ref[...]) + b_ref[...].astype(F32)
    normed, inv_scale = norm_parts(first_sum)
    normed_ref[...] = normed
    scale_ref[...] = jnp.broadcast_to(inv_scale, scale_ref.shape)


def norm_back(grad_out, normed, inv_scale, gain):
    grad_normed = grad_out * gain
    centered = grad_normed - jnp.mean(grad_normed, -1, keepdims=True)
    return inv_scale * (centered - normed * jnp.mean(grad_normed * normed, -1, keepdims=True))


def ffn_phase(
    normed_ref, scale_ref, gain_one_ref, shift_one_ref, up_ref, b_up_ref, down_ref, b_down_ref,
    gain_two_ref, shift_two_ref, cot_ref, layer_ref, first_ref, low_ref, vec_ref, gup_ref, gdown_ref,
    gbias_ref, act_ref, slope_ref, acc_ref,
):
    shards = up_ref.shape[0]
    normed_one = normed_ref[...]
    hidden_one = normed_one * gain_one_ref[...] + shift_one_ref[...]
    hidden = hidden_one.astype(BF16)
    acc_ref[...] = hidden_one + b_down_ref[...].astype(F32)

    @pl.loop(0, shards)
    def _(shard):
        pre = nn(hidden, up_ref[shard]) + b_up_ref[shard, 0:1, :].astype(F32)
        phi = 0.5 * (1.0 + lax.erf(pre * ROOT_HALF))
        act = (pre * phi).astype(BF16)
        act_ref[shard] = act
        slope_ref[shard] = (phi + pre * INV_ROOT_TAU * jnp.exp(-0.5 * pre * pre)).astype(BF16)
        acc_ref[...] += nt(act, down_ref[shard])

    normed_two, scale_two = norm_parts(acc_ref[...])
    layer_ref[...] = (normed_two * gain_two_ref[...] + shift_two_ref[...]).astype(BF16)
    cot = cot_ref[...].astype(F32)
    grad_second = norm_back(cot, normed_two, scale_two, gain_two_ref[...])
    grad_ffn = grad_second.astype(BF16)
    vec_ref[0:1, :] = jnp.sum(cot * normed_two, 0, keepdims=True)
    vec_ref[1:2, :] = jnp.sum(cot, 0, keepdims=True)
    vec_ref[2:3, :] = jnp.sum(grad_ffn.astype(F32), 0, keepdims=True)
    acc_ref[...] = grad_second
    grad_turned = grad_ffn.T
    hidden_turned = hidden.T

    @pl.loop(0, shards)
    def _(shard):
        grad_act = nn(grad_ffn, down_ref[shard])
        grad_pre = (grad_act * slope_ref[shard].astype(F32)).astype(BF16)
        gdown_ref[shard] = nn(grad_turned, act_ref[shard]).astype(BF16)
        gup_ref[shard] = nn(hidden_turned, grad_pre).astype(BF16)
        gbias_ref[shard] = jnp.broadcast_to(
            jnp.sum(grad_pre.astype(F32), 0, keepdims=True), gbias_ref.shape[1:]
        )
        acc_ref[...] += nt(grad_pre, up_ref[shard])

    grad_hidden = acc_ref[...]
    grad_first = norm_back(grad_hidden, normed_one, scale_ref[:, 0:1], gain_one_ref[...])
    grad_low = grad_first.astype(BF16)
    first_ref[...] = grad_first
    low_ref[...] = grad_low
    vec_ref[3:4, :] = jnp.sum(grad_hidden * normed_one, 0, keepdims=True)
    vec_ref[4:5, :] = jnp.sum(grad_hidden, 0, keepdims=True)
    vec_ref[5:6, :] = jnp.sum(grad_low.astype(F32), 0, keepdims=True)
    vec_ref[6:8, :] = jnp.zeros((2, vec_ref.shape[1]), F32)


def out_back_phase(
    glow_ref, w_ref, low_ref, out_ref, denom_ref, qf_ref, gnum_ref, gden_ref, gw_ref, dnum_ref,
    dden_ref, total_ref, pairs, head_dim,
):
    rows_all = glow_ref.shape[0]
    blocks = rows_all // WINDOW
    half = LANES // 2
    ones = block_ones(LANES, head_dim).astype(BF16)
    grad_low = glow_ref[...]
    gw_ref[...] = tn(low_ref[...], grad_low)
    for pair in range(pairs):
        cols = slice(pair * LANES, (pair + 1) * LANES)
        grad_attn = nt(grad_low, w_ref[cols, :])
        inverse = 1.0 / denom_ref[:, cols]
        grad_num = (grad_attn * inverse).astype(BF16)
        grad_den = -head_sums(grad_num.astype(F32) * out_ref[:, cols], ones)
        gnum_ref[:, cols] = grad_num
        gden_ref[:, cols] = grad_den
        total = jnp.zeros((half, LANES), F32)
        total_den = jnp.zeros((1, LANES), F32)
        for block in range(blocks):
            rows = slice(block * WINDOW, (block + 1) * WINDOW)
            query = qf_ref[rows, cols]
            num = compact(tn(query, grad_num[rows]))
            den = jnp.sum(query.astype(F32) * grad_den[rows], 0, keepdims=True)
            dnum_ref[pair * blocks + block] = num
            dden_ref[pair * blocks + block : pair * blocks + block + 1, :] = den
            total = total + num
            total_den = total_den + den
        total_ref[pair * half : (pair + 1) * half, :] = total
        total_ref[pairs * half + pair : pairs * half + pair + 1, :] = total_den


def row_grads(keys, values, num, den, ones_f32):
    upper, lower = halves(expand(num, ones_f32))
    grad_keys = nt(values, upper) + nt(values, lower) + den
    grad_values = nn(keys, upper) + nn(keys, lower)
    return grad_keys, grad_values


def band_backward_phase(
    qf_ref, ke_ref, ve_ref, line_ref, gnum_ref, gden_ref, dnum_ref, dden_ref, left_ref, right_ref,
    left_den_ref, right_den_ref, gq_ref, gk_ref, gv_ref, gline_ref, coef_grad_ref, pairs, head_dim,
):
    blocks = qf_ref.shape[0] // WINDOW

    @pl.loop(0, pairs)
    def _(pair):
        ones_f32 = block_ones(LANES, head_dim)
        cols = lanes(pair)
        coef = coef_tile(line_ref, pair)
        left_coef, right_coef = far_coefs(line_ref, pair)
        gk_ref[:, cols] = jnp.zeros((gk_ref.shape[0], LANES), F32)
        gv_ref[:, cols] = jnp.zeros((gv_ref.shape[0], LANES), F32)
        coef_grad_ref[...] = jnp.zeros(coef_grad_ref.shape, F32)
        left_sum = jnp.zeros((1, LANES), F32)
        right_sum = jnp.zeros((1, LANES), F32)
        for block in range(blocks):
            rows = slice(block * WINDOW, (block + 1) * WINDOW)
            window = slice(block * WINDOW, (block + 3) * WINDOW)
            index = pair * blocks + block
            query = qf_ref[rows, cols]
            keys = ke_ref[window, cols]
            values = ve_ref[window, cols]
            grad_num = gnum_ref[rows, cols]
            grad_den = gden_ref[rows, cols]
            queries = both_heads(query)
            grads = both_heads(grad_num)
            weights = coef * nt(queries, keys)
            den_column = jnp.concatenate(
                [grad_den[:, 0:1], grad_den[:, LANES // 2 : LANES // 2 + 1]], 0
            )
            grad_weights = nt(grads, values) + den_column
            coef_grad_ref[...] += grad_weights * weights
            grad_scores = (coef * grad_weights).astype(BF16)
            gv_ref[window, cols] += tn(weights.astype(BF16), grads)
            gk_ref[window, cols] += tn(grad_scores, queries)
            grad_query = per_head(nn(grad_scores, keys))
            left, right = left_ref[index], right_ref[index]
            left_den = left_den_ref[pl.ds(index, 1), :]
            right_den = right_den_ref[pl.ds(index, 1), :]
            upper, lower = halves(expand(left_coef * left + right_coef * right, ones_f32))
            den_far = left_coef * left_den + right_coef * right_den
            grad_query = grad_query + nt(grad_num, upper) + nt(grad_num, lower) + grad_den * den_far
            gq_ref[rows, cols] = grad_query
            dnum = dnum_ref[index]
            dden = dden_ref[pl.ds(index, 1), :]
            left_sum = left_sum + jnp.sum(dnum * left, 0, keepdims=True) + dden * left_den
            right_sum = right_sum + jnp.sum(dnum * right, 0, keepdims=True) + dden * right_den
        for edge, block, scale in ((0, 0, left_coef), (blocks + 1, blocks - 1, right_coef)):
            rows = slice(edge * WINDOW, (edge + 1) * WINDOW)
            index = pair * blocks + block
            edge_k, edge_v = row_grads(
                ke_ref[rows, cols],
                ve_ref[rows, cols],
                scale * dnum_ref[index],
                scale * dden_ref[pl.ds(index, 1), :],
                ones_f32,
            )
            gk_ref[rows, cols] -= edge_k
            gv_ref[rows, cols] -= edge_v
        first = first_half((1, LANES))
        positions = lax.broadcasted_iota(jnp.int32, (1, LINE), 1)
        left_all = left_coef * left_sum
        right_all = right_coef * right_sum
        for head in range(2):
            keep = first if head == 0 else jnp.logical_not(first)
            left_one = jnp.sum(jnp.where(keep, left_all, 0.0), 1, keepdims=True)
            right_one = jnp.sum(jnp.where(keep, right_all, 0.0), 1, keepdims=True)
            line = unskew_sum(coef_grad_ref[head * WINDOW : (head + 1) * WINDOW, :])
            line = line + jnp.where(positions == 0, left_one, 0.0)
            line = line + jnp.where(positions == LINE - 2, right_one, 0.0)
            gline_ref[pl.ds(2 * pair + head, 1), :] = line


def key_back_phase(
    kf_ref, v_ref, line_ref, dnum_ref, dden_ref, past_ref, future_ref, low_in_ref, high_in_ref,
    gk_ref, gv_ref, pairs, head_dim,
):
    blocks = kf_ref.shape[0] // WINDOW
    half = LANES // 2

    @pl.loop(0, pairs)
    def _(pair):
        ones_f32 = block_ones(LANES, head_dim)
        cols = lanes(pair)
        left_coef, right_coef = far_coefs(line_ref, pair)
        state_rows = pl.ds(pl.multiple_of(pair * half, half), half)
        den_row = pl.ds(pairs * half + pair, 1)
        nums = [dnum_ref[pair * blocks + block] for block in range(blocks)]
        dens = [dden_ref[pl.ds(pair * blocks + block, 1), :] for block in range(blocks)]
        for block in range(blocks):
            num_left, den_left = future_ref[state_rows, :], future_ref[den_row, :]
            num_right, den_right = past_ref[state_rows, :], past_ref[den_row, :]
            for other in range(blocks):
                if other >= block + 2:
                    num_left, den_left = num_left + nums[other], den_left + dens[other]
                if other <= block - 2:
                    num_right, den_right = num_right + nums[other], den_right + dens[other]
            rows = slice(block * WINDOW, (block + 1) * WINDOW)
            outer = slice((block + 1) * WINDOW, (block + 2) * WINDOW)
            far_k, far_v = row_grads(
                kf_ref[rows, cols],
                v_ref[rows, cols],
                left_coef * num_left + right_coef * num_right,
                left_coef * den_left + right_coef * den_right,
                ones_f32,
            )
            if block == 0:
                far_k = far_k + low_in_ref[0, :, cols].astype(F32)
                far_v = far_v + low_in_ref[1, :, cols].astype(F32)
            if block == blocks - 1:
                far_k = far_k + high_in_ref[0, :, cols].astype(F32)
                far_v = far_v + high_in_ref[1, :, cols].astype(F32)
            gk_ref[outer, cols] += far_k
            gv_ref[outer, cols] += far_v


def qkv_back_phase(
    x_ref, w_ref, omega_ref, q_ref, k_ref, qf_ref, kf_ref, gq_ref, gk_ref, gv_ref, first_ref,
    gqkv_ref, gtok_ref, gw_ref, gb_ref, head_dim,
):
    rows_all, width = x_ref.shape
    own = slice(WINDOW, WINDOW + rows_all)
    ones = block_ones(CHUNK, head_dim).astype(BF16)
    factor = head_dim ** (-0.25) / SPREAD
    for part, low_ref, feat_ref, grad_ref in (
        (0, q_ref, qf_ref, gq_ref), (1, k_ref, kf_ref, gk_ref), (2, None, None, gv_ref),
    ):
        rows = slice(0, rows_all) if part == 0 else own
        for chunk in range(width // CHUNK):
            cols = slice(chunk * CHUNK, (chunk + 1) * CHUNK)
            wide = slice(part * width + chunk * CHUNK, part * width + (chunk + 1) * CHUNK)
            grad = grad_ref[rows, cols]
            if part < 2:
                inner_up, inner_low = halves(grad * feat_ref[:, cols].astype(F32))
                omega = omega_ref[chunk]
                projected = (nt(inner_up, omega) + nt(inner_low, omega)) * factor
                sums = nn(inner_up, ones) + nn(inner_low, ones)
                grad = projected - sums * head_dim ** (-0.5) * low_ref[:, cols].astype(F32)
            gqkv_ref[:, wide] = grad.astype(BF16)
    gb_ref[...] = jnp.zeros(gb_ref.shape, F32)
    turned = x_ref[...].T
    total = first_ref[...]
    for chunk in range(3 * width // CHUNK):
        wide = slice(chunk * CHUNK, (chunk + 1) * CHUNK)
        grad = gqkv_ref[:, wide]
        gb_ref[0:1, wide] = jnp.sum(grad.astype(F32), 0, keepdims=True)
        gw_ref[:, wide] = nn(turned, grad)
        total = total + nt(grad, w_ref[:, wide])
    gtok_ref[...] = total


def table_phase(gline_ref, bucket_ref, gtable_ref):
    buckets = gtable_ref.shape[1]
    one_hot = jnp.where(
        lax.broadcasted_iota(jnp.int32, (buckets, LINE), 0) == bucket_ref[...], 1.0, 0.0
    )
    gtable_ref[...] = lax.dot_general(
        gline_ref[...],
        one_hot,
        (((1,), (1,)), ((), ())),
        precision=lax.Precision.HIGHEST,
        preferred_element_type=F32,
    )


def call(body, outs, operands, scratch=(), limit=60):
    return pl.pallas_call(
        body,
        out_shape=[jax.ShapeDtypeStruct(shape, dtype) for shape, dtype in outs],
        in_specs=[pl.BlockSpec(memory_space=pltpu.VMEM)] * len(operands),
        out_specs=[pl.BlockSpec(memory_space=pltpu.VMEM)] * len(outs),
        scratch_shapes=list(scratch),
        compiler_params=pltpu.CompilerParams(vmem_limit_bytes=limit * MIB),
    )(*operands)


def shards(
    tokens, cotangent, w_qkv, b_qkv, w_out, b_out, gain_one, shift_one, w_up, b_up, w_down, b_down,
    gain_two, shift_two, feature_codes, bias_table, offset_bucket,
):
    rows, width = tokens.shape[1:]
    heads, head_dim, feats = feature_codes.shape
    buckets = bias_table.shape[1]
    pairs = heads // 2
    blocks = rows // WINDOW
    half = LANES // 2
    hidden_units = w_up.shape[1]
    length = (offset_bucket.shape[0] + 1) // 2
    count = lax.axis_size("seq")
    x = tokens[0]
    omega_int = (feature_codes.astype(F32) - CENTER).astype(BF16)
    group = CHUNK // head_dim
    eye = jnp.eye(group, dtype=BF16)
    omega = (
        omega_int.reshape(heads // group, group, head_dim, 1, feats)
        * eye[None, :, None, :, None]
    ).reshape(heads // group, CHUNK, CHUNK)
    bucket_line = offset_bucket[length - LINE // 2 : length + LINE // 2][None]
    state = (pairs * half + 8, LANES)
    stacked = (pairs * blocks, half, LANES)
    flat = (pairs * blocks, LANES)
    wide = (rows, width)

    def body_one(x_r, w_r, b_r, o_r, bu_r, ta_r, q_r, k_r, v_r, qf_r, kf_r, line_r, num_r, den_r, tot_r):
        qkv_phase(x_r, w_r, b_r, o_r, q_r, k_r, v_r, qf_r, kf_r, head_dim)
        line_phase(bu_r, ta_r, line_r)
        state_phase(kf_r, v_r, num_r, den_r, tot_r, pairs)

    q, k, v, qf, kf, line, num, den, total = call(
        body_one,
        [(wide, BF16)] * 5
        + [((heads, LINE), F32), (stacked, F32), (flat, F32), (state, F32)],
        (x, w_qkv, b_qkv[None], omega, bucket_line, bias_table),
    )
    up_all = lax.all_gather(w_up, "seq", axis=0)
    down_all = lax.all_gather(jnp.transpose(w_down), "seq", axis=0)
    b_up_all = jnp.broadcast_to(lax.all_gather(b_up, "seq", axis=0)[:, None, :], (count, 8, hidden_units))

    def halo(block):
        forward = [(i, i + 1) for i in range(count - 1)]
        backward = [(target, source) for source, target in forward]
        low = lax.ppermute(block[rows - WINDOW :], "seq", forward)
        high = lax.ppermute(block[:WINDOW], "seq", backward)
        return jnp.concatenate([low, block, high], 0)

    me = lax.axis_index("seq")
    ids = jnp.arange(count)

    def prefix(message):
        every = lax.all_gather(message, "seq", axis=0)
        before = jnp.sum(jnp.where((ids < me)[:, None, None], every, 0.0), 0)
        after = jnp.sum(jnp.where((ids > me)[:, None, None], every, 0.0), 0)
        return before, after

    ke, ve = halo(kf), halo(v)
    before, after = prefix(total)

    def body_two(*refs):
        ins, outs = refs[:12], refs[12:]
        qf_r, ke_r, ve_r, line_r, num_r, den_r, bef_r, aft_r, x_r, w_r, b_r, _ = ins
        out_r, low_r, dnm_r, l_r, r_r, ld_r, rd_r, nrm_r, sc_r = outs
        band_forward_phase(
            qf_r, ke_r, ve_r, line_r, num_r, den_r, bef_r, aft_r,
            out_r, low_r, dnm_r, l_r, r_r, ld_r, rd_r, pairs, head_dim,
        )
        out_phase(x_r, low_r, w_r, b_r, nrm_r, sc_r)

    attn, attn_low, denom, left, right, left_den, right_den, normed, scale = call(
        body_two,
        [(wide, F32), (wide, BF16), (wide, F32), (stacked, F32), (stacked, F32), (flat, F32),
         (flat, F32), (wide, F32), ((rows, LANES), F32)],
        (qf, ke, ve, line, num, den, before, after, x, w_out, b_out[None], gain_one[None]),
    )
    layer, first, first_low, vec, gup, gdown, gbias = call(
        ffn_phase,
        [(wide, BF16), (wide, F32), (wide, BF16), ((8, width), F32),
         ((count, width, hidden_units), BF16), ((count, width, hidden_units), BF16),
         ((count, 8, hidden_units), F32)],
        (normed, scale, gain_one[None], shift_one[None], up_all, b_up_all, down_all, b_down[None],
         gain_two[None], shift_two[None], cotangent[0]),
        (pltpu.VMEM((count, rows, hidden_units), BF16), pltpu.VMEM((count, rows, hidden_units), BF16),
         pltpu.VMEM(wide, F32)),
    )

    def reduced(part):
        return lax.psum(lax.psum_scatter(part, "seq", scatter_dimension=0), "row").astype(F32)

    grad_w_up = reduced(gup)
    grad_w_down = jnp.transpose(reduced(gdown))
    grad_b_up = reduced(gbias[:, 0])
    ext = (rows + 2 * WINDOW, width)

    def body_four(*refs):
        (gl_r, w_r, lo_r, ou_r, dn_r, qf_r, ke_r, ve_r, li_r, l_r, r_r, ld_r, rd_r, bu_r) = refs[:14]
        gw_r, gq_r, gk_r, gv_r, dnum_r, dden_r, tot_r, gt_r, gnum_r, gden_r, gline_r, cg_r = refs[14:]
        out_back_phase(
            gl_r, w_r, lo_r, ou_r, dn_r, qf_r, gnum_r, gden_r, gw_r, dnum_r, dden_r, tot_r, pairs, head_dim
        )
        band_backward_phase(
            qf_r, ke_r, ve_r, li_r, gnum_r, gden_r, dnum_r, dden_r, l_r, r_r, ld_r, rd_r,
            gq_r, gk_r, gv_r, gline_r, cg_r, pairs, head_dim,
        )
        table_phase(gline_r, bu_r, gt_r)

    gw_out, gq, gk, gv, dnum, dden, gtotal, gtable = call(
        body_four,
        [((width, width), F32), (wide, F32), (ext, F32), (ext, F32), (stacked, F32), (flat, F32),
         (state, F32), (bias_table.shape, F32)],
        (first_low, w_out, attn_low, attn, denom, qf, ke, ve, line, left, right, left_den, right_den,
         bucket_line),
        (pltpu.VMEM(wide, BF16), pltpu.VMEM(wide, F32), pltpu.VMEM((heads, LINE), F32),
         pltpu.VMEM((2 * WINDOW, 3 * WINDOW), F32)),
    )
    past, future = prefix(gtotal)
    forward = [(i, i + 1) for i in range(count - 1)]
    backward = [(target, source) for source, target in forward]
    to_left = jnp.stack([gk[:WINDOW], gv[:WINDOW]]).astype(BF16)
    to_right = jnp.stack([gk[rows + WINDOW :], gv[rows + WINDOW :]]).astype(BF16)
    low_in = lax.ppermute(to_right, "seq", forward)
    high_in = lax.ppermute(to_left, "seq", backward)

    def body_five(*refs):
        (x_r, w_r, o_r, q_r, k_r, v_r, qf_r, kf_r, li_r, dn_r, dd_r, pa_r, fu_r, lo_r, hi_r, gq_r,
         gki_r, gvi_r, fi_r) = refs[:19]
        gt_r, gw_r, gb_r, gqkv_r, gk_r, gv_r = refs[19:]
        gk_r[...] = gki_r[...]
        gv_r[...] = gvi_r[...]
        key_back_phase(
            kf_r, v_r, li_r, dn_r, dd_r, pa_r, fu_r, lo_r, hi_r, gk_r, gv_r, pairs, head_dim
        )
        qkv_back_phase(
            x_r, w_r, o_r, q_r, k_r, qf_r, kf_r, gq_r, gk_r, gv_r, fi_r, gqkv_r, gt_r, gw_r, gb_r,
            head_dim,
        )

    gtok, gw_qkv, gb_qkv = call(
        body_five,
        [(wide, F32), ((width, 3 * width), F32), ((8, 3 * width), F32)],
        (x, w_qkv, omega, q, k, v, qf, kf, line, dnum, dden, past, future, low_in, high_in, gq, gk, gv,
         first),
        (pltpu.VMEM((rows, 3 * width), BF16), pltpu.VMEM(ext, F32), pltpu.VMEM(ext, F32)),
    )
    summed = lax.psum((gw_qkv, gb_qkv[0], gw_out, vec, gtable), ("row", "seq"))
    gw_qkv, gb_qkv, gw_out, vec, gtable = summed
    return (
        layer[None], gtok[None], gw_qkv, gb_qkv, gw_out, vec[5], vec[3], vec[4], grad_w_up, grad_b_up,
        grad_w_down, vec[2], vec[0], vec[1], gtable,
    )


def solution(mesh):
    placed = (
        P("row", "seq", None), P("row", "seq", None), P(), P(), P(), P(), P(), P(), P(None, "seq"),
        P("seq"), P("seq", None), P(), P(), P(), P(), P(), P(),
    )
    return jax.shard_map(
        shards,
        mesh=mesh,
        in_specs=placed,
        out_specs=(
            P("row", "seq", None), P("row", "seq", None), P(), P(), P(), P(), P(), P(), P(None, "seq"),
            P("seq"), P("seq", None), P(), P(), P(), P(),
        ),
        check_vma=False,
    )
```

```python
import functools
import math

import jax
import jax.numpy as jnp
from jax import lax
from jax.experimental import pallas as pl
from jax.experimental.pallas import tpu as pltpu
from jax.sharding import PartitionSpec as P

WINDOW = 128
LANES = 128
LINE = 512
CHUNK = 256
EPS = 1e-06
CENTER = 7.5
SPREAD = math.sqrt(21.25)
ROOT_HALF = 0.7071067811865476
INV_ROOT_TAU = 0.3989422804014327
MIB = 1 << 20
F32 = jnp.float32
BF16 = jnp.bfloat16


def nn(a, b):
    return lax.dot_general(a, b, (((1,), (0,)), ((), ())), preferred_element_type=F32)


def nt(a, b):
    return lax.dot_general(a, b, (((1,), (1,)), ((), ())), preferred_element_type=F32)


def tn(a, b):
    return lax.dot_general(a, b, (((0,), (0,)), ((), ())), preferred_element_type=F32)


def halves(values):
    upper = values.astype(BF16)
    return upper, (values - upper.astype(F32)).astype(BF16)


def block_ones(size, head_dim):
    rows = lax.broadcasted_iota(jnp.int32, (size, size), 0) // head_dim
    cols = lax.broadcasted_iota(jnp.int32, (size, size), 1) // head_dim
    return jnp.where(rows == cols, 1.0, 0.0)


def head_sums(values, ones):
    upper, lower = halves(values)
    return nn(upper, ones) + nn(lower, ones)


def first_half(shape):
    return lax.broadcasted_iota(jnp.int32, shape, len(shape) - 1) < LANES // 2


def both_heads(pair):
    first = first_half((1, LANES))
    mask_a = jnp.where(first, 1.0, 0.0).astype(pair.dtype)
    mask_b = jnp.where(first, 0.0, 1.0).astype(pair.dtype)
    return jnp.concatenate([pair * mask_a, pair * mask_b], 0)


def per_head(stacked):
    rows = stacked.shape[0] // 2
    return jnp.where(first_half((rows, LANES)), stacked[:rows], stacked[rows:])


def compact(full):
    half = LANES // 2
    return jnp.where(first_half((half, LANES)), full[:half], full[half:])


def expand(small, ones):
    return jnp.concatenate([small, small], 0) * ones


def block_state(keys, values):
    return compact(tn(keys, values)), jnp.sum(keys.astype(F32), 0, keepdims=True)


def coef_tile(line_ref, pair):
    tiles = []
    for head in range(2):
        row = line_ref[pl.ds(2 * pair + head, 1), :]
        wide = pltpu.roll(
            jnp.broadcast_to(row, (WINDOW, LINE)), LINE - WINDOW + 1, 1, stride=1, stride_axis=0
        )
        tiles.append(wide[:, : 3 * WINDOW])
    return jnp.concatenate(tiles, 0)


def far_coefs(line_ref, pair):
    first = first_half((1, LANES))
    row_a = line_ref[pl.ds(2 * pair, 1), :]
    row_b = line_ref[pl.ds(2 * pair + 1, 1), :]
    left = jnp.where(first, row_a[:, 0:1], row_b[:, 0:1])
    right = jnp.where(first, row_a[:, LINE - 2 : LINE - 1], row_b[:, LINE - 2 : LINE - 1])
    return left, right


def unskew_sum(tile):
    rows = tile.shape[0]
    padded = jnp.concatenate([tile, jnp.zeros((rows, LINE - tile.shape[1]), F32)], 1)
    while rows > 8:
        rows = rows // 2
        padded = pltpu.roll(padded[:rows], rows, 1) + padded[rows:]
    while rows > 1:
        rows = rows // 2
        padded = pltpu.roll(padded[:rows], rows, 1) + padded[rows:]
    return padded


def lanes(pair):
    return pl.ds(pl.multiple_of(pair * LANES, LANES), LANES)


def qkv_phase(x_ref, w_ref, b_ref, omega_ref, parts, head_dim):
    width = x_ref.shape[1]
    x = x_ref[...]
    ones = block_ones(CHUNK, head_dim).astype(BF16)
    factor = head_dim ** (-0.25) / SPREAD
    for part, low_ref, feat_ref in parts:
        for chunk in range(width // CHUNK):
            cols = slice(chunk * CHUNK, (chunk + 1) * CHUNK)
            wide = slice(part * width + chunk * CHUNK, part * width + (chunk + 1) * CHUNK)
            low = (nn(x, w_ref[:, wide]) + b_ref[:, wide].astype(F32)).astype(BF16)
            low_ref[:, cols] = low
            if feat_ref is not None:
                projected = nn(low, omega_ref[chunk]) * factor
                widened = low.astype(F32)
                half_norm = head_sums(widened * widened, ones) * (0.5 * head_dim ** (-0.5))
                feat_ref[:, cols] = (
                    jnp.exp(projected - half_norm) * head_dim ** (-0.5)
                ).astype(BF16)


def line_phase(bucket_ref, table_ref, line_ref):
    buckets = table_ref.shape[1]
    one_hot = jnp.where(
        lax.broadcasted_iota(jnp.int32, (buckets, LINE), 0) == bucket_ref[...], 1.0, 0.0
    )
    logs = lax.dot_general(
        table_ref[...],
        one_hot,
        (((1,), (0,)), ((), ())),
        precision=lax.Precision.HIGHEST,
        preferred_element_type=F32,
    )
    line_ref[...] = jnp.exp(logs)


def state_phase(kf_ref, v_ref, num_ref, den_ref, total_ref, pairs):
    blocks = kf_ref.shape[0] // WINDOW
    half = LANES // 2

    @pl.loop(0, pairs)
    def _(pair):
        total = jnp.zeros((half, LANES), F32)
        total_den = jnp.zeros((1, LANES), F32)
        for block in range(blocks):
            rows = slice(block * WINDOW, (block + 1) * WINDOW)
            num, den = block_state(kf_ref[rows, lanes(pair)], v_ref[rows, lanes(pair)])
            num_ref[pair * blocks + block] = num
            den_ref[pl.ds(pair * blocks + block, 1), :] = den
            total = total + num
            total_den = total_den + den
        total_ref[pl.ds(pl.multiple_of(pair * half, half), half), :] = total
        total_ref[pl.ds(pairs * half + pair, 1), :] = total_den


def band_forward_phase(qf_ref, ke_ref, ve_ref, line_ref, out_ref, denom_ref, first, last):
    blocks = qf_ref.shape[0] // WINDOW

    @pl.loop(first, last)
    def _(pair):
        cols = lanes(pair)
        coef = coef_tile(line_ref, pair)
        for block in range(blocks):
            rows = slice(block * WINDOW, (block + 1) * WINDOW)
            window = slice(block * WINDOW, (block + 3) * WINDOW)
            scores = nt(both_heads(qf_ref[rows, cols]), ke_ref[window, cols])
            weights = (coef * scores).astype(BF16)
            values = ve_ref[window, cols]
            summed = nn(weights, jnp.concatenate([values, jnp.ones_like(values)], 1))
            out_ref[rows, cols] = per_head(summed[:, :LANES])
            denom_ref[rows, cols] = per_head(summed[:, LANES:])


def far_forward_phase(
    qf_ref, ke_ref, ve_ref, line_ref, num_ref, den_ref, before_ref, after_ref,
    out_ref, low_ref, denom_ref, left_ref, right_ref, left_den_ref, right_den_ref, pairs, head_dim,
):
    blocks = qf_ref.shape[0] // WINDOW
    half = LANES // 2

    @pl.loop(0, pairs)
    def _(pair):
        ones_f32 = block_ones(LANES, head_dim)
        ones = ones_f32.astype(BF16)
        cols = lanes(pair)
        left_coef, right_coef = far_coefs(line_ref, pair)
        state_rows = pl.ds(pl.multiple_of(pair * half, half), half)
        den_row = pl.ds(pairs * half + pair, 1)
        edge_low = block_state(ke_ref[:WINDOW, cols], ve_ref[:WINDOW, cols])
        edge_high = block_state(
            ke_ref[(blocks + 1) * WINDOW :, cols], ve_ref[(blocks + 1) * WINDOW :, cols]
        )
        past = (before_ref[state_rows, :], before_ref[den_row, :])
        future = (after_ref[state_rows, :], after_ref[den_row, :])

        def block_of(block):
            index = pair * blocks + block
            return num_ref[index], den_ref[pl.ds(index, 1), :]

        def add(one, two, sign=1.0):
            return tuple(a + sign * b for a, b in zip(one, two))

        lefts = [add(past, edge_low, -1.0), past]
        for block in range(2, blocks):
            lefts.append(add(lefts[-1], block_of(block - 2)))
        rights = [add(future, edge_high, -1.0), future]
        for block in range(2, blocks):
            rights.append(add(rights[-1], block_of(blocks + 1 - block)))
        rights = rights[::-1]
        for block in range(blocks):
            rows = slice(block * WINDOW, (block + 1) * WINDOW)
            index = pair * blocks + block
            query = qf_ref[rows, cols]
            left, left_den = lefts[block]
            right, right_den = rights[block]
            left_ref[index] = left
            right_ref[index] = right
            left_den_ref[pl.ds(index, 1), :] = left_den
            right_den_ref[pl.ds(index, 1), :] = right_den
            upper, lower = halves(expand(left_coef * left + right_coef * right, ones_f32))
            numer = out_ref[rows, cols] + nn(query, upper) + nn(query, lower)
            den_far = left_coef * left_den + right_coef * right_den
            denom = denom_ref[rows, cols] + head_sums(query.astype(F32) * den_far, ones)
            out = numer / denom
            out_ref[rows, cols] = out
            low_ref[rows, cols] = out.astype(BF16)
            denom_ref[rows, cols] = denom


def norm_parts(values):
    center = values - jnp.mean(values, -1, keepdims=True)
    inv_scale = lax.rsqrt(jnp.mean(center * center, -1, keepdims=True) + EPS)
    return center * inv_scale, inv_scale


def out_phase(x_ref, low_ref, w_ref, b_ref, normed_ref, scale_ref):
    first_sum = x_ref[...].astype(F32) + nn(low_ref[...], w_ref[...]) + b_ref[...].astype(F32)
    normed, inv_scale = norm_parts(first_sum)
    normed_ref[...] = normed
    scale_ref[...] = jnp.broadcast_to(inv_scale, scale_ref.shape)


def norm_back(grad_out, normed, inv_scale, gain):
    grad_normed = grad_out * gain
    centered = grad_normed - jnp.mean(grad_normed, -1, keepdims=True)
    return inv_scale * (centered - normed * jnp.mean(grad_normed * normed, -1, keepdims=True))


def ffn_phase(
    normed_ref, scale_ref, gain_one_ref, shift_one_ref, up_ref, b_up_ref, down_ref, b_down_ref,
    gain_two_ref, shift_two_ref, cot_ref, layer_ref, first_ref, low_ref, vec_ref, gup_ref, gdown_ref,
    gbias_ref, act_ref, slope_ref, acc_ref,
):
    shards = up_ref.shape[0]
    normed_one = normed_ref[...]
    hidden_one = normed_one * gain_one_ref[...] + shift_one_ref[...]
    hidden = hidden_one.astype(BF16)
    acc_ref[...] = hidden_one + b_down_ref[...].astype(F32)

    @pl.loop(0, shards)
    def _(shard):
        pre = nn(hidden, up_ref[shard]) + b_up_ref[shard, 0:1, :].astype(F32)
        phi = 0.5 * (1.0 + lax.erf(pre * ROOT_HALF))
        act = (pre * phi).astype(BF16)
        act_ref[shard] = act
        slope_ref[shard] = (phi + pre * INV_ROOT_TAU * jnp.exp(-0.5 * pre * pre)).astype(BF16)
        acc_ref[...] += nt(act, down_ref[shard])

    normed_two, scale_two = norm_parts(acc_ref[...])
    layer_ref[...] = (normed_two * gain_two_ref[...] + shift_two_ref[...]).astype(BF16)
    cot = cot_ref[...].astype(F32)
    grad_second = norm_back(cot, normed_two, scale_two, gain_two_ref[...])
    grad_ffn = grad_second.astype(BF16)
    vec_ref[0:1, :] = jnp.sum(cot * normed_two, 0, keepdims=True)
    vec_ref[1:2, :] = jnp.sum(cot, 0, keepdims=True)
    vec_ref[2:3, :] = jnp.sum(grad_ffn.astype(F32), 0, keepdims=True)
    acc_ref[...] = grad_second
    grad_turned = grad_ffn.T
    hidden_turned = hidden.T

    @pl.loop(0, shards)
    def _(shard):
        grad_act = nn(grad_ffn, down_ref[shard])
        grad_pre = (grad_act * slope_ref[shard].astype(F32)).astype(BF16)
        gdown_ref[shard] = nn(grad_turned, act_ref[shard]).astype(BF16)
        gup_ref[shard] = nn(hidden_turned, grad_pre).astype(BF16)
        gbias_ref[shard] = jnp.broadcast_to(
            jnp.sum(grad_pre.astype(F32), 0, keepdims=True), gbias_ref.shape[1:]
        )
        acc_ref[...] += nt(grad_pre, up_ref[shard])

    grad_hidden = acc_ref[...]
    grad_first = norm_back(grad_hidden, normed_one, scale_ref[:, 0:1], gain_one_ref[...])
    grad_low = grad_first.astype(BF16)
    first_ref[...] = grad_first
    low_ref[...] = grad_low
    vec_ref[3:4, :] = jnp.sum(grad_hidden * normed_one, 0, keepdims=True)
    vec_ref[4:5, :] = jnp.sum(grad_hidden, 0, keepdims=True)
    vec_ref[5:6, :] = jnp.sum(grad_low.astype(F32), 0, keepdims=True)
    vec_ref[6:8, :] = jnp.zeros((2, vec_ref.shape[1]), F32)


def out_back_phase(
    glow_ref, w_ref, low_ref, out_ref, denom_ref, qf_ref, gnum_ref, gden_ref, gw_ref, dnum_ref,
    dden_ref, total_ref, pairs, head_dim,
):
    rows_all = glow_ref.shape[0]
    blocks = rows_all // WINDOW
    half = LANES // 2
    ones = block_ones(LANES, head_dim).astype(BF16)
    grad_low = glow_ref[...]
    gw_ref[...] = tn(low_ref[...], grad_low).astype(gw_ref.dtype)
    for pair in range(pairs):
        cols = slice(pair * LANES, (pair + 1) * LANES)
        grad_attn = nt(grad_low, w_ref[cols, :])
        inverse = 1.0 / denom_ref[:, cols]
        grad_num = (grad_attn * inverse).astype(BF16)
        grad_den = -head_sums(grad_num.astype(F32) * out_ref[:, cols], ones)
        gnum_ref[:, cols] = grad_num
        gden_ref[:, cols] = grad_den
        total = jnp.zeros((half, LANES), F32)
        total_den = jnp.zeros((1, LANES), F32)
        for block in range(blocks):
            rows = slice(block * WINDOW, (block + 1) * WINDOW)
            query = qf_ref[rows, cols]
            num = compact(tn(query, grad_num[rows]))
            den = jnp.sum(query.astype(F32) * grad_den[rows], 0, keepdims=True)
            dnum_ref[pair * blocks + block] = num
            dden_ref[pair * blocks + block : pair * blocks + block + 1, :] = den
            total = total + num
            total_den = total_den + den
        total_ref[pair * half : (pair + 1) * half, :] = total
        total_ref[pairs * half + pair : pairs * half + pair + 1, :] = total_den


def row_grads(keys, values, num, den, ones_f32):
    upper, lower = halves(expand(num, ones_f32))
    grad_keys = nt(values, upper) + nt(values, lower) + den
    grad_values = nn(keys, upper) + nn(keys, lower)
    return grad_keys, grad_values


def band_backward_phase(
    qf_ref, ke_ref, ve_ref, line_ref, gnum_ref, gden_ref, dnum_ref, dden_ref, left_ref, right_ref,
    left_den_ref, right_den_ref, gq_ref, gk_ref, gv_ref, gline_ref, coef_grad_ref, start, stop, head_dim,
):
    blocks = qf_ref.shape[0] // WINDOW

    @pl.loop(start, stop)
    def _(pair):
        ones_f32 = block_ones(LANES, head_dim)
        cols = lanes(pair)
        coef = coef_tile(line_ref, pair)
        left_coef, right_coef = far_coefs(line_ref, pair)
        gk_ref[:, cols] = jnp.zeros((gk_ref.shape[0], LANES), F32)
        gv_ref[:, cols] = jnp.zeros((gv_ref.shape[0], LANES), F32)
        coef_grad_ref[...] = jnp.zeros(coef_grad_ref.shape, F32)
        left_sum = jnp.zeros((1, LANES), F32)
        right_sum = jnp.zeros((1, LANES), F32)
        for block in range(blocks):
            rows = slice(block * WINDOW, (block + 1) * WINDOW)
            window = slice(block * WINDOW, (block + 3) * WINDOW)
            index = pair * blocks + block
            query = qf_ref[rows, cols]
            keys = ke_ref[window, cols]
            values = ve_ref[window, cols]
            grad_num = gnum_ref[rows, cols]
            grad_den = gden_ref[rows, cols]
            queries = both_heads(query)
            grads = both_heads(grad_num)
            weights = coef * nt(queries, keys)
            den_column = jnp.concatenate(
                [grad_den[:, 0:1], grad_den[:, LANES // 2 : LANES // 2 + 1]], 0
            )
            grad_weights = nt(grads, values) + den_column
            coef_grad_ref[...] += grad_weights * weights
            grad_scores = (coef * grad_weights).astype(BF16)
            gv_ref[window, cols] += tn(weights.astype(BF16), grads)
            gk_ref[window, cols] += tn(grad_scores, queries)
            grad_query = per_head(nn(grad_scores, keys))
            left, right = left_ref[index], right_ref[index]
            left_den = left_den_ref[pl.ds(index, 1), :]
            right_den = right_den_ref[pl.ds(index, 1), :]
            upper, lower = halves(expand(left_coef * left + right_coef * right, ones_f32))
            den_far = left_coef * left_den + right_coef * right_den
            grad_query = grad_query + nt(grad_num, upper) + nt(grad_num, lower) + grad_den * den_far
            gq_ref[rows, cols] = grad_query
            dnum = dnum_ref[index]
            dden = dden_ref[pl.ds(index, 1), :]
            left_sum = left_sum + jnp.sum(dnum * left, 0, keepdims=True) + dden * left_den
            right_sum = right_sum + jnp.sum(dnum * right, 0, keepdims=True) + dden * right_den
        for edge, block, scale in ((0, 0, left_coef), (blocks + 1, blocks - 1, right_coef)):
            rows = slice(edge * WINDOW, (edge + 1) * WINDOW)
            index = pair * blocks + block
            edge_k, edge_v = row_grads(
                ke_ref[rows, cols],
                ve_ref[rows, cols],
                scale * dnum_ref[index],
                scale * dden_ref[pl.ds(index, 1), :],
                ones_f32,
            )
            gk_ref[rows, cols] -= edge_k
            gv_ref[rows, cols] -= edge_v
        first = first_half((1, LANES))
        positions = lax.broadcasted_iota(jnp.int32, (1, LINE), 1)
        left_all = left_coef * left_sum
        right_all = right_coef * right_sum
        for head in range(2):
            keep = first if head == 0 else jnp.logical_not(first)
            left_one = jnp.sum(jnp.where(keep, left_all, 0.0), 1, keepdims=True)
            right_one = jnp.sum(jnp.where(keep, right_all, 0.0), 1, keepdims=True)
            line = unskew_sum(coef_grad_ref[head * WINDOW : (head + 1) * WINDOW, :])
            line = line + jnp.where(positions == 0, left_one, 0.0)
            line = line + jnp.where(positions == LINE - 2, right_one, 0.0)
            gline_ref[pl.ds(2 * pair + head, 1), :] = line


def key_back_phase(
    kf_ref, v_ref, line_ref, dnum_ref, dden_ref, past_ref, future_ref, low_in_ref, high_in_ref,
    gk_ref, gv_ref, pairs, start, stop, head_dim,
):
    blocks = kf_ref.shape[0] // WINDOW
    half = LANES // 2

    @pl.loop(start, stop)
    def _(pair):
        ones_f32 = block_ones(LANES, head_dim)
        cols = lanes(pair)
        left_coef, right_coef = far_coefs(line_ref, pair)
        state_rows = pl.ds(pl.multiple_of(pair * half, half), half)
        den_row = pl.ds(pairs * half + pair, 1)
        nums = [dnum_ref[pair * blocks + block] for block in range(blocks)]
        dens = [dden_ref[pl.ds(pair * blocks + block, 1), :] for block in range(blocks)]
        for block in range(blocks):
            num_left, den_left = future_ref[state_rows, :], future_ref[den_row, :]
            num_right, den_right = past_ref[state_rows, :], past_ref[den_row, :]
            for other in range(blocks):
                if other >= block + 2:
                    num_left, den_left = num_left + nums[other], den_left + dens[other]
                if other <= block - 2:
                    num_right, den_right = num_right + nums[other], den_right + dens[other]
            rows = slice(block * WINDOW, (block + 1) * WINDOW)
            outer = slice((block + 1) * WINDOW, (block + 2) * WINDOW)
            far_k, far_v = row_grads(
                kf_ref[rows, cols],
                v_ref[rows, cols],
                left_coef * num_left + right_coef * num_right,
                left_coef * den_left + right_coef * den_right,
                ones_f32,
            )
            if block == 0:
                far_k = far_k + low_in_ref[0, :, cols].astype(F32)
                far_v = far_v + low_in_ref[1, :, cols].astype(F32)
            if block == blocks - 1:
                far_k = far_k + high_in_ref[0, :, cols].astype(F32)
                far_v = far_v + high_in_ref[1, :, cols].astype(F32)
            gk_ref[outer, cols] += far_k
            gv_ref[outer, cols] += far_v


def qkv_back_phase(
    turned_ref, w_ref, omega_ref, q_ref, k_ref, qf_ref, kf_ref, gq_ref, gk_ref, gv_ref, gtok_ref, parts_ref,
    small_ref, group, head_dim,
):
    width, rows_all = turned_ref.shape
    own = slice(WINDOW, WINDOW + rows_all)
    ones = block_ones(CHUNK, head_dim).astype(BF16)
    factor = head_dim ** (-0.25) / SPREAD
    cols = slice(group * CHUNK, (group + 1) * CHUNK)
    omega = omega_ref[group]
    lows = []
    total = gtok_ref[...]
    for part, low_ref, feat_ref, grad in (
        (0, q_ref, qf_ref, gq_ref[:, cols]), (1, k_ref, kf_ref, gk_ref[own, cols]), (2, None, None, gv_ref[own, cols]),
    ):
        if part < 2:
            inner_up, inner_low = halves(grad * feat_ref[:, cols].astype(F32))
            projected = (nt(inner_up, omega) + nt(inner_low, omega)) * factor
            sums = nn(inner_up, ones) + nn(inner_low, ones)
            grad = projected - sums * head_dim ** (-0.5) * low_ref[:, cols].astype(F32)
        low = grad.astype(BF16)
        lows.append(low)
        total = total + nt(low, w_ref[:, part * width + group * CHUNK : part * width + (group + 1) * CHUNK])
    gtok_ref[...] = total
    joined = jnp.concatenate(lows, 1)
    small_ref[8 + group : 9 + group, :] = jnp.sum(joined.astype(F32), 0, keepdims=True)
    parts_ref[:, (group + 1) * width : (group + 2) * width] = nn(turned_ref[...], joined).astype(parts_ref.dtype)


def table_phase(gline_ref, bucket_ref, buckets):
    one_hot = jnp.where(
        lax.broadcasted_iota(jnp.int32, (buckets, LINE), 0) == bucket_ref[...], 1.0, 0.0
    )
    return lax.dot_general(
        gline_ref[...],
        one_hot,
        (((1,), (1,)), ((), ())),
        precision=lax.Precision.HIGHEST,
        preferred_element_type=F32,
    )


MESH = pl.DeviceIdType.MESH


class Place:
    def __init__(self, shards):
        self.row, self.seq = lax.axis_index("row"), lax.axis_index("seq")
        self.count_b = 2
        self.count_a = shards // self.count_b
        self.shards = shards
        self.x, self.core = self.row // 2, self.row % 2
        self.a, self.b = self.seq // self.count_b, self.seq % self.count_b

    def at(self, x=None, core=None, a=None, b=None):
        x = self.x if x is None else x
        core = self.core if core is None else core
        a = self.a if a is None else a
        b = self.b if b is None else b
        return (x * 2 + core, a * self.count_b + b)

    def beside(self, seq):
        return (self.row, seq)


class Sends:
    def __init__(self):
        self.started = []

    def send(self, src, dst, send_sem, recv_sem, device, when=None):
        copy = pltpu.make_async_remote_copy(
            src_ref=src, dst_ref=dst, send_sem=send_sem, recv_sem=recv_sem, device_id=device,
            device_id_type=MESH,
        )
        guarded(when, copy.start)
        self.started.append((when, copy))

    def drain(self):
        for when, copy in self.started:
            guarded(when, copy.wait_send)
        self.started = []


def guarded(when, action):
    if when is None:
        action()
    else:
        pl.when(when)(action)


def arrive(dst, sem, device, when=None):
    copy = pltpu.make_async_remote_copy(
        src_ref=dst, dst_ref=dst, send_sem=sem, recv_sem=sem, device_id=device, device_id_type=MESH
    )
    guarded(when, copy.wait_recv)


def greet(devices):
    barrier = pltpu.get_barrier_semaphore()
    for device in devices:
        pl.semaphore_signal(barrier, inc=1, device_id=device, device_id_type=MESH)
    pl.semaphore_wait(barrier, len(devices))


class WeightGather:
    def __init__(self, place, sends, mats, sems):
        self.place, self.sends, self.mats = place, sends, mats
        self.z_send, self.z_recv, self.y_send, self.y_recv, self.x_send, self.x_recv, self.c_send, self.c_recv = sems
        third = mats.shape[3] // 3
        self.third = third

    def window(self, a, b, core=None, x=None):
        p = self.place
        x = p.x if x is None else x
        core = p.core if core is None else core
        return self.mats.at[core, a, b, pl.ds(pl.multiple_of(x * self.third, self.third), 2 * self.third), :]

    def piece(self, a, b, x, core=None):
        p = self.place
        core = p.core if core is None else core
        return self.mats.at[core, a, b, pl.ds(pl.multiple_of(x * 2 * self.third, self.third), self.third), :]

    def sides(self, step):
        p = self.place
        if step == 0:
            return [(0, p.a, None)]
        low, high = p.a - step, p.a + step
        return [
            (0, jnp.maximum(low, 0), low >= 0),
            (1, jnp.minimum(high, p.count_a - 1), high <= p.count_a - 1),
        ]

    def along_a(self, step):
        p = self.place
        for side, a, when in self.sides(step):
            here = self.window(a, p.b)
            if step > 0:
                arrive(here, self.z_recv.at[side, step], p.at(), when)
            targets = ((0, 1), (1, -1)) if step == 0 else (((0, 1),) if side == 0 else ((1, -1),))
            if step < p.count_a - 1:
                for out, move in targets:
                    target = p.a + move
                    ok = jnp.logical_and(target >= 0, target <= p.count_a - 1)
                    both = ok if when is None else jnp.logical_and(ok, when)
                    target = jnp.clip(target, 0, p.count_a - 1)
                    self.sends.send(
                        here, here, self.z_send.at[out, step], self.z_recv.at[out, step + 1],
                        p.at(a=target), both,
                    )
            self.sends.send(
                here, here, self.y_send.at[side, step], self.y_recv.at[side, step], p.at(b=1 - p.b), when
            )
            if step > 0:
                self.pass_on(side, step, 0, a, p.b, when)

    def pass_on(self, side, step, column, a, b, when):
        p = self.place
        piece = self.piece(a, b, p.x)
        index = (side, step, column)
        self.sends.send(
            piece, piece, self.x_send.at[index], self.x_recv.at[index], p.at(x=1 - p.x), when
        )
        here = self.window(a, b)
        self.sends.send(
            here, here, self.c_send.at[(0, *index)], self.c_recv.at[(0, *index)], p.at(core=1 - p.core), when
        )

    def along_b(self, step):
        p = self.place
        for side, a, when in self.sides(step):
            arrive(self.window(a, 1 - p.b), self.y_recv.at[side, step], p.at(), when)
            self.pass_on(side, step, 1, a, 1 - p.b, when)

    def columns(self, step):
        p = self.place
        return ((1, 1 - p.b),) if step == 0 else ((0, p.b), (1, 1 - p.b))

    def along_x(self, step):
        p = self.place
        for column, b in self.columns(step):
            for side, a, when in self.sides(step):
                index = (side, step, column)
                piece = self.piece(a, b, 1 - p.x)
                arrive(piece, self.x_recv.at[index], p.at(), when)
                self.sends.send(
                    piece, piece, self.c_send.at[(1, *index)], self.c_recv.at[(1, *index)],
                    p.at(core=1 - p.core), when,
                )

    def finish(self, step):
        p = self.place
        for column, b in self.columns(step):
            for side, a, when in self.sides(step):
                index = (side, step, column)
                other = 1 - p.core
                arrive(self.window(a, b, other), self.c_recv.at[(0, *index)], p.at(), when)
                arrive(self.piece(a, b, 1 - p.x, other), self.c_recv.at[(1, *index)], p.at(), when)


def gather_sems(count_a):
    dma = pltpu.SemaphoreType.DMA
    return [
        dma((2, count_a)), dma((2, count_a)), dma((2, count_a)), dma((2, count_a)),
        dma((2, count_a, 2)), dma((2, count_a, 2)), dma((2, 2, count_a, 2)), dma((2, 2, count_a, 2)),
    ]


class StateGather:
    def __init__(self, place, sends, states, sems):
        self.place, self.sends, self.states = place, sends, states
        self.z_send, self.z_recv, self.y_send, self.y_recv = sems

    def source(self, offset):
        p = self.place
        return lax.rem(p.a + (p.count_a - offset), p.count_a)

    def along_a(self):
        p = self.place
        here = self.states.at[p.a, p.b]
        for offset in range(1, p.count_a):
            target = lax.rem(p.a + offset, p.count_a)
            self.sends.send(here, here, self.z_send.at[offset], self.z_recv.at[offset], p.at(a=target))
        self.sends.send(here, here, self.y_send.at[0], self.y_recv.at[0], p.at(b=1 - p.b))

    def along_b(self):
        p = self.place
        for offset in range(1, p.count_a):
            here = self.states.at[self.source(offset), p.b]
            arrive(here, self.z_recv.at[offset], p.at())
            self.sends.send(here, here, self.y_send.at[offset], self.y_recv.at[offset], p.at(b=1 - p.b))

    def finish(self):
        p = self.place
        for offset in range(p.count_a):
            arrive(self.states.at[self.source(offset), 1 - p.b], self.y_recv.at[offset], p.at())


def state_sems(count_a):
    return [pltpu.SemaphoreType.DMA((count_a,)) for _ in range(4)]


def prefix_phase(place, states, before_ref, after_ref):
    before = jnp.zeros(before_ref.shape, F32)
    after = jnp.zeros(after_ref.shape, F32)
    for a in range(place.count_a):
        for b in range(place.count_b):
            seq = a * place.count_b + b
            value = states[a, b].astype(F32)
            before = before + jnp.where(seq < place.seq, 1.0, 0.0) * value
            after = after + jnp.where(seq > place.seq, 1.0, 0.0) * value
    before_ref[...] = before
    after_ref[...] = after


def forward_kernel(pairs, head_dim, shards_axis, *refs):
    (x_r, w_r, b_r, o_r, bu_r, ta_r, wo_r, bo_r, up_r, down_r, bup_r) = refs[:11]
    (q_r, k_r, qf_r, kv_r, line_r, out_r, low_r, dnm_r, l_r, r_r, ld_r, rd_r, nrm_r, sc_r, mats,
     bups_r) = refs[11:27]
    num_r, den_r, tot_r, states, bef_r, aft_r = refs[27:33]
    w_sems, s_sems, (h_send, h_recv) = refs[33:41], refs[41:45], refs[45:47]
    place = Place(shards_axis)
    sends = Sends()
    rows = x_r.shape[0]
    seq = place.seq
    greet(
        [place.beside(lax.rem(seq + o, shards_axis)) for o in range(1, shards_axis)]
        + [place.at(core=1 - place.core), place.at(x=1 - place.x)]
    )
    weights = WeightGather(place, sends, mats, w_sems)
    gather = StateGather(place, sends, states, s_sems)
    mats[0, place.a, place.b] = up_r[...]
    mats[1, place.a, place.b] = down_r[...].T
    weights.along_a(0)
    ke_r, ve_r = kv_r.at[0], kv_r.at[1]
    own = pl.ds(WINDOW, rows)
    qkv_phase(
        x_r, w_r, b_r, o_r, ((1, k_r, ke_r.at[own]), (2, ve_r.at[own], None)), head_dim
    )
    is_first, is_last = seq == 0, seq == shards_axis - 1
    low_edge, high_edge = kv_r.at[:, pl.ds(0, WINDOW), :], kv_r.at[:, pl.ds(rows + WINDOW, WINDOW), :]
    to_right = jnp.minimum(seq + 1, shards_axis - 1)
    to_left = jnp.maximum(seq - 1, 0)
    sends.send(
        kv_r.at[:, pl.ds(rows, WINDOW), :], low_edge, h_send.at[0], h_recv.at[0], place.beside(to_right),
        jnp.logical_not(is_last),
    )
    sends.send(
        kv_r.at[:, pl.ds(WINDOW, WINDOW), :], high_edge, h_send.at[1], h_recv.at[1],
        place.beside(to_left), jnp.logical_not(is_first),
    )

    @pl.when(is_first)
    def _():
        kv_r[:, 0:WINDOW, :] = jnp.zeros((2, WINDOW, kv_r.shape[2]), BF16)

    @pl.when(is_last)
    def _():
        kv_r[:, rows + WINDOW :, :] = jnp.zeros((2, WINDOW, kv_r.shape[2]), BF16)

    half = LANES // 2
    tot_r[pairs * half :, :] = jnp.zeros((tot_r.shape[0] - pairs * half, LANES), F32)
    state_phase(ke_r.at[own], ve_r.at[own], num_r, den_r, tot_r, pairs)
    bias_rows = bup_r.shape[1] // LANES
    for index in range(bias_rows):
        at = pairs * (half + 1) + index
        tot_r[at : at + 1, :] = bup_r[:, index * LANES : (index + 1) * LANES].astype(F32)
    states[place.a, place.b] = tot_r[...].astype(BF16)
    gather.along_a()
    weights.along_b(0)
    qkv_phase(x_r, w_r, b_r, o_r, ((0, q_r, qf_r),), head_dim)
    line_phase(bu_r, ta_r, line_r)
    gather.along_b()
    weights.along_a(1)
    weights.along_x(0)
    arrive(low_edge, h_recv.at[0], place.at(), jnp.logical_not(is_first))
    arrive(high_edge, h_recv.at[1], place.at(), jnp.logical_not(is_last))
    third = pairs // 3
    band_forward_phase(qf_r, ke_r, ve_r, line_r, out_r, dnm_r, 0, third)
    weights.along_b(1)
    weights.along_a(2)
    band_forward_phase(qf_r, ke_r, ve_r, line_r, out_r, dnm_r, third, 2 * third)
    weights.along_x(1)
    weights.along_b(2)
    gather.finish()
    prefix_phase(place, states, bef_r, aft_r)
    for a in range(place.count_a):
        for b in range(place.count_b):
            tail = states[a, b, pairs * half :, :].astype(F32)
            first = pairs
            bups_r[a * place.count_b + b] = jnp.broadcast_to(
                jnp.concatenate([tail[first + i : first + i + 1] for i in range(bias_rows)], 1),
                bups_r.shape[1:],
            )
    band_forward_phase(qf_r, ke_r, ve_r, line_r, out_r, dnm_r, 2 * third, pairs)
    weights.along_a(3)
    weights.along_x(2)
    far_forward_phase(
        qf_r, ke_r, ve_r, line_r, num_r, den_r, bef_r, aft_r, out_r, low_r, dnm_r, l_r, r_r, ld_r, rd_r,
        pairs, head_dim,
    )
    weights.along_b(3)
    out_phase(x_r, low_r, wo_r, bo_r, nrm_r, sc_r)
    weights.along_x(3)
    for step in range(place.count_a):
        weights.finish(step)
    sends.drain()


class GradScatter:
    def __init__(self, place, sends, grads, own, total, lands, sems):
        self.place, self.sends, self.grads, self.own, self.total = place, sends, grads, own, total
        self.core_land, self.x_land, self.y_land, self.z_land, self.last_land = lands
        (self.copy, self.c_send, self.c_recv, self.x_send, self.x_recv, self.y_send, self.y_recv, self.z_send,
         self.z_recv, self.l_send, self.l_recv) = sems
        self.third = own.shape[2] // 3
        self.order = list(range(1, place.count_a)) + [0]

    def shard(self, offset):
        p = self.place
        return lax.rem(p.a + offset, p.count_a)

    def outer(self, x):
        return pl.ds(pl.multiple_of(x * 2 * self.third, self.third), self.third)

    def window(self):
        return pl.ds(pl.multiple_of(self.place.x * self.third, self.third), 2 * self.third)

    def start(self):
        p = self.place
        for offset in self.order:
            a = self.shard(offset)
            self.sends.send(
                self.grads.at[1 - p.core, a], self.core_land.at[a], self.c_send.at[offset],
                self.c_recv.at[offset], p.at(core=1 - p.core),
            )
            pltpu.make_async_copy(self.grads.at[p.core, a], self.own.at[a], self.copy.at[offset]).start()

    def add(self, ref, land):
        ref[...] = (ref[...].astype(F32) + land[...].astype(F32)).astype(BF16)

    def chip(self, offset):
        p = self.place
        a = self.shard(offset)
        pltpu.make_async_copy(self.grads.at[p.core, a], self.own.at[a], self.copy.at[offset]).wait()
        arrive(self.core_land.at[a], self.c_recv.at[offset], p.at())
        self.add(self.own.at[a], self.core_land.at[a])
        self.sends.send(
            self.own.at[a, :, self.outer(1 - p.x), :], self.x_land.at[a], self.x_send.at[offset],
            self.x_recv.at[offset], p.at(x=1 - p.x),
        )

    def along_x(self, offset):
        p = self.place
        a = self.shard(offset)
        arrive(self.x_land.at[a], self.x_recv.at[offset], p.at())
        self.add(self.own.at[a, :, self.outer(p.x), :], self.x_land.at[a])
        self.sends.send(
            self.own.at[a, 1 - p.b, self.window(), :], self.y_land.at[a], self.y_send.at[offset],
            self.y_recv.at[offset], p.at(b=1 - p.b),
        )

    def along_b(self, offset):
        p = self.place
        a = self.shard(offset)
        arrive(self.y_land.at[a], self.y_recv.at[offset], p.at())
        mine = self.own.at[a, p.b, self.window(), :]
        self.add(mine, self.y_land.at[a])
        if offset:
            self.sends.send(
                mine, self.z_land.at[offset], self.z_send.at[offset], self.z_recv.at[offset], p.at(a=a)
            )

    def along_a(self):
        p = self.place
        mine = self.own.at[p.a, p.b, self.window(), :]
        for offset in range(1, p.count_a):
            arrive(self.z_land.at[offset], self.z_recv.at[offset], p.at())
        total = mine[...].astype(F32)
        for offset in range(1, p.count_a):
            total = total + self.z_land[offset].astype(F32)
        mine[...] = total.astype(BF16)
        middle = pl.ds(self.third, self.third)
        outer = self.outer(p.x)
        self.total[p.core, outer, :] = self.own[p.a, p.b, outer, :]
        self.sends.send(
            self.own.at[p.a, p.b, middle, :], self.last_land, self.l_send.at[0], self.l_recv.at[0],
            p.at(x=1 - p.x),
        )
        self.sends.send(
            self.total.at[p.core, outer, :], self.total.at[p.core, outer, :], self.l_send.at[1],
            self.l_recv.at[1], p.at(x=1 - p.x),
        )

    def last_x(self):
        p = self.place
        middle = pl.ds(self.third, self.third)
        arrive(self.last_land, self.l_recv.at[0], p.at())
        self.total[p.core, middle, :] = (
            self.own[p.a, p.b, middle, :].astype(F32) + self.last_land[...].astype(F32)
        ).astype(BF16)
        arrive(self.total.at[p.core, self.outer(1 - p.x), :], self.l_recv.at[1], p.at())
        here = self.total.at[p.core]
        self.sends.send(here, here, self.l_send.at[2], self.l_recv.at[2], p.at(core=1 - p.core))

    def finish(self):
        arrive(self.total.at[1 - self.place.core], self.l_recv.at[2], self.place.at())


def scatter_sems(count_a):
    dma = pltpu.SemaphoreType.DMA
    return [dma((count_a,)) for _ in range(9)] + [dma((3,)), dma((3,))]


class AllReduce:
    def __init__(self, place, sends, parts, result, lands, done, chunk, sems):
        self.place, self.sends, self.parts, self.result, self.chunk = place, sends, parts, result, chunk
        self.core_land, self.one_land, self.two_land, self.a_land = lands
        self.done = done
        self.s_send, self.s_recv, self.z_send, self.z_recv, self.g_send, self.g_recv, self.zg_send, self.zg_recv, self.copy = sems
        p = place
        straight = p.core == 0
        self.half = parts.shape[0] // 2
        self.quarter = self.half // 2
        self.slim = self.quarter // p.count_a
        self.one = jnp.where(straight, p.x, p.b)
        self.two = jnp.where(straight, p.b, p.x)
        other_x, other_b = p.at(x=1 - p.x), p.at(b=1 - p.b)
        self.one_device = tuple(jnp.where(straight, u, w) for u, w in zip(other_x, other_b))
        self.two_device = tuple(jnp.where(straight, w, u) for u, w in zip(other_x, other_b))
        self.core_device = p.at(core=1 - p.core)

    def cols(self, index):
        return pl.ds(index * self.chunk, self.chunk)

    def side(self, index, two):
        width = self.chunk // 2
        return pl.ds(pl.multiple_of(index * self.chunk + two * width, LANES), width)

    def half_rows(self, core):
        return pl.ds(pl.multiple_of(core * self.half, self.half), self.half)

    def quarter_rows(self, one):
        start = self.place.core * self.half + one * self.quarter
        return pl.ds(pl.multiple_of(start, self.quarter), self.quarter)

    def slim_rows(self, a):
        start = self.place.core * self.half + self.one * self.quarter + a * self.slim
        return pl.ds(pl.multiple_of(start, self.slim), self.slim)

    def push(self, index):
        p = self.place
        self.sends.send(
            self.parts.at[self.half_rows(1 - p.core), self.cols(index)], self.core_land.at[:, self.cols(index)],
            self.s_send.at[0, index], self.s_recv.at[0, index], self.core_device,
        )

    def add(self, rows, cols, land):
        self.parts[rows, cols] = (self.parts[rows, cols].astype(F32) + land[...].astype(F32)).astype(BF16)

    def stage(self, index, number):
        p = self.place
        cols = self.cols(index)
        mine, other = self.side(index, self.two), self.side(index, 1 - self.two)
        if number == 1:
            land = self.core_land.at[:, cols]
            arrive(land, self.s_recv.at[0, index], p.at())
            self.add(self.half_rows(p.core), cols, land)
            self.sends.send(
                self.parts.at[self.quarter_rows(1 - self.one), cols], self.one_land.at[:, cols],
                self.s_send.at[1, index], self.s_recv.at[1, index], self.one_device,
            )
        elif number == 2:
            land = self.one_land.at[:, cols]
            arrive(land, self.s_recv.at[1, index], p.at())
            self.add(self.quarter_rows(self.one), cols, land)
            self.sends.send(
                self.parts.at[self.quarter_rows(self.one), other], self.two_land.at[index],
                self.s_send.at[2, index], self.s_recv.at[2, index], self.two_device,
            )
        elif number == 3:
            land = self.two_land.at[index]
            arrive(land, self.s_recv.at[2, index], p.at())
            self.add(self.quarter_rows(self.one), mine, land)
            for offset in range(1, p.count_a):
                a = lax.rem(p.a + offset, p.count_a)
                self.sends.send(
                    self.parts.at[self.slim_rows(a), mine], self.a_land.at[index, offset],
                    self.z_send.at[index, offset], self.z_recv.at[index, offset], p.at(a=a),
                )
        elif number == 4:
            for offset in range(1, p.count_a):
                arrive(self.a_land.at[index, offset], self.z_recv.at[index, offset], p.at())
            rows = self.slim_rows(p.a)
            total = self.parts[rows, mine].astype(F32)
            for offset in range(1, p.count_a):
                total = total + self.a_land[index, offset].astype(F32)
            self.done[index] = total.astype(BF16)
            here = self.result.at[rows, mine]
            pltpu.make_async_copy(self.done.at[index], here, self.copy.at[index]).start()
            for offset in range(1, p.count_a):
                a = lax.rem(p.a + offset, p.count_a)
                self.sends.send(
                    self.done.at[index], here, self.zg_send.at[index, offset], self.zg_recv.at[index, offset],
                    p.at(a=a),
                )
        elif number == 5:
            pltpu.make_async_copy(
                self.done.at[index], self.result.at[self.slim_rows(p.a), mine], self.copy.at[index]
            ).wait()
            for offset in range(1, p.count_a):
                a = lax.rem(p.a + p.count_a - offset, p.count_a)
                arrive(self.result.at[self.slim_rows(a), mine], self.zg_recv.at[index, offset], p.at())
            here = self.result.at[self.quarter_rows(self.one), mine]
            self.sends.send(
                here, here, self.g_send.at[0, index], self.g_recv.at[0, index], self.two_device
            )
        elif number == 6:
            arrive(
                self.result.at[self.quarter_rows(self.one), other], self.g_recv.at[0, index], p.at()
            )
            here = self.result.at[self.quarter_rows(self.one), cols]
            self.sends.send(
                here, here, self.g_send.at[1, index], self.g_recv.at[1, index], self.one_device
            )
        elif number == 7:
            arrive(
                self.result.at[self.quarter_rows(1 - self.one), cols], self.g_recv.at[1, index], p.at()
            )
            here = self.result.at[self.half_rows(p.core), cols]
            self.sends.send(
                here, here, self.g_send.at[2, index], self.g_recv.at[2, index], self.core_device
            )
        elif number == 8:
            arrive(self.result.at[self.half_rows(1 - p.core), cols], self.g_recv.at[2, index], p.at())


def reduce_sems(chunks, count_a):
    dma = pltpu.SemaphoreType.DMA
    return [
        dma((3, chunks)), dma((3, chunks)), dma((chunks, count_a)), dma((chunks, count_a)),
        dma((3, chunks)), dma((3, chunks)), dma((chunks, count_a)), dma((chunks, count_a)), dma((chunks,)),
    ]


class SmallReduce:
    def __init__(self, place, sends, held, land, sems):
        self.place, self.sends, self.held, self.land = place, sends, held, land
        self.out_sem, self.in_sem = sems
        p = place
        self.devices = [p.at(core=1 - p.core), p.at(x=1 - p.x), p.at(b=1 - p.b)]

    def send(self, step):
        if step < 3:
            self.sends.send(
                self.held.at[step], self.land.at[step], self.out_sem.at[step], self.in_sem.at[step],
                self.devices[step],
            )
            return
        p = self.place
        for offset in range(1, p.count_a):
            self.sends.send(
                self.held.at[3], self.land.at[3 + offset], self.out_sem.at[3 + offset],
                self.in_sem.at[3 + offset], p.at(a=lax.rem(p.a + offset, p.count_a)),
            )

    def receive(self, step):
        p = self.place
        if step < 3:
            arrive(self.land.at[step], self.in_sem.at[step], p.at())
            self.held[step + 1] = self.held[step] + self.land[step]
            return
        for offset in range(1, p.count_a):
            arrive(self.land.at[3 + offset], self.in_sem.at[3 + offset], p.at())
        self.land[3] = self.held[3]

    def total(self):
        p = self.place
        total = self.land[3 + lax.rem(p.a, p.count_a)]
        for a in range(1, p.count_a):
            total = total + self.land[3 + lax.rem(p.a + p.count_a - a, p.count_a)]
        return total


def backward_kernel(pairs, head_dim, buckets, shards_axis, *refs):
    (x_r, w_r, o_r, wo_r, q_r, k_r, qf_r, kv_r, line_r, out_r, low_r, dnm_r, l_r, r_r, ld_r, rd_r, glow_r,
     vec_r, gbias_r, bu_r, first_r, grads_r) = refs[:22]
    gtok_r, gup_r, gdown_r, small_r, result_r = refs[22:27]
    (gnum_r, gden_r, dnum_r, dden_r, tot_r, states, past_r, future_r, gq_r, gk_r, gv_r, gline_r, cg_r,
     edge_out, edge_in, parts_r, turned_r) = refs[27:44]
    own_r, total_r = refs[44:46]
    rs_lands, ar_lands, done_r, held_r, land_r = refs[46:51], refs[51:55], refs[55], refs[56], refs[57]
    sems = refs[58:]
    s_sems, sems = sems[:4], sems[4:]
    rs_sems, sems = sems[:11], sems[11:]
    ar_sems, sems = sems[:9], sems[9:]
    sm_sems, sems = sems[:2], sems[2:]
    e_send, e_recv, load_sem = sems
    rows, width = x_r.shape
    half = LANES // 2
    place = Place(shards_axis)
    sends = Sends()
    seq = place.seq
    load = pltpu.make_async_copy(first_r, gtok_r, load_sem.at[0])
    out_v, dnm_v = gq_r, gk_r.at[pl.ds(0, rows)]
    load_out = pltpu.make_async_copy(out_r, out_v, load_sem.at[1])
    load_dnm = pltpu.make_async_copy(dnm_r, dnm_v, load_sem.at[2])
    load_out.start()
    load_dnm.start()
    load.start()
    greet(
        [place.beside(lax.rem(seq + o, shards_axis)) for o in range(1, shards_axis)]
        + [place.at(core=1 - place.core), place.at(x=1 - place.x)]
    )
    scatter = GradScatter(place, sends, grads_r, own_r, total_r, rs_lands, rs_sems)
    gather = StateGather(place, sends, states, s_sems)
    reduce = AllReduce(place, sends, parts_r, result_r, ar_lands, done_r, width, ar_sems)
    little = SmallReduce(place, sends, held_r, land_r, sm_sems)
    ke_r, ve_r = kv_r.at[0], kv_r.at[1]
    own = pl.ds(WINDOW, rows)
    kf_r, v_r = ke_r.at[own], ve_r.at[own]
    is_first, is_last = seq == 0, seq == shards_axis - 1
    to_right = place.beside(jnp.minimum(seq + 1, shards_axis - 1))
    to_left = place.beside(jnp.maximum(seq - 1, 0))
    groups = pairs * LANES // CHUNK
    in_group = CHUNK // LANES

    scatter.start()
    turned_r[...] = x_r[...].T
    tot_r[pairs * half :, :] = jnp.zeros((tot_r.shape[0] - pairs * half, LANES), F32)
    load_out.wait()
    load_dnm.wait()
    out_back_phase(
        glow_r, wo_r, low_r, out_v, dnm_v, qf_r, gnum_r, gden_r, parts_r.at[:, pl.ds(0, width)], dnum_r, dden_r, tot_r, pairs, head_dim
    )
    states[place.a, place.b] = tot_r[...].astype(BF16)
    gather.along_a()
    reduce.push(0)

    def band(group):
        band_backward_phase(
            qf_r, ke_r, ve_r, line_r, gnum_r, gden_r, dnum_r, dden_r, l_r, r_r, ld_r, rd_r, gq_r, gk_r, gv_r,
            gline_r, cg_r, group * in_group, (group + 1) * in_group, head_dim,
        )
        cols = slice(group * CHUNK, (group + 1) * CHUNK)
        for index, ref in ((0, gk_r), (1, gv_r)):
            edge_out[0, index, :, cols] = ref[0:WINDOW, cols].astype(BF16)
            edge_out[1, index, :, cols] = ref[rows + WINDOW :, cols].astype(BF16)
        lane = pl.ds(group * CHUNK, CHUNK)
        for side, device, when in ((0, to_left, jnp.logical_not(is_first)), (1, to_right, jnp.logical_not(is_last))):
            sends.send(
                edge_out.at[side, :, :, lane], edge_in.at[1 - side, :, :, lane], e_send.at[side, group],
                e_recv.at[1 - side, group], device, when,
            )

    def keys(group):
        lane = pl.ds(group * CHUNK, CHUNK)
        for side, when in ((0, jnp.logical_not(is_first)), (1, jnp.logical_not(is_last))):
            arrive(edge_in.at[side, :, :, lane], e_recv.at[side, group], place.at(), when)
        key_back_phase(
            kf_r, v_r, line_r, dnum_r, dden_r, past_r, future_r, edge_in.at[0], edge_in.at[1], gk_r, gv_r,
            pairs, group * in_group, (group + 1) * in_group, head_dim,
        )
        qkv_back_phase(
            turned_r, w_r, o_r, q_r, k_r, qf_r, kf_r, gq_r, gk_r, gv_r, gtok_r, parts_r, small_r, group, head_dim,
        )
        reduce.push(group + 1)

    @pl.when(is_first)
    def _():
        edge_in[0] = jnp.zeros(edge_in.shape[1:], BF16)

    @pl.when(is_last)
    def _():
        edge_in[1] = jnp.zeros(edge_in.shape[1:], BF16)

    small_r[...] = jnp.zeros(small_r.shape, F32)
    scatter.chip(1)
    gather.along_b()
    scatter.chip(2)
    reduce.stage(0, 1)
    band(0)
    scatter.along_x(1)
    scatter.chip(3)
    scatter.along_x(2)
    scatter.chip(0)
    reduce.stage(0, 2)
    gather.finish()
    prefix_phase(place, states, past_r, future_r)
    load.wait()
    band(1)
    scatter.along_b(1)
    scatter.along_x(3)
    scatter.along_b(2)
    scatter.along_x(0)
    reduce.stage(0, 3)
    keys(0)
    scatter.along_b(3)
    reduce.stage(0, 4)
    reduce.stage(1, 1)
    band(2)
    scatter.along_b(0)
    reduce.stage(0, 5)
    reduce.stage(1, 2)
    keys(1)
    reduce.stage(0, 6)
    reduce.stage(1, 3)
    reduce.stage(2, 1)
    scatter.along_a()
    keys(2)
    small_r[16 : 16 + gline_r.shape[0], 0:buckets] = table_phase(gline_r, bu_r, buckets)
    small_r[0:8, :] = vec_r[...]
    shards = gbias_r.shape[0]
    per_row = width // gbias_r.shape[2]
    for index in range(shards // per_row):
        small_r[12 + index : 13 + index, :] = jnp.concatenate(
            [gbias_r[index * per_row + i, 0:1, :] for i in range(per_row)], 1
        )
    held_r[0] = small_r[...]
    little.send(0)
    scatter.last_x()
    reduce.stage(0, 7)
    reduce.stage(1, 4)
    reduce.stage(2, 2)
    reduce.stage(3, 1)
    little.receive(0)
    little.send(1)
    for step in range(7):
        if step < 1:
            reduce.stage(0, 8)
        if step < 4:
            reduce.stage(1, 5 + step)
        if step < 6:
            reduce.stage(2, 3 + step)
        reduce.stage(3, 2 + step)
        if step < 3:
            little.receive(1 + step)
        if step < 2:
            little.send(2 + step)
    small_r[...] = little.total()
    scatter.finish()
    gup_r[...] = total_r[0].astype(F32)
    gdown_r[...] = total_r[1].T.astype(F32)
    sends.drain()


def in_parts(grouped):
    groups = grouped.shape[1] // (3 * CHUNK)
    starts = [(group * 3 + part) * CHUNK for part in range(3) for group in range(groups)]
    return jnp.concatenate([grouped[:, start : start + CHUNK].astype(F32) for start in starts], 1)


def call(body, outs, operands, scratch=(), limit=60, collective_id=None, in_place=(), out_place=()):
    return pl.pallas_call(
        body,
        out_shape=[jax.ShapeDtypeStruct(shape, dtype) for shape, dtype in outs],
        in_specs=[
            pl.BlockSpec(memory_space=pl.ANY if i in in_place else pltpu.VMEM) for i in range(len(operands))
        ],
        out_specs=[
            pl.BlockSpec(memory_space=pl.ANY if i in out_place else pltpu.VMEM) for i in range(len(outs))
        ],
        scratch_shapes=list(scratch),
        compiler_params=pltpu.CompilerParams(
            vmem_limit_bytes=limit * MIB,
            collective_id=collective_id,
            has_side_effects=collective_id is not None,
        ),
    )(*operands)


def shards(
    tokens, cotangent, w_qkv, b_qkv, w_out, b_out, gain_one, shift_one, w_up, b_up, w_down, b_down,
    gain_two, shift_two, feature_codes, bias_table, offset_bucket,
):
    rows, width = tokens.shape[1:]
    heads, head_dim, feats = feature_codes.shape
    buckets = bias_table.shape[1]
    pairs = heads // 2
    blocks = rows // WINDOW
    half = LANES // 2
    hidden_units = w_up.shape[1]
    length = (offset_bucket.shape[0] + 1) // 2
    count = lax.axis_size("seq")
    x = tokens[0]
    omega_int = (feature_codes.astype(F32) - CENTER).astype(BF16)
    group = CHUNK // head_dim
    eye = jnp.eye(group, dtype=BF16)
    omega = (
        omega_int.reshape(heads // group, group, head_dim, 1, feats)
        * eye[None, :, None, :, None]
    ).reshape(heads // group, CHUNK, CHUNK)
    bucket_line = offset_bucket[length - LINE // 2 : length + LINE // 2][None]
    state = (pairs * half + 8, LANES)
    stacked = (pairs * blocks, half, LANES)
    flat = (pairs * blocks, LANES)
    wide = (rows, width)

    def halo(block):
        forward = [(i, i + 1) for i in range(count - 1)]
        backward = [(target, source) for source, target in forward]
        low = lax.ppermute(block[rows - WINDOW :], "seq", forward)
        high = lax.ppermute(block[:WINDOW], "seq", backward)
        return jnp.concatenate([low, block, high], 0)

    me = lax.axis_index("seq")
    ids = jnp.arange(count)

    def prefix(message):
        every = lax.all_gather(message, "seq", axis=0)
        before = jnp.sum(jnp.where((ids < me)[:, None, None], every, 0.0), 0)
        after = jnp.sum(jnp.where((ids > me)[:, None, None], every, 0.0), 0)
        return before, after

    if lax.axis_size("row") == 4 and count == 8:
        count_a = count // 2
        ext = (rows + 2 * WINDOW, width)
        message = (pairs * half + 16, LANES)
        dma = pltpu.SemaphoreType.DMA
        (q, k, qf, kve, line, attn, attn_low, denom, left, right, left_den, right_den, normed, scale,
         mats, b_up_all) = call(
            functools.partial(forward_kernel, pairs, head_dim, count),
            [(wide, BF16), (wide, BF16), (wide, BF16), ((2, *ext), BF16), ((heads, LINE), F32),
             (wide, F32), (wide, BF16), (wide, F32), (stacked, F32), (stacked, F32), (flat, F32),
             (flat, F32), (wide, F32), ((rows, LANES), F32),
             ((2, count_a, 2, width, hidden_units), BF16), ((count, 8, hidden_units), F32)],
            (x, w_qkv, b_qkv[None], omega, bucket_line, bias_table, w_out, b_out[None], w_up, w_down,
             b_up[None]),
            [pltpu.VMEM(stacked, F32), pltpu.VMEM(flat, F32), pltpu.VMEM(message, F32),
             pltpu.VMEM((count_a, 2, *message), BF16), pltpu.VMEM(message, F32),
             pltpu.VMEM(message, F32)]
            + gather_sems(count_a) + state_sems(count_a) + [dma((2,)), dma((2,))],
            collective_id=0,
        )
        def ffn_body(*refs):
            up_r, down_r = refs[4].at[0], refs[4].at[1]
            ins = refs[:4] + (up_r, refs[5], down_r) + refs[6:10]
            outs = refs[10:]
            ffn_phase(*ins, *outs[:4], outs[4].at[0], outs[4].at[1], *outs[5:])

        layer, first, first_low, vec, grads, gbias = call(
            ffn_body,
            [(wide, BF16), (wide, F32), (wide, BF16), ((8, width), F32),
             ((2, count, width, hidden_units), BF16), ((count, 8, hidden_units), F32)],
            (normed, scale, gain_one[None], shift_one[None], mats.reshape(2, count, width, hidden_units),
             b_up_all, b_down[None], gain_two[None], shift_two[None], cotangent[0]),
            (pltpu.VMEM((count, rows, hidden_units), BF16), pltpu.VMEM((count, rows, hidden_units), BF16),
             pltpu.VMEM(wide, F32)),
        )
        third = width // 3
        chunks = 1 + width // CHUNK
        quarter = width // 4
        gtok, grad_w_up, grad_w_down, small, result = call(
            functools.partial(backward_kernel, pairs, head_dim, buckets, count),
            [(wide, F32), ((width, hidden_units), F32), ((hidden_units, width), F32), ((32, width), F32),
             ((width, chunks * width), BF16)],
            (x, w_qkv, omega, w_out, q, k, qf, kve, line, attn, attn_low, denom, left, right, left_den,
             right_den, first_low, vec, gbias, bucket_line, first,
             grads.reshape(2, count_a, 2, width, hidden_units)),
            [pltpu.VMEM(wide, BF16), pltpu.VMEM(wide, F32), pltpu.VMEM(stacked, F32), pltpu.VMEM(flat, F32),
             pltpu.VMEM(message, F32), pltpu.VMEM((count_a, 2, *message), BF16), pltpu.VMEM(message, F32),
             pltpu.VMEM(message, F32), pltpu.VMEM(wide, F32), pltpu.VMEM(ext, F32), pltpu.VMEM(ext, F32),
             pltpu.VMEM((heads, LINE), F32), pltpu.VMEM((2 * WINDOW, 3 * WINDOW), F32),
             pltpu.VMEM((2, 2, WINDOW, width), BF16), pltpu.VMEM((2, 2, WINDOW, width), BF16),
             pltpu.VMEM((width, chunks * width), BF16), pltpu.VMEM((width, rows), BF16),
             pltpu.VMEM((count_a, 2, width, hidden_units), BF16), pltpu.VMEM((2, width, hidden_units), BF16),
             pltpu.VMEM((count_a, 2, width, hidden_units), BF16),
             pltpu.VMEM((count_a, 2, third, hidden_units), BF16),
             pltpu.VMEM((count_a, 2 * third, hidden_units), BF16),
             pltpu.VMEM((count_a, 2 * third, hidden_units), BF16),
             pltpu.VMEM((third, hidden_units), BF16),
             pltpu.VMEM((2 * quarter, chunks * width), BF16), pltpu.VMEM((quarter, chunks * width), BF16),
             pltpu.VMEM((chunks, quarter, width // 2), BF16),
             pltpu.VMEM((chunks, count_a, quarter // count_a, width // 2), BF16),
             pltpu.VMEM((chunks, quarter // count_a, width // 2), BF16),
             pltpu.VMEM((4, 32, width), F32), pltpu.VMEM((3 + count_a, 32, width), F32)]
            + state_sems(count_a) + scatter_sems(count_a) + reduce_sems(chunks, count_a)
            + [dma((3 + count_a,)), dma((3 + count_a,)), dma((2, chunks)), dma((2, chunks)), dma((3,))],
            limit=62,
            collective_id=1,
            in_place=(9, 11, 20, 21),
            out_place=(4,),
        )
        gw_qkv = in_parts(result[:, width:])
        gw_out = result[:, :width].astype(F32)
        gb_qkv = in_parts(small[8 : 8 + width // CHUNK].reshape(1, -1))[0]
        units = count * hidden_units // width
        grad_b_up = lax.dynamic_slice_in_dim(
            small[12 : 12 + units].reshape(-1), lax.axis_index("seq") * hidden_units, hidden_units
        )
        gtable = small[16 : 16 + heads, :buckets]
        return (
            layer[None], gtok[None], gw_qkv, gb_qkv, gw_out, small[5], small[3], small[4], grad_w_up, grad_b_up,
            grad_w_down, small[2], small[0], small[1], gtable,
        )

    def body_one(x_r, w_r, b_r, o_r, bu_r, ta_r, q_r, k_r, v_r, qf_r, kf_r, line_r, num_r, den_r, tot_r):
        parts = ((1, k_r, kf_r), (2, v_r, None), (0, q_r, qf_r))
        qkv_phase(x_r, w_r, b_r, o_r, parts, head_dim)
        line_phase(bu_r, ta_r, line_r)
        state_phase(kf_r, v_r, num_r, den_r, tot_r, pairs)

    q, k, v, qf, kf, line, num, den, total = call(
        body_one,
        [(wide, BF16)] * 5
        + [((heads, LINE), F32), (stacked, F32), (flat, F32), (state, F32)],
        (x, w_qkv, b_qkv[None], omega, bucket_line, bias_table),
    )
    up_all = lax.all_gather(w_up, "seq", axis=0)
    down_all = lax.all_gather(jnp.transpose(w_down), "seq", axis=0)
    b_up_all = jnp.broadcast_to(lax.all_gather(b_up, "seq", axis=0)[:, None, :], (count, 8, hidden_units))

    ke, ve = halo(kf), halo(v)
    before, after = prefix(total)

    def body_two(*refs):
        ins, outs = refs[:12], refs[12:]
        qf_r, ke_r, ve_r, line_r, num_r, den_r, bef_r, aft_r, x_r, w_r, b_r, _ = ins
        out_r, low_r, dnm_r, l_r, r_r, ld_r, rd_r, nrm_r, sc_r = outs
        band_forward_phase(qf_r, ke_r, ve_r, line_r, out_r, dnm_r, 0, pairs)
        far_forward_phase(
            qf_r, ke_r, ve_r, line_r, num_r, den_r, bef_r, aft_r,
            out_r, low_r, dnm_r, l_r, r_r, ld_r, rd_r, pairs, head_dim,
        )
        out_phase(x_r, low_r, w_r, b_r, nrm_r, sc_r)

    attn, attn_low, denom, left, right, left_den, right_den, normed, scale = call(
        body_two,
        [(wide, F32), (wide, BF16), (wide, F32), (stacked, F32), (stacked, F32), (flat, F32),
         (flat, F32), (wide, F32), ((rows, LANES), F32)],
        (qf, ke, ve, line, num, den, before, after, x, w_out, b_out[None], gain_one[None]),
    )
    layer, first, first_low, vec, gup, gdown, gbias = call(
        ffn_phase,
        [(wide, BF16), (wide, F32), (wide, BF16), ((8, width), F32),
         ((count, width, hidden_units), BF16), ((count, width, hidden_units), BF16),
         ((count, 8, hidden_units), F32)],
        (normed, scale, gain_one[None], shift_one[None], up_all, b_up_all, down_all, b_down[None],
         gain_two[None], shift_two[None], cotangent[0]),
        (pltpu.VMEM((count, rows, hidden_units), BF16), pltpu.VMEM((count, rows, hidden_units), BF16),
         pltpu.VMEM(wide, F32)),
    )

    def reduced(part):
        return lax.psum(lax.psum_scatter(part, "seq", scatter_dimension=0), "row").astype(F32)

    grad_w_up = reduced(gup)
    grad_w_down = jnp.transpose(reduced(gdown))
    grad_b_up = reduced(gbias[:, 0])
    ext = (rows + 2 * WINDOW, width)

    def body_four(*refs):
        (gl_r, w_r, lo_r, ou_r, dn_r, qf_r, ke_r, ve_r, li_r, l_r, r_r, ld_r, rd_r, bu_r) = refs[:14]
        gw_r, gq_r, gk_r, gv_r, dnum_r, dden_r, tot_r, gt_r, gnum_r, gden_r, gline_r, cg_r = refs[14:]
        out_back_phase(
            gl_r, w_r, lo_r, ou_r, dn_r, qf_r, gnum_r, gden_r, gw_r, dnum_r, dden_r, tot_r, pairs, head_dim
        )
        band_backward_phase(
            qf_r, ke_r, ve_r, li_r, gnum_r, gden_r, dnum_r, dden_r, l_r, r_r, ld_r, rd_r,
            gq_r, gk_r, gv_r, gline_r, cg_r, 0, pairs, head_dim,
        )
        gt_r[...] = table_phase(gline_r, bu_r, buckets)

    gw_out, gq, gk, gv, dnum, dden, gtotal, gtable = call(
        body_four,
        [((width, width), F32), (wide, F32), (ext, F32), (ext, F32), (stacked, F32), (flat, F32),
         (state, F32), (bias_table.shape, F32)],
        (first_low, w_out, attn_low, attn, denom, qf, ke, ve, line, left, right, left_den, right_den,
         bucket_line),
        (pltpu.VMEM(wide, BF16), pltpu.VMEM(wide, F32), pltpu.VMEM((heads, LINE), F32),
         pltpu.VMEM((2 * WINDOW, 3 * WINDOW), F32)),
    )
    past, future = prefix(gtotal)
    forward = [(i, i + 1) for i in range(count - 1)]
    backward = [(target, source) for source, target in forward]
    to_left = jnp.stack([gk[:WINDOW], gv[:WINDOW]]).astype(BF16)
    to_right = jnp.stack([gk[rows + WINDOW :], gv[rows + WINDOW :]]).astype(BF16)
    low_in = lax.ppermute(to_right, "seq", forward)
    high_in = lax.ppermute(to_left, "seq", backward)

    def body_five(*refs):
        (x_r, w_r, o_r, q_r, k_r, v_r, qf_r, kf_r, li_r, dn_r, dd_r, pa_r, fu_r, lo_r, hi_r, gq_r,
         gki_r, gvi_r, fi_r) = refs[:19]
        gt_r, gw_r, gb_r, gk_r, gv_r, turned_r = refs[19:]
        gk_r[...] = gki_r[...]
        gv_r[...] = gvi_r[...]
        gt_r[...] = fi_r[...]
        turned_r[...] = x_r[...].T
        key_back_phase(
            kf_r, v_r, li_r, dn_r, dd_r, pa_r, fu_r, lo_r, hi_r, gk_r, gv_r, pairs, 0, pairs, head_dim
        )
        for group in range(width // CHUNK):
            qkv_back_phase(
                turned_r, w_r, o_r, q_r, k_r, qf_r, kf_r, gq_r, gk_r, gv_r, gt_r, gw_r, gb_r, group, head_dim
            )

    gtok, gw_qkv, small = call(
        body_five,
        [(wide, F32), ((width, 4 * width), F32), ((16, width), F32)],
        (x, w_qkv, omega, q, k, v, qf, kf, line, dnum, dden, past, future, low_in, high_in, gq, gk, gv,
         first),
        (pltpu.VMEM(ext, F32), pltpu.VMEM(ext, F32), pltpu.VMEM((width, rows), BF16)),
    )
    gw_qkv = in_parts(gw_qkv[:, width:])
    gb_qkv = in_parts(small[8 : 8 + width // CHUNK].reshape(1, -1))
    summed = lax.psum((gw_qkv, gb_qkv[0], gw_out, vec, gtable), ("row", "seq"))
    gw_qkv, gb_qkv, gw_out, vec, gtable = summed
    return (
        layer[None], gtok[None], gw_qkv, gb_qkv, gw_out, vec[5], vec[3], vec[4], grad_w_up, grad_b_up,
        grad_w_down, vec[2], vec[0], vec[1], gtable,
    )


def solution(mesh):
    placed = (
        P("row", "seq", None), P("row", "seq", None), P(), P(), P(), P(), P(), P(), P(None, "seq"),
        P("seq"), P("seq", None), P(), P(), P(), P(), P(), P(),
    )
    return jax.shard_map(
        shards,
        mesh=mesh,
        in_specs=placed,
        out_specs=(
            P("row", "seq", None), P("row", "seq", None), P(), P(), P(), P(), P(), P(), P(None, "seq"),
            P("seq"), P("seq", None), P(), P(), P(), P(),
        ),
        check_vma=False,
    )
```

```python
import functools
import math

import jax
import jax.numpy as jnp
from jax import lax
from jax.experimental import pallas as pl
from jax.experimental.pallas import tpu as pltpu
from jax.sharding import PartitionSpec as P

WINDOW = 128
LANES = 128
LINE = 512
CHUNK = 256
EPS = 1e-06
CENTER = 7.5
SPREAD = math.sqrt(21.25)
ROOT_HALF = 0.7071067811865476
INV_ROOT_TAU = 0.3989422804014327
MIB = 1 << 20
F32 = jnp.float32
BF16 = jnp.bfloat16


def nn(a, b):
    return lax.dot_general(a, b, (((1,), (0,)), ((), ())), preferred_element_type=F32)


def nt(a, b):
    return lax.dot_general(a, b, (((1,), (1,)), ((), ())), preferred_element_type=F32)


def tn(a, b):
    return lax.dot_general(a, b, (((0,), (0,)), ((), ())), preferred_element_type=F32)


def halves(values):
    upper = values.astype(BF16)
    return upper, (values - upper.astype(F32)).astype(BF16)


def block_ones(size, head_dim):
    rows = lax.broadcasted_iota(jnp.int32, (size, size), 0) // head_dim
    cols = lax.broadcasted_iota(jnp.int32, (size, size), 1) // head_dim
    return jnp.where(rows == cols, 1.0, 0.0)


def head_sums(values, ones):
    upper, lower = halves(values)
    return nn(upper, ones) + nn(lower, ones)


def first_half(shape):
    return lax.broadcasted_iota(jnp.int32, shape, len(shape) - 1) < LANES // 2


def both_heads(pair):
    first = first_half((1, LANES))
    mask_a = jnp.where(first, 1.0, 0.0).astype(pair.dtype)
    mask_b = jnp.where(first, 0.0, 1.0).astype(pair.dtype)
    return jnp.concatenate([pair * mask_a, pair * mask_b], 0)


def per_head(stacked):
    rows = stacked.shape[0] // 2
    return jnp.where(first_half((rows, LANES)), stacked[:rows], stacked[rows:])


def compact(full):
    half = LANES // 2
    return jnp.where(first_half((half, LANES)), full[:half], full[half:])


def expand(small, ones):
    return jnp.concatenate([small, small], 0) * ones


def block_state(keys, values):
    return compact(tn(keys, values)), jnp.sum(keys.astype(F32), 0, keepdims=True)


def coef_tile(line_ref, pair):
    tiles = []
    for head in range(2):
        row = line_ref[pl.ds(2 * pair + head, 1), :]
        wide = pltpu.roll(
            jnp.broadcast_to(row, (WINDOW, LINE)), LINE - WINDOW + 1, 1, stride=1, stride_axis=0
        )
        tiles.append(wide[:, : 3 * WINDOW])
    return jnp.concatenate(tiles, 0)


def far_coefs(line_ref, pair):
    first = first_half((1, LANES))
    row_a = line_ref[pl.ds(2 * pair, 1), :]
    row_b = line_ref[pl.ds(2 * pair + 1, 1), :]
    left = jnp.where(first, row_a[:, 0:1], row_b[:, 0:1])
    right = jnp.where(first, row_a[:, LINE - 2 : LINE - 1], row_b[:, LINE - 2 : LINE - 1])
    return left, right


def unskew_sum(tile):
    rows = tile.shape[0]
    padded = jnp.concatenate([tile, jnp.zeros((rows, LINE - tile.shape[1]), F32)], 1)
    while rows > 8:
        rows = rows // 2
        padded = pltpu.roll(padded[:rows], rows, 1) + padded[rows:]
    while rows > 1:
        rows = rows // 2
        padded = pltpu.roll(padded[:rows], rows, 1) + padded[rows:]
    return padded


def lanes(pair):
    return pl.ds(pl.multiple_of(pair * LANES, LANES), LANES)


def qkv_phase(x_ref, w_ref, b_ref, omega_ref, parts, head_dim):
    width = x_ref.shape[1]
    x = x_ref[...]
    ones = block_ones(CHUNK, head_dim).astype(BF16)
    factor = head_dim ** (-0.25) / SPREAD
    for part, low_ref, feat_ref in parts:
        for chunk in range(width // CHUNK):
            cols = slice(chunk * CHUNK, (chunk + 1) * CHUNK)
            wide = slice(part * width + chunk * CHUNK, part * width + (chunk + 1) * CHUNK)
            low = (nn(x, w_ref[:, wide]) + b_ref[part][:, cols]).astype(BF16)
            low_ref[:, cols] = low
            if feat_ref is not None:
                projected = nn(low, omega_ref[chunk]) * factor
                widened = low.astype(F32)
                half_norm = head_sums(widened * widened, ones) * (0.5 * head_dim ** (-0.5))
                feat_ref[:, cols] = (
                    jnp.exp(projected - half_norm) * head_dim ** (-0.5)
                ).astype(BF16)


def line_phase(bucket_ref, table_ref, line_ref):
    buckets = table_ref.shape[1]
    one_hot = jnp.where(
        lax.broadcasted_iota(jnp.int32, (buckets, LINE), 0) == bucket_ref[...].astype(jnp.int32), 1.0, 0.0
    )
    logs = lax.dot_general(
        table_ref[...],
        one_hot,
        (((1,), (0,)), ((), ())),
        precision=lax.Precision.HIGHEST,
        preferred_element_type=F32,
    )
    line_ref[...] = jnp.exp(logs)


def state_phase(kf_ref, v_ref, num_ref, den_ref, total_ref, pairs):
    blocks = kf_ref.shape[0] // WINDOW
    half = LANES // 2

    @pl.loop(0, pairs)
    def _(pair):
        total = jnp.zeros((half, LANES), F32)
        total_den = jnp.zeros((1, LANES), F32)
        for block in range(blocks):
            rows = slice(block * WINDOW, (block + 1) * WINDOW)
            num, den = block_state(kf_ref[rows, lanes(pair)], v_ref[rows, lanes(pair)])
            num_ref[pair * blocks + block] = num
            den_ref[pl.ds(pair * blocks + block, 1), :] = den
            total = total + num
            total_den = total_den + den
        total_ref[pl.ds(pl.multiple_of(pair * half, half), half), :] = total
        total_ref[pl.ds(pairs * half + pair, 1), :] = total_den


def band_forward_phase(qf_ref, ke_ref, ve_ref, line_ref, out_ref, denom_ref, first, last):
    blocks = qf_ref.shape[0] // WINDOW

    @pl.loop(first, last)
    def _(pair):
        cols = lanes(pair)
        coef = coef_tile(line_ref, pair)
        for block in range(blocks):
            rows = slice(block * WINDOW, (block + 1) * WINDOW)
            window = slice(block * WINDOW, (block + 3) * WINDOW)
            scores = nt(both_heads(qf_ref[rows, cols]), ke_ref[window, cols])
            weights = (coef * scores).astype(BF16)
            values = ve_ref[window, cols]
            summed = nn(weights, jnp.concatenate([values, jnp.ones_like(values)], 1))
            out_ref[rows, cols] = per_head(summed[:, :LANES])
            denom_ref[rows, cols] = per_head(summed[:, LANES:])


def far_forward_phase(
    qf_ref, ke_ref, ve_ref, line_ref, num_ref, den_ref, before_ref, after_ref,
    out_ref, low_ref, denom_ref, left_ref, right_ref, left_den_ref, right_den_ref, pairs, head_dim,
):
    blocks = qf_ref.shape[0] // WINDOW
    half = LANES // 2

    @pl.loop(0, pairs)
    def _(pair):
        ones_f32 = block_ones(LANES, head_dim)
        ones = ones_f32.astype(BF16)
        cols = lanes(pair)
        left_coef, right_coef = far_coefs(line_ref, pair)
        state_rows = pl.ds(pl.multiple_of(pair * half, half), half)
        den_row = pl.ds(pairs * half + pair, 1)
        edge_low = block_state(ke_ref[:WINDOW, cols], ve_ref[:WINDOW, cols])
        edge_high = block_state(
            ke_ref[(blocks + 1) * WINDOW :, cols], ve_ref[(blocks + 1) * WINDOW :, cols]
        )
        past = (before_ref[state_rows, :], before_ref[den_row, :])
        future = (after_ref[state_rows, :], after_ref[den_row, :])

        def block_of(block):
            index = pair * blocks + block
            return num_ref[index], den_ref[pl.ds(index, 1), :]

        def add(one, two, sign=1.0):
            return tuple(a + sign * b for a, b in zip(one, two))

        lefts = [add(past, edge_low, -1.0), past]
        for block in range(2, blocks):
            lefts.append(add(lefts[-1], block_of(block - 2)))
        rights = [add(future, edge_high, -1.0), future]
        for block in range(2, blocks):
            rights.append(add(rights[-1], block_of(blocks + 1 - block)))
        rights = rights[::-1]
        for block in range(blocks):
            rows = slice(block * WINDOW, (block + 1) * WINDOW)
            index = pair * blocks + block
            query = qf_ref[rows, cols]
            left, left_den = lefts[block]
            right, right_den = rights[block]
            left_ref[index] = left
            right_ref[index] = right
            left_den_ref[pl.ds(index, 1), :] = left_den
            right_den_ref[pl.ds(index, 1), :] = right_den
            upper, lower = halves(expand(left_coef * left + right_coef * right, ones_f32))
            numer = out_ref[rows, cols] + nn(query, upper) + nn(query, lower)
            den_far = left_coef * left_den + right_coef * right_den
            denom = denom_ref[rows, cols] + head_sums(query.astype(F32) * den_far, ones)
            out = numer / denom
            out_ref[rows, cols] = out
            low_ref[rows, cols] = out.astype(BF16)
            denom_ref[rows, cols] = denom


def norm_parts(values):
    center = values - jnp.mean(values, -1, keepdims=True)
    inv_scale = lax.rsqrt(jnp.mean(center * center, -1, keepdims=True) + EPS)
    return center * inv_scale, inv_scale


def out_phase(x_ref, low_ref, w_ref, b_ref, normed_ref, scale_ref):
    first_sum = x_ref[...].astype(F32) + nn(low_ref[...], w_ref[...]) + b_ref[...].astype(F32)
    normed, inv_scale = norm_parts(first_sum)
    normed_ref[...] = normed
    scale_ref[...] = jnp.broadcast_to(inv_scale, scale_ref.shape)


def norm_back(grad_out, normed, inv_scale, gain):
    grad_normed = grad_out * gain
    centered = grad_normed - jnp.mean(grad_normed, -1, keepdims=True)
    return inv_scale * (centered - normed * jnp.mean(grad_normed * normed, -1, keepdims=True))


def ffn_phase(
    normed_ref, scale_ref, gain_one_ref, shift_one_ref, up_ref, b_up_ref, down_ref, b_down_ref,
    gain_two_ref, shift_two_ref, cot_ref, layer_ref, first_ref, low_ref, vec_ref, gup_ref, gdown_ref,
    gbias_ref, act_ref, slope_ref, acc_ref,
):
    shards = up_ref.shape[0]
    normed_one = normed_ref[...]
    hidden_one = normed_one * gain_one_ref[...] + shift_one_ref[...]
    hidden = hidden_one.astype(BF16)
    acc_ref[...] = hidden_one + b_down_ref[...].astype(F32)

    @pl.loop(0, shards)
    def _(shard):
        pre = nn(hidden, up_ref[shard]) + b_up_ref[shard, 0:1, :].astype(F32)
        phi = 0.5 * (1.0 + lax.erf(pre * ROOT_HALF))
        act = (pre * phi).astype(BF16)
        act_ref[shard] = act
        slope_ref[shard] = (phi + pre * INV_ROOT_TAU * jnp.exp(-0.5 * pre * pre)).astype(BF16)
        acc_ref[...] += nt(act, down_ref[shard])

    normed_two, scale_two = norm_parts(acc_ref[...])
    layer_ref[...] = (normed_two * gain_two_ref[...] + shift_two_ref[...]).astype(BF16)
    cot = cot_ref[...].astype(F32)
    grad_second = norm_back(cot, normed_two, scale_two, gain_two_ref[...])
    grad_ffn = grad_second.astype(BF16)
    vec_ref[0:1, :] = jnp.sum(cot * normed_two, 0, keepdims=True)
    vec_ref[1:2, :] = jnp.sum(cot, 0, keepdims=True)
    vec_ref[2:3, :] = jnp.sum(grad_ffn.astype(F32), 0, keepdims=True)
    acc_ref[...] = grad_second
    grad_turned = grad_ffn.T
    hidden_turned = hidden.T

    @pl.loop(0, shards)
    def _(shard):
        grad_act = nn(grad_ffn, down_ref[shard])
        grad_pre = (grad_act * slope_ref[shard].astype(F32)).astype(BF16)
        gdown_ref[shard] = nn(grad_turned, act_ref[shard]).astype(BF16)
        gup_ref[shard] = nn(hidden_turned, grad_pre).astype(BF16)
        gbias_ref[shard] = jnp.broadcast_to(
            jnp.sum(grad_pre.astype(F32), 0, keepdims=True), gbias_ref.shape[1:]
        )
        acc_ref[...] += nt(grad_pre, up_ref[shard])

    grad_hidden = acc_ref[...]
    grad_first = norm_back(grad_hidden, normed_one, scale_ref[:, 0:1], gain_one_ref[...])
    grad_low = grad_first.astype(BF16)
    first_ref[...] = grad_first
    low_ref[...] = grad_low
    vec_ref[3:4, :] = jnp.sum(grad_hidden * normed_one, 0, keepdims=True)
    vec_ref[4:5, :] = jnp.sum(grad_hidden, 0, keepdims=True)
    vec_ref[5:6, :] = jnp.sum(grad_low.astype(F32), 0, keepdims=True)
    vec_ref[6:8, :] = jnp.zeros((2, vec_ref.shape[1]), F32)


def out_back_phase(
    glow_ref, w_ref, low_ref, out_ref, denom_ref, qf_ref, gnum_ref, gden_ref, gw_ref, dnum_ref,
    dden_ref, total_ref, pairs, head_dim,
):
    rows_all = glow_ref.shape[0]
    blocks = rows_all // WINDOW
    half = LANES // 2
    ones = block_ones(LANES, head_dim).astype(BF16)
    grad_low = glow_ref[...]
    gw_ref[...] = tn(low_ref[...], grad_low).astype(gw_ref.dtype)
    for pair in range(pairs):
        cols = slice(pair * LANES, (pair + 1) * LANES)
        grad_attn = nt(grad_low, w_ref[cols, :])
        inverse = 1.0 / denom_ref[:, cols]
        grad_num = (grad_attn * inverse).astype(BF16)
        grad_den = -head_sums(grad_num.astype(F32) * out_ref[:, cols], ones)
        gnum_ref[:, cols] = grad_num
        gden_ref[:, cols] = grad_den
        total = jnp.zeros((half, LANES), F32)
        total_den = jnp.zeros((1, LANES), F32)
        for block in range(blocks):
            rows = slice(block * WINDOW, (block + 1) * WINDOW)
            query = qf_ref[rows, cols]
            num = compact(tn(query, grad_num[rows]))
            den = jnp.sum(query.astype(F32) * grad_den[rows], 0, keepdims=True)
            dnum_ref[pair * blocks + block] = num
            dden_ref[pair * blocks + block : pair * blocks + block + 1, :] = den
            total = total + num
            total_den = total_den + den
        total_ref[pair * half : (pair + 1) * half, :] = total
        total_ref[pairs * half + pair : pairs * half + pair + 1, :] = total_den


def row_grads(keys, values, num, den, ones_f32):
    upper, lower = halves(expand(num, ones_f32))
    grad_keys = nt(values, upper) + nt(values, lower) + den
    grad_values = nn(keys, upper) + nn(keys, lower)
    return grad_keys, grad_values


def band_backward_phase(
    qf_ref, ke_ref, ve_ref, line_ref, gnum_ref, gden_ref, dnum_ref, dden_ref, left_ref, right_ref,
    left_den_ref, right_den_ref, gq_ref, gk_ref, gv_ref, gline_ref, coef_grad_ref, start, stop, first_col, head_dim,
):
    blocks = qf_ref.shape[0] // WINDOW

    @pl.loop(start, stop)
    def _(pair):
        ones_f32 = block_ones(LANES, head_dim)
        cols = lanes(pair)
        out = lanes(pair - first_col)
        coef = coef_tile(line_ref, pair)
        left_coef, right_coef = far_coefs(line_ref, pair)
        gk_ref[:, out] = jnp.zeros((gk_ref.shape[0], LANES), F32)
        gv_ref[:, out] = jnp.zeros((gv_ref.shape[0], LANES), F32)
        coef_grad_ref[...] = jnp.zeros(coef_grad_ref.shape, F32)
        left_sum = jnp.zeros((1, LANES), F32)
        right_sum = jnp.zeros((1, LANES), F32)
        for block in range(blocks):
            rows = slice(block * WINDOW, (block + 1) * WINDOW)
            window = slice(block * WINDOW, (block + 3) * WINDOW)
            index = pair * blocks + block
            query = qf_ref[rows, cols]
            keys = ke_ref[window, cols]
            values = ve_ref[window, cols]
            grad_num = gnum_ref[rows, cols]
            grad_den = gden_ref[rows, cols]
            queries = both_heads(query)
            grads = both_heads(grad_num)
            weights = coef * nt(queries, keys)
            den_column = jnp.concatenate(
                [grad_den[:, 0:1], grad_den[:, LANES // 2 : LANES // 2 + 1]], 0
            )
            grad_weights = nt(grads, values) + den_column
            coef_grad_ref[...] += grad_weights * weights
            grad_scores = (coef * grad_weights).astype(BF16)
            gv_ref[window, out] += tn(weights.astype(BF16), grads)
            gk_ref[window, out] += tn(grad_scores, queries)
            grad_query = per_head(nn(grad_scores, keys))
            left, right = left_ref[index], right_ref[index]
            left_den = left_den_ref[pl.ds(index, 1), :]
            right_den = right_den_ref[pl.ds(index, 1), :]
            upper, lower = halves(expand(left_coef * left + right_coef * right, ones_f32))
            den_far = left_coef * left_den + right_coef * right_den
            grad_query = grad_query + nt(grad_num, upper) + nt(grad_num, lower) + grad_den * den_far
            gq_ref[rows, cols] = grad_query
            dnum = dnum_ref[index]
            dden = dden_ref[pl.ds(index, 1), :]
            left_sum = left_sum + jnp.sum(dnum * left, 0, keepdims=True) + dden * left_den
            right_sum = right_sum + jnp.sum(dnum * right, 0, keepdims=True) + dden * right_den
        for edge, block, scale in ((0, 0, left_coef), (blocks + 1, blocks - 1, right_coef)):
            rows = slice(edge * WINDOW, (edge + 1) * WINDOW)
            index = pair * blocks + block
            edge_k, edge_v = row_grads(
                ke_ref[rows, cols],
                ve_ref[rows, cols],
                scale * dnum_ref[index],
                scale * dden_ref[pl.ds(index, 1), :],
                ones_f32,
            )
            gk_ref[rows, out] -= edge_k
            gv_ref[rows, out] -= edge_v
        first = first_half((1, LANES))
        positions = lax.broadcasted_iota(jnp.int32, (1, LINE), 1)
        left_all = left_coef * left_sum
        right_all = right_coef * right_sum
        for head in range(2):
            keep = first if head == 0 else jnp.logical_not(first)
            left_one = jnp.sum(jnp.where(keep, left_all, 0.0), 1, keepdims=True)
            right_one = jnp.sum(jnp.where(keep, right_all, 0.0), 1, keepdims=True)
            line = unskew_sum(coef_grad_ref[head * WINDOW : (head + 1) * WINDOW, :])
            line = line + jnp.where(positions == 0, left_one, 0.0)
            line = line + jnp.where(positions == LINE - 2, right_one, 0.0)
            gline_ref[pl.ds(2 * pair + head, 1), :] = line


def key_back_phase(
    kf_ref, v_ref, line_ref, dnum_ref, dden_ref, past_ref, future_ref, low_in_ref, high_in_ref,
    gk_ref, gv_ref, pairs, start, stop, head_dim,
):
    blocks = kf_ref.shape[0] // WINDOW
    half = LANES // 2

    @pl.loop(start, stop)
    def _(pair):
        ones_f32 = block_ones(LANES, head_dim)
        cols = lanes(pair)
        left_coef, right_coef = far_coefs(line_ref, pair)
        state_rows = pl.ds(pl.multiple_of(pair * half, half), half)
        den_row = pl.ds(pairs * half + pair, 1)
        nums = [dnum_ref[pair * blocks + block] for block in range(blocks)]
        dens = [dden_ref[pl.ds(pair * blocks + block, 1), :] for block in range(blocks)]
        for block in range(blocks):
            num_left, den_left = future_ref[state_rows, :], future_ref[den_row, :]
            num_right, den_right = past_ref[state_rows, :], past_ref[den_row, :]
            for other in range(blocks):
                if other >= block + 2:
                    num_left, den_left = num_left + nums[other], den_left + dens[other]
                if other <= block - 2:
                    num_right, den_right = num_right + nums[other], den_right + dens[other]
            rows = slice(block * WINDOW, (block + 1) * WINDOW)
            outer = slice((block + 1) * WINDOW, (block + 2) * WINDOW)
            far_k, far_v = row_grads(
                kf_ref[rows, cols],
                v_ref[rows, cols],
                left_coef * num_left + right_coef * num_right,
                left_coef * den_left + right_coef * den_right,
                ones_f32,
            )
            if block == 0:
                far_k = far_k + low_in_ref[0, :, cols].astype(F32)
                far_v = far_v + low_in_ref[1, :, cols].astype(F32)
            if block == blocks - 1:
                far_k = far_k + high_in_ref[0, :, cols].astype(F32)
                far_v = far_v + high_in_ref[1, :, cols].astype(F32)
            gk_ref[outer, cols] += far_k
            gv_ref[outer, cols] += far_v


def qkv_back_phase(
    turned_ref, w_ref, omega_ref, q_ref, k_ref, qf_ref, kf_ref, gq_ref, gk_ref, gv_ref, gtok_ref, parts_ref,
    small_ref, group, head_dim,
):
    width, rows_all = turned_ref.shape
    own = slice(WINDOW, WINDOW + rows_all)
    ones = block_ones(CHUNK, head_dim).astype(BF16)
    factor = head_dim ** (-0.25) / SPREAD
    cols = slice(group * CHUNK, (group + 1) * CHUNK)
    omega = omega_ref[group]
    lows = []
    total = gtok_ref[...]
    for part, low_ref, feat_ref, grad in (
        (0, q_ref, qf_ref, gq_ref[:, cols]), (1, k_ref, kf_ref, gk_ref[own, cols]), (2, None, None, gv_ref[own, cols]),
    ):
        if part < 2:
            inner_up, inner_low = halves(grad * feat_ref[:, cols].astype(F32))
            projected = (nt(inner_up, omega) + nt(inner_low, omega)) * factor
            sums = nn(inner_up, ones) + nn(inner_low, ones)
            grad = projected - sums * head_dim ** (-0.5) * low_ref[:, cols].astype(F32)
        low = grad.astype(BF16)
        lows.append(low)
        total = total + nt(low, w_ref[:, part * width + group * CHUNK : part * width + (group + 1) * CHUNK])
    gtok_ref[...] = total
    joined = jnp.concatenate(lows, 1)
    small_ref[8 + group : 9 + group, :] = jnp.sum(joined.astype(F32), 0, keepdims=True)
    parts_ref[:, (group + 1) * width : (group + 2) * width] = nn(turned_ref[...], joined).astype(parts_ref.dtype)


def table_phase(gline_ref, bucket_ref, buckets):
    one_hot = jnp.where(
        lax.broadcasted_iota(jnp.int32, (buckets, LINE), 0) == bucket_ref[...].astype(jnp.int32), 1.0, 0.0
    )
    return lax.dot_general(
        gline_ref[...],
        one_hot,
        (((1,), (1,)), ((), ())),
        precision=lax.Precision.HIGHEST,
        preferred_element_type=F32,
    )


MESH = pl.DeviceIdType.MESH


def guarded(when, action):
    if when is None:
        action()
    else:
        pl.when(when)(action)


class Place:
    def __init__(self, shards):
        self.row, self.seq = lax.axis_index("row"), lax.axis_index("seq")
        self.count_b = 2
        self.count_a = shards // self.count_b
        self.shards = shards
        self.x, self.core = self.row // 2, self.row % 2
        self.a, self.b = self.seq // self.count_b, self.seq % self.count_b
        self.is_first, self.is_last = self.seq == 0, self.seq == shards - 1
        self.not_first, self.not_last = self.seq > 0, self.seq < shards - 1

    def at(self, x=None, core=None, a=None, b=None):
        x = self.x if x is None else x
        core = self.core if core is None else core
        a = self.a if a is None else a
        b = self.b if b is None else b
        return (x * 2 + core, a * self.count_b + b)

    def beside(self, seq):
        return (self.row, seq)

    def shard(self, offset):
        return lax.rem(self.a + offset, self.count_a)

    def nearest(self, step):
        orders = []
        for a in range(self.count_a):
            orders.append(sorted(range(self.count_a), key=lambda other: (abs(other - a), other)))
        index = jnp.int32(orders[0][step])
        for a in range(1, self.count_a):
            index = jnp.where(self.a == a, orders[a][step], index)
        return index


class Sends:
    def __init__(self):
        self.started = []

    def send(self, src, dst, send_sem, recv_sem, device, when=None):
        copy = pltpu.make_async_remote_copy(
            src_ref=src, dst_ref=dst, send_sem=send_sem, recv_sem=recv_sem, device_id=device,
            device_id_type=MESH,
        )
        guarded(when, copy.start)
        self.started.append((when, copy))

    def drain(self):
        for when, copy in self.started:
            guarded(when, copy.wait_send)
        self.started = []


def arrive(dst, sem, device, when=None):
    copy = pltpu.make_async_remote_copy(
        src_ref=dst, dst_ref=dst, send_sem=sem, recv_sem=sem, device_id=device, device_id_type=MESH
    )
    guarded(when, copy.wait_recv)


class WeightGather:
    def __init__(self, place, sends, mats, sems):
        self.place, self.sends, self.mats = place, sends, mats
        self.z_send, self.z_recv, self.y_send, self.y_recv, self.x_send, self.x_recv, self.c_send, self.c_recv = sems
        self.third = mats.shape[3] // 3

    def outer(self, a, b, x, core=None):
        core = self.place.core if core is None else core
        return self.mats.at[core, a, b, pl.ds(pl.multiple_of(x * 2 * self.third, self.third), self.third), :]

    def middle(self, a, b, core=None):
        core = self.place.core if core is None else core
        return self.mats.at[core, a, b, pl.ds(self.third, self.third), :]

    def both(self, a, b, core=None):
        return ((0, self.outer(a, b, self.place.x, core)), (1, self.middle(a, b, core)))

    def along_a(self, step):
        p = self.place
        a = p.nearest(step)
        for kind, here in self.both(a, p.b):
            if step > 0:
                arrive(here, self.z_recv.at[kind, a], p.at())
            for out, move in ((0, 1), (1, -1)):
                target = p.a + move
                ok = jnp.logical_and(target >= 0, target <= p.count_a - 1)
                if step > 0:
                    ok = jnp.logical_and(ok, a < p.a if move == 1 else a > p.a)
                self.sends.send(
                    here, here, self.z_send.at[out, kind, a], self.z_recv.at[kind, a],
                    p.at(a=jnp.clip(target, 0, p.count_a - 1)), ok,
                )
            self.sends.send(here, here, self.y_send.at[kind, a], self.y_recv.at[kind, a], p.at(b=1 - p.b))
            if step > 0:
                self.pass_on(kind, 0, a, here)

    def pass_on(self, kind, column, a, here):
        p = self.place
        if kind == 0:
            self.sends.send(
                here, here, self.x_send.at[column, a], self.x_recv.at[column, a], p.at(x=1 - p.x)
            )
        self.sends.send(
            here, here, self.c_send.at[kind, column, a], self.c_recv.at[kind, column, a], p.at(core=1 - p.core)
        )

    def along_b(self, step):
        p = self.place
        a = p.nearest(step)
        for kind, here in self.both(a, 1 - p.b):
            arrive(here, self.y_recv.at[kind, a], p.at())
            self.pass_on(kind, 1, a, here)

    def columns(self, step):
        p = self.place
        return ((1, 1 - p.b),) if step == 0 else ((0, p.b), (1, 1 - p.b))

    def along_x(self, step):
        p = self.place
        a = p.nearest(step)
        for column, b in self.columns(step):
            here = self.outer(a, b, 1 - p.x)
            arrive(here, self.x_recv.at[column, a], p.at())
            self.sends.send(
                here, here, self.c_send.at[2, column, a], self.c_recv.at[2, column, a], p.at(core=1 - p.core)
            )

    def finish(self, step):
        p = self.place
        a = p.nearest(step)
        other = 1 - p.core
        for column, b in self.columns(step):
            for kind, here in self.both(a, b, other) + ((2, self.outer(a, b, 1 - p.x, other)),):
                arrive(here, self.c_recv.at[kind, column, a], p.at())


def gather_sems(count_a):
    dma = pltpu.SemaphoreType.DMA
    return [
        dma((2, 2, count_a)), dma((2, count_a)), dma((2, count_a)), dma((2, count_a)),
        dma((2, count_a)), dma((2, count_a)), dma((3, 2, count_a)), dma((3, 2, count_a)),
    ]


class StateGather:
    def __init__(self, place, sends, states, sems):
        self.place, self.sends, self.states = place, sends, states
        self.z_send, self.z_recv, self.y_send, self.y_recv = sems

    def source(self, offset):
        p = self.place
        return lax.rem(p.a + (p.count_a - offset), p.count_a)

    def along_a(self):
        p = self.place
        here = self.states.at[p.a, p.b]
        for offset in range(1, p.count_a):
            self.sends.send(
                here, here, self.z_send.at[offset], self.z_recv.at[offset], p.at(a=p.shard(offset))
            )
        self.sends.send(here, here, self.y_send.at[0], self.y_recv.at[0], p.at(b=1 - p.b))

    def along_b(self):
        p = self.place
        for offset in range(1, p.count_a):
            here = self.states.at[self.source(offset), p.b]
            arrive(here, self.z_recv.at[offset], p.at())
            self.sends.send(here, here, self.y_send.at[offset], self.y_recv.at[offset], p.at(b=1 - p.b))

    def finish(self):
        p = self.place
        for offset in range(p.count_a):
            arrive(self.states.at[self.source(offset), 1 - p.b], self.y_recv.at[offset], p.at())


def state_sems(count_a):
    return [pltpu.SemaphoreType.DMA((count_a,)) for _ in range(4)]


def prefix_phase(place, states, before_ref, after_ref):
    before = jnp.zeros(before_ref.shape, F32)
    after = jnp.zeros(after_ref.shape, F32)
    for a in range(place.count_a):
        for b in range(place.count_b):
            seq = a * place.count_b + b
            value = states[a, b].astype(F32)
            before = before + jnp.where(seq < place.seq, 1.0, 0.0) * value
            after = after + jnp.where(seq > place.seq, 1.0, 0.0) * value
    before_ref[...] = before
    after_ref[...] = after


class GradScatter:
    def __init__(self, place, sends, grads, total, lands, sems):
        self.place, self.sends, self.grads, self.total = place, sends, grads, total
        self.core_land, self.stage, self.x_land, self.y_land, self.z_land, self.last_land = lands
        (self.copy, self.c_send, self.c_recv, self.x_send, self.x_recv, self.y_send, self.y_recv, self.z_send,
         self.z_recv, self.l_send, self.l_recv) = sems
        self.third = grads.shape[3] // 3

    def outer(self, x):
        return pl.ds(pl.multiple_of(x * 2 * self.third, self.third), self.third)

    def window(self):
        return pl.ds(pl.multiple_of(self.place.x * self.third, self.third), 2 * self.third)

    def start(self, offset):
        p = self.place
        a = p.shard(offset)
        self.sends.send(
            self.grads.at[1 - p.core, a], self.core_land.at[a], self.c_send.at[offset],
            self.c_recv.at[offset], p.at(core=1 - p.core),
        )

    def add(self, ref, land):
        ref[...] = (ref[...].astype(F32) + land[...].astype(F32)).astype(BF16)

    def staged(self, offset):
        return pltpu.make_async_copy(
            self.core_land.at[self.place.shard(offset)], self.stage, self.copy.at[offset]
        )

    def fetch(self, offset):
        arrive(self.core_land.at[self.place.shard(offset)], self.c_recv.at[offset], self.place.at())
        self.staged(offset).start()

    def chip(self, offset):
        p = self.place
        a = p.shard(offset)
        self.staged(offset).wait()
        self.add(self.grads.at[p.core, a], self.stage)
        self.sends.send(
            self.grads.at[p.core, a, :, self.outer(1 - p.x), :], self.x_land.at[a], self.x_send.at[offset],
            self.x_recv.at[offset], p.at(x=1 - p.x),
        )

    def along_x(self, offset):
        p = self.place
        a = p.shard(offset)
        arrive(self.x_land.at[a], self.x_recv.at[offset], p.at())
        self.add(self.grads.at[p.core, a, :, self.outer(p.x), :], self.x_land.at[a])
        self.sends.send(
            self.grads.at[p.core, a, 1 - p.b, self.window(), :], self.y_land.at[a], self.y_send.at[offset],
            self.y_recv.at[offset], p.at(b=1 - p.b),
        )

    def along_b(self, offset):
        p = self.place
        a = p.shard(offset)
        arrive(self.y_land.at[a], self.y_recv.at[offset], p.at())
        mine = self.grads.at[p.core, a, p.b, self.window(), :]
        self.add(mine, self.y_land.at[a])
        if offset:
            self.sends.send(
                mine, self.z_land.at[offset - 1], self.z_send.at[offset], self.z_recv.at[offset], p.at(a=a)
            )

    def along_a(self):
        p = self.place
        own = self.grads.at[p.core, p.a, p.b]
        mine = own.at[self.window(), :]
        total = mine[...].astype(F32)
        for offset in range(1, p.count_a):
            arrive(self.z_land.at[offset - 1], self.z_recv.at[offset], p.at())
            total = total + self.z_land[offset - 1].astype(F32)
        mine[...] = total.astype(BF16)
        middle = pl.ds(self.third, self.third)
        outer = self.outer(p.x)
        self.total[p.core, outer, :] = self.grads[p.core, p.a, p.b, outer, :]
        self.sends.send(
            own.at[middle, :], self.last_land, self.l_send.at[0], self.l_recv.at[0], p.at(x=1 - p.x)
        )
        here = self.total.at[p.core, outer, :]
        self.sends.send(here, here, self.l_send.at[1], self.l_recv.at[1], p.at(x=1 - p.x))

    def last_x(self):
        p = self.place
        middle = pl.ds(self.third, self.third)
        arrive(self.last_land, self.l_recv.at[0], p.at())
        self.total[p.core, middle, :] = (
            self.grads[p.core, p.a, p.b, middle, :].astype(F32) + self.last_land[...].astype(F32)
        ).astype(BF16)
        arrive(self.total.at[p.core, self.outer(1 - p.x), :], self.l_recv.at[1], p.at())
        here = self.total.at[p.core]
        self.sends.send(here, here, self.l_send.at[2], self.l_recv.at[2], p.at(core=1 - p.core))

    def finish(self):
        arrive(self.total.at[1 - self.place.core], self.l_recv.at[2], self.place.at())


def scatter_sems(count_a):
    dma = pltpu.SemaphoreType.DMA
    return [dma((count_a,)) for _ in range(9)] + [dma((3,)), dma((3,))]


class AllReduce:
    def __init__(self, place, sends, parts, result, lands, done, mixed, sems):
        self.place, self.sends, self.parts, self.result = place, sends, parts, result
        self.core_land, self.staged, self.one_land, self.two_land, self.a_land = lands
        self.done, self.mixed = done, mixed
        (self.s_send, self.s_recv, self.z_send, self.z_recv, self.g_send, self.g_recv, self.zg_send, self.zg_recv,
         self.copy) = sems
        self.half = result.shape[1] // 2
        self.quarter = self.half // 2
        self.slim = self.quarter // place.count_a

    def ways(self, index):
        p = self.place
        other_x, other_b = p.at(x=1 - p.x), p.at(b=1 - p.b)
        if index not in self.mixed:
            return p.x, p.b, other_x, other_b
        straight = p.core == 0
        one = tuple(jnp.where(straight, u, w) for u, w in zip(other_x, other_b))
        two = tuple(jnp.where(straight, w, u) for u, w in zip(other_x, other_b))
        return jnp.where(straight, p.x, p.b), jnp.where(straight, p.b, p.x), one, two

    def half_rows(self, core):
        return pl.ds(pl.multiple_of(core * self.half, self.half), self.half)

    def quarter_rows(self, one):
        start = self.place.core * self.half + one * self.quarter
        return pl.ds(pl.multiple_of(start, self.quarter), self.quarter)

    def slim_rows(self, one, a):
        start = self.place.core * self.half + one * self.quarter + a * self.slim
        return pl.ds(pl.multiple_of(start, self.slim), self.slim)

    def push(self, index):
        p = self.place
        blocks = pl.ds(2 * index, 2)
        self.sends.send(
            self.parts.at[blocks, self.half_rows(1 - p.core), :], self.core_land.at[blocks],
            self.s_send.at[0, index], self.s_recv.at[0, index], p.at(core=1 - p.core),
        )

    def add(self, ref, land):
        ref[...] = (ref[...].astype(F32) + land[...].astype(F32)).astype(BF16)

    def stage(self, index, number):
        p = self.place
        one, two, one_device, two_device = self.ways(index)
        blocks = pl.ds(2 * index, 2)
        mine, other = 2 * index + two, 2 * index + 1 - two
        parts, result = self.parts, self.result
        if number == 1:
            land = self.core_land.at[blocks]
            arrive(land, self.s_recv.at[0, index], p.at())
            fetch = pltpu.make_async_copy(land, self.staged, self.copy.at[index])
            fetch.start()
            fetch.wait()
            self.add(parts.at[blocks, self.half_rows(p.core), :], self.staged)
            self.sends.send(
                parts.at[blocks, self.quarter_rows(1 - one), :], self.one_land.at[blocks],
                self.s_send.at[1, index], self.s_recv.at[1, index], one_device,
            )
        elif number == 2:
            land = self.one_land.at[blocks]
            arrive(land, self.s_recv.at[1, index], p.at())
            self.add(parts.at[blocks, self.quarter_rows(one), :], land)
            self.sends.send(
                parts.at[other, self.quarter_rows(one), :], self.two_land.at[index],
                self.s_send.at[2, index], self.s_recv.at[2, index], two_device,
            )
        elif number == 3:
            land = self.two_land.at[index]
            arrive(land, self.s_recv.at[2, index], p.at())
            self.add(parts.at[mine, self.quarter_rows(one), :], land)
            for offset in range(1, p.count_a):
                a = p.shard(offset)
                self.sends.send(
                    parts.at[mine, self.slim_rows(one, a), :], self.a_land.at[index, offset - 1],
                    self.z_send.at[index, offset], self.z_recv.at[index, offset], p.at(a=a),
                )
        elif number == 4:
            rows = self.slim_rows(one, p.a)
            total = parts[mine, rows, :].astype(F32)
            for offset in range(1, p.count_a):
                arrive(self.a_land.at[index, offset - 1], self.z_recv.at[index, offset], p.at())
                total = total + self.a_land[index, offset - 1].astype(F32)
            self.done[index] = total.astype(BF16)
            here = result.at[mine, rows, :]
            pltpu.make_async_copy(self.done.at[index], here, self.copy.at[index]).start()
            for offset in range(1, p.count_a):
                self.sends.send(
                    self.done.at[index], here, self.zg_send.at[index, offset], self.zg_recv.at[index, offset],
                    p.at(a=p.shard(offset)),
                )
        elif number == 5:
            pltpu.make_async_copy(
                self.done.at[index], result.at[mine, self.slim_rows(one, p.a), :], self.copy.at[index]
            ).wait()
            for offset in range(1, p.count_a):
                a = lax.rem(p.a + p.count_a - offset, p.count_a)
                arrive(result.at[mine, self.slim_rows(one, a), :], self.zg_recv.at[index, offset], p.at())
            here = result.at[mine, self.quarter_rows(one), :]
            self.sends.send(here, here, self.g_send.at[0, index], self.g_recv.at[0, index], two_device)
        elif number == 6:
            arrive(result.at[other, self.quarter_rows(one), :], self.g_recv.at[0, index], p.at())
            here = result.at[blocks, self.quarter_rows(one), :]
            self.sends.send(here, here, self.g_send.at[1, index], self.g_recv.at[1, index], one_device)
        elif number == 7:
            arrive(result.at[blocks, self.quarter_rows(1 - one), :], self.g_recv.at[1, index], p.at())
            here = result.at[blocks, self.half_rows(p.core), :]
            self.sends.send(here, here, self.g_send.at[2, index], self.g_recv.at[2, index], p.at(core=1 - p.core))
        elif number == 8:
            arrive(result.at[blocks, self.half_rows(1 - p.core), :], self.g_recv.at[2, index], p.at())


def reduce_sems(chunks, count_a):
    dma = pltpu.SemaphoreType.DMA
    return [
        dma((3, chunks)), dma((3, chunks)), dma((chunks, count_a)), dma((chunks, count_a)),
        dma((3, chunks)), dma((3, chunks)), dma((chunks, count_a)), dma((chunks, count_a)), dma((chunks,)),
    ]


class SmallReduce:
    def __init__(self, place, sends, held, land, sems):
        self.place, self.sends, self.held, self.land = place, sends, held, land
        self.out_sem, self.in_sem = sems
        p = place
        self.devices = [p.at(core=1 - p.core), p.at(x=1 - p.x), p.at(b=1 - p.b)]

    def send(self, step):
        if step < 3:
            self.sends.send(
                self.held.at[step], self.land.at[step], self.out_sem.at[step], self.in_sem.at[step],
                self.devices[step],
            )
            return
        p = self.place
        for offset in range(1, p.count_a):
            self.sends.send(
                self.held.at[3], self.land.at[3 + offset], self.out_sem.at[3 + offset],
                self.in_sem.at[3 + offset], p.at(a=p.shard(offset)),
            )

    def receive(self, step):
        p = self.place
        if step < 3:
            arrive(self.land.at[step], self.in_sem.at[step], p.at())
            self.held[step + 1] = self.held[step] + self.land[step]
            return
        for offset in range(1, p.count_a):
            arrive(self.land.at[3 + offset], self.in_sem.at[3 + offset], p.at())
        self.land[3] = self.held[3]

    def total(self):
        p = self.place
        total = self.land[3 + lax.rem(p.a, p.count_a)]
        for a in range(1, p.count_a):
            total = total + self.land[3 + lax.rem(p.a + p.count_a - a, p.count_a)]
        return total


def halo_phase(x_ref, w_ref, b_ref, omega_ref, k_ref, kv_ref, place, head_dim):
    rows_ext, width = x_ref.shape
    low, high = slice(0, WINDOW), slice(rows_ext - WINDOW, rows_ext)
    x = jnp.concatenate([x_ref[low, :], x_ref[high, :]], 0)
    ones = block_ones(CHUNK, head_dim).astype(BF16)
    factor = head_dim ** (-0.25) / SPREAD
    row = lax.broadcasted_iota(jnp.int32, (2 * WINDOW, 1), 0)
    inside = jnp.logical_or(
        jnp.logical_and(row < WINDOW, place.seq > 0),
        jnp.logical_and(row >= WINDOW, place.seq < place.shards - 1),
    )
    for part in (1, 2):
        for chunk in range(width // CHUNK):
            cols = slice(chunk * CHUNK, (chunk + 1) * CHUNK)
            wide = slice(part * width + chunk * CHUNK, part * width + (chunk + 1) * CHUNK)
            value = (nn(x, w_ref[:, wide]) + b_ref[part][:, cols]).astype(BF16)
            if part == 1:
                k_ref[low, cols], k_ref[high, cols] = value[:WINDOW], value[WINDOW:]
                widened = value.astype(F32)
                half_norm = head_sums(widened * widened, ones) * (0.5 * head_dim ** (-0.5))
                value = jnp.exp(nn(value, omega_ref[chunk]) * factor - half_norm) * head_dim ** (-0.5)
            value = jnp.where(inside, value.astype(F32), 0.0).astype(BF16)
            kv_ref[part - 1, low, cols], kv_ref[part - 1, high, cols] = value[:WINDOW], value[WINDOW:]


def ffn_forward_shard(hidden_ref, mats, a, b, shard, bias_ref, pool, acc_ref):
    rows = hidden_ref.shape[0]
    pre = nn(hidden_ref[...], mats[0, a, b]) + bias_ref[shard, 0:1, :]
    phi = 0.5 * (1.0 + lax.erf(pre * ROOT_HALF))
    act = (pre * phi).astype(BF16)
    pool[shard, 0:rows, :] = act
    pool[shard, rows : 2 * rows, :] = (phi + pre * INV_ROOT_TAU * jnp.exp(-0.5 * pre * pre)).astype(BF16)
    acc_ref[...] += nt(act, mats[1, a, b])


def ffn_backward_shard(grad_ref, grad_turned_ref, hidden_turned_ref, mats, a, b, shard, pool, acc_ref, gbias_ref):
    rows = grad_ref.shape[0]
    grad_act = nn(grad_ref[...], mats[1, a, b])
    grad_pre = (grad_act * pool[shard, rows : 2 * rows, :].astype(F32)).astype(BF16)
    gbias_ref[shard] = jnp.broadcast_to(
        jnp.sum(grad_pre.astype(F32), 0, keepdims=True), gbias_ref.shape[1:]
    )
    acc_ref[...] += nt(grad_pre, mats[0, a, b])
    mats[1, a, b] = nn(grad_turned_ref[...], pool[shard, 0:rows, :]).astype(BF16)
    mats[0, a, b] = nn(hidden_turned_ref[...], grad_pre).astype(BF16)


def row_blocks(rows, body, size=CHUNK):
    @pl.loop(0, rows // size)
    def _(index):
        body(pl.ds(pl.multiple_of(index * size, size), size))


def hidden_phase(
    x_ref, low_ref, w_ref, b_ref, gain_ref, shift_ref, b_down_ref, normed_refs, scale_ref, hidden_ref, turned_ref, acc_ref
):
    def body(rows):
        first_sum = x_ref[rows, :].astype(F32) + nn(low_ref[rows, :], w_ref[...]) + b_ref[...].astype(F32)
        normed, inv_scale = norm_parts(first_sum)
        normed_refs[0][rows, :], normed_refs[1][rows, :], normed_refs[2][rows, :] = jnp.split(normed, 3, 1)
        scale_ref[rows, :] = jnp.broadcast_to(inv_scale, (first_sum.shape[0], scale_ref.shape[1]))
        hidden_one = normed * gain_ref[...] + shift_ref[...]
        hidden = hidden_one.astype(BF16)
        hidden_ref[rows, :] = hidden
        turned_ref[:, rows] = hidden.T
        acc_ref[rows, :] = hidden_one + b_down_ref[...].astype(F32)

    row_blocks(x_ref.shape[0], body)


def middle_phase(acc_ref, cot_ref, gain_two_ref, shift_two_ref, grad_ref, grad_turned_ref, vec_ref):
    def body(rows):
        normed_two, scale_two = norm_parts(acc_ref[rows, :])
        cot = cot_ref[rows, :].astype(F32)
        cot_ref[rows, :] = (normed_two * gain_two_ref[...] + shift_two_ref[...]).astype(BF16)
        grad_second = norm_back(cot, normed_two, scale_two, gain_two_ref[...])
        grad_ffn = grad_second.astype(BF16)
        vec_ref[0:1, :] += jnp.sum(cot * normed_two, 0, keepdims=True)
        vec_ref[1:2, :] += jnp.sum(cot, 0, keepdims=True)
        vec_ref[2:3, :] += jnp.sum(grad_ffn.astype(F32), 0, keepdims=True)
        acc_ref[rows, :] = grad_second
        grad_ref[rows, :] = grad_ffn
        grad_turned_ref[:, rows] = grad_ffn.T

    row_blocks(cot_ref.shape[0], body)


def first_back_phase(acc_ref, normed_refs, scale_ref, gain_one_ref, low_ref, vec_ref):
    def body(rows):
        grad_hidden = acc_ref[rows, :]
        normed = jnp.concatenate([ref[rows, :] for ref in normed_refs], 1)
        grad_first = norm_back(grad_hidden, normed, scale_ref[rows, 0:1], gain_one_ref[...])
        grad_low = grad_first.astype(BF16)
        acc_ref[rows, :] = grad_first
        low_ref[rows, :] = grad_low
        vec_ref[3:4, :] += jnp.sum(grad_hidden * normed, 0, keepdims=True)
        vec_ref[4:5, :] += jnp.sum(grad_hidden, 0, keepdims=True)
        vec_ref[5:6, :] += jnp.sum(grad_low.astype(F32), 0, keepdims=True)

    row_blocks(low_ref.shape[0], body)


def attn_back_phase(glow_ref, w_ref, out_ref, denom_ref, low_ref, qf_ref, dnum_ref, dden_ref, total_ref, pairs, head_dim):
    rows_all = glow_ref.shape[0]
    blocks = rows_all // WINDOW
    half = LANES // 2
    ones = block_ones(LANES, head_dim).astype(BF16)
    grad_low = glow_ref[...]
    for pair in range(pairs):
        cols = slice(pair * LANES, (pair + 1) * LANES)
        grad_attn = nt(grad_low, w_ref[cols, :])
        grad_num = (grad_attn / denom_ref[:, cols]).astype(BF16)
        grad_den = -head_sums(grad_num.astype(F32) * out_ref[:, cols], ones)
        low_ref[:, cols] = grad_num
        denom_ref[:, cols] = grad_den
        total = jnp.zeros((half, LANES), F32)
        total_den = jnp.zeros((1, LANES), F32)
        for block in range(blocks):
            rows = slice(block * WINDOW, (block + 1) * WINDOW)
            query = qf_ref[rows, cols]
            num = compact(tn(query, grad_num[rows]))
            den = jnp.sum(query.astype(F32) * grad_den[rows], 0, keepdims=True)
            dnum_ref[pair * blocks + block] = num
            dden_ref[pair * blocks + block : pair * blocks + block + 1, :] = den
            total = total + num
            total_den = total_den + den
        total_ref[pair * half : (pair + 1) * half, :] = total
        total_ref[pairs * half + pair : pairs * half + pair + 1, :] = total_den


def far_back_phase(ke_ref, ve_ref, line_ref, dnum_ref, dden_ref, past_ref, future_ref, gk_ref, gv_ref, pairs, start, stop, first_col, head_dim):
    blocks = ke_ref.shape[0] // WINDOW - 2
    half = LANES // 2

    @pl.loop(start, stop)
    def _(pair):
        ones_f32 = block_ones(LANES, head_dim)
        cols = lanes(pair)
        out = lanes(pair - first_col)
        left_coef, right_coef = far_coefs(line_ref, pair)
        state_rows = pl.ds(pl.multiple_of(pair * half, half), half)
        den_row = pl.ds(pairs * half + pair, 1)
        nums = [dnum_ref[pair * blocks + block] for block in range(blocks)]
        dens = [dden_ref[pl.ds(pair * blocks + block, 1), :] for block in range(blocks)]
        for block in range(blocks):
            num_left, den_left = future_ref[state_rows, :], future_ref[den_row, :]
            num_right, den_right = past_ref[state_rows, :], past_ref[den_row, :]
            for other in range(blocks):
                if other >= block + 2:
                    num_left, den_left = num_left + nums[other], den_left + dens[other]
                if other <= block - 2:
                    num_right, den_right = num_right + nums[other], den_right + dens[other]
            rows = slice((block + 1) * WINDOW, (block + 2) * WINDOW)
            far_k, far_v = row_grads(
                ke_ref[rows, cols],
                ve_ref[rows, cols],
                left_coef * num_left + right_coef * num_right,
                left_coef * den_left + right_coef * den_right,
                ones_f32,
            )
            gk_ref[rows, out] += far_k
            gv_ref[rows, out] += far_v


def qkv_grad_phase(
    turned_ref, w_ref, omega_ref, q_ref, k_ref, qf_ref, kf_ref, gq_ref, gk_ref, gv_ref, grads_ref, parts, small_ref,
    group, place, head_dim,
):
    width, rows_ext = turned_ref.shape
    rows_all = rows_ext - 2 * WINDOW
    own = slice(WINDOW, WINDOW + rows_all)
    ones = block_ones(CHUNK, head_dim).astype(BF16)
    factor = head_dim ** (-0.25) / SPREAD
    cols = slice(group * CHUNK, (group + 1) * CHUNK)
    omega = omega_ref[group]
    base = group * 3 * CHUNK
    block = parts.shape[2]
    for part, low_ref, feat_ref in ((0, q_ref, qf_ref), (1, k_ref, kf_ref), (2, None, None)):
        out = slice(part * CHUNK, (part + 1) * CHUNK)

        def body(rows):
            if part == 0:
                grad = gq_ref[rows, cols]
            else:
                grad = (gk_ref if part == 1 else gv_ref)[rows, :]
            if part < 2:
                inner_up, inner_low = halves(grad * feat_ref[rows, cols].astype(F32))
                projected = (nt(inner_up, omega) + nt(inner_low, omega)) * factor
                sums = nn(inner_up, ones) + nn(inner_low, ones)
                grad = projected - sums * head_dim ** (-0.5) * low_ref[rows, cols].astype(F32)
            if part > 0:
                row = lax.broadcasted_iota(jnp.int32, (CHUNK, 1), 0) + rows.start
                inside = jnp.logical_and(
                    jnp.logical_or(row >= WINDOW, place.seq > 0),
                    jnp.logical_or(row < rows_ext - WINDOW, place.seq < place.shards - 1),
                )
                grad = jnp.where(inside, grad, 0.0)
            low = grad.astype(BF16)
            if part == 0:
                rows = pl.ds(pl.multiple_of(rows.start + WINDOW, WINDOW), CHUNK)
            grads_ref[rows, out] = low
            small_ref[6 + group : 7 + group, out] += jnp.sum(low.astype(F32), 0, keepdims=True)

        row_blocks(rows_all if part == 0 else rows_ext, body)
        rows = own if part == 0 else slice(0, rows_ext)
        weight = nn(turned_ref[:, rows], grads_ref[rows, out]).astype(BF16)
        start = width + base + part * CHUNK
        done = 0
        while done < CHUNK:
            index, at = (start + done) // block, (start + done) % block
            size = min(CHUNK - done, block - at)
            parts[index, 0:width, at : at + size] = weight[:, done : done + size]
            done += size


def table_grads(gline_ref, bucket_ref, buckets, small_ref):
    heads = gline_ref.shape[0]
    head = lax.broadcasted_iota(jnp.int32, (heads, LANES), 0)
    lane_bucket = lax.broadcasted_iota(jnp.int32, (LANES, LINE), 0)
    total = jnp.zeros((heads, LANES), F32)
    per_row = LANES // buckets
    for place in range(per_row):
        one_hot = jnp.where(lane_bucket - place * buckets == bucket_ref[...].astype(jnp.int32), 1.0, 0.0)
        sums = lax.dot_general(
            gline_ref[...], one_hot, (((1,), (1,)), ((), ())), precision=lax.Precision.HIGHEST,
            preferred_element_type=F32,
        )
        total = total + jnp.where(head % per_row == place, sums, 0.0)
    for index in range(heads // per_row):
        small_ref[13 + index : 14 + index, 0:LANES] = jnp.sum(
            total[index * per_row : (index + 1) * per_row], 0, keepdims=True
        )


def layer_kernel(pairs, head_dim, buckets, shards, *refs):
    x_h, cot_h, up_h, down_h, w_r, omega_r, table_r, wo_r, packed_r = refs[:9]
    layer_h, gtok_h, total_r, small_r, result_h, core_h, ac_h = refs[9:16]
    (x_r, q_r, k_r, qf_r, kv_r, line_r, num_r, den_r, tot_r, states, states_two, before_r, after_r, left_r, right_r,
     lden_r, rden_r, attn_r, denom_r, low_r, scale_r, hidden_r, turned_r, cot_r, acc_r,
     mats, pool, bias_r, gbias_r, gk_r, gv_r, gline_r, cg_r, gqkv_r) = refs[16:50]
    stage_r, xl_r, yl_r, zl_r, ll_r = refs[50:55]
    ac_r, ao_r, at_r, aa_r, done_r, held_r, land_r = refs[55:62]
    sems = refs[62:]
    all_rows = pl.ds(0, q_r.shape[0])
    normed_r = (gk_r.at[0, all_rows], gk_r.at[1, all_rows], gv_r.at[0, all_rows])
    gturned_r = gqkv_r.at[:, all_rows]
    edge_r, tail_r = cot_r.at[pl.ds(0, 2 * WINDOW)], cot_r.at[pl.ds(2 * WINDOW, 2 * WINDOW)]
    w_sems, s_sems, s2_sems, rs_sems = sems[:8], sems[8:12], sems[12:16], sems[16:27]
    ar_sems, sm_sems = sems[27:36], sems[36:38]
    h_send, h_recv, t_send, t_recv, load_sem = sems[38:]
    rows, width = q_r.shape
    half = LANES // 2
    line = [packed_r.at[pl.ds(index, 1)] for index in range(packed_r.shape[0])]
    b_r, bo_r, g1_r, s1_r, bdown_r, g2_r, s2_r = line[:3], *line[3:9]
    bup_r, bucket_r = line[9].at[:, pl.ds(0, up_h.shape[1])], line[10].at[:, pl.ds(0, LINE)]
    own = pl.ds(WINDOW, rows)
    place = Place(shards)
    sends = Sends()
    seq = place.seq
    peers = [place.beside(lax.rem(seq + o, shards)) for o in range(1, shards)]
    peers += [place.at(core=1 - place.core), place.at(x=1 - place.x)]
    barrier = pltpu.get_barrier_semaphore()
    for peer in peers:
        pl.semaphore_signal(barrier, inc=1, device_id=peer, device_id_type=MESH)
    loads = [
        pltpu.make_async_copy(src, dst, load_sem.at[i])
        for i, (src, dst) in enumerate((
            (down_h, hidden_r.at[pl.ds(0, down_h.shape[0])]), (up_h, mats.at[0, place.a, place.b]),
            (x_h, x_r.at[own]), (cot_h, cot_r),
        ))
    ]
    for load in loads:
        load.start()
    gather = WeightGather(place, sends, mats, w_sems)
    keys_gather = StateGather(place, sends, states, s_sems)
    grads_gather = StateGather(place, sends, states_two, s2_sems)
    scatter = GradScatter(place, sends, mats, total_r, (core_h, stage_r, xl_r, yl_r, zl_r, ll_r), rs_sems)
    chunks = done_r.shape[0]
    reduce = AllReduce(place, sends, pool, result_h, (ac_h, ac_r, ao_r, at_r, aa_r), done_r, (chunks - 1,), ar_sems)
    little = SmallReduce(place, sends, held_r, land_r, sm_sems)
    to_right = place.beside(jnp.minimum(seq + 1, shards - 1))
    to_left = place.beside(jnp.maximum(seq - 1, 0))
    low_edge, high_edge = pl.ds(0, WINDOW), pl.ds(rows + WINDOW, WINDOW)

    small_r[...] = jnp.zeros(small_r.shape, F32)
    acc_r[0:WINDOW, :] = jnp.zeros((WINDOW, width), F32)
    acc_r[rows + WINDOW :, :] = jnp.zeros((WINDOW, width), F32)
    loads[0].wait()
    mats[1, place.a, place.b] = hidden_r[0 : down_h.shape[0], :].T
    loads[1].wait()
    loads[2].wait()
    pl.semaphore_wait(barrier, len(peers))
    sends.send(
        x_r.at[pl.ds(rows, WINDOW)], x_r.at[low_edge], h_send.at[0], h_recv.at[0], to_right, place.not_last
    )
    sends.send(
        x_r.at[pl.ds(WINDOW, WINDOW)], x_r.at[high_edge], h_send.at[1], h_recv.at[1], to_left, place.not_first
    )
    gather.along_a(0)

    @pl.when(place.is_first)
    def _():
        x_r[0:WINDOW, :] = jnp.zeros((WINDOW, width), BF16)

    @pl.when(place.is_last)
    def _():
        x_r[rows + WINDOW :, :] = jnp.zeros((WINDOW, width), BF16)

    ke_r, ve_r = kv_r.at[0], kv_r.at[1]
    qkv_phase(
        x_r.at[own], w_r, b_r, omega_r, ((1, k_r.at[own], ke_r.at[own]), (2, ve_r.at[own], None)), head_dim
    )
    tot_r[pairs * half :, :] = jnp.zeros((tot_r.shape[0] - pairs * half, LANES), F32)
    state_phase(ke_r.at[own], ve_r.at[own], num_r, den_r, tot_r, pairs)
    bias_rows = bup_r.shape[1] // LANES
    for index in range(bias_rows):
        at = pairs * (half + 1) + index
        tot_r[at : at + 1, :] = bup_r[:, index * LANES : (index + 1) * LANES].astype(F32)
    states[place.a, place.b] = tot_r[...].astype(BF16)
    keys_gather.along_a()
    gather.along_b(0)
    qkv_phase(x_r.at[own], w_r, b_r, omega_r, ((0, q_r, qf_r),), head_dim)
    gather.along_a(1)
    line_phase(bucket_r, table_r, line_r)
    arrive(x_r.at[low_edge], h_recv.at[0], place.at(), place.not_first)
    arrive(x_r.at[high_edge], h_recv.at[1], place.at(), place.not_last)
    halo_phase(x_r, w_r, b_r, omega_r, k_r, kv_r, place, head_dim)
    gather.along_x(0)
    keys_gather.along_b()
    third = pairs // 3
    band_forward_phase(qf_r, ke_r, ve_r, line_r, attn_r, denom_r, 0, third)
    gather.along_b(1)
    gather.along_a(2)
    band_forward_phase(qf_r, ke_r, ve_r, line_r, attn_r, denom_r, third, 2 * third)
    gather.along_x(1)
    band_forward_phase(qf_r, ke_r, ve_r, line_r, attn_r, denom_r, 2 * third, pairs)
    gather.along_b(2)
    keys_gather.finish()
    prefix_phase(place, states, before_r, after_r)
    for a in range(place.count_a):
        for b in range(place.count_b):
            tail = states[a, b, pairs * half :, :].astype(F32)
            bias_r[a * place.count_b + b] = jnp.broadcast_to(
                jnp.concatenate([tail[pairs + i : pairs + i + 1] for i in range(bias_rows)], 1), bias_r.shape[1:]
            )
    far_forward_phase(
        qf_r, ke_r, ve_r, line_r, num_r, den_r, before_r, after_r, attn_r, low_r, denom_r, left_r, right_r, lden_r,
        rden_r, pairs, head_dim,
    )
    gather.along_a(3)
    gather.along_x(2)
    hidden_turned = turned_r.at[:, pl.ds(0, rows)]
    acc = acc_r.at[own]
    hidden_phase(
        x_r.at[own], low_r, wo_r, bo_r, g1_r, s1_r, bdown_r, normed_r, scale_r, hidden_r, hidden_turned, acc
    )

    def ffn(step, forward):
        a = place.nearest(step) if forward else place.shard(step)

        @pl.loop(0, place.count_b)
        def _(index):
            b = lax.rem(place.b + index, place.count_b)
            shard = a * place.count_b + b
            if forward:
                ffn_forward_shard(hidden_r, mats, a, b, shard, bias_r, pool, acc)
            else:
                ffn_backward_shard(hidden_r, gturned_r, hidden_turned, mats, a, b, shard, pool, acc, gbias_r)

    gather.finish(0)
    ffn(0, True)
    gather.along_b(3)
    gather.finish(1)
    ffn(1, True)
    gather.along_x(3)
    gather.finish(2)
    ffn(2, True)
    gather.finish(3)
    ffn(3, True)
    sends.drain()
    loads[3].wait()
    middle_phase(acc, cot_r, g2_r, s2_r, hidden_r, gturned_r, small_r)
    layer_out = pltpu.make_async_copy(cot_r, layer_h, load_sem.at[4])
    layer_out.start()
    ffn(1, False)
    scatter.start(1)
    ffn(2, False)
    scatter.start(2)
    scatter.fetch(1)
    ffn(3, False)
    scatter.start(3)
    scatter.chip(1)
    scatter.fetch(2)
    ffn(0, False)
    scatter.start(0)
    scatter.chip(2)
    scatter.along_x(1)
    scatter.fetch(3)
    first_back_phase(acc, normed_r, scale_r, g1_r, hidden_r, small_r)
    tot_r[pairs * half :, :] = jnp.zeros((tot_r.shape[0] - pairs * half, LANES), F32)
    block = pool.shape[2]
    for index in range(width // block):
        cols = slice(index * block, (index + 1) * block)
        pool[index, 0:width, :] = tn(low_r[...], hidden_r[:, cols]).astype(BF16)
    reduce.push(0)
    attn_back_phase(hidden_r, wo_r, attn_r, denom_r, low_r, qf_r, num_r, den_r, tot_r, pairs, head_dim)
    layer_out.wait()
    states_two[place.a, place.b] = tot_r[...].astype(BF16)
    grads_gather.along_a()
    scatter.chip(3)
    scatter.along_x(2)
    scatter.fetch(0)

    def turn(block):
        turned_r[:, block] = x_r[block, :].T

    row_blocks(rows + 2 * WINDOW, turn)
    groups = pairs * LANES // CHUNK
    in_group = CHUNK // LANES

    def band(group):
        gk, gv = gk_r.at[group % 2], gv_r.at[group % 2]
        band_backward_phase(
            qf_r, ke_r, ve_r, line_r, low_r, denom_r, num_r, den_r, left_r, right_r, lden_r, rden_r, attn_r, gk, gv,
            gline_r, cg_r, group * in_group, (group + 1) * in_group, group * in_group, head_dim,
        )

    def keys(group):
        gk, gv = gk_r.at[group % 2], gv_r.at[group % 2]
        far_back_phase(
            ke_r, ve_r, line_r, num_r, den_r, before_r, after_r, gk, gv, pairs, group * in_group,
            (group + 1) * in_group, group * in_group, head_dim,
        )
        qkv_grad_phase(
            turned_r, w_r, omega_r, q_r, k_r, qf_r, ke_r, attn_r, gk, gv, gqkv_r, pool, small_r, group, place,
            head_dim,
        )
        reduce.push(group + 1)

    def tokens_part(group):
        def body(block):
            total = acc_r[block, :]
            for part in range(3):
                cols = slice(part * CHUNK, (part + 1) * CHUNK)
                wide = slice(part * width + group * CHUNK, part * width + (group + 1) * CHUNK)
                total = total + nt(gqkv_r[block, cols], w_r[:, wide])
            acc_r[block, :] = total

        row_blocks(rows + 2 * WINDOW, body)

    gqkv_r[0:WINDOW, 0:CHUNK] = jnp.zeros((WINDOW, CHUNK), BF16)
    gqkv_r[rows + WINDOW :, 0:CHUNK] = jnp.zeros((WINDOW, CHUNK), BF16)
    band(0)
    scatter.along_b(1)
    scatter.chip(0)
    scatter.along_x(3)
    reduce.stage(0, 1)
    grads_gather.along_b()
    band(1)
    scatter.along_b(2)
    scatter.along_x(0)
    reduce.stage(0, 2)
    grads_gather.finish()
    prefix_phase(place, states_two, before_r, after_r)
    keys(0)
    scatter.along_b(3)
    reduce.stage(0, 3)
    reduce.stage(1, 1)
    tokens_part(0)
    band(2)
    scatter.along_b(0)
    reduce.stage(0, 4)
    reduce.stage(1, 2)
    keys(1)
    reduce.stage(0, 5)
    reduce.stage(1, 3)
    reduce.stage(2, 1)
    tokens_part(1)
    keys(2)
    scatter.along_a()
    table_grads(gline_r, bucket_r, buckets, small_r)
    per_row = width // gbias_r.shape[2]
    for index in range(shards // per_row):
        small_r[9 + index : 10 + index, :] = jnp.concatenate(
            [gbias_r[index * per_row + i, 0:1, :] for i in range(per_row)], 1
        )
    held_r[0] = small_r[...]
    little.send(0)
    reduce.stage(3, 1)
    reduce.stage(0, 6)
    reduce.stage(1, 4)
    reduce.stage(2, 2)
    little.receive(0)
    little.send(1)

    reduce.stage(3, 2)
    reduce.stage(2, 3)
    reduce.stage(1, 5)
    reduce.stage(0, 7)
    scatter.last_x()
    little.receive(1)
    little.send(2)
    reduce.stage(3, 3)
    reduce.stage(2, 4)
    reduce.stage(1, 6)
    tokens_part(2)
    edge_r[0:WINDOW, :] = acc_r[0:WINDOW, :].astype(BF16)
    edge_r[WINDOW:, :] = acc_r[rows + WINDOW :, :].astype(BF16)
    top, bottom = pl.ds(0, WINDOW), pl.ds(WINDOW, WINDOW)
    sends.send(edge_r.at[top], tail_r.at[bottom], t_send.at[0], t_recv.at[1], to_left, place.not_first)
    sends.send(edge_r.at[bottom], tail_r.at[top], t_send.at[1], t_recv.at[0], to_right, place.not_last)
    reduce.stage(3, 4)
    reduce.stage(2, 5)
    reduce.stage(1, 7)
    little.receive(2)
    little.send(3)
    reduce.stage(3, 5)
    reduce.stage(2, 6)
    arrive(tail_r.at[top], t_recv.at[0], place.at(), place.not_first)
    arrive(tail_r.at[bottom], t_recv.at[1], place.at(), place.not_last)

    @pl.when(place.not_first)
    def _():
        acc_r[WINDOW : 2 * WINDOW, :] += tail_r[0:WINDOW, :].astype(F32)

    @pl.when(place.not_last)
    def _():
        acc_r[rows : rows + WINDOW, :] += tail_r[WINDOW:, :].astype(F32)

    tokens_out = pltpu.make_async_copy(acc, gtok_h, load_sem.at[5])
    tokens_out.start()
    reduce.stage(3, 6)
    reduce.stage(2, 7)
    little.receive(3)
    small_r[...] = little.total()
    reduce.stage(3, 7)
    scatter.finish()
    for index in range(chunks):
        reduce.stage(index, 8)
    tokens_out.wait()
    sends.drain()


def in_parts(grouped):
    groups = grouped.shape[1] // (3 * CHUNK)
    starts = [(group * 3 + part) * CHUNK for part in range(3) for group in range(groups)]
    return jnp.concatenate([grouped[:, start : start + CHUNK].astype(F32) for start in starts], 1)


def call(body, outs, operands, scratch=(), limit=60, collective_id=None, in_place=(), out_place=()):
    return pl.pallas_call(
        body,
        out_shape=[jax.ShapeDtypeStruct(shape, dtype) for shape, dtype in outs],
        in_specs=[
            pl.BlockSpec(memory_space=pl.ANY if i in in_place else pltpu.VMEM) for i in range(len(operands))
        ],
        out_specs=[
            pl.BlockSpec(memory_space=pl.ANY if i in out_place else pltpu.VMEM) for i in range(len(outs))
        ],
        scratch_shapes=list(scratch),
        compiler_params=pltpu.CompilerParams(
            vmem_limit_bytes=limit * MIB,
            collective_id=collective_id,
            has_side_effects=collective_id is not None,
        ),
    )(*operands)


def unpack_kernel(
    result_r, total_r, tokens_r, layer_r, small_r, gw_r, gwo_r, gup_r, gdown_r, gtok_r, out_r, gb_r, gbu_r, *vector_rs
):
    blocks, width, block = result_r.shape
    for index in range(blocks):
        at = 0
        while at < block:
            column = index * block + at
            if column < width:
                target, place, size = gwo_r, column, block - at
            else:
                group, rest = divmod(column - width, 3 * CHUNK)
                part, inner = divmod(rest, CHUNK)
                target, place = gw_r, part * width + group * CHUNK + inner
                size = min(block - at, CHUNK - inner)
            target[:, place : place + size] = result_r[index, :, at : at + size].astype(F32)
            at += size
    gup_r[...] = total_r[0].astype(F32)
    gdown_r[...] = total_r[1].T.astype(F32)
    gtok_r[...] = tokens_r[...]
    out_r[...] = layer_r[...]
    for index, ref in enumerate(vector_rs):
        ref[...] = small_r[index, :]
    for group in range(width // CHUNK):
        for part in range(3):
            start = part * width + group * CHUNK
            gb_r[start : start + CHUNK] = small_r[6 + group, part * CHUNK : (part + 1) * CHUNK]
    units = gbu_r.shape[0]
    seq = lax.axis_index("seq")
    per_row = width // units
    for shard in range(lax.axis_size("seq")):
        @pl.when(seq == shard)
        def _():
            at = shard % per_row * units
            gbu_r[...] = small_r[9 + shard // per_row, at : at + units]


def fused(
    x, cot, w_up, w_down, w_qkv, b_qkv, omega, bucket_line, bias_table, w_out, b_out, gain_one, shift_one, b_up, b_down,
    gain_two, shift_two, pairs, head_dim,
):
    rows, width = x.shape
    units = w_up.shape[1]
    heads, buckets = bias_table.shape
    count = lax.axis_size("seq")
    count_a = count // 2
    blocks, half = rows // WINDOW, LANES // 2
    third, quarter = width // 3, width // 4
    groups = width // CHUNK
    chunks = 1 + groups
    columns = chunks * width // units
    wide, ext = (rows, width), (rows + 2 * WINDOW, width)
    stacked, flat = (pairs * blocks, half, LANES), (pairs * blocks, LANES)
    message = (pairs * half + 16, LANES)
    mats = (2, count_a, 2, width, units)
    dma = pltpu.SemaphoreType.DMA
    vmem = pltpu.VMEM
    vectors = [b_qkv, b_out, gain_one, shift_one, b_down, gain_two, shift_two]
    vectors += [jnp.pad(vector, (0, width - vector.shape[0])) for vector in (b_up, bucket_line[0])]
    packed = jnp.concatenate([vector.astype(F32) for vector in vectors]).reshape(-1, width)
    layer, gtok, total, small, result, _, _ = call(
        functools.partial(layer_kernel, pairs, head_dim, buckets, count),
        [(wide, BF16), (wide, F32), ((2, width, units), BF16), ((16, width), F32), ((columns, width, units), BF16),
         (mats[1:], BF16), ((columns, 2 * quarter, units), BF16)],
        (x, cot, w_up, w_down, w_qkv, omega, bias_table, w_out, packed),
        [vmem(ext, BF16), vmem(wide, BF16), vmem(ext, BF16), vmem(wide, BF16), vmem((2, *ext), BF16),
         vmem((heads, LINE), F32), vmem(stacked, F32), vmem(flat, F32), vmem(message, F32),
         vmem((count_a, 2, *message), BF16), vmem((count_a, 2, *message), BF16), vmem(message, F32),
         vmem(message, F32), vmem(stacked, F32), vmem(stacked, F32), vmem(flat, F32), vmem(flat, F32),
         vmem(wide, F32), vmem(wide, F32), vmem(wide, BF16), vmem((rows, LANES), F32),
         vmem(wide, BF16), vmem((width, ext[0]), BF16),
         vmem(wide, BF16), vmem(ext, F32), vmem(mats, BF16), vmem((columns, 2 * rows, units), BF16),
         vmem((count, 8, units), F32), vmem((count, 8, units), F32), vmem((2, ext[0], CHUNK), F32),
         vmem((2, ext[0], CHUNK), F32), vmem((heads, LINE), F32), vmem((2 * WINDOW, 3 * WINDOW), F32),
         vmem(ext, BF16), vmem((2, width, units), BF16), vmem((count_a, 2, third, units), BF16),
         vmem((count_a, 2 * third, units), BF16), vmem((count_a - 1, 2 * third, units), BF16),
         vmem((third, units), BF16),
         vmem((2, 2 * quarter, units), BF16), vmem((columns, quarter, units), BF16),
         vmem((chunks, quarter, units), BF16), vmem((chunks, count_a - 1, quarter // count_a, units), BF16),
         vmem((chunks, quarter // count_a, units), BF16), vmem((4, 16, width), F32),
         vmem((3 + count_a, 16, width), F32)]
        + gather_sems(count_a) + state_sems(count_a) + state_sems(count_a) + scatter_sems(count_a)
        + reduce_sems(chunks, count_a)
        + [dma((3 + count_a,)), dma((3 + count_a,)), dma((2,)), dma((2,)), dma((2,)), dma((2,)), dma((6,))],
        limit=62,
        collective_id=0,
        in_place=(0, 1, 2, 3),
        out_place=(0, 1, 4, 5, 6),
    )
    vector = ((width,), F32)
    gw_qkv, gw_out, gup, gdown, gtok, layer, gb_qkv, grad_b_up, g2, s2, bd, g1, s1, bo = call(
        unpack_kernel,
        [((width, 3 * width), F32), ((width, width), F32), ((width, units), F32), ((units, width), F32), (wide, F32),
         (wide, BF16), ((3 * width,), F32), ((units,), F32)] + [vector] * 6,
        (result, total, gtok, layer, small),
    )
    gtable = small[13 : 13 + heads * buckets // LANES, :LANES].reshape(heads, buckets)
    return (
        layer[None], gtok[None], gw_qkv, gb_qkv, gw_out, bo, g1, s1, gup, grad_b_up, gdown, bd, g2, s2, gtable,
    )


def shards(
    tokens, cotangent, w_qkv, b_qkv, w_out, b_out, gain_one, shift_one, w_up, b_up, w_down, b_down,
    gain_two, shift_two, feature_codes, bias_table, offset_bucket,
):
    rows, width = tokens.shape[1:]
    heads, head_dim, feats = feature_codes.shape
    buckets = bias_table.shape[1]
    pairs = heads // 2
    blocks = rows // WINDOW
    half = LANES // 2
    hidden_units = w_up.shape[1]
    length = (offset_bucket.shape[0] + 1) // 2
    count = lax.axis_size("seq")
    x = tokens[0]
    omega_int = (feature_codes.astype(F32) - CENTER).astype(BF16)
    group = CHUNK // head_dim
    eye = jnp.eye(group, dtype=BF16)
    omega = (
        omega_int.reshape(heads // group, group, head_dim, 1, feats)
        * eye[None, :, None, :, None]
    ).reshape(heads // group, CHUNK, CHUNK)
    bucket_line = offset_bucket[length - LINE // 2 : length + LINE // 2][None]
    state = (pairs * half + 8, LANES)
    stacked = (pairs * blocks, half, LANES)
    flat = (pairs * blocks, LANES)
    wide = (rows, width)

    def halo(block):
        forward = [(i, i + 1) for i in range(count - 1)]
        backward = [(target, source) for source, target in forward]
        low = lax.ppermute(block[rows - WINDOW :], "seq", forward)
        high = lax.ppermute(block[:WINDOW], "seq", backward)
        return jnp.concatenate([low, block, high], 0)

    me = lax.axis_index("seq")
    ids = jnp.arange(count)

    def prefix(message):
        every = lax.all_gather(message, "seq", axis=0)
        before = jnp.sum(jnp.where((ids < me)[:, None, None], every, 0.0), 0)
        after = jnp.sum(jnp.where((ids > me)[:, None, None], every, 0.0), 0)
        return before, after

    if lax.axis_size("row") == 4 and count == 8:
        return fused(
            x, cotangent[0], w_up, w_down, w_qkv, b_qkv, omega, bucket_line, bias_table, w_out, b_out, gain_one,
            shift_one, b_up, b_down, gain_two, shift_two, pairs, head_dim,
        )

    def body_one(x_r, w_r, b_r, o_r, bu_r, ta_r, q_r, k_r, v_r, qf_r, kf_r, line_r, num_r, den_r, tot_r):
        parts = ((1, k_r, kf_r), (2, v_r, None), (0, q_r, qf_r))
        qkv_phase(x_r, w_r, [b_r.at[pl.ds(i, 1)] for i in range(3)], o_r, parts, head_dim)
        line_phase(bu_r, ta_r, line_r)
        state_phase(kf_r, v_r, num_r, den_r, tot_r, pairs)

    q, k, v, qf, kf, line, num, den, total = call(
        body_one,
        [(wide, BF16)] * 5
        + [((heads, LINE), F32), (stacked, F32), (flat, F32), (state, F32)],
        (x, w_qkv, b_qkv.astype(F32).reshape(3, width), omega, bucket_line, bias_table),
    )
    up_all = lax.all_gather(w_up, "seq", axis=0)
    down_all = lax.all_gather(jnp.transpose(w_down), "seq", axis=0)
    b_up_all = jnp.broadcast_to(lax.all_gather(b_up, "seq", axis=0)[:, None, :], (count, 8, hidden_units))

    ke, ve = halo(kf), halo(v)
    before, after = prefix(total)

    def body_two(*refs):
        ins, outs = refs[:12], refs[12:]
        qf_r, ke_r, ve_r, line_r, num_r, den_r, bef_r, aft_r, x_r, w_r, b_r, _ = ins
        out_r, low_r, dnm_r, l_r, r_r, ld_r, rd_r, nrm_r, sc_r = outs
        band_forward_phase(qf_r, ke_r, ve_r, line_r, out_r, dnm_r, 0, pairs)
        far_forward_phase(
            qf_r, ke_r, ve_r, line_r, num_r, den_r, bef_r, aft_r,
            out_r, low_r, dnm_r, l_r, r_r, ld_r, rd_r, pairs, head_dim,
        )
        out_phase(x_r, low_r, w_r, b_r, nrm_r, sc_r)

    attn, attn_low, denom, left, right, left_den, right_den, normed, scale = call(
        body_two,
        [(wide, F32), (wide, BF16), (wide, F32), (stacked, F32), (stacked, F32), (flat, F32),
         (flat, F32), (wide, F32), ((rows, LANES), F32)],
        (qf, ke, ve, line, num, den, before, after, x, w_out, b_out[None], gain_one[None]),
    )
    layer, first, first_low, vec, gup, gdown, gbias = call(
        ffn_phase,
        [(wide, BF16), (wide, F32), (wide, BF16), ((8, width), F32),
         ((count, width, hidden_units), BF16), ((count, width, hidden_units), BF16),
         ((count, 8, hidden_units), F32)],
        (normed, scale, gain_one[None], shift_one[None], up_all, b_up_all, down_all, b_down[None],
         gain_two[None], shift_two[None], cotangent[0]),
        (pltpu.VMEM((count, rows, hidden_units), BF16), pltpu.VMEM((count, rows, hidden_units), BF16),
         pltpu.VMEM(wide, F32)),
    )

    def reduced(part):
        return lax.psum(lax.psum_scatter(part, "seq", scatter_dimension=0), "row").astype(F32)

    grad_w_up = reduced(gup)
    grad_w_down = jnp.transpose(reduced(gdown))
    grad_b_up = reduced(gbias[:, 0])
    ext = (rows + 2 * WINDOW, width)

    def body_four(*refs):
        (gl_r, w_r, lo_r, ou_r, dn_r, qf_r, ke_r, ve_r, li_r, l_r, r_r, ld_r, rd_r, bu_r) = refs[:14]
        gw_r, gq_r, gk_r, gv_r, dnum_r, dden_r, tot_r, gt_r, gnum_r, gden_r, gline_r, cg_r = refs[14:]
        out_back_phase(
            gl_r, w_r, lo_r, ou_r, dn_r, qf_r, gnum_r, gden_r, gw_r, dnum_r, dden_r, tot_r, pairs, head_dim
        )
        band_backward_phase(
            qf_r, ke_r, ve_r, li_r, gnum_r, gden_r, dnum_r, dden_r, l_r, r_r, ld_r, rd_r,
            gq_r, gk_r, gv_r, gline_r, cg_r, 0, pairs, 0, head_dim,
        )
        gt_r[...] = table_phase(gline_r, bu_r, buckets)

    gw_out, gq, gk, gv, dnum, dden, gtotal, gtable = call(
        body_four,
        [((width, width), F32), (wide, F32), (ext, F32), (ext, F32), (stacked, F32), (flat, F32),
         (state, F32), (bias_table.shape, F32)],
        (first_low, w_out, attn_low, attn, denom, qf, ke, ve, line, left, right, left_den, right_den,
         bucket_line),
        (pltpu.VMEM(wide, BF16), pltpu.VMEM(wide, F32), pltpu.VMEM((heads, LINE), F32),
         pltpu.VMEM((2 * WINDOW, 3 * WINDOW), F32)),
    )
    past, future = prefix(gtotal)
    forward = [(i, i + 1) for i in range(count - 1)]
    backward = [(target, source) for source, target in forward]
    to_left = jnp.stack([gk[:WINDOW], gv[:WINDOW]]).astype(BF16)
    to_right = jnp.stack([gk[rows + WINDOW :], gv[rows + WINDOW :]]).astype(BF16)
    low_in = lax.ppermute(to_right, "seq", forward)
    high_in = lax.ppermute(to_left, "seq", backward)

    def body_five(*refs):
        (x_r, w_r, o_r, q_r, k_r, v_r, qf_r, kf_r, li_r, dn_r, dd_r, pa_r, fu_r, lo_r, hi_r, gq_r,
         gki_r, gvi_r, fi_r) = refs[:19]
        gt_r, gw_r, gb_r, gk_r, gv_r, turned_r = refs[19:]
        gk_r[...] = gki_r[...]
        gv_r[...] = gvi_r[...]
        gt_r[...] = fi_r[...]
        turned_r[...] = x_r[...].T
        key_back_phase(
            kf_r, v_r, li_r, dn_r, dd_r, pa_r, fu_r, lo_r, hi_r, gk_r, gv_r, pairs, 0, pairs, head_dim
        )
        for group in range(width // CHUNK):
            qkv_back_phase(
                turned_r, w_r, o_r, q_r, k_r, qf_r, kf_r, gq_r, gk_r, gv_r, gt_r, gw_r, gb_r, group, head_dim
            )

    gtok, gw_qkv, small = call(
        body_five,
        [(wide, F32), ((width, 4 * width), F32), ((16, width), F32)],
        (x, w_qkv, omega, q, k, v, qf, kf, line, dnum, dden, past, future, low_in, high_in, gq, gk, gv,
         first),
        (pltpu.VMEM(ext, F32), pltpu.VMEM(ext, F32), pltpu.VMEM((width, rows), BF16)),
    )
    gw_qkv = in_parts(gw_qkv[:, width:])
    gb_qkv = in_parts(small[6 : 6 + width // CHUNK].reshape(1, -1))
    summed = lax.psum((gw_qkv, gb_qkv[0], gw_out, vec, gtable), ("row", "seq"))
    gw_qkv, gb_qkv, gw_out, vec, gtable = summed
    return (
        layer[None], gtok[None], gw_qkv, gb_qkv, gw_out, vec[5], vec[3], vec[4], grad_w_up, grad_b_up,
        grad_w_down, vec[2], vec[0], vec[1], gtable,
    )


def solution(mesh):
    placed = (
        P("row", "seq", None), P("row", "seq", None), P(), P(), P(), P(), P(), P(), P(None, "seq"),
        P("seq"), P("seq", None), P(), P(), P(), P(), P(), P(),
    )
    return jax.shard_map(
        shards,
        mesh=mesh,
        in_specs=placed,
        out_specs=(
            P("row", "seq", None), P("row", "seq", None), P(), P(), P(), P(), P(), P(), P(None, "seq"),
            P("seq"), P("seq", None), P(), P(), P(), P(),
        ),
        check_vma=False,
    )
```

```python
import functools
import math

import jax
import jax.numpy as jnp
from jax import lax
from jax.experimental import pallas as pl
from jax.experimental.pallas import tpu as pltpu
from jax.sharding import PartitionSpec as P

WINDOW = 128
LANES = 128
LINE = 512
CHUNK = 256
EPS = 1e-06
CENTER = 7.5
SPREAD = math.sqrt(21.25)
ROOT_HALF = 0.7071067811865476
INV_ROOT_TAU = 0.3989422804014327
MIB = 1 << 20
F32 = jnp.float32
BF16 = jnp.bfloat16


def nn(a, b):
    return lax.dot_general(a, b, (((1,), (0,)), ((), ())), preferred_element_type=F32)


def nt(a, b):
    return lax.dot_general(a, b, (((1,), (1,)), ((), ())), preferred_element_type=F32)


def tn(a, b):
    return lax.dot_general(a, b, (((0,), (0,)), ((), ())), preferred_element_type=F32)


def halves(values):
    upper = values.astype(BF16)
    return upper, (values - upper.astype(F32)).astype(BF16)


def block_ones(size, head_dim):
    rows = lax.broadcasted_iota(jnp.int32, (size, size), 0) // head_dim
    cols = lax.broadcasted_iota(jnp.int32, (size, size), 1) // head_dim
    return jnp.where(rows == cols, 1.0, 0.0)


def head_sums(values, ones):
    upper, lower = halves(values)
    return nn(upper, ones) + nn(lower, ones)


def first_half(shape):
    return lax.broadcasted_iota(jnp.int32, shape, len(shape) - 1) < LANES // 2


def both_heads(pair):
    first = first_half((1, LANES))
    mask_a = jnp.where(first, 1.0, 0.0).astype(pair.dtype)
    mask_b = jnp.where(first, 0.0, 1.0).astype(pair.dtype)
    return jnp.concatenate([pair * mask_a, pair * mask_b], 0)


def per_head(stacked):
    rows = stacked.shape[0] // 2
    return jnp.where(first_half((rows, LANES)), stacked[:rows], stacked[rows:])


def compact(full):
    half = LANES // 2
    return jnp.where(first_half((half, LANES)), full[:half], full[half:])


def expand(small, ones):
    return jnp.concatenate([small, small], 0) * ones


def block_state(keys, values):
    return compact(tn(keys, values)), jnp.sum(keys.astype(F32), 0, keepdims=True)


def coef_tile(line_ref, pair):
    tiles = []
    for head in range(2):
        row = line_ref[pl.ds(2 * pair + head, 1), :]
        wide = pltpu.roll(
            jnp.broadcast_to(row, (WINDOW, LINE)), LINE - WINDOW + 1, 1, stride=1, stride_axis=0
        )
        tiles.append(wide[:, : 3 * WINDOW])
    return jnp.concatenate(tiles, 0)


def far_coefs(line_ref, pair):
    first = first_half((1, LANES))
    row_a = line_ref[pl.ds(2 * pair, 1), :]
    row_b = line_ref[pl.ds(2 * pair + 1, 1), :]
    left = jnp.where(first, row_a[:, 0:1], row_b[:, 0:1])
    right = jnp.where(first, row_a[:, LINE - 2 : LINE - 1], row_b[:, LINE - 2 : LINE - 1])
    return left, right


def unskew_sum(tile):
    rows = tile.shape[0]
    padded = jnp.concatenate([tile, jnp.zeros((rows, LINE - tile.shape[1]), F32)], 1)
    while rows > 8:
        rows = rows // 2
        padded = pltpu.roll(padded[:rows], rows, 1) + padded[rows:]
    while rows > 1:
        rows = rows // 2
        padded = pltpu.roll(padded[:rows], rows, 1) + padded[rows:]
    return padded


def lanes(pair):
    return pl.ds(pl.multiple_of(pair * LANES, LANES), LANES)


def qkv_phase(x_ref, w_ref, b_ref, omega_ref, parts, head_dim):
    width = x_ref.shape[1]
    x = x_ref[...]
    ones = block_ones(CHUNK, head_dim).astype(BF16)
    factor = head_dim ** (-0.25) / SPREAD
    for part, low_ref, feat_ref in parts:
        for chunk in range(width // CHUNK):
            cols = slice(chunk * CHUNK, (chunk + 1) * CHUNK)
            wide = slice(part * width + chunk * CHUNK, part * width + (chunk + 1) * CHUNK)
            low = (nn(x, w_ref[:, wide]) + b_ref[part][:, cols]).astype(BF16)
            low_ref[:, cols] = low
            if feat_ref is not None:
                projected = nn(low, omega_ref[chunk]) * factor
                widened = low.astype(F32)
                half_norm = head_sums(widened * widened, ones) * (0.5 * head_dim ** (-0.5))
                feat_ref[:, cols] = (
                    jnp.exp(projected - half_norm) * head_dim ** (-0.5)
                ).astype(BF16)


def line_phase(bucket_ref, table_ref, line_ref):
    buckets = table_ref.shape[1]
    one_hot = jnp.where(
        lax.broadcasted_iota(jnp.int32, (buckets, LINE), 0) == bucket_ref[...].astype(jnp.int32), 1.0, 0.0
    )
    logs = lax.dot_general(
        table_ref[...],
        one_hot,
        (((1,), (0,)), ((), ())),
        precision=lax.Precision.HIGHEST,
        preferred_element_type=F32,
    )
    line_ref[...] = jnp.exp(logs)


def state_phase(kf_ref, v_ref, num_ref, den_ref, total_ref, pairs):
    blocks = kf_ref.shape[0] // WINDOW
    half = LANES // 2

    @pl.loop(0, pairs)
    def _(pair):
        total = jnp.zeros((half, LANES), F32)
        total_den = jnp.zeros((1, LANES), F32)
        for block in range(blocks):
            rows = slice(block * WINDOW, (block + 1) * WINDOW)
            num, den = block_state(kf_ref[rows, lanes(pair)], v_ref[rows, lanes(pair)])
            num_ref[pair * blocks + block] = num
            den_ref[pl.ds(pair * blocks + block, 1), :] = den
            total = total + num
            total_den = total_den + den
        total_ref[pl.ds(pl.multiple_of(pair * half, half), half), :] = total
        total_ref[pl.ds(pairs * half + pair, 1), :] = total_den


def band_forward_phase(qf_ref, ke_ref, ve_ref, line_ref, out_ref, denom_ref, first, last):
    blocks = qf_ref.shape[0] // WINDOW

    @pl.loop(first, last)
    def _(pair):
        cols = lanes(pair)
        coef = coef_tile(line_ref, pair)
        for block in range(blocks):
            rows = slice(block * WINDOW, (block + 1) * WINDOW)
            window = slice(block * WINDOW, (block + 3) * WINDOW)
            scores = nt(both_heads(qf_ref[rows, cols]), ke_ref[window, cols])
            weights = (coef * scores).astype(BF16)
            values = ve_ref[window, cols]
            summed = nn(weights, jnp.concatenate([values, jnp.ones_like(values)], 1))
            out_ref[rows, cols] = per_head(summed[:, :LANES])
            denom_ref[rows, cols] = per_head(summed[:, LANES:])


def far_forward_phase(
    qf_ref, ke_ref, ve_ref, line_ref, num_ref, den_ref, before_ref, after_ref,
    out_ref, low_ref, denom_ref, left_ref, right_ref, left_den_ref, right_den_ref, pairs, head_dim,
):
    blocks = qf_ref.shape[0] // WINDOW
    half = LANES // 2

    @pl.loop(0, pairs)
    def _(pair):
        ones_f32 = block_ones(LANES, head_dim)
        ones = ones_f32.astype(BF16)
        cols = lanes(pair)
        left_coef, right_coef = far_coefs(line_ref, pair)
        state_rows = pl.ds(pl.multiple_of(pair * half, half), half)
        den_row = pl.ds(pairs * half + pair, 1)
        edge_low = block_state(ke_ref[:WINDOW, cols], ve_ref[:WINDOW, cols])
        edge_high = block_state(
            ke_ref[(blocks + 1) * WINDOW :, cols], ve_ref[(blocks + 1) * WINDOW :, cols]
        )
        past = (before_ref[state_rows, :], before_ref[den_row, :])
        future = (after_ref[state_rows, :], after_ref[den_row, :])

        def block_of(block):
            index = pair * blocks + block
            return num_ref[index], den_ref[pl.ds(index, 1), :]

        def add(one, two, sign=1.0):
            return tuple(a + sign * b for a, b in zip(one, two))

        lefts = [add(past, edge_low, -1.0), past]
        for block in range(2, blocks):
            lefts.append(add(lefts[-1], block_of(block - 2)))
        rights = [add(future, edge_high, -1.0), future]
        for block in range(2, blocks):
            rights.append(add(rights[-1], block_of(blocks + 1 - block)))
        rights = rights[::-1]
        for block in range(blocks):
            rows = slice(block * WINDOW, (block + 1) * WINDOW)
            index = pair * blocks + block
            query = qf_ref[rows, cols]
            left, left_den = lefts[block]
            right, right_den = rights[block]
            left_ref[index] = left
            right_ref[index] = right
            left_den_ref[pl.ds(index, 1), :] = left_den
            right_den_ref[pl.ds(index, 1), :] = right_den
            upper, lower = halves(expand(left_coef * left + right_coef * right, ones_f32))
            numer = out_ref[rows, cols] + nn(query, upper) + nn(query, lower)
            den_far = left_coef * left_den + right_coef * right_den
            denom = denom_ref[rows, cols] + head_sums(query.astype(F32) * den_far, ones)
            out = numer / denom
            out_ref[rows, cols] = out
            low_ref[rows, cols] = out.astype(BF16)
            denom_ref[rows, cols] = denom


def norm_parts(values):
    center = values - jnp.mean(values, -1, keepdims=True)
    inv_scale = lax.rsqrt(jnp.mean(center * center, -1, keepdims=True) + EPS)
    return center * inv_scale, inv_scale


def out_phase(x_ref, low_ref, w_ref, b_ref, normed_ref, scale_ref):
    first_sum = x_ref[...].astype(F32) + nn(low_ref[...], w_ref[...]) + b_ref[...].astype(F32)
    normed, inv_scale = norm_parts(first_sum)
    normed_ref[...] = normed
    scale_ref[...] = jnp.broadcast_to(inv_scale, scale_ref.shape)


def norm_back(grad_out, normed, inv_scale, gain):
    grad_normed = grad_out * gain
    centered = grad_normed - jnp.mean(grad_normed, -1, keepdims=True)
    return inv_scale * (centered - normed * jnp.mean(grad_normed * normed, -1, keepdims=True))


def ffn_phase(
    normed_ref, scale_ref, gain_one_ref, shift_one_ref, up_ref, b_up_ref, down_ref, b_down_ref,
    gain_two_ref, shift_two_ref, cot_ref, layer_ref, first_ref, low_ref, vec_ref, gup_ref, gdown_ref,
    gbias_ref, act_ref, slope_ref, acc_ref,
):
    shards = up_ref.shape[0]
    normed_one = normed_ref[...]
    hidden_one = normed_one * gain_one_ref[...] + shift_one_ref[...]
    hidden = hidden_one.astype(BF16)
    acc_ref[...] = hidden_one + b_down_ref[...].astype(F32)

    @pl.loop(0, shards)
    def _(shard):
        pre = nn(hidden, up_ref[shard]) + b_up_ref[shard, 0:1, :].astype(F32)
        phi = 0.5 * (1.0 + lax.erf(pre * ROOT_HALF))
        act = (pre * phi).astype(BF16)
        act_ref[shard] = act
        slope_ref[shard] = (phi + pre * INV_ROOT_TAU * jnp.exp(-0.5 * pre * pre)).astype(BF16)
        acc_ref[...] += nt(act, down_ref[shard])

    normed_two, scale_two = norm_parts(acc_ref[...])
    layer_ref[...] = (normed_two * gain_two_ref[...] + shift_two_ref[...]).astype(BF16)
    cot = cot_ref[...].astype(F32)
    grad_second = norm_back(cot, normed_two, scale_two, gain_two_ref[...])
    grad_ffn = grad_second.astype(BF16)
    vec_ref[0:1, :] = jnp.sum(cot * normed_two, 0, keepdims=True)
    vec_ref[1:2, :] = jnp.sum(cot, 0, keepdims=True)
    vec_ref[2:3, :] = jnp.sum(grad_ffn.astype(F32), 0, keepdims=True)
    acc_ref[...] = grad_second
    grad_turned = grad_ffn.T
    hidden_turned = hidden.T

    @pl.loop(0, shards)
    def _(shard):
        grad_act = nn(grad_ffn, down_ref[shard])
        grad_pre = (grad_act * slope_ref[shard].astype(F32)).astype(BF16)
        gdown_ref[shard] = nn(grad_turned, act_ref[shard]).astype(BF16)
        gup_ref[shard] = nn(hidden_turned, grad_pre).astype(BF16)
        gbias_ref[shard] = jnp.broadcast_to(
            jnp.sum(grad_pre.astype(F32), 0, keepdims=True), gbias_ref.shape[1:]
        )
        acc_ref[...] += nt(grad_pre, up_ref[shard])

    grad_hidden = acc_ref[...]
    grad_first = norm_back(grad_hidden, normed_one, scale_ref[:, 0:1], gain_one_ref[...])
    grad_low = grad_first.astype(BF16)
    first_ref[...] = grad_first
    low_ref[...] = grad_low
    vec_ref[3:4, :] = jnp.sum(grad_hidden * normed_one, 0, keepdims=True)
    vec_ref[4:5, :] = jnp.sum(grad_hidden, 0, keepdims=True)
    vec_ref[5:6, :] = jnp.sum(grad_low.astype(F32), 0, keepdims=True)
    vec_ref[6:8, :] = jnp.zeros((2, vec_ref.shape[1]), F32)


def out_back_phase(
    glow_ref, w_ref, low_ref, out_ref, denom_ref, qf_ref, gnum_ref, gden_ref, gw_ref, dnum_ref,
    dden_ref, total_ref, pairs, head_dim,
):
    rows_all = glow_ref.shape[0]
    blocks = rows_all // WINDOW
    half = LANES // 2
    ones = block_ones(LANES, head_dim).astype(BF16)
    grad_low = glow_ref[...]
    gw_ref[...] = tn(low_ref[...], grad_low).astype(gw_ref.dtype)
    for pair in range(pairs):
        cols = slice(pair * LANES, (pair + 1) * LANES)
        grad_attn = nt(grad_low, w_ref[cols, :])
        inverse = 1.0 / denom_ref[:, cols]
        grad_num = (grad_attn * inverse).astype(BF16)
        grad_den = -head_sums(grad_num.astype(F32) * out_ref[:, cols], ones)
        gnum_ref[:, cols] = grad_num
        gden_ref[:, cols] = grad_den
        total = jnp.zeros((half, LANES), F32)
        total_den = jnp.zeros((1, LANES), F32)
        for block in range(blocks):
            rows = slice(block * WINDOW, (block + 1) * WINDOW)
            query = qf_ref[rows, cols]
            num = compact(tn(query, grad_num[rows]))
            den = jnp.sum(query.astype(F32) * grad_den[rows], 0, keepdims=True)
            dnum_ref[pair * blocks + block] = num
            dden_ref[pair * blocks + block : pair * blocks + block + 1, :] = den
            total = total + num
            total_den = total_den + den
        total_ref[pair * half : (pair + 1) * half, :] = total
        total_ref[pairs * half + pair : pairs * half + pair + 1, :] = total_den


def row_grads(keys, values, num, den, ones_f32):
    upper, lower = halves(expand(num, ones_f32))
    grad_keys = nt(values, upper) + nt(values, lower) + den
    grad_values = nn(keys, upper) + nn(keys, lower)
    return grad_keys, grad_values


def band_backward_phase(
    qf_ref, ke_ref, ve_ref, line_ref, gnum_ref, gden_ref, dnum_ref, dden_ref, left_ref, right_ref,
    left_den_ref, right_den_ref, gq_ref, gk_ref, gv_ref, gline_ref, coef_grad_ref, start, stop, first_col, head_dim,
):
    blocks = qf_ref.shape[0] // WINDOW

    @pl.loop(start, stop)
    def _(pair):
        ones_f32 = block_ones(LANES, head_dim)
        cols = lanes(pair)
        out = lanes(pair - first_col)
        coef = coef_tile(line_ref, pair)
        left_coef, right_coef = far_coefs(line_ref, pair)
        gk_ref[:, out] = jnp.zeros((gk_ref.shape[0], LANES), F32)
        gv_ref[:, out] = jnp.zeros((gv_ref.shape[0], LANES), F32)
        coef_grad_ref[...] = jnp.zeros(coef_grad_ref.shape, F32)
        left_sum = jnp.zeros((1, LANES), F32)
        right_sum = jnp.zeros((1, LANES), F32)
        for block in range(blocks):
            rows = slice(block * WINDOW, (block + 1) * WINDOW)
            window = slice(block * WINDOW, (block + 3) * WINDOW)
            index = pair * blocks + block
            query = qf_ref[rows, cols]
            keys = ke_ref[window, cols]
            values = ve_ref[window, cols]
            grad_num = gnum_ref[rows, cols]
            grad_den = gden_ref[rows, cols]
            queries = both_heads(query)
            grads = both_heads(grad_num)
            weights = coef * nt(queries, keys)
            den_column = jnp.concatenate(
                [grad_den[:, 0:1], grad_den[:, LANES // 2 : LANES // 2 + 1]], 0
            )
            grad_weights = nt(grads, values) + den_column
            coef_grad_ref[...] += grad_weights * weights
            grad_scores = (coef * grad_weights).astype(BF16)
            gv_ref[window, out] += tn(weights.astype(BF16), grads)
            gk_ref[window, out] += tn(grad_scores, queries)
            grad_query = per_head(nn(grad_scores, keys))
            left, right = left_ref[index], right_ref[index]
            left_den = left_den_ref[pl.ds(index, 1), :]
            right_den = right_den_ref[pl.ds(index, 1), :]
            upper, lower = halves(expand(left_coef * left + right_coef * right, ones_f32))
            den_far = left_coef * left_den + right_coef * right_den
            grad_query = grad_query + nt(grad_num, upper) + nt(grad_num, lower) + grad_den * den_far
            gq_ref[rows, cols] = grad_query
            dnum = dnum_ref[index]
            dden = dden_ref[pl.ds(index, 1), :]
            left_sum = left_sum + jnp.sum(dnum * left, 0, keepdims=True) + dden * left_den
            right_sum = right_sum + jnp.sum(dnum * right, 0, keepdims=True) + dden * right_den
        for edge, block, scale in ((0, 0, left_coef), (blocks + 1, blocks - 1, right_coef)):
            rows = slice(edge * WINDOW, (edge + 1) * WINDOW)
            index = pair * blocks + block
            edge_k, edge_v = row_grads(
                ke_ref[rows, cols],
                ve_ref[rows, cols],
                scale * dnum_ref[index],
                scale * dden_ref[pl.ds(index, 1), :],
                ones_f32,
            )
            gk_ref[rows, out] -= edge_k
            gv_ref[rows, out] -= edge_v
        first = first_half((1, LANES))
        positions = lax.broadcasted_iota(jnp.int32, (1, LINE), 1)
        left_all = left_coef * left_sum
        right_all = right_coef * right_sum
        for head in range(2):
            keep = first if head == 0 else jnp.logical_not(first)
            left_one = jnp.sum(jnp.where(keep, left_all, 0.0), 1, keepdims=True)
            right_one = jnp.sum(jnp.where(keep, right_all, 0.0), 1, keepdims=True)
            line = unskew_sum(coef_grad_ref[head * WINDOW : (head + 1) * WINDOW, :])
            line = line + jnp.where(positions == 0, left_one, 0.0)
            line = line + jnp.where(positions == LINE - 2, right_one, 0.0)
            gline_ref[pl.ds(2 * pair + head, 1), :] = line


def key_back_phase(
    kf_ref, v_ref, line_ref, dnum_ref, dden_ref, past_ref, future_ref, low_in_ref, high_in_ref,
    gk_ref, gv_ref, pairs, start, stop, head_dim,
):
    blocks = kf_ref.shape[0] // WINDOW
    half = LANES // 2

    @pl.loop(start, stop)
    def _(pair):
        ones_f32 = block_ones(LANES, head_dim)
        cols = lanes(pair)
        left_coef, right_coef = far_coefs(line_ref, pair)
        state_rows = pl.ds(pl.multiple_of(pair * half, half), half)
        den_row = pl.ds(pairs * half + pair, 1)
        nums = [dnum_ref[pair * blocks + block] for block in range(blocks)]
        dens = [dden_ref[pl.ds(pair * blocks + block, 1), :] for block in range(blocks)]
        for block in range(blocks):
            num_left, den_left = future_ref[state_rows, :], future_ref[den_row, :]
            num_right, den_right = past_ref[state_rows, :], past_ref[den_row, :]
            for other in range(blocks):
                if other >= block + 2:
                    num_left, den_left = num_left + nums[other], den_left + dens[other]
                if other <= block - 2:
                    num_right, den_right = num_right + nums[other], den_right + dens[other]
            rows = slice(block * WINDOW, (block + 1) * WINDOW)
            outer = slice((block + 1) * WINDOW, (block + 2) * WINDOW)
            far_k, far_v = row_grads(
                kf_ref[rows, cols],
                v_ref[rows, cols],
                left_coef * num_left + right_coef * num_right,
                left_coef * den_left + right_coef * den_right,
                ones_f32,
            )
            if block == 0:
                far_k = far_k + low_in_ref[0, :, cols].astype(F32)
                far_v = far_v + low_in_ref[1, :, cols].astype(F32)
            if block == blocks - 1:
                far_k = far_k + high_in_ref[0, :, cols].astype(F32)
                far_v = far_v + high_in_ref[1, :, cols].astype(F32)
            gk_ref[outer, cols] += far_k
            gv_ref[outer, cols] += far_v


def qkv_back_phase(
    turned_ref, w_ref, omega_ref, q_ref, k_ref, qf_ref, kf_ref, gq_ref, gk_ref, gv_ref, gtok_ref, parts_ref,
    small_ref, group, head_dim,
):
    width, rows_all = turned_ref.shape
    own = slice(WINDOW, WINDOW + rows_all)
    ones = block_ones(CHUNK, head_dim).astype(BF16)
    factor = head_dim ** (-0.25) / SPREAD
    cols = slice(group * CHUNK, (group + 1) * CHUNK)
    omega = omega_ref[group]
    lows = []
    total = gtok_ref[...]
    for part, low_ref, feat_ref, grad in (
        (0, q_ref, qf_ref, gq_ref[:, cols]), (1, k_ref, kf_ref, gk_ref[own, cols]), (2, None, None, gv_ref[own, cols]),
    ):
        if part < 2:
            inner_up, inner_low = halves(grad * feat_ref[:, cols].astype(F32))
            projected = (nt(inner_up, omega) + nt(inner_low, omega)) * factor
            sums = nn(inner_up, ones) + nn(inner_low, ones)
            grad = projected - sums * head_dim ** (-0.5) * low_ref[:, cols].astype(F32)
        low = grad.astype(BF16)
        lows.append(low)
        total = total + nt(low, w_ref[:, part * width + group * CHUNK : part * width + (group + 1) * CHUNK])
    gtok_ref[...] = total
    joined = jnp.concatenate(lows, 1)
    small_ref[8 + group : 9 + group, :] = jnp.sum(joined.astype(F32), 0, keepdims=True)
    parts_ref[:, (group + 1) * width : (group + 2) * width] = nn(turned_ref[...], joined).astype(parts_ref.dtype)


def table_phase(gline_ref, bucket_ref, buckets):
    one_hot = jnp.where(
        lax.broadcasted_iota(jnp.int32, (buckets, LINE), 0) == bucket_ref[...].astype(jnp.int32), 1.0, 0.0
    )
    return lax.dot_general(
        gline_ref[...],
        one_hot,
        (((1,), (1,)), ((), ())),
        precision=lax.Precision.HIGHEST,
        preferred_element_type=F32,
    )


MESH = pl.DeviceIdType.MESH


def guarded(when, action):
    if when is None:
        action()
    else:
        pl.when(when)(action)


class Place:
    def __init__(self, shards):
        self.row, self.seq = lax.axis_index("row"), lax.axis_index("seq")
        self.count_b = 2
        self.count_a = shards // self.count_b
        self.shards = shards
        self.x, self.core = self.row // 2, self.row % 2
        self.a, self.b = self.seq // self.count_b, self.seq % self.count_b
        self.is_first, self.is_last = self.seq == 0, self.seq == shards - 1
        self.not_first, self.not_last = self.seq > 0, self.seq < shards - 1

    def at(self, x=None, core=None, a=None, b=None):
        x = self.x if x is None else x
        core = self.core if core is None else core
        a = self.a if a is None else a
        b = self.b if b is None else b
        return (x * 2 + core, a * self.count_b + b)

    def beside(self, seq):
        return (self.row, seq)

    def shard(self, offset):
        return lax.rem(self.a + offset, self.count_a)

    def nearest(self, step):
        orders = []
        for a in range(self.count_a):
            orders.append(sorted(range(self.count_a), key=lambda other: (abs(other - a), other)))
        index = jnp.int32(orders[0][step])
        for a in range(1, self.count_a):
            index = jnp.where(self.a == a, orders[a][step], index)
        return index


class Sends:
    def __init__(self):
        self.started = []

    def send(self, src, dst, send_sem, recv_sem, device, when=None):
        copy = pltpu.make_async_remote_copy(
            src_ref=src, dst_ref=dst, send_sem=send_sem, recv_sem=recv_sem, device_id=device,
            device_id_type=MESH,
        )
        guarded(when, copy.start)
        self.started.append((when, copy))

    def drain(self):
        for when, copy in self.started:
            guarded(when, copy.wait_send)
        self.started = []


def arrive(dst, sem, device, when=None):
    copy = pltpu.make_async_remote_copy(
        src_ref=dst, dst_ref=dst, send_sem=sem, recv_sem=sem, device_id=device, device_id_type=MESH
    )
    guarded(when, copy.wait_recv)


class WeightGather:
    def __init__(self, place, sends, mats, middle, sems):
        self.place, self.sends, self.mats, self.mid = place, sends, mats, middle
        self.z_send, self.z_recv, self.y_send, self.y_recv, self.x_send, self.x_recv, self.c_send, self.c_recv = sems
        self.side = (mats.shape[3] - middle) // 2

    def outer(self, a, b, x, core=None):
        core = self.place.core if core is None else core
        start = pl.multiple_of(x * (self.side + self.mid), 16)
        return self.mats.at[core, a, b, pl.ds(start, self.side), :]

    def both(self, a, b, core=None):
        core = self.place.core if core is None else core
        kinds = [(0, self.outer(a, b, self.place.x, core))]
        if self.mid:
            kinds.append((1, self.mats.at[core, a, b, pl.ds(self.side, self.mid), :]))
        return kinds

    def column(self, column):
        return 1 - self.place.b if column else self.place.b

    def rounds(self, step):
        p = self.place
        if step == 0:
            return [(p.a, None, (1, -1))]
        last = p.count_a - 1
        return [
            (jnp.maximum(p.a - step, 0), p.a - step >= 0, (1,)),
            (jnp.minimum(p.a + step, last), p.a + step <= last, (-1,)),
        ]

    def along_a(self, step):
        p = self.place
        for a, there, moves in self.rounds(step):
            for kind, here in self.both(a, p.b):
                if step > 0:
                    arrive(here, self.z_recv.at[kind, a], p.at(), there)
                for move in moves:
                    target = p.a + move
                    ok = target <= p.count_a - 1 if move > 0 else target >= 0
                    if there is not None:
                        ok = jnp.logical_and(ok, there)
                    self.sends.send(
                        here, here, self.z_send.at[(1 - move) // 2, kind, a], self.z_recv.at[kind, a],
                        p.at(a=jnp.clip(target, 0, p.count_a - 1)), ok,
                    )
                if step > 0:
                    self.pass_on(kind, 0, a, here, there)

    def across(self, step):
        p = self.place
        for a, there, _ in self.rounds(step):
            for kind, here in self.both(a, p.b):
                self.sends.send(
                    here, here, self.y_send.at[kind, a], self.y_recv.at[kind, a], p.at(b=1 - p.b), there
                )

    def pass_on(self, kind, column, a, here, when=None):
        p = self.place
        if kind == 0:
            self.sends.send(
                here, here, self.x_send.at[column, a], self.x_recv.at[column, a], p.at(x=1 - p.x), when
            )
        self.sends.send(
            here, here, self.c_send.at[kind, column, a], self.c_recv.at[kind, column, a], p.at(core=1 - p.core), when
        )

    def along_b(self, step):
        p = self.place
        a = p.nearest(step)
        for kind, here in self.both(a, 1 - p.b):
            arrive(here, self.y_recv.at[kind, a], p.at())
            self.pass_on(kind, 1, a, here)

    def along_x(self, step, column):
        p = self.place
        a = p.nearest(step)
        here = self.outer(a, self.column(column), 1 - p.x)
        arrive(here, self.x_recv.at[column, a], p.at())
        self.sends.send(
            here, here, self.c_send.at[2, column, a], self.c_recv.at[2, column, a], p.at(core=1 - p.core)
        )

    def finish(self, step, column):
        p = self.place
        a = p.nearest(step)
        other, b = 1 - p.core, self.column(column)
        for kind, here in self.both(a, b, other) + [(2, self.outer(a, b, 1 - p.x, other))]:
            arrive(here, self.c_recv.at[kind, column, a], p.at())


def gather_sems(count_a):
    dma = pltpu.SemaphoreType.DMA
    return [
        dma((2, 2, count_a)), dma((2, count_a)), dma((2, count_a)), dma((2, count_a)),
        dma((2, count_a)), dma((2, count_a)), dma((3, 2, count_a)), dma((3, 2, count_a)),
    ]


class StateSums:
    def __init__(self, place, sends, buffers, sems):
        self.place, self.sends = place, sends
        self.own, self.peer, self.pair, self.far, self.sums, self.land = buffers
        self.y_send, self.y_recv, self.z_send, self.z_recv = sems
        self.half = self.pair.shape[0]

    def rows(self, b):
        return pl.ds(pl.multiple_of(b * self.half, 16), self.half)

    def start(self, message_ref):
        p = self.place
        self.own[...] = message_ref[...].astype(BF16)
        self.sends.send(self.own, self.peer, self.y_send.at[0], self.y_recv.at[0], p.at(b=1 - p.b))

    def along_a(self):
        p = self.place
        arrive(self.peer, self.y_recv.at[0], p.at())
        mine = self.rows(p.b)
        self.pair[...] = (self.own[mine, :].astype(F32) + self.peer[mine, :].astype(F32)).astype(BF16)
        for offset in range(1, p.count_a):
            self.sends.send(
                self.pair, self.far.at[p.a], self.z_send.at[offset], self.z_recv.at[offset],
                p.at(a=p.shard(offset)),
            )

    def along_b(self):
        p = self.place
        self.far[p.a] = jnp.zeros(self.pair.shape, BF16)
        for offset in range(1, p.count_a):
            source = p.shard(p.count_a - offset)
            arrive(self.far.at[source], self.z_recv.at[offset], p.at())
        for index in range(2):
            total = jnp.zeros(self.pair.shape, F32)
            for a in range(p.count_a):
                keep = a < p.a if index == 0 else a > p.a
                total = total + jnp.where(keep, 1.0, 0.0) * self.far[a].astype(F32)
            self.sums[index] = total.astype(BF16)
        self.sends.send(self.sums, self.land, self.y_send.at[1], self.y_recv.at[1], p.at(b=1 - p.b))

    def finish(self, before_ref, after_ref):
        p = self.place
        arrive(self.land, self.y_recv.at[1], p.at())
        for index, ref in ((0, before_ref), (1, after_ref)):
            ref[self.rows(p.b), :] = self.sums[index].astype(F32)
            ref[self.rows(1 - p.b), :] = self.land[index].astype(F32)
        peer = self.peer[...].astype(F32)
        before_ref[...] += jnp.where(p.b == 1, 1.0, 0.0) * peer
        after_ref[...] += jnp.where(p.b == 0, 1.0, 0.0) * peer


def sums_sems(count_a):
    dma = pltpu.SemaphoreType.DMA
    return [dma((2,)), dma((2,)), dma((count_a,)), dma((count_a,))]


class GradScatter:
    def __init__(self, place, sends, grads, total, middle, lands, sems):
        self.place, self.sends, self.grads, self.total, self.mid = place, sends, grads, total, middle
        self.core_land, self.stage, self.x_land, self.y_land, self.z_land, self.last_land = lands
        (self.copy, self.c_send, self.c_recv, self.x_send, self.x_recv, self.y_send, self.y_recv, self.z_send,
         self.z_recv, self.l_send, self.l_recv) = sems
        self.side = (grads.shape[3] - middle) // 2

    def outer(self, x):
        return pl.ds(pl.multiple_of(x * (self.side + self.mid), 16), self.side)

    def window(self):
        return pl.ds(pl.multiple_of(self.place.x * self.side, 16), self.side + self.mid)

    def column(self, column):
        return 1 - self.place.b if column else self.place.b

    def start(self, offset, column):
        p = self.place
        item = (offset, column)
        self.sends.send(
            self.grads.at[1 - p.core, p.shard(offset), self.column(column)], self.core_land.at[item],
            self.c_send.at[item], self.c_recv.at[item], p.at(core=1 - p.core),
        )

    def add(self, ref, land):
        ref[...] = (ref[...].astype(F32) + land[...].astype(F32)).astype(BF16)

    def staged(self, offset, column):
        item = (offset, column)
        return pltpu.make_async_copy(self.core_land.at[item], self.stage.at[1 - column], self.copy.at[item])

    def fetch(self, offset, column):
        item = (offset, column)
        arrive(self.core_land.at[item], self.c_recv.at[item], self.place.at())
        self.staged(offset, column).start()

    def chip(self, offset, column):
        p = self.place
        item = (offset, column)
        self.staged(offset, column).wait()
        here = self.grads.at[p.core, p.shard(offset), self.column(column)]
        self.add(here, self.stage.at[1 - column])
        self.sends.send(
            here.at[self.outer(1 - p.x), :], self.x_land.at[item], self.x_send.at[item], self.x_recv.at[item],
            p.at(x=1 - p.x),
        )

    def along_x(self, offset, column):
        p = self.place
        item = (offset, column)
        here = self.grads.at[p.core, p.shard(offset), self.column(column)]
        arrive(self.x_land.at[item], self.x_recv.at[item], p.at())
        self.add(here.at[self.outer(p.x), :], self.x_land.at[item])
        if column:
            self.sends.send(
                here.at[self.window(), :], self.y_land.at[offset], self.y_send.at[offset], self.y_recv.at[offset],
                p.at(b=1 - p.b),
            )

    def along_b(self, offset):
        p = self.place
        a = p.shard(offset)
        arrive(self.y_land.at[offset], self.y_recv.at[offset], p.at())
        mine = self.grads.at[p.core, a, p.b, self.window(), :]
        self.add(mine, self.y_land.at[offset])
        if offset:
            self.sends.send(
                mine, self.z_land.at[offset - 1], self.z_send.at[offset], self.z_recv.at[offset], p.at(a=a)
            )

    def along_a(self):
        p = self.place
        own = self.grads.at[p.core, p.a, p.b]
        mine = own.at[self.window(), :]
        total = mine[...].astype(F32)
        for offset in range(1, p.count_a):
            arrive(self.z_land.at[offset - 1], self.z_recv.at[offset], p.at())
            total = total + self.z_land[offset - 1].astype(F32)
        mine[...] = total.astype(BF16)
        middle = pl.ds(self.side, self.mid)
        outer = self.outer(p.x)
        self.total[p.core, outer, :] = self.grads[p.core, p.a, p.b, outer, :]
        self.sends.send(
            own.at[middle, :], self.last_land, self.l_send.at[0], self.l_recv.at[0], p.at(x=1 - p.x)
        )
        here = self.total.at[p.core, outer, :]
        self.sends.send(here, here, self.l_send.at[1], self.l_recv.at[1], p.at(x=1 - p.x))

    def last_x(self):
        p = self.place
        middle = pl.ds(self.side, self.mid)
        arrive(self.last_land, self.l_recv.at[0], p.at())
        self.total[p.core, middle, :] = (
            self.grads[p.core, p.a, p.b, middle, :].astype(F32) + self.last_land[...].astype(F32)
        ).astype(BF16)
        arrive(self.total.at[p.core, self.outer(1 - p.x), :], self.l_recv.at[1], p.at())
        here = self.total.at[p.core]
        self.sends.send(here, here, self.l_send.at[2], self.l_recv.at[2], p.at(core=1 - p.core))

    def finish(self):
        arrive(self.total.at[1 - self.place.core], self.l_recv.at[2], self.place.at())


def scatter_sems(count_a):
    dma = pltpu.SemaphoreType.DMA
    return [dma((count_a, 2)) for _ in range(5)] + [dma((count_a,)) for _ in range(4)] + [dma((3,)), dma((3,))]


class AllReduce:
    def __init__(self, place, sends, parts, result, lands, done, mixed, sems):
        self.place, self.sends, self.parts, self.result = place, sends, parts, result
        self.core_land, self.staged, self.one_land, self.two_land, self.a_land = lands
        self.done, self.mixed = done, mixed
        (self.s_send, self.s_recv, self.z_send, self.z_recv, self.g_send, self.g_recv, self.zg_send, self.zg_recv,
         self.copy) = sems
        self.half = result.shape[1] // 2
        self.quarter = self.half // 2
        self.slim = self.quarter // place.count_a

    def ways(self, index):
        p = self.place
        other_x, other_b = p.at(x=1 - p.x), p.at(b=1 - p.b)
        if index not in self.mixed:
            return p.x, p.b, other_x, other_b
        straight = p.core == 0
        one = tuple(jnp.where(straight, u, w) for u, w in zip(other_x, other_b))
        two = tuple(jnp.where(straight, w, u) for u, w in zip(other_x, other_b))
        return jnp.where(straight, p.x, p.b), jnp.where(straight, p.b, p.x), one, two

    def half_rows(self, core):
        return pl.ds(pl.multiple_of(core * self.half, self.half), self.half)

    def quarter_rows(self, one):
        start = self.place.core * self.half + one * self.quarter
        return pl.ds(pl.multiple_of(start, self.quarter), self.quarter)

    def slim_rows(self, one, a):
        start = self.place.core * self.half + one * self.quarter + a * self.slim
        return pl.ds(pl.multiple_of(start, self.slim), self.slim)

    def push(self, index):
        p = self.place
        blocks = pl.ds(2 * index, 2)
        self.sends.send(
            self.parts.at[blocks, self.half_rows(1 - p.core), :], self.core_land.at[blocks],
            self.s_send.at[0, index], self.s_recv.at[0, index], p.at(core=1 - p.core),
        )

    def add(self, ref, land):
        ref[...] = (ref[...].astype(F32) + land[...].astype(F32)).astype(BF16)

    def stage(self, index, number):
        p = self.place
        one, two, one_device, two_device = self.ways(index)
        blocks = pl.ds(2 * index, 2)
        mine, other = 2 * index + two, 2 * index + 1 - two
        parts, result = self.parts, self.result
        if number == 1:
            land = self.core_land.at[blocks]
            arrive(land, self.s_recv.at[0, index], p.at())
            fetch = pltpu.make_async_copy(land, self.staged, self.copy.at[index])
            fetch.start()
            fetch.wait()
            self.add(parts.at[blocks, self.half_rows(p.core), :], self.staged)
            self.sends.send(
                parts.at[blocks, self.quarter_rows(1 - one), :], self.one_land.at[blocks],
                self.s_send.at[1, index], self.s_recv.at[1, index], one_device,
            )
        elif number == 2:
            land = self.one_land.at[blocks]
            arrive(land, self.s_recv.at[1, index], p.at())
            self.add(parts.at[blocks, self.quarter_rows(one), :], land)
            self.sends.send(
                parts.at[other, self.quarter_rows(one), :], self.two_land.at[index],
                self.s_send.at[2, index], self.s_recv.at[2, index], two_device,
            )
        elif number == 3:
            land = self.two_land.at[index]
            arrive(land, self.s_recv.at[2, index], p.at())
            self.add(parts.at[mine, self.quarter_rows(one), :], land)
            for offset in range(1, p.count_a):
                a = p.shard(offset)
                self.sends.send(
                    parts.at[mine, self.slim_rows(one, a), :], self.a_land.at[index, offset - 1],
                    self.z_send.at[index, offset], self.z_recv.at[index, offset], p.at(a=a),
                )
        elif number == 4:
            rows = self.slim_rows(one, p.a)
            total = parts[mine, rows, :].astype(F32)
            for offset in range(1, p.count_a):
                arrive(self.a_land.at[index, offset - 1], self.z_recv.at[index, offset], p.at())
                total = total + self.a_land[index, offset - 1].astype(F32)
            self.done[index] = total.astype(BF16)
            here = result.at[mine, rows, :]
            pltpu.make_async_copy(self.done.at[index], here, self.copy.at[index]).start()
            for offset in range(1, p.count_a):
                self.sends.send(
                    self.done.at[index], here, self.zg_send.at[index, offset], self.zg_recv.at[index, offset],
                    p.at(a=p.shard(offset)),
                )
        elif number == 5:
            pltpu.make_async_copy(
                self.done.at[index], result.at[mine, self.slim_rows(one, p.a), :], self.copy.at[index]
            ).wait()
            for offset in range(1, p.count_a):
                a = lax.rem(p.a + p.count_a - offset, p.count_a)
                arrive(result.at[mine, self.slim_rows(one, a), :], self.zg_recv.at[index, offset], p.at())
            here = result.at[mine, self.quarter_rows(one), :]
            self.sends.send(here, here, self.g_send.at[0, index], self.g_recv.at[0, index], two_device)
        elif number == 6:
            arrive(result.at[other, self.quarter_rows(one), :], self.g_recv.at[0, index], p.at())
            here = result.at[blocks, self.quarter_rows(one), :]
            self.sends.send(here, here, self.g_send.at[1, index], self.g_recv.at[1, index], one_device)
        elif number == 7:
            arrive(result.at[blocks, self.quarter_rows(1 - one), :], self.g_recv.at[1, index], p.at())
            here = result.at[blocks, self.half_rows(p.core), :]
            self.sends.send(here, here, self.g_send.at[2, index], self.g_recv.at[2, index], p.at(core=1 - p.core))
        elif number == 8:
            arrive(result.at[blocks, self.half_rows(1 - p.core), :], self.g_recv.at[2, index], p.at())


def reduce_sems(chunks, count_a):
    dma = pltpu.SemaphoreType.DMA
    return [
        dma((3, chunks)), dma((3, chunks)), dma((chunks, count_a)), dma((chunks, count_a)),
        dma((3, chunks)), dma((3, chunks)), dma((chunks, count_a)), dma((chunks, count_a)), dma((chunks,)),
    ]


class SmallReduce:
    def __init__(self, place, sends, held, land, sems):
        self.place, self.sends, self.held, self.land = place, sends, held, land
        self.out_sem, self.in_sem = sems
        p = place
        self.devices = [p.at(core=1 - p.core), p.at(x=1 - p.x), p.at(b=1 - p.b)]

    def send(self, step):
        if step < 3:
            self.sends.send(
                self.held.at[step], self.land.at[step], self.out_sem.at[step], self.in_sem.at[step],
                self.devices[step],
            )
            return
        p = self.place
        for offset in range(1, p.count_a):
            self.sends.send(
                self.held.at[3], self.land.at[3 + offset], self.out_sem.at[3 + offset],
                self.in_sem.at[3 + offset], p.at(a=p.shard(offset)),
            )

    def receive(self, step):
        p = self.place
        if step < 3:
            arrive(self.land.at[step], self.in_sem.at[step], p.at())
            self.held[step + 1] = self.held[step] + self.land[step]
            return
        for offset in range(1, p.count_a):
            arrive(self.land.at[3 + offset], self.in_sem.at[3 + offset], p.at())
        self.land[3] = self.held[3]

    def total(self):
        p = self.place
        total = self.land[3 + lax.rem(p.a, p.count_a)]
        for a in range(1, p.count_a):
            total = total + self.land[3 + lax.rem(p.a + p.count_a - a, p.count_a)]
        return total


def halo_phase(x_ref, w_ref, b_ref, omega_ref, k_ref, kv_ref, place, head_dim):
    rows_ext, width = x_ref.shape
    low, high = slice(0, WINDOW), slice(rows_ext - WINDOW, rows_ext)
    x = jnp.concatenate([x_ref[low, :], x_ref[high, :]], 0)
    ones = block_ones(CHUNK, head_dim).astype(BF16)
    factor = head_dim ** (-0.25) / SPREAD
    row = lax.broadcasted_iota(jnp.int32, (2 * WINDOW, 1), 0)
    inside = jnp.logical_or(
        jnp.logical_and(row < WINDOW, place.seq > 0),
        jnp.logical_and(row >= WINDOW, place.seq < place.shards - 1),
    )
    for part in (1, 2):
        for chunk in range(width // CHUNK):
            cols = slice(chunk * CHUNK, (chunk + 1) * CHUNK)
            wide = slice(part * width + chunk * CHUNK, part * width + (chunk + 1) * CHUNK)
            value = (nn(x, w_ref[:, wide]) + b_ref[part][:, cols]).astype(BF16)
            if part == 1:
                k_ref[low, cols], k_ref[high, cols] = value[:WINDOW], value[WINDOW:]
                widened = value.astype(F32)
                half_norm = head_sums(widened * widened, ones) * (0.5 * head_dim ** (-0.5))
                value = jnp.exp(nn(value, omega_ref[chunk]) * factor - half_norm) * head_dim ** (-0.5)
            value = jnp.where(inside, value.astype(F32), 0.0).astype(BF16)
            kv_ref[part - 1, low, cols], kv_ref[part - 1, high, cols] = value[:WINDOW], value[WINDOW:]


def ffn_forward_shard(hidden_ref, mats, a, b, shard, bias_ref, pool, acc_ref):
    rows = hidden_ref.shape[0]
    pre = nn(hidden_ref[...], mats[0, a, b]) + bias_ref[shard, 0:1, :]
    phi = 0.5 * (1.0 + lax.erf(pre * ROOT_HALF))
    act = (pre * phi).astype(BF16)
    pool[shard, 0:rows, :] = act
    pool[shard, rows : 2 * rows, :] = (phi + pre * INV_ROOT_TAU * jnp.exp(-0.5 * pre * pre)).astype(BF16)
    acc_ref[...] += nt(act, mats[1, a, b])


def ffn_backward_shard(grad_ref, grad_turned_ref, hidden_turned_ref, mats, a, b, shard, pool, acc_ref, gbias_ref):
    rows = grad_ref.shape[0]
    grad_act = nn(grad_ref[...], mats[1, a, b])
    grad_pre = (grad_act * pool[shard, rows : 2 * rows, :].astype(F32)).astype(BF16)
    gbias_ref[shard] = jnp.broadcast_to(
        jnp.sum(grad_pre.astype(F32), 0, keepdims=True), gbias_ref.shape[1:]
    )
    acc_ref[...] += nt(grad_pre, mats[0, a, b])
    mats[1, a, b] = nn(grad_turned_ref[...], pool[shard, 0:rows, :]).astype(BF16)
    mats[0, a, b] = nn(hidden_turned_ref[...], grad_pre).astype(BF16)


def row_blocks(rows, body, size=CHUNK):
    @pl.loop(0, rows // size)
    def _(index):
        body(pl.ds(pl.multiple_of(index * size, size), size))


def hidden_phase(
    x_ref, low_ref, w_ref, b_ref, gain_ref, shift_ref, b_down_ref, normed_refs, scale_ref, hidden_ref, turned_ref, acc_ref
):
    def body(rows):
        first_sum = x_ref[rows, :].astype(F32) + nn(low_ref[rows, :], w_ref[...]) + b_ref[...].astype(F32)
        normed, inv_scale = norm_parts(first_sum)
        normed_refs[0][rows, :], normed_refs[1][rows, :], normed_refs[2][rows, :] = jnp.split(normed, 3, 1)
        scale_ref[rows, :] = jnp.broadcast_to(inv_scale, (first_sum.shape[0], scale_ref.shape[1]))
        hidden_one = normed * gain_ref[...] + shift_ref[...]
        hidden = hidden_one.astype(BF16)
        hidden_ref[rows, :] = hidden
        turned_ref[:, rows] = hidden.T
        acc_ref[rows, :] = hidden_one + b_down_ref[...].astype(F32)

    row_blocks(x_ref.shape[0], body)


def middle_phase(acc_ref, cot_ref, gain_two_ref, shift_two_ref, grad_ref, grad_turned_ref, vec_ref):
    def body(rows):
        normed_two, scale_two = norm_parts(acc_ref[rows, :])
        cot = cot_ref[rows, :].astype(F32)
        cot_ref[rows, :] = (normed_two * gain_two_ref[...] + shift_two_ref[...]).astype(BF16)
        grad_second = norm_back(cot, normed_two, scale_two, gain_two_ref[...])
        grad_ffn = grad_second.astype(BF16)
        vec_ref[0:1, :] += jnp.sum(cot * normed_two, 0, keepdims=True)
        vec_ref[1:2, :] += jnp.sum(cot, 0, keepdims=True)
        vec_ref[2:3, :] += jnp.sum(grad_ffn.astype(F32), 0, keepdims=True)
        acc_ref[rows, :] = grad_second
        grad_ref[rows, :] = grad_ffn
        grad_turned_ref[:, rows] = grad_ffn.T

    row_blocks(cot_ref.shape[0], body)


def first_back_phase(acc_ref, normed_refs, scale_ref, gain_one_ref, low_ref, vec_ref):
    def body(rows):
        grad_hidden = acc_ref[rows, :]
        normed = jnp.concatenate([ref[rows, :] for ref in normed_refs], 1)
        grad_first = norm_back(grad_hidden, normed, scale_ref[rows, 0:1], gain_one_ref[...])
        grad_low = grad_first.astype(BF16)
        acc_ref[rows, :] = grad_first
        low_ref[rows, :] = grad_low
        vec_ref[3:4, :] += jnp.sum(grad_hidden * normed, 0, keepdims=True)
        vec_ref[4:5, :] += jnp.sum(grad_hidden, 0, keepdims=True)
        vec_ref[5:6, :] += jnp.sum(grad_low.astype(F32), 0, keepdims=True)

    row_blocks(low_ref.shape[0], body)


def attn_back_phase(glow_ref, w_ref, out_ref, denom_ref, low_ref, qf_ref, dnum_ref, dden_ref, total_ref, pairs, head_dim):
    rows_all = glow_ref.shape[0]
    blocks = rows_all // WINDOW
    half = LANES // 2
    ones = block_ones(LANES, head_dim).astype(BF16)
    grad_low = glow_ref[...]
    for pair in range(pairs):
        cols = slice(pair * LANES, (pair + 1) * LANES)
        grad_attn = nt(grad_low, w_ref[cols, :])
        grad_num = (grad_attn / denom_ref[:, cols]).astype(BF16)
        grad_den = -head_sums(grad_num.astype(F32) * out_ref[:, cols], ones)
        low_ref[:, cols] = grad_num
        denom_ref[:, cols] = grad_den
        total = jnp.zeros((half, LANES), F32)
        total_den = jnp.zeros((1, LANES), F32)
        for block in range(blocks):
            rows = slice(block * WINDOW, (block + 1) * WINDOW)
            query = qf_ref[rows, cols]
            num = compact(tn(query, grad_num[rows]))
            den = jnp.sum(query.astype(F32) * grad_den[rows], 0, keepdims=True)
            dnum_ref[pair * blocks + block] = num
            dden_ref[pair * blocks + block : pair * blocks + block + 1, :] = den
            total = total + num
            total_den = total_den + den
        total_ref[pair * half : (pair + 1) * half, :] = total
        total_ref[pairs * half + pair : pairs * half + pair + 1, :] = total_den


def far_back_phase(ke_ref, ve_ref, line_ref, dnum_ref, dden_ref, past_ref, future_ref, gk_ref, gv_ref, pairs, start, stop, first_col, head_dim):
    blocks = ke_ref.shape[0] // WINDOW - 2
    half = LANES // 2

    @pl.loop(start, stop)
    def _(pair):
        ones_f32 = block_ones(LANES, head_dim)
        cols = lanes(pair)
        out = lanes(pair - first_col)
        left_coef, right_coef = far_coefs(line_ref, pair)
        state_rows = pl.ds(pl.multiple_of(pair * half, half), half)
        den_row = pl.ds(pairs * half + pair, 1)
        nums = [dnum_ref[pair * blocks + block] for block in range(blocks)]
        dens = [dden_ref[pl.ds(pair * blocks + block, 1), :] for block in range(blocks)]
        for block in range(blocks):
            num_left, den_left = future_ref[state_rows, :], future_ref[den_row, :]
            num_right, den_right = past_ref[state_rows, :], past_ref[den_row, :]
            for other in range(blocks):
                if other >= block + 2:
                    num_left, den_left = num_left + nums[other], den_left + dens[other]
                if other <= block - 2:
                    num_right, den_right = num_right + nums[other], den_right + dens[other]
            rows = slice((block + 1) * WINDOW, (block + 2) * WINDOW)
            far_k, far_v = row_grads(
                ke_ref[rows, cols],
                ve_ref[rows, cols],
                left_coef * num_left + right_coef * num_right,
                left_coef * den_left + right_coef * den_right,
                ones_f32,
            )
            gk_ref[rows, out] += far_k
            gv_ref[rows, out] += far_v


def qkv_grad_phase(
    turned_ref, w_ref, omega_ref, q_ref, k_ref, qf_ref, kf_ref, gq_ref, gk_ref, gv_ref, grads_ref, parts, small_ref,
    group, wanted, place, head_dim,
):
    width, rows_ext = turned_ref.shape
    rows_all = rows_ext - 2 * WINDOW
    own = slice(WINDOW, WINDOW + rows_all)
    ones = block_ones(CHUNK, head_dim).astype(BF16)
    factor = head_dim ** (-0.25) / SPREAD
    cols = slice(group * CHUNK, (group + 1) * CHUNK)
    omega = omega_ref[group]
    base = group * 3 * CHUNK
    block = parts.shape[2]
    for part, low_ref, feat_ref in ((0, q_ref, qf_ref), (1, k_ref, kf_ref), (2, None, None)):
        if part not in wanted:
            continue
        out = slice(part * CHUNK, (part + 1) * CHUNK)

        def body(rows):
            if part == 0:
                grad = gq_ref[rows, cols]
            else:
                grad = (gk_ref if part == 1 else gv_ref)[rows, :]
            if part < 2:
                inner_up, inner_low = halves(grad * feat_ref[rows, cols].astype(F32))
                projected = (nt(inner_up, omega) + nt(inner_low, omega)) * factor
                sums = nn(inner_up, ones) + nn(inner_low, ones)
                grad = projected - sums * head_dim ** (-0.5) * low_ref[rows, cols].astype(F32)
            if part > 0:
                row = lax.broadcasted_iota(jnp.int32, (CHUNK, 1), 0) + rows.start
                inside = jnp.logical_and(
                    jnp.logical_or(row >= WINDOW, place.seq > 0),
                    jnp.logical_or(row < rows_ext - WINDOW, place.seq < place.shards - 1),
                )
                grad = jnp.where(inside, grad, 0.0)
            low = grad.astype(BF16)
            if part == 0:
                rows = pl.ds(pl.multiple_of(rows.start + WINDOW, WINDOW), CHUNK)
            grads_ref[rows, out] = low
            small_ref[6 + group : 7 + group, out] += jnp.sum(low.astype(F32), 0, keepdims=True)

        row_blocks(rows_all if part == 0 else rows_ext, body)
        rows = own if part == 0 else slice(0, rows_ext)
        weight = nn(turned_ref[:, rows], grads_ref[rows, out]).astype(BF16)
        start = width + base + part * CHUNK
        done = 0
        while done < CHUNK:
            index, at = (start + done) // block, (start + done) % block
            size = min(CHUNK - done, block - at)
            parts[index, 0:width, at : at + size] = weight[:, done : done + size]
            done += size


def table_grads(gline_ref, bucket_ref, buckets, small_ref):
    heads = gline_ref.shape[0]
    head = lax.broadcasted_iota(jnp.int32, (heads, LANES), 0)
    lane_bucket = lax.broadcasted_iota(jnp.int32, (LANES, LINE), 0)
    total = jnp.zeros((heads, LANES), F32)
    per_row = LANES // buckets
    for place in range(per_row):
        one_hot = jnp.where(lane_bucket - place * buckets == bucket_ref[...].astype(jnp.int32), 1.0, 0.0)
        sums = lax.dot_general(
            gline_ref[...], one_hot, (((1,), (1,)), ((), ())), precision=lax.Precision.HIGHEST,
            preferred_element_type=F32,
        )
        total = total + jnp.where(head % per_row == place, sums, 0.0)
    for index in range(heads // per_row):
        small_ref[13 + index : 14 + index, 0:LANES] = jnp.sum(
            total[index * per_row : (index + 1) * per_row], 0, keepdims=True
        )


def layer_kernel(pairs, head_dim, buckets, shards, *refs):
    x_h, cot_h, up_h, down_h, w_r, omega_r, table_r, wo_r, packed_r = refs[:9]
    layer_h, gtok_h, total_r, small_r, result_h, core_h, ac_h = refs[9:16]
    (x_r, q_r, k_r, qf_r, kv_r, line_r, num_r, den_r, tot_r, biases, before_r, after_r, left_r, right_r,
     lden_r, rden_r, attn_r, denom_r, low_r, scale_r, hidden_r, turned_r, cot_r, acc_r,
     mats, pool, bias_r, gbias_r, gk_r, gv_r, gline_r, cg_r, gqkv_r) = refs[16:49]
    stage_r, xl_r, yl_r, zl_r, ll_r = refs[49:54]
    ac_r, ao_r, at_r, aa_r, done_r, held_r, land_r = refs[54:61]
    sum_buffers, sum_two_buffers = refs[61:67], refs[67:73]
    sems = refs[73:]
    all_rows = pl.ds(0, q_r.shape[0])
    normed_r = (gk_r.at[0, all_rows], gk_r.at[1, all_rows], gv_r.at[0, all_rows])
    gturned_r = gqkv_r.at[:, all_rows]
    edge_r, tail_r = cot_r.at[pl.ds(0, 2 * WINDOW)], cot_r.at[pl.ds(2 * WINDOW, 2 * WINDOW)]
    w_sems, s_sems, s2_sems, rs_sems = sems[:8], sems[8:12], sems[12:16], sems[16:27]
    ar_sems, sm_sems, bias_sems = sems[27:36], sems[36:38], sems[38:40]
    h_send, h_recv, t_send, t_recv, load_sem = sems[40:]
    rows, width = q_r.shape
    half = LANES // 2
    line = [packed_r.at[pl.ds(index, 1)] for index in range(packed_r.shape[0])]
    b_r, bo_r, g1_r, s1_r, bdown_r, g2_r, s2_r = line[:3], *line[3:9]
    bup_r, bucket_r = line[9].at[:, pl.ds(0, up_h.shape[1])], line[10].at[:, pl.ds(0, LINE)]
    own = pl.ds(WINDOW, rows)
    place = Place(shards)
    sends = Sends()
    seq = place.seq
    peers = [place.beside(lax.rem(seq + o, shards)) for o in range(1, shards)]
    peers += [place.at(core=1 - place.core), place.at(x=1 - place.x)]
    barrier = pltpu.get_barrier_semaphore()
    for peer in peers:
        pl.semaphore_signal(barrier, inc=1, device_id=peer, device_id_type=MESH)
    loads = [
        pltpu.make_async_copy(src, dst, load_sem.at[i])
        for i, (src, dst) in enumerate((
            (down_h, hidden_r.at[pl.ds(0, down_h.shape[0])]), (up_h, mats.at[0, place.a, place.b]),
            (x_h, x_r.at[own]), (cot_h, cot_r),
        ))
    ]
    for load in loads:
        load.start()
    gather = WeightGather(place, sends, mats, width // 3, w_sems)
    key_sums = StateSums(place, sends, sum_buffers, s_sems)
    grad_sums = StateSums(place, sends, sum_two_buffers, s2_sems)
    scatter = GradScatter(place, sends, mats, total_r, ll_r.shape[0], (core_h, stage_r, xl_r, yl_r, zl_r, ll_r), rs_sems)
    chunks = done_r.shape[0]
    reduce = AllReduce(place, sends, pool, result_h, (ac_h, ac_r, ao_r, at_r, aa_r), done_r, (1, chunks - 1), ar_sems)
    little = SmallReduce(place, sends, held_r, land_r, sm_sems)
    to_right = place.beside(jnp.minimum(seq + 1, shards - 1))
    to_left = place.beside(jnp.maximum(seq - 1, 0))
    low_edge, high_edge = pl.ds(0, WINDOW), pl.ds(rows + WINDOW, WINDOW)

    small_r[...] = jnp.zeros(small_r.shape, F32)
    acc_r[0:WINDOW, :] = jnp.zeros((WINDOW, width), F32)
    acc_r[rows + WINDOW :, :] = jnp.zeros((WINDOW, width), F32)
    loads[0].wait()
    mats[1, place.a, place.b] = hidden_r[0 : down_h.shape[0], :].T
    loads[1].wait()
    loads[2].wait()
    pl.semaphore_wait(barrier, len(peers))
    sends.send(
        x_r.at[pl.ds(rows, WINDOW)], x_r.at[low_edge], h_send.at[0], h_recv.at[0], to_right, place.not_last
    )
    sends.send(
        x_r.at[pl.ds(WINDOW, WINDOW)], x_r.at[high_edge], h_send.at[1], h_recv.at[1], to_left, place.not_first
    )
    biases[seq] = jnp.broadcast_to(bup_r[...], biases.shape[1:]).astype(BF16)
    for offset in range(1, shards):
        sends.send(
            biases.at[seq], biases.at[seq], bias_sems[0].at[offset], bias_sems[1].at[offset],
            place.beside(lax.rem(seq + offset, shards)),
        )
    gather.along_a(0)

    @pl.when(place.is_first)
    def _():
        x_r[0:WINDOW, :] = jnp.zeros((WINDOW, width), BF16)

    @pl.when(place.is_last)
    def _():
        x_r[rows + WINDOW :, :] = jnp.zeros((WINDOW, width), BF16)

    ke_r, ve_r = kv_r.at[0], kv_r.at[1]
    qkv_phase(
        x_r.at[own], w_r, b_r, omega_r, ((1, k_r.at[own], ke_r.at[own]), (2, ve_r.at[own], None)), head_dim
    )
    tot_r[pairs * half :, :] = jnp.zeros((tot_r.shape[0] - pairs * half, LANES), F32)
    state_phase(ke_r.at[own], ve_r.at[own], num_r, den_r, tot_r, pairs)
    key_sums.start(tot_r)
    gather.across(0)
    qkv_phase(x_r.at[own], w_r, b_r, omega_r, ((0, q_r, qf_r),), head_dim)
    line_phase(bucket_r, table_r, line_r)
    arrive(x_r.at[low_edge], h_recv.at[0], place.at(), place.not_first)
    arrive(x_r.at[high_edge], h_recv.at[1], place.at(), place.not_last)
    halo_phase(x_r, w_r, b_r, omega_r, k_r, kv_r, place, head_dim)
    third = pairs // 3

    def ffn(step, column, forward):
        a = place.nearest(step) if forward else place.shard(step)
        b = 1 - place.b if column else place.b
        shard = a * place.count_b + b
        if forward:
            ffn_forward_shard(hidden_r, mats, a, b, shard, bias_r, pool, acc)
        else:
            ffn_backward_shard(hidden_r, gturned_r, hidden_turned, mats, a, b, shard, pool, acc, gbias_r)

    key_sums.along_a()
    band_forward_phase(qf_r, ke_r, ve_r, line_r, attn_r, denom_r, 0, third)
    gather.along_a(1)
    band_forward_phase(qf_r, ke_r, ve_r, line_r, attn_r, denom_r, third, 2 * third)
    band_forward_phase(qf_r, ke_r, ve_r, line_r, attn_r, denom_r, 2 * third, pairs)
    key_sums.along_b()
    gather.across(1)
    gather.along_b(0)
    key_sums.finish(before_r, after_r)
    gather.along_a(2)
    gather.across(2)
    far_forward_phase(
        qf_r, ke_r, ve_r, line_r, num_r, den_r, before_r, after_r, attn_r, low_r, denom_r, left_r, right_r, lden_r,
        rden_r, pairs, head_dim,
    )
    hidden_turned = turned_r.at[:, pl.ds(0, rows)]
    acc = acc_r.at[own]
    hidden_phase(
        x_r.at[own], low_r, wo_r, bo_r, g1_r, s1_r, bdown_r, normed_r, scale_r, hidden_r, hidden_turned, acc
    )
    for offset in range(1, shards):
        arrive(biases.at[lax.rem(seq + shards - offset, shards)], bias_sems[1].at[offset], place.at())
    for shard in range(shards):
        bias_r[shard] = biases[shard, 0:8, :].astype(F32)
    ffn(0, 0, True)
    gather.along_b(1)
    gather.along_x(1, 0)
    gather.along_x(0, 1)
    gather.finish(0, 1)
    ffn(0, 1, True)
    gather.along_a(3)
    gather.across(3)
    gather.finish(1, 0)
    ffn(1, 0, True)
    gather.along_x(1, 1)
    gather.along_b(2)
    gather.along_x(2, 0)
    gather.finish(1, 1)
    ffn(1, 1, True)
    gather.finish(2, 0)
    ffn(2, 0, True)
    gather.along_x(2, 1)
    gather.along_x(3, 0)
    gather.along_b(3)
    gather.finish(2, 1)
    ffn(2, 1, True)
    gather.finish(3, 0)
    ffn(3, 0, True)
    gather.along_x(3, 1)
    gather.finish(3, 1)
    ffn(3, 1, True)
    sends.drain()
    loads[3].wait()
    middle_phase(acc, cot_r, g2_r, s2_r, hidden_r, gturned_r, small_r)
    layer_out = pltpu.make_async_copy(cot_r, layer_h, load_sem.at[4])
    layer_out.start()
    items = [(offset, column) for offset in (1, 2, 3, 0) for column in (1, 0)]
    for index, item in enumerate(items):
        ffn(*item, False)
        scatter.start(*item)
        if index > 1:
            scatter.chip(*items[index - 2])
        if index > 0:
            scatter.fetch(*items[index - 1])
        if index == 6:
            scatter.along_x(*items[0])
    first_back_phase(acc, normed_r, scale_r, g1_r, hidden_r, small_r)
    tot_r[pairs * half :, :] = jnp.zeros((tot_r.shape[0] - pairs * half, LANES), F32)
    block = pool.shape[2]
    for index in range(width // block):
        cols = slice(index * block, (index + 1) * block)
        pool[index, 0:width, :] = tn(low_r[...], hidden_r[:, cols]).astype(BF16)
    reduce.push(0)
    scatter.chip(*items[6])
    scatter.fetch(*items[7])
    scatter.along_x(*items[1])
    attn_back_phase(hidden_r, wo_r, attn_r, denom_r, low_r, qf_r, num_r, den_r, tot_r, pairs, head_dim)
    layer_out.wait()
    grad_sums.start(tot_r)
    scatter.chip(*items[7])
    scatter.along_x(*items[2])
    reduce.stage(0, 1)

    def turn(block):
        turned_r[:, block] = x_r[block, :].T

    row_blocks(rows + 2 * WINDOW, turn)
    groups = pairs * LANES // CHUNK
    in_group = CHUNK // LANES

    def band(pair):
        group = pair // in_group
        band_backward_phase(
            qf_r, ke_r, ve_r, line_r, low_r, denom_r, num_r, den_r, left_r, right_r, lden_r, rden_r, attn_r,
            gk_r.at[group % 2], gv_r.at[group % 2], gline_r, cg_r, pair, pair + 1, group * in_group, head_dim,
        )

    def far(group):
        far_back_phase(
            ke_r, ve_r, line_r, num_r, den_r, before_r, after_r, gk_r.at[group % 2], gv_r.at[group % 2], pairs,
            group * in_group, (group + 1) * in_group, group * in_group, head_dim,
        )

    def grads(group, wanted):
        qkv_grad_phase(
            turned_r, w_r, omega_r, q_r, k_r, qf_r, ke_r, attn_r, gk_r.at[group % 2], gv_r.at[group % 2], gqkv_r,
            pool, small_r, group, wanted, place, head_dim,
        )

    def tokens_part(group, wanted):
        def body(block):
            if 1 not in wanted:
                block = pl.ds(pl.multiple_of(block.start + WINDOW, WINDOW), CHUNK)
            total = acc_r[block, :]
            for part in wanted:
                cols = slice(part * CHUNK, (part + 1) * CHUNK)
                wide = slice(part * width + group * CHUNK, part * width + (group + 1) * CHUNK)
                total = total + nt(gqkv_r[block, cols], w_r[:, wide])
            acc_r[block, :] = total

        row_blocks(rows + 2 * WINDOW if 1 in wanted else rows, body)

    band(0)
    grad_sums.along_a()
    scatter.along_x(*items[3])
    band(1)
    grads(0, (0,))
    tokens_part(0, (0,))
    band(2)
    grad_sums.along_b()
    scatter.along_b(1)
    scatter.along_x(*items[4])
    band(3)
    grad_sums.finish(before_r, after_r)
    scatter.along_x(*items[5])
    far(0)
    scatter.along_b(2)
    grads(0, (1, 2))
    reduce.push(1)
    tokens_part(0, (1, 2))
    scatter.along_x(*items[6])
    grads(1, (0,))
    tokens_part(1, (0,))
    scatter.along_x(*items[7])
    band(4)
    reduce.stage(1, 1)
    reduce.stage(0, 2)
    band(5)
    scatter.along_b(3)
    far(1)
    grads(1, (1, 2))
    reduce.push(2)
    reduce.stage(0, 3)
    scatter.along_b(0)
    tokens_part(1, (1, 2))
    grads(2, (0,))
    tokens_part(2, (0,))
    reduce.stage(2, 1)
    reduce.stage(1, 2)
    far(2)
    grads(2, (1, 2))
    reduce.push(3)
    table_grads(gline_r, bucket_r, buckets, small_r)
    per_row = width // gbias_r.shape[2]
    for index in range(shards // per_row):
        small_r[9 + index : 10 + index, :] = jnp.concatenate(
            [gbias_r[index * per_row + i, 0:1, :] for i in range(per_row)], 1
        )
    held_r[0] = small_r[...]
    little.send(0)
    reduce.stage(1, 3)
    reduce.stage(3, 1)
    tokens_part(2, (1, 2))
    edge_r[0:WINDOW, :] = acc_r[0:WINDOW, :].astype(BF16)
    edge_r[WINDOW:, :] = acc_r[rows + WINDOW :, :].astype(BF16)
    top, bottom = pl.ds(0, WINDOW), pl.ds(WINDOW, WINDOW)
    sends.send(edge_r.at[top], tail_r.at[bottom], t_send.at[0], t_recv.at[1], to_left, place.not_first)
    sends.send(edge_r.at[bottom], tail_r.at[top], t_send.at[1], t_recv.at[0], to_right, place.not_last)
    reduce.stage(2, 2)
    reduce.stage(0, 4)
    reduce.stage(3, 2)
    little.receive(0)
    little.send(1)
    reduce.stage(2, 3)
    reduce.stage(1, 4)
    reduce.stage(3, 3)
    reduce.stage(0, 5)
    scatter.along_a()
    reduce.stage(2, 4)
    reduce.stage(1, 5)
    little.receive(1)
    little.send(2)
    reduce.stage(3, 4)
    reduce.stage(0, 6)
    reduce.stage(2, 5)
    reduce.stage(1, 6)
    reduce.stage(3, 5)
    little.receive(2)
    little.send(3)
    arrive(tail_r.at[top], t_recv.at[0], place.at(), place.not_first)
    arrive(tail_r.at[bottom], t_recv.at[1], place.at(), place.not_last)

    @pl.when(place.not_first)
    def _():
        acc_r[WINDOW : 2 * WINDOW, :] += tail_r[0:WINDOW, :].astype(F32)

    @pl.when(place.not_last)
    def _():
        acc_r[rows : rows + WINDOW, :] += tail_r[WINDOW:, :].astype(F32)

    tokens_out = pltpu.make_async_copy(acc, gtok_h, load_sem.at[5])
    tokens_out.start()
    reduce.stage(2, 6)
    reduce.stage(3, 6)
    scatter.last_x()
    reduce.stage(0, 7)
    reduce.stage(1, 7)
    little.receive(3)
    small_r[...] = little.total()
    reduce.stage(3, 7)
    reduce.stage(2, 7)
    scatter.finish()
    for index in range(chunks):
        reduce.stage(index, 8)
    tokens_out.wait()
    sends.drain()


def in_parts(grouped):
    groups = grouped.shape[1] // (3 * CHUNK)
    starts = [(group * 3 + part) * CHUNK for part in range(3) for group in range(groups)]
    return jnp.concatenate([grouped[:, start : start + CHUNK].astype(F32) for start in starts], 1)


def call(body, outs, operands, scratch=(), limit=60, collective_id=None, in_place=(), out_place=()):
    return pl.pallas_call(
        body,
        out_shape=[jax.ShapeDtypeStruct(shape, dtype) for shape, dtype in outs],
        in_specs=[
            pl.BlockSpec(memory_space=pl.ANY if i in in_place else pltpu.VMEM) for i in range(len(operands))
        ],
        out_specs=[
            pl.BlockSpec(memory_space=pl.ANY if i in out_place else pltpu.VMEM) for i in range(len(outs))
        ],
        scratch_shapes=list(scratch),
        compiler_params=pltpu.CompilerParams(
            vmem_limit_bytes=limit * MIB,
            collective_id=collective_id,
            has_side_effects=collective_id is not None,
        ),
    )(*operands)


def unpack_kernel(
    result_r, total_r, tokens_r, layer_r, small_r, gw_r, gwo_r, gup_r, gdown_r, gtok_r, out_r, gb_r, gbu_r, *vector_rs
):
    blocks, width, block = result_r.shape
    for index in range(blocks):
        at = 0
        while at < block:
            column = index * block + at
            if column < width:
                target, place, size = gwo_r, column, block - at
            else:
                group, rest = divmod(column - width, 3 * CHUNK)
                part, inner = divmod(rest, CHUNK)
                target, place = gw_r, part * width + group * CHUNK + inner
                size = min(block - at, CHUNK - inner)
            target[:, place : place + size] = result_r[index, :, at : at + size].astype(F32)
            at += size
    gup_r[...] = total_r[0].astype(F32)
    gdown_r[...] = total_r[1].T.astype(F32)
    gtok_r[...] = tokens_r[...]
    out_r[...] = layer_r[...]
    for index, ref in enumerate(vector_rs):
        ref[...] = small_r[index, :]
    for group in range(width // CHUNK):
        for part in range(3):
            start = part * width + group * CHUNK
            gb_r[start : start + CHUNK] = small_r[6 + group, part * CHUNK : (part + 1) * CHUNK]
    units = gbu_r.shape[0]
    seq = lax.axis_index("seq")
    per_row = width // units
    for shard in range(lax.axis_size("seq")):
        @pl.when(seq == shard)
        def _():
            at = shard % per_row * units
            gbu_r[...] = small_r[9 + shard // per_row, at : at + units]


def fused(
    x, cot, w_up, w_down, w_qkv, b_qkv, omega, bucket_line, bias_table, w_out, b_out, gain_one, shift_one, b_up, b_down,
    gain_two, shift_two, pairs, head_dim,
):
    rows, width = x.shape
    units = w_up.shape[1]
    heads, buckets = bias_table.shape
    count = lax.axis_size("seq")
    count_a = count // 2
    blocks, half = rows // WINDOW, LANES // 2
    middle, quarter = width // 6, width // 4
    side = (width - middle) // 2
    groups = width // CHUNK
    chunks = 1 + groups
    columns = chunks * width // units
    wide, ext = (rows, width), (rows + 2 * WINDOW, width)
    stacked, flat = (pairs * blocks, half, LANES), (pairs * blocks, LANES)
    message = (pairs * half + 32, LANES)
    mats = (2, count_a, 2, width, units)
    dma = pltpu.SemaphoreType.DMA
    vmem = pltpu.VMEM
    part = (message[0] // 2, LANES)
    sums = [vmem(shape, BF16) for shape in (message, message, part, (count_a, *part), (2, *part), (2, *part))]
    vectors = [b_qkv, b_out, gain_one, shift_one, b_down, gain_two, shift_two]
    vectors += [jnp.pad(vector, (0, width - vector.shape[0])) for vector in (b_up, bucket_line[0])]
    packed = jnp.concatenate([vector.astype(F32) for vector in vectors]).reshape(-1, width)
    layer, gtok, total, small, result, _, _ = call(
        functools.partial(layer_kernel, pairs, head_dim, buckets, count),
        [(wide, BF16), (wide, F32), ((2, width, units), BF16), ((16, width), F32), ((columns, width, units), BF16),
         (mats[1:], BF16), ((columns, 2 * quarter, units), BF16)],
        (x, cot, w_up, w_down, w_qkv, omega, bias_table, w_out, packed),
        [vmem(ext, BF16), vmem(wide, BF16), vmem(ext, BF16), vmem(wide, BF16), vmem((2, *ext), BF16),
         vmem((heads, LINE), F32), vmem(stacked, F32), vmem(flat, F32), vmem(message, F32),
         vmem((count, 16, units), BF16), vmem(message, F32),
         vmem(message, F32), vmem(stacked, F32), vmem(stacked, F32), vmem(flat, F32), vmem(flat, F32),
         vmem(wide, F32), vmem(wide, F32), vmem(wide, BF16), vmem((rows, LANES), F32),
         vmem(wide, BF16), vmem((width, ext[0]), BF16),
         vmem(wide, BF16), vmem(ext, F32), vmem(mats, BF16), vmem((columns, 2 * rows, units), BF16),
         vmem((count, 8, units), F32), vmem((count, 8, units), F32), vmem((2, ext[0], CHUNK), F32),
         vmem((2, ext[0], CHUNK), F32), vmem((heads, LINE), F32), vmem((2 * WINDOW, 3 * WINDOW), F32),
         vmem(ext, BF16), vmem((2, width, units), BF16), vmem((count_a, 2, side, units), BF16),
         vmem((count_a, side + middle, units), BF16), vmem((count_a - 1, side + middle, units), BF16),
         vmem((middle, units), BF16),
         vmem((2, 2 * quarter, units), BF16), vmem((columns, quarter, units), BF16),
         vmem((chunks, quarter, units), BF16), vmem((chunks, count_a - 1, quarter // count_a, units), BF16),
         vmem((chunks, quarter // count_a, units), BF16), vmem((4, 16, width), F32),
         vmem((3 + count_a, 16, width), F32)]
        + sums + sums
        + gather_sems(count_a) + sums_sems(count_a) + sums_sems(count_a) + scatter_sems(count_a)
        + reduce_sems(chunks, count_a)
        + [dma((3 + count_a,)), dma((3 + count_a,))] + [dma((count,)), dma((count,))] + [ dma((2,)), dma((2,)), dma((2,)), dma((2,)), dma((6,))],
        limit=62,
        collective_id=0,
        in_place=(0, 1, 2, 3),
        out_place=(0, 1, 4, 5, 6),
    )
    vector = ((width,), F32)
    gw_qkv, gw_out, gup, gdown, gtok, layer, gb_qkv, grad_b_up, g2, s2, bd, g1, s1, bo = call(
        unpack_kernel,
        [((width, 3 * width), F32), ((width, width), F32), ((width, units), F32), ((units, width), F32), (wide, F32),
         (wide, BF16), ((3 * width,), F32), ((units,), F32)] + [vector] * 6,
        (result, total, gtok, layer, small),
    )
    gtable = small[13 : 13 + heads * buckets // LANES, :LANES].reshape(heads, buckets)
    return (
        layer[None], gtok[None], gw_qkv, gb_qkv, gw_out, bo, g1, s1, gup, grad_b_up, gdown, bd, g2, s2, gtable,
    )


def shards(
    tokens, cotangent, w_qkv, b_qkv, w_out, b_out, gain_one, shift_one, w_up, b_up, w_down, b_down,
    gain_two, shift_two, feature_codes, bias_table, offset_bucket,
):
    rows, width = tokens.shape[1:]
    heads, head_dim, feats = feature_codes.shape
    buckets = bias_table.shape[1]
    pairs = heads // 2
    blocks = rows // WINDOW
    half = LANES // 2
    hidden_units = w_up.shape[1]
    length = (offset_bucket.shape[0] + 1) // 2
    count = lax.axis_size("seq")
    x = tokens[0]
    omega_int = (feature_codes.astype(F32) - CENTER).astype(BF16)
    group = CHUNK // head_dim
    eye = jnp.eye(group, dtype=BF16)
    omega = (
        omega_int.reshape(heads // group, group, head_dim, 1, feats)
        * eye[None, :, None, :, None]
    ).reshape(heads // group, CHUNK, CHUNK)
    bucket_line = offset_bucket[length - LINE // 2 : length + LINE // 2][None]
    state = (pairs * half + 8, LANES)
    stacked = (pairs * blocks, half, LANES)
    flat = (pairs * blocks, LANES)
    wide = (rows, width)

    def halo(block):
        forward = [(i, i + 1) for i in range(count - 1)]
        backward = [(target, source) for source, target in forward]
        low = lax.ppermute(block[rows - WINDOW :], "seq", forward)
        high = lax.ppermute(block[:WINDOW], "seq", backward)
        return jnp.concatenate([low, block, high], 0)

    me = lax.axis_index("seq")
    ids = jnp.arange(count)

    def prefix(message):
        every = lax.all_gather(message, "seq", axis=0)
        before = jnp.sum(jnp.where((ids < me)[:, None, None], every, 0.0), 0)
        after = jnp.sum(jnp.where((ids > me)[:, None, None], every, 0.0), 0)
        return before, after

    if lax.axis_size("row") == 4 and count == 8:
        return fused(
            x, cotangent[0], w_up, w_down, w_qkv, b_qkv, omega, bucket_line, bias_table, w_out, b_out, gain_one,
            shift_one, b_up, b_down, gain_two, shift_two, pairs, head_dim,
        )

    def body_one(x_r, w_r, b_r, o_r, bu_r, ta_r, q_r, k_r, v_r, qf_r, kf_r, line_r, num_r, den_r, tot_r):
        parts = ((1, k_r, kf_r), (2, v_r, None), (0, q_r, qf_r))
        qkv_phase(x_r, w_r, [b_r.at[pl.ds(i, 1)] for i in range(3)], o_r, parts, head_dim)
        line_phase(bu_r, ta_r, line_r)
        state_phase(kf_r, v_r, num_r, den_r, tot_r, pairs)

    q, k, v, qf, kf, line, num, den, total = call(
        body_one,
        [(wide, BF16)] * 5
        + [((heads, LINE), F32), (stacked, F32), (flat, F32), (state, F32)],
        (x, w_qkv, b_qkv.astype(F32).reshape(3, width), omega, bucket_line, bias_table),
    )
    up_all = lax.all_gather(w_up, "seq", axis=0)
    down_all = lax.all_gather(jnp.transpose(w_down), "seq", axis=0)
    b_up_all = jnp.broadcast_to(lax.all_gather(b_up, "seq", axis=0)[:, None, :], (count, 8, hidden_units))

    ke, ve = halo(kf), halo(v)
    before, after = prefix(total)

    def body_two(*refs):
        ins, outs = refs[:12], refs[12:]
        qf_r, ke_r, ve_r, line_r, num_r, den_r, bef_r, aft_r, x_r, w_r, b_r, _ = ins
        out_r, low_r, dnm_r, l_r, r_r, ld_r, rd_r, nrm_r, sc_r = outs
        band_forward_phase(qf_r, ke_r, ve_r, line_r, out_r, dnm_r, 0, pairs)
        far_forward_phase(
            qf_r, ke_r, ve_r, line_r, num_r, den_r, bef_r, aft_r,
            out_r, low_r, dnm_r, l_r, r_r, ld_r, rd_r, pairs, head_dim,
        )
        out_phase(x_r, low_r, w_r, b_r, nrm_r, sc_r)

    attn, attn_low, denom, left, right, left_den, right_den, normed, scale = call(
        body_two,
        [(wide, F32), (wide, BF16), (wide, F32), (stacked, F32), (stacked, F32), (flat, F32),
         (flat, F32), (wide, F32), ((rows, LANES), F32)],
        (qf, ke, ve, line, num, den, before, after, x, w_out, b_out[None], gain_one[None]),
    )
    layer, first, first_low, vec, gup, gdown, gbias = call(
        ffn_phase,
        [(wide, BF16), (wide, F32), (wide, BF16), ((8, width), F32),
         ((count, width, hidden_units), BF16), ((count, width, hidden_units), BF16),
         ((count, 8, hidden_units), F32)],
        (normed, scale, gain_one[None], shift_one[None], up_all, b_up_all, down_all, b_down[None],
         gain_two[None], shift_two[None], cotangent[0]),
        (pltpu.VMEM((count, rows, hidden_units), BF16), pltpu.VMEM((count, rows, hidden_units), BF16),
         pltpu.VMEM(wide, F32)),
    )

    def reduced(part):
        return lax.psum(lax.psum_scatter(part, "seq", scatter_dimension=0), "row").astype(F32)

    grad_w_up = reduced(gup)
    grad_w_down = jnp.transpose(reduced(gdown))
    grad_b_up = reduced(gbias[:, 0])
    ext = (rows + 2 * WINDOW, width)

    def body_four(*refs):
        (gl_r, w_r, lo_r, ou_r, dn_r, qf_r, ke_r, ve_r, li_r, l_r, r_r, ld_r, rd_r, bu_r) = refs[:14]
        gw_r, gq_r, gk_r, gv_r, dnum_r, dden_r, tot_r, gt_r, gnum_r, gden_r, gline_r, cg_r = refs[14:]
        out_back_phase(
            gl_r, w_r, lo_r, ou_r, dn_r, qf_r, gnum_r, gden_r, gw_r, dnum_r, dden_r, tot_r, pairs, head_dim
        )
        band_backward_phase(
            qf_r, ke_r, ve_r, li_r, gnum_r, gden_r, dnum_r, dden_r, l_r, r_r, ld_r, rd_r,
            gq_r, gk_r, gv_r, gline_r, cg_r, 0, pairs, 0, head_dim,
        )
        gt_r[...] = table_phase(gline_r, bu_r, buckets)

    gw_out, gq, gk, gv, dnum, dden, gtotal, gtable = call(
        body_four,
        [((width, width), F32), (wide, F32), (ext, F32), (ext, F32), (stacked, F32), (flat, F32),
         (state, F32), (bias_table.shape, F32)],
        (first_low, w_out, attn_low, attn, denom, qf, ke, ve, line, left, right, left_den, right_den,
         bucket_line),
        (pltpu.VMEM(wide, BF16), pltpu.VMEM(wide, F32), pltpu.VMEM((heads, LINE), F32),
         pltpu.VMEM((2 * WINDOW, 3 * WINDOW), F32)),
    )
    past, future = prefix(gtotal)
    forward = [(i, i + 1) for i in range(count - 1)]
    backward = [(target, source) for source, target in forward]
    to_left = jnp.stack([gk[:WINDOW], gv[:WINDOW]]).astype(BF16)
    to_right = jnp.stack([gk[rows + WINDOW :], gv[rows + WINDOW :]]).astype(BF16)
    low_in = lax.ppermute(to_right, "seq", forward)
    high_in = lax.ppermute(to_left, "seq", backward)

    def body_five(*refs):
        (x_r, w_r, o_r, q_r, k_r, v_r, qf_r, kf_r, li_r, dn_r, dd_r, pa_r, fu_r, lo_r, hi_r, gq_r,
         gki_r, gvi_r, fi_r) = refs[:19]
        gt_r, gw_r, gb_r, gk_r, gv_r, turned_r = refs[19:]
        gk_r[...] = gki_r[...]
        gv_r[...] = gvi_r[...]
        gt_r[...] = fi_r[...]
        turned_r[...] = x_r[...].T
        key_back_phase(
            kf_r, v_r, li_r, dn_r, dd_r, pa_r, fu_r, lo_r, hi_r, gk_r, gv_r, pairs, 0, pairs, head_dim
        )
        for group in range(width // CHUNK):
            qkv_back_phase(
                turned_r, w_r, o_r, q_r, k_r, qf_r, kf_r, gq_r, gk_r, gv_r, gt_r, gw_r, gb_r, group, head_dim
            )

    gtok, gw_qkv, small = call(
        body_five,
        [(wide, F32), ((width, 4 * width), F32), ((16, width), F32)],
        (x, w_qkv, omega, q, k, v, qf, kf, line, dnum, dden, past, future, low_in, high_in, gq, gk, gv,
         first),
        (pltpu.VMEM(ext, F32), pltpu.VMEM(ext, F32), pltpu.VMEM((width, rows), BF16)),
    )
    gw_qkv = in_parts(gw_qkv[:, width:])
    gb_qkv = in_parts(small[6 : 6 + width // CHUNK].reshape(1, -1))
    summed = lax.psum((gw_qkv, gb_qkv[0], gw_out, vec, gtable), ("row", "seq"))
    gw_qkv, gb_qkv, gw_out, vec, gtable = summed
    return (
        layer[None], gtok[None], gw_qkv, gb_qkv, gw_out, vec[5], vec[3], vec[4], grad_w_up, grad_b_up,
        grad_w_down, vec[2], vec[0], vec[1], gtable,
    )


def solution(mesh):
    placed = (
        P("row", "seq", None), P("row", "seq", None), P(), P(), P(), P(), P(), P(), P(None, "seq"),
        P("seq"), P("seq", None), P(), P(), P(), P(), P(), P(),
    )
    return jax.shard_map(
        shards,
        mesh=mesh,
        in_specs=placed,
        out_specs=(
            P("row", "seq", None), P("row", "seq", None), P(), P(), P(), P(), P(), P(), P(None, "seq"),
            P("seq"), P("seq", None), P(), P(), P(), P(),
        ),
        check_vma=False,
    )
```

```python
import functools
import math

import jax
import jax.numpy as jnp
from jax import lax
from jax.experimental import pallas as pl
from jax.experimental.pallas import tpu as pltpu
from jax.sharding import PartitionSpec as P

WINDOW = 128
LANES = 128
LINE = 512
CHUNK = 256
EPS = 1e-06
CENTER = 7.5
SPREAD = math.sqrt(21.25)
ROOT_HALF = 0.7071067811865476
INV_ROOT_TAU = 0.3989422804014327
MIB = 1 << 20
F32 = jnp.float32
BF16 = jnp.bfloat16


def nn(a, b):
    return lax.dot_general(a, b, (((1,), (0,)), ((), ())), preferred_element_type=F32)


def nt(a, b):
    return lax.dot_general(a, b, (((1,), (1,)), ((), ())), preferred_element_type=F32)


def tn(a, b):
    return lax.dot_general(a, b, (((0,), (0,)), ((), ())), preferred_element_type=F32)


def halves(values):
    upper = values.astype(BF16)
    return upper, (values - upper.astype(F32)).astype(BF16)


def block_ones(size, head_dim):
    rows = lax.broadcasted_iota(jnp.int32, (size, size), 0) // head_dim
    cols = lax.broadcasted_iota(jnp.int32, (size, size), 1) // head_dim
    return jnp.where(rows == cols, 1.0, 0.0)


def head_sums(values, ones):
    upper, lower = halves(values)
    return nn(upper, ones) + nn(lower, ones)


def first_half(shape):
    return lax.broadcasted_iota(jnp.int32, shape, len(shape) - 1) < LANES // 2


def both_heads(pair):
    first = first_half((1, LANES))
    mask_a = jnp.where(first, 1.0, 0.0).astype(pair.dtype)
    mask_b = jnp.where(first, 0.0, 1.0).astype(pair.dtype)
    return jnp.concatenate([pair * mask_a, pair * mask_b], 0)


def per_head(stacked):
    rows = stacked.shape[0] // 2
    return jnp.where(first_half((rows, LANES)), stacked[:rows], stacked[rows:])


def compact(full):
    half = LANES // 2
    return jnp.where(first_half((half, LANES)), full[:half], full[half:])


def expand(small, ones):
    return jnp.concatenate([small, small], 0) * ones


def block_state(keys, values):
    return compact(tn(keys, values)), jnp.sum(keys.astype(F32), 0, keepdims=True)


def coef_tile(line_ref, pair):
    tiles = []
    for head in range(2):
        row = line_ref[pl.ds(2 * pair + head, 1), :]
        wide = pltpu.roll(
            jnp.broadcast_to(row, (WINDOW, LINE)), LINE - WINDOW + 1, 1, stride=1, stride_axis=0
        )
        tiles.append(wide[:, : 3 * WINDOW])
    return jnp.concatenate(tiles, 0)


def far_coefs(line_ref, pair):
    first = first_half((1, LANES))
    row_a = line_ref[pl.ds(2 * pair, 1), :]
    row_b = line_ref[pl.ds(2 * pair + 1, 1), :]
    left = jnp.where(first, row_a[:, 0:1], row_b[:, 0:1])
    right = jnp.where(first, row_a[:, LINE - 2 : LINE - 1], row_b[:, LINE - 2 : LINE - 1])
    return left, right


def unskew_sum(tile):
    rows = tile.shape[0]
    padded = jnp.concatenate([tile, jnp.zeros((rows, LINE - tile.shape[1]), F32)], 1)
    while rows > 8:
        rows = rows // 2
        padded = pltpu.roll(padded[:rows], rows, 1) + padded[rows:]
    while rows > 1:
        rows = rows // 2
        padded = pltpu.roll(padded[:rows], rows, 1) + padded[rows:]
    return padded


def lanes(pair):
    return pl.ds(pl.multiple_of(pair * LANES, LANES), LANES)


def qkv_phase(x_ref, w_ref, b_ref, omega_ref, parts, head_dim):
    width = x_ref.shape[1]
    x = x_ref[...]
    ones = block_ones(CHUNK, head_dim).astype(BF16)
    factor = head_dim ** (-0.25) / SPREAD
    for part, low_ref, feat_ref in parts:
        for chunk in range(width // CHUNK):
            cols = slice(chunk * CHUNK, (chunk + 1) * CHUNK)
            wide = slice(part * width + chunk * CHUNK, part * width + (chunk + 1) * CHUNK)
            low = (nn(x, w_ref[:, wide]) + b_ref[part][:, cols]).astype(BF16)
            low_ref[:, cols] = low
            if feat_ref is not None:
                projected = nn(low, omega_ref[chunk]) * factor
                widened = low.astype(F32)
                half_norm = head_sums(widened * widened, ones) * (0.5 * head_dim ** (-0.5))
                feat_ref[:, cols] = (
                    jnp.exp(projected - half_norm) * head_dim ** (-0.5)
                ).astype(BF16)


def line_phase(bucket_ref, table_ref, line_ref):
    buckets = table_ref.shape[1]
    one_hot = jnp.where(
        lax.broadcasted_iota(jnp.int32, (buckets, LINE), 0) == bucket_ref[...].astype(jnp.int32), 1.0, 0.0
    )
    logs = lax.dot_general(
        table_ref[...],
        one_hot,
        (((1,), (0,)), ((), ())),
        precision=lax.Precision.HIGHEST,
        preferred_element_type=F32,
    )
    line_ref[...] = jnp.exp(logs)


def state_phase(kf_ref, v_ref, num_ref, den_ref, total_ref, pairs):
    blocks = kf_ref.shape[0] // WINDOW
    half = LANES // 2

    @pl.loop(0, pairs)
    def _(pair):
        total = jnp.zeros((half, LANES), F32)
        total_den = jnp.zeros((1, LANES), F32)
        for block in range(blocks):
            rows = slice(block * WINDOW, (block + 1) * WINDOW)
            num, den = block_state(kf_ref[rows, lanes(pair)], v_ref[rows, lanes(pair)])
            num_ref[pair * blocks + block] = num
            den_ref[pl.ds(pair * blocks + block, 1), :] = den
            total = total + num
            total_den = total_den + den
        total_ref[pl.ds(pl.multiple_of(pair * half, half), half), :] = total
        total_ref[pl.ds(pairs * half + pair, 1), :] = total_den


def band_forward_phase(qf_ref, ke_ref, ve_ref, line_ref, out_ref, denom_ref, first, last):
    blocks = qf_ref.shape[0] // WINDOW

    @pl.loop(first, last)
    def _(pair):
        cols = lanes(pair)
        coef = coef_tile(line_ref, pair)
        for block in range(blocks):
            rows = slice(block * WINDOW, (block + 1) * WINDOW)
            window = slice(block * WINDOW, (block + 3) * WINDOW)
            scores = nt(both_heads(qf_ref[rows, cols]), ke_ref[window, cols])
            weights = (coef * scores).astype(BF16)
            values = ve_ref[window, cols]
            summed = nn(weights, jnp.concatenate([values, jnp.ones_like(values)], 1))
            out_ref[rows, cols] = per_head(summed[:, :LANES])
            denom_ref[rows, cols] = per_head(summed[:, LANES:])


def far_forward_phase(
    qf_ref, ke_ref, ve_ref, line_ref, num_ref, den_ref, before_ref, after_ref,
    out_ref, low_ref, denom_ref, left_ref, right_ref, left_den_ref, right_den_ref, pairs, head_dim,
):
    blocks = qf_ref.shape[0] // WINDOW
    half = LANES // 2

    @pl.loop(0, pairs)
    def _(pair):
        ones_f32 = block_ones(LANES, head_dim)
        ones = ones_f32.astype(BF16)
        cols = lanes(pair)
        left_coef, right_coef = far_coefs(line_ref, pair)
        state_rows = pl.ds(pl.multiple_of(pair * half, half), half)
        den_row = pl.ds(pairs * half + pair, 1)
        edge_low = block_state(ke_ref[:WINDOW, cols], ve_ref[:WINDOW, cols])
        edge_high = block_state(
            ke_ref[(blocks + 1) * WINDOW :, cols], ve_ref[(blocks + 1) * WINDOW :, cols]
        )
        past = (before_ref[state_rows, :], before_ref[den_row, :])
        future = (after_ref[state_rows, :], after_ref[den_row, :])

        def block_of(block):
            index = pair * blocks + block
            return num_ref[index], den_ref[pl.ds(index, 1), :]

        def add(one, two, sign=1.0):
            return tuple(a + sign * b for a, b in zip(one, two))

        lefts = [add(past, edge_low, -1.0), past]
        for block in range(2, blocks):
            lefts.append(add(lefts[-1], block_of(block - 2)))
        rights = [add(future, edge_high, -1.0), future]
        for block in range(2, blocks):
            rights.append(add(rights[-1], block_of(blocks + 1 - block)))
        rights = rights[::-1]
        for block in range(blocks):
            rows = slice(block * WINDOW, (block + 1) * WINDOW)
            index = pair * blocks + block
            query = qf_ref[rows, cols]
            left, left_den = lefts[block]
            right, right_den = rights[block]
            left_ref[index] = left
            right_ref[index] = right
            left_den_ref[pl.ds(index, 1), :] = left_den
            right_den_ref[pl.ds(index, 1), :] = right_den
            upper, lower = halves(expand(left_coef * left + right_coef * right, ones_f32))
            numer = out_ref[rows, cols] + nn(query, upper) + nn(query, lower)
            den_far = left_coef * left_den + right_coef * right_den
            denom = denom_ref[rows, cols] + head_sums(query.astype(F32) * den_far, ones)
            out = numer / denom
            out_ref[rows, cols] = out
            low_ref[rows, cols] = out.astype(BF16)
            denom_ref[rows, cols] = denom


def norm_parts(values):
    center = values - jnp.mean(values, -1, keepdims=True)
    inv_scale = lax.rsqrt(jnp.mean(center * center, -1, keepdims=True) + EPS)
    return center * inv_scale, inv_scale


def out_phase(x_ref, low_ref, w_ref, b_ref, normed_ref, scale_ref):
    first_sum = x_ref[...].astype(F32) + nn(low_ref[...], w_ref[...]) + b_ref[...].astype(F32)
    normed, inv_scale = norm_parts(first_sum)
    normed_ref[...] = normed
    scale_ref[...] = jnp.broadcast_to(inv_scale, scale_ref.shape)


def norm_back(grad_out, normed, inv_scale, gain):
    grad_normed = grad_out * gain
    centered = grad_normed - jnp.mean(grad_normed, -1, keepdims=True)
    return inv_scale * (centered - normed * jnp.mean(grad_normed * normed, -1, keepdims=True))


def ffn_phase(
    normed_ref, scale_ref, gain_one_ref, shift_one_ref, up_ref, b_up_ref, down_ref, b_down_ref,
    gain_two_ref, shift_two_ref, cot_ref, layer_ref, first_ref, low_ref, vec_ref, gup_ref, gdown_ref,
    gbias_ref, act_ref, slope_ref, acc_ref,
):
    shards = up_ref.shape[0]
    normed_one = normed_ref[...]
    hidden_one = normed_one * gain_one_ref[...] + shift_one_ref[...]
    hidden = hidden_one.astype(BF16)
    acc_ref[...] = hidden_one + b_down_ref[...].astype(F32)

    @pl.loop(0, shards)
    def _(shard):
        pre = nn(hidden, up_ref[shard]) + b_up_ref[shard, 0:1, :].astype(F32)
        phi = 0.5 * (1.0 + lax.erf(pre * ROOT_HALF))
        act = (pre * phi).astype(BF16)
        act_ref[shard] = act
        slope_ref[shard] = (phi + pre * INV_ROOT_TAU * jnp.exp(-0.5 * pre * pre)).astype(BF16)
        acc_ref[...] += nt(act, down_ref[shard])

    normed_two, scale_two = norm_parts(acc_ref[...])
    layer_ref[...] = (normed_two * gain_two_ref[...] + shift_two_ref[...]).astype(BF16)
    cot = cot_ref[...].astype(F32)
    grad_second = norm_back(cot, normed_two, scale_two, gain_two_ref[...])
    grad_ffn = grad_second.astype(BF16)
    vec_ref[0:1, :] = jnp.sum(cot * normed_two, 0, keepdims=True)
    vec_ref[1:2, :] = jnp.sum(cot, 0, keepdims=True)
    vec_ref[2:3, :] = jnp.sum(grad_ffn.astype(F32), 0, keepdims=True)
    acc_ref[...] = grad_second
    grad_turned = grad_ffn.T
    hidden_turned = hidden.T

    @pl.loop(0, shards)
    def _(shard):
        grad_act = nn(grad_ffn, down_ref[shard])
        grad_pre = (grad_act * slope_ref[shard].astype(F32)).astype(BF16)
        gdown_ref[shard] = nn(grad_turned, act_ref[shard]).astype(BF16)
        gup_ref[shard] = nn(hidden_turned, grad_pre).astype(BF16)
        gbias_ref[shard] = jnp.broadcast_to(
            jnp.sum(grad_pre.astype(F32), 0, keepdims=True), gbias_ref.shape[1:]
        )
        acc_ref[...] += nt(grad_pre, up_ref[shard])

    grad_hidden = acc_ref[...]
    grad_first = norm_back(grad_hidden, normed_one, scale_ref[:, 0:1], gain_one_ref[...])
    grad_low = grad_first.astype(BF16)
    first_ref[...] = grad_first
    low_ref[...] = grad_low
    vec_ref[3:4, :] = jnp.sum(grad_hidden * normed_one, 0, keepdims=True)
    vec_ref[4:5, :] = jnp.sum(grad_hidden, 0, keepdims=True)
    vec_ref[5:6, :] = jnp.sum(grad_low.astype(F32), 0, keepdims=True)
    vec_ref[6:8, :] = jnp.zeros((2, vec_ref.shape[1]), F32)


def out_back_phase(
    glow_ref, w_ref, low_ref, out_ref, denom_ref, qf_ref, gnum_ref, gden_ref, gw_ref, dnum_ref,
    dden_ref, total_ref, pairs, head_dim,
):
    rows_all = glow_ref.shape[0]
    blocks = rows_all // WINDOW
    half = LANES // 2
    ones = block_ones(LANES, head_dim).astype(BF16)
    grad_low = glow_ref[...]
    gw_ref[...] = tn(low_ref[...], grad_low).astype(gw_ref.dtype)
    for pair in range(pairs):
        cols = slice(pair * LANES, (pair + 1) * LANES)
        grad_attn = nt(grad_low, w_ref[cols, :])
        inverse = 1.0 / denom_ref[:, cols]
        grad_num = (grad_attn * inverse).astype(BF16)
        grad_den = -head_sums(grad_num.astype(F32) * out_ref[:, cols], ones)
        gnum_ref[:, cols] = grad_num
        gden_ref[:, cols] = grad_den
        total = jnp.zeros((half, LANES), F32)
        total_den = jnp.zeros((1, LANES), F32)
        for block in range(blocks):
            rows = slice(block * WINDOW, (block + 1) * WINDOW)
            query = qf_ref[rows, cols]
            num = compact(tn(query, grad_num[rows]))
            den = jnp.sum(query.astype(F32) * grad_den[rows], 0, keepdims=True)
            dnum_ref[pair * blocks + block] = num
            dden_ref[pair * blocks + block : pair * blocks + block + 1, :] = den
            total = total + num
            total_den = total_den + den
        total_ref[pair * half : (pair + 1) * half, :] = total
        total_ref[pairs * half + pair : pairs * half + pair + 1, :] = total_den


def row_grads(keys, values, num, den, ones_f32):
    upper, lower = halves(expand(num, ones_f32))
    grad_keys = nt(values, upper) + nt(values, lower) + den
    grad_values = nn(keys, upper) + nn(keys, lower)
    return grad_keys, grad_values


def band_backward_phase(
    qf_ref, ke_ref, ve_ref, line_ref, gnum_ref, gden_ref, dnum_ref, dden_ref, left_ref, right_ref,
    left_den_ref, right_den_ref, gq_ref, gk_ref, gv_ref, gline_ref, coef_grad_ref, start, stop, first_col, head_dim,
):
    blocks = qf_ref.shape[0] // WINDOW

    @pl.loop(start, stop)
    def _(pair):
        ones_f32 = block_ones(LANES, head_dim)
        cols = lanes(pair)
        out = lanes(pair - first_col)
        coef = coef_tile(line_ref, pair)
        left_coef, right_coef = far_coefs(line_ref, pair)
        gk_ref[:, out] = jnp.zeros((gk_ref.shape[0], LANES), F32)
        gv_ref[:, out] = jnp.zeros((gv_ref.shape[0], LANES), F32)
        coef_grad_ref[...] = jnp.zeros(coef_grad_ref.shape, F32)
        left_sum = jnp.zeros((1, LANES), F32)
        right_sum = jnp.zeros((1, LANES), F32)
        for block in range(blocks):
            rows = slice(block * WINDOW, (block + 1) * WINDOW)
            window = slice(block * WINDOW, (block + 3) * WINDOW)
            index = pair * blocks + block
            query = qf_ref[rows, cols]
            keys = ke_ref[window, cols]
            values = ve_ref[window, cols]
            grad_num = gnum_ref[rows, cols]
            grad_den = gden_ref[rows, cols]
            queries = both_heads(query)
            grads = both_heads(grad_num)
            weights = coef * nt(queries, keys)
            den_column = jnp.concatenate(
                [grad_den[:, 0:1], grad_den[:, LANES // 2 : LANES // 2 + 1]], 0
            )
            grad_weights = nt(grads, values) + den_column
            coef_grad_ref[...] += grad_weights * weights
            grad_scores = (coef * grad_weights).astype(BF16)
            gv_ref[window, out] += tn(weights.astype(BF16), grads)
            gk_ref[window, out] += tn(grad_scores, queries)
            grad_query = per_head(nn(grad_scores, keys))
            left, right = left_ref[index], right_ref[index]
            left_den = left_den_ref[pl.ds(index, 1), :]
            right_den = right_den_ref[pl.ds(index, 1), :]
            upper, lower = halves(expand(left_coef * left + right_coef * right, ones_f32))
            den_far = left_coef * left_den + right_coef * right_den
            grad_query = grad_query + nt(grad_num, upper) + nt(grad_num, lower) + grad_den * den_far
            gq_ref[rows, cols] = grad_query
            dnum = dnum_ref[index]
            dden = dden_ref[pl.ds(index, 1), :]
            left_sum = left_sum + jnp.sum(dnum * left, 0, keepdims=True) + dden * left_den
            right_sum = right_sum + jnp.sum(dnum * right, 0, keepdims=True) + dden * right_den
        for edge, block, scale in ((0, 0, left_coef), (blocks + 1, blocks - 1, right_coef)):
            rows = slice(edge * WINDOW, (edge + 1) * WINDOW)
            index = pair * blocks + block
            edge_k, edge_v = row_grads(
                ke_ref[rows, cols],
                ve_ref[rows, cols],
                scale * dnum_ref[index],
                scale * dden_ref[pl.ds(index, 1), :],
                ones_f32,
            )
            gk_ref[rows, out] -= edge_k
            gv_ref[rows, out] -= edge_v
        first = first_half((1, LANES))
        positions = lax.broadcasted_iota(jnp.int32, (1, LINE), 1)
        left_all = left_coef * left_sum
        right_all = right_coef * right_sum
        for head in range(2):
            keep = first if head == 0 else jnp.logical_not(first)
            left_one = jnp.sum(jnp.where(keep, left_all, 0.0), 1, keepdims=True)
            right_one = jnp.sum(jnp.where(keep, right_all, 0.0), 1, keepdims=True)
            line = unskew_sum(coef_grad_ref[head * WINDOW : (head + 1) * WINDOW, :])
            line = line + jnp.where(positions == 0, left_one, 0.0)
            line = line + jnp.where(positions == LINE - 2, right_one, 0.0)
            gline_ref[pl.ds(2 * pair + head, 1), :] = line


def key_back_phase(
    kf_ref, v_ref, line_ref, dnum_ref, dden_ref, past_ref, future_ref, low_in_ref, high_in_ref,
    gk_ref, gv_ref, pairs, start, stop, head_dim,
):
    blocks = kf_ref.shape[0] // WINDOW
    half = LANES // 2

    @pl.loop(start, stop)
    def _(pair):
        ones_f32 = block_ones(LANES, head_dim)
        cols = lanes(pair)
        left_coef, right_coef = far_coefs(line_ref, pair)
        state_rows = pl.ds(pl.multiple_of(pair * half, half), half)
        den_row = pl.ds(pairs * half + pair, 1)
        nums = [dnum_ref[pair * blocks + block] for block in range(blocks)]
        dens = [dden_ref[pl.ds(pair * blocks + block, 1), :] for block in range(blocks)]
        for block in range(blocks):
            num_left, den_left = future_ref[state_rows, :], future_ref[den_row, :]
            num_right, den_right = past_ref[state_rows, :], past_ref[den_row, :]
            for other in range(blocks):
                if other >= block + 2:
                    num_left, den_left = num_left + nums[other], den_left + dens[other]
                if other <= block - 2:
                    num_right, den_right = num_right + nums[other], den_right + dens[other]
            rows = slice(block * WINDOW, (block + 1) * WINDOW)
            outer = slice((block + 1) * WINDOW, (block + 2) * WINDOW)
            far_k, far_v = row_grads(
                kf_ref[rows, cols],
                v_ref[rows, cols],
                left_coef * num_left + right_coef * num_right,
                left_coef * den_left + right_coef * den_right,
                ones_f32,
            )
            if block == 0:
                far_k = far_k + low_in_ref[0, :, cols].astype(F32)
                far_v = far_v + low_in_ref[1, :, cols].astype(F32)
            if block == blocks - 1:
                far_k = far_k + high_in_ref[0, :, cols].astype(F32)
                far_v = far_v + high_in_ref[1, :, cols].astype(F32)
            gk_ref[outer, cols] += far_k
            gv_ref[outer, cols] += far_v


def qkv_back_phase(
    turned_ref, w_ref, omega_ref, q_ref, k_ref, qf_ref, kf_ref, gq_ref, gk_ref, gv_ref, gtok_ref, parts_ref,
    small_ref, group, head_dim,
):
    width, rows_all = turned_ref.shape
    own = slice(WINDOW, WINDOW + rows_all)
    ones = block_ones(CHUNK, head_dim).astype(BF16)
    factor = head_dim ** (-0.25) / SPREAD
    cols = slice(group * CHUNK, (group + 1) * CHUNK)
    omega = omega_ref[group]
    lows = []
    total = gtok_ref[...]
    for part, low_ref, feat_ref, grad in (
        (0, q_ref, qf_ref, gq_ref[:, cols]), (1, k_ref, kf_ref, gk_ref[own, cols]), (2, None, None, gv_ref[own, cols]),
    ):
        if part < 2:
            inner_up, inner_low = halves(grad * feat_ref[:, cols].astype(F32))
            projected = (nt(inner_up, omega) + nt(inner_low, omega)) * factor
            sums = nn(inner_up, ones) + nn(inner_low, ones)
            grad = projected - sums * head_dim ** (-0.5) * low_ref[:, cols].astype(F32)
        low = grad.astype(BF16)
        lows.append(low)
        total = total + nt(low, w_ref[:, part * width + group * CHUNK : part * width + (group + 1) * CHUNK])
    gtok_ref[...] = total
    joined = jnp.concatenate(lows, 1)
    small_ref[8 + group : 9 + group, :] = jnp.sum(joined.astype(F32), 0, keepdims=True)
    parts_ref[:, (group + 1) * width : (group + 2) * width] = nn(turned_ref[...], joined).astype(parts_ref.dtype)


def table_phase(gline_ref, bucket_ref, buckets):
    one_hot = jnp.where(
        lax.broadcasted_iota(jnp.int32, (buckets, LINE), 0) == bucket_ref[...].astype(jnp.int32), 1.0, 0.0
    )
    return lax.dot_general(
        gline_ref[...],
        one_hot,
        (((1,), (1,)), ((), ())),
        precision=lax.Precision.HIGHEST,
        preferred_element_type=F32,
    )


MESH = pl.DeviceIdType.MESH


def guarded(when, action):
    if when is None:
        action()
    else:
        pl.when(when)(action)


class Place:
    def __init__(self, shards):
        self.row, self.seq = lax.axis_index("row"), lax.axis_index("seq")
        self.count_b = 2
        self.count_a = shards // self.count_b
        self.shards = shards
        self.x, self.core = self.row // 2, self.row % 2
        self.a, self.b = self.seq // self.count_b, self.seq % self.count_b
        self.is_first, self.is_last = self.seq == 0, self.seq == shards - 1
        self.not_first, self.not_last = self.seq > 0, self.seq < shards - 1

    def at(self, x=None, core=None, a=None, b=None):
        x = self.x if x is None else x
        core = self.core if core is None else core
        a = self.a if a is None else a
        b = self.b if b is None else b
        return (x * 2 + core, a * self.count_b + b)

    def beside(self, seq):
        return (self.row, seq)

    def shard(self, offset):
        return lax.rem(self.a + offset, self.count_a)

    def nearest(self, step):
        orders = []
        for a in range(self.count_a):
            orders.append(sorted(range(self.count_a), key=lambda other: (abs(other - a), other)))
        index = jnp.int32(orders[0][step])
        for a in range(1, self.count_a):
            index = jnp.where(self.a == a, orders[a][step], index)
        return index


class Sends:
    def __init__(self):
        self.started = []

    def send(self, src, dst, send_sem, recv_sem, device, when=None):
        copy = pltpu.make_async_remote_copy(
            src_ref=src, dst_ref=dst, send_sem=send_sem, recv_sem=recv_sem, device_id=device,
            device_id_type=MESH,
        )
        guarded(when, copy.start)
        self.started.append((when, copy))

    def drain(self):
        for when, copy in self.started:
            guarded(when, copy.wait_send)
        self.started = []


def arrive(dst, sem, device, when=None):
    copy = pltpu.make_async_remote_copy(
        src_ref=dst, dst_ref=dst, send_sem=sem, recv_sem=sem, device_id=device, device_id_type=MESH
    )
    guarded(when, copy.wait_recv)


class WeightGather:
    def __init__(self, place, sends, mats, middle, sems):
        self.place, self.sends, self.mats, self.mid = place, sends, mats, middle
        self.z_send, self.z_recv, self.y_send, self.y_recv, self.x_send, self.x_recv, self.c_send, self.c_recv = sems
        self.side = (mats.shape[3] - middle) // 2

    def outer(self, a, b, x, core=None):
        core = self.place.core if core is None else core
        start = pl.multiple_of(x * (self.side + self.mid), 16)
        return self.mats.at[core, a, b, pl.ds(start, self.side), :]

    def both(self, a, b, core=None):
        core = self.place.core if core is None else core
        kinds = [(0, self.outer(a, b, self.place.x, core))]
        if self.mid:
            kinds.append((1, self.mats.at[core, a, b, pl.ds(self.side, self.mid), :]))
        return kinds

    def column(self, column):
        return 1 - self.place.b if column else self.place.b

    def rounds(self, step):
        p = self.place
        if step == 0:
            return [(p.a, None, (1, -1))]
        last = p.count_a - 1
        return [
            (jnp.maximum(p.a - step, 0), p.a - step >= 0, (1,)),
            (jnp.minimum(p.a + step, last), p.a + step <= last, (-1,)),
        ]

    def along_a(self, step, wanted):
        p = self.place
        for a, there, moves in self.rounds(step):
            for kind, here in self.both(a, p.b):
                if kind not in wanted:
                    continue
                if step > 0:
                    arrive(here, self.z_recv.at[kind, a], p.at(), there)
                for move in moves:
                    target = p.a + move
                    ok = target <= p.count_a - 1 if move > 0 else target >= 0
                    if there is not None:
                        ok = jnp.logical_and(ok, there)
                    self.sends.send(
                        here, here, self.z_send.at[(1 - move) // 2, kind, a], self.z_recv.at[kind, a],
                        p.at(a=jnp.clip(target, 0, p.count_a - 1)), ok,
                    )
                if step > 0:
                    self.pass_on(kind, 0, a, here, there)

    def across(self, step):
        p = self.place
        for a, there, _ in self.rounds(step):
            for kind, here in self.both(a, p.b):
                self.sends.send(
                    here, here, self.y_send.at[kind, a], self.y_recv.at[kind, a], p.at(b=1 - p.b), there
                )

    def pass_on(self, kind, column, a, here, when=None):
        p = self.place
        if kind == 0:
            self.sends.send(
                here, here, self.x_send.at[column, a], self.x_recv.at[column, a], p.at(x=1 - p.x), when
            )
        self.sends.send(
            here, here, self.c_send.at[kind, column, a], self.c_recv.at[kind, column, a], p.at(core=1 - p.core), when
        )

    def along_b(self, step, wanted):
        p = self.place
        a = p.nearest(step)
        for kind, here in self.both(a, 1 - p.b):
            if kind in wanted:
                arrive(here, self.y_recv.at[kind, a], p.at())
                self.pass_on(kind, 1, a, here)

    def along_x(self, step, column):
        p = self.place
        a = p.nearest(step)
        here = self.outer(a, self.column(column), 1 - p.x)
        arrive(here, self.x_recv.at[column, a], p.at())
        self.sends.send(
            here, here, self.c_send.at[2, column, a], self.c_recv.at[2, column, a], p.at(core=1 - p.core)
        )

    def finish(self, step, column):
        p = self.place
        a = p.nearest(step)
        other, b = 1 - p.core, self.column(column)
        for kind, here in self.both(a, b, other) + [(2, self.outer(a, b, 1 - p.x, other))]:
            arrive(here, self.c_recv.at[kind, column, a], p.at())


def gather_sems(count_a):
    dma = pltpu.SemaphoreType.DMA
    return [
        dma((2, 2, count_a)), dma((2, count_a)), dma((2, count_a)), dma((2, count_a)),
        dma((2, count_a)), dma((2, count_a)), dma((3, 2, count_a)), dma((3, 2, count_a)),
    ]


class StateSums:
    def __init__(self, place, sends, buffers, sems):
        self.place, self.sends = place, sends
        self.own, self.peer, self.pair, self.far, self.sums, self.land = buffers
        self.y_send, self.y_recv, self.z_send, self.z_recv = sems
        self.half = self.pair.shape[0]

    def rows(self, b):
        return pl.ds(pl.multiple_of(b * self.half, 16), self.half)

    def start(self, message_ref):
        p = self.place
        self.own[...] = message_ref[...].astype(BF16)
        self.sends.send(self.own, self.peer, self.y_send.at[0], self.y_recv.at[0], p.at(b=1 - p.b))

    def along_a(self):
        p = self.place
        arrive(self.peer, self.y_recv.at[0], p.at())
        mine = self.rows(p.b)
        self.pair[...] = (self.own[mine, :].astype(F32) + self.peer[mine, :].astype(F32)).astype(BF16)
        for offset in range(1, p.count_a):
            self.sends.send(
                self.pair, self.far.at[p.a], self.z_send.at[offset], self.z_recv.at[offset],
                p.at(a=p.shard(offset)),
            )

    def along_b(self):
        p = self.place
        self.far[p.a] = jnp.zeros(self.pair.shape, BF16)
        for offset in range(1, p.count_a):
            source = p.shard(p.count_a - offset)
            arrive(self.far.at[source], self.z_recv.at[offset], p.at())
        for index in range(2):
            total = jnp.zeros(self.pair.shape, F32)
            for a in range(p.count_a):
                keep = a < p.a if index == 0 else a > p.a
                total = total + jnp.where(keep, 1.0, 0.0) * self.far[a].astype(F32)
            self.sums[index] = total.astype(BF16)
        self.sends.send(self.sums, self.land, self.y_send.at[1], self.y_recv.at[1], p.at(b=1 - p.b))

    def finish(self, before_ref, after_ref):
        p = self.place
        arrive(self.land, self.y_recv.at[1], p.at())
        for index, ref in ((0, before_ref), (1, after_ref)):
            ref[self.rows(p.b), :] = self.sums[index].astype(F32)
            ref[self.rows(1 - p.b), :] = self.land[index].astype(F32)
        peer = self.peer[...].astype(F32)
        before_ref[...] += jnp.where(p.b == 1, 1.0, 0.0) * peer
        after_ref[...] += jnp.where(p.b == 0, 1.0, 0.0) * peer


def sums_sems(count_a):
    dma = pltpu.SemaphoreType.DMA
    return [dma((2,)), dma((2,)), dma((count_a,)), dma((count_a,))]


class GradScatter:
    def __init__(self, place, sends, grads, total, middle, lands, sems):
        self.place, self.sends, self.grads, self.total, self.mid = place, sends, grads, total, middle
        self.core_land, self.stage, self.x_land, self.y_land, self.z_land, self.last_land = lands
        (self.copy, self.c_send, self.c_recv, self.x_send, self.x_recv, self.y_send, self.y_recv, self.z_send,
         self.z_recv, self.l_send, self.l_recv) = sems
        self.side = (grads.shape[3] - middle) // 2

    def outer(self, x):
        return pl.ds(pl.multiple_of(x * (self.side + self.mid), 16), self.side)

    def window(self):
        return pl.ds(pl.multiple_of(self.place.x * self.side, 16), self.side + self.mid)

    def column(self, column):
        return 1 - self.place.b if column else self.place.b

    def start(self, offset, column):
        p = self.place
        item = (offset, column)
        self.sends.send(
            self.grads.at[1 - p.core, p.shard(offset), self.column(column)], self.core_land.at[item],
            self.c_send.at[item], self.c_recv.at[item], p.at(core=1 - p.core),
        )

    def add(self, ref, land):
        ref[...] = (ref[...].astype(F32) + land[...].astype(F32)).astype(BF16)

    def staged(self, offset, column):
        item = (offset, column)
        return pltpu.make_async_copy(self.core_land.at[item], self.stage.at[1 - column], self.copy.at[item])

    def fetch(self, offset, column):
        item = (offset, column)
        arrive(self.core_land.at[item], self.c_recv.at[item], self.place.at())
        self.staged(offset, column).start()

    def chip(self, offset, column):
        p = self.place
        item = (offset, column)
        self.staged(offset, column).wait()
        here = self.grads.at[p.core, p.shard(offset), self.column(column)]
        self.add(here, self.stage.at[1 - column])
        self.sends.send(
            here.at[self.outer(1 - p.x), :], self.x_land.at[item], self.x_send.at[item], self.x_recv.at[item],
            p.at(x=1 - p.x),
        )

    def along_x(self, offset, column):
        p = self.place
        item = (offset, column)
        here = self.grads.at[p.core, p.shard(offset), self.column(column)]
        arrive(self.x_land.at[item], self.x_recv.at[item], p.at())
        self.add(here.at[self.outer(p.x), :], self.x_land.at[item])
        if column:
            self.sends.send(
                here.at[self.window(), :], self.y_land.at[offset], self.y_send.at[offset], self.y_recv.at[offset],
                p.at(b=1 - p.b),
            )

    def along_b(self, offset):
        p = self.place
        a = p.shard(offset)
        arrive(self.y_land.at[offset], self.y_recv.at[offset], p.at())
        mine = self.grads.at[p.core, a, p.b, self.window(), :]
        self.add(mine, self.y_land.at[offset])
        if offset:
            self.sends.send(
                mine, self.z_land.at[offset - 1], self.z_send.at[offset], self.z_recv.at[offset], p.at(a=a)
            )

    def along_a(self):
        p = self.place
        own = self.grads.at[p.core, p.a, p.b]
        mine = own.at[self.window(), :]
        total = mine[...].astype(F32)
        for offset in range(1, p.count_a):
            arrive(self.z_land.at[offset - 1], self.z_recv.at[offset], p.at())
            total = total + self.z_land[offset - 1].astype(F32)
        mine[...] = total.astype(BF16)
        middle = pl.ds(self.side, self.mid)
        outer = self.outer(p.x)
        self.total[p.core, outer, :] = self.grads[p.core, p.a, p.b, outer, :]
        self.sends.send(
            own.at[middle, :], self.last_land, self.l_send.at[0], self.l_recv.at[0], p.at(x=1 - p.x)
        )
        here = self.total.at[p.core, outer, :]
        self.sends.send(here, here, self.l_send.at[1], self.l_recv.at[1], p.at(x=1 - p.x))

    def last_x(self):
        p = self.place
        middle = pl.ds(self.side, self.mid)
        arrive(self.last_land, self.l_recv.at[0], p.at())
        self.total[p.core, middle, :] = (
            self.grads[p.core, p.a, p.b, middle, :].astype(F32) + self.last_land[...].astype(F32)
        ).astype(BF16)
        arrive(self.total.at[p.core, self.outer(1 - p.x), :], self.l_recv.at[1], p.at())
        here = self.total.at[p.core]
        self.sends.send(here, here, self.l_send.at[2], self.l_recv.at[2], p.at(core=1 - p.core))

    def finish(self):
        arrive(self.total.at[1 - self.place.core], self.l_recv.at[2], self.place.at())


def scatter_sems(count_a):
    dma = pltpu.SemaphoreType.DMA
    return [dma((count_a, 2)) for _ in range(5)] + [dma((count_a,)) for _ in range(4)] + [dma((3,)), dma((3,))]


class AllReduce:
    def __init__(self, place, sends, parts, result, lands, done, orders, sems):
        self.place, self.sends, self.parts, self.result = place, sends, parts, result
        self.core_land, self.staged, self.one_land, self.two_land, self.a_land = lands
        self.done, self.orders = done, orders
        (self.s_send, self.s_recv, self.z_send, self.z_recv, self.g_send, self.g_recv, self.zg_send, self.zg_recv,
         self.copy) = sems
        self.half = result.shape[1] // 2
        self.quarter = self.half // 2
        self.slim = self.quarter // place.count_a

    def ways(self, index):
        p = self.place
        other_x, other_b = p.at(x=1 - p.x), p.at(b=1 - p.b)
        straight = {"x": True, "b": False}.get(self.orders[index], p.core == 0)
        one = tuple(jnp.where(straight, u, w) for u, w in zip(other_x, other_b))
        two = tuple(jnp.where(straight, w, u) for u, w in zip(other_x, other_b))
        return jnp.where(straight, p.x, p.b), jnp.where(straight, p.b, p.x), one, two

    def half_rows(self, core):
        return pl.ds(pl.multiple_of(core * self.half, self.half), self.half)

    def quarter_rows(self, one):
        start = self.place.core * self.half + one * self.quarter
        return pl.ds(pl.multiple_of(start, self.quarter), self.quarter)

    def slim_rows(self, one, a):
        start = self.place.core * self.half + one * self.quarter + a * self.slim
        return pl.ds(pl.multiple_of(start, self.slim), self.slim)

    def push(self, index):
        p = self.place
        blocks = pl.ds(2 * index, 2)
        self.sends.send(
            self.parts.at[blocks, self.half_rows(1 - p.core), :], self.core_land.at[blocks],
            self.s_send.at[0, index], self.s_recv.at[0, index], p.at(core=1 - p.core),
        )

    def add(self, ref, land):
        ref[...] = (ref[...].astype(F32) + land[...].astype(F32)).astype(BF16)

    def stage(self, index, number):
        p = self.place
        one, two, one_device, two_device = self.ways(index)
        blocks = pl.ds(2 * index, 2)
        mine, other = 2 * index + two, 2 * index + 1 - two
        parts, result = self.parts, self.result
        if number == 1:
            land = self.core_land.at[blocks]
            arrive(land, self.s_recv.at[0, index], p.at())
            fetch = pltpu.make_async_copy(land, self.staged, self.copy.at[index])
            fetch.start()
            fetch.wait()
            self.add(parts.at[blocks, self.half_rows(p.core), :], self.staged)
            self.sends.send(
                parts.at[blocks, self.quarter_rows(1 - one), :], self.one_land.at[blocks],
                self.s_send.at[1, index], self.s_recv.at[1, index], one_device,
            )
        elif number == 2:
            land = self.one_land.at[blocks]
            arrive(land, self.s_recv.at[1, index], p.at())
            self.add(parts.at[blocks, self.quarter_rows(one), :], land)
            self.sends.send(
                parts.at[other, self.quarter_rows(one), :], self.two_land.at[index],
                self.s_send.at[2, index], self.s_recv.at[2, index], two_device,
            )
        elif number == 3:
            land = self.two_land.at[index]
            arrive(land, self.s_recv.at[2, index], p.at())
            self.add(parts.at[mine, self.quarter_rows(one), :], land)
            for offset in range(1, p.count_a):
                a = p.shard(offset)
                self.sends.send(
                    parts.at[mine, self.slim_rows(one, a), :], self.a_land.at[index, offset - 1],
                    self.z_send.at[index, offset], self.z_recv.at[index, offset], p.at(a=a),
                )
        elif number == 4:
            rows = self.slim_rows(one, p.a)
            total = parts[mine, rows, :].astype(F32)
            for offset in range(1, p.count_a):
                arrive(self.a_land.at[index, offset - 1], self.z_recv.at[index, offset], p.at())
                total = total + self.a_land[index, offset - 1].astype(F32)
            self.done[index] = total.astype(BF16)
            here = result.at[mine, rows, :]
            pltpu.make_async_copy(self.done.at[index], here, self.copy.at[index]).start()
            for offset in range(1, p.count_a):
                self.sends.send(
                    self.done.at[index], here, self.zg_send.at[index, offset], self.zg_recv.at[index, offset],
                    p.at(a=p.shard(offset)),
                )
        elif number == 5:
            pltpu.make_async_copy(
                self.done.at[index], result.at[mine, self.slim_rows(one, p.a), :], self.copy.at[index]
            ).wait()
            for offset in range(1, p.count_a):
                a = lax.rem(p.a + p.count_a - offset, p.count_a)
                arrive(result.at[mine, self.slim_rows(one, a), :], self.zg_recv.at[index, offset], p.at())
            here = result.at[mine, self.quarter_rows(one), :]
            self.sends.send(here, here, self.g_send.at[0, index], self.g_recv.at[0, index], two_device)
        elif number == 6:
            arrive(result.at[other, self.quarter_rows(one), :], self.g_recv.at[0, index], p.at())
            here = result.at[blocks, self.quarter_rows(one), :]
            self.sends.send(here, here, self.g_send.at[1, index], self.g_recv.at[1, index], one_device)
        elif number == 7:
            arrive(result.at[blocks, self.quarter_rows(1 - one), :], self.g_recv.at[1, index], p.at())
            here = result.at[blocks, self.half_rows(p.core), :]
            self.sends.send(here, here, self.g_send.at[2, index], self.g_recv.at[2, index], p.at(core=1 - p.core))
        elif number == 8:
            arrive(result.at[blocks, self.half_rows(1 - p.core), :], self.g_recv.at[2, index], p.at())


def reduce_sems(chunks, count_a):
    dma = pltpu.SemaphoreType.DMA
    return [
        dma((3, chunks)), dma((3, chunks)), dma((chunks, count_a)), dma((chunks, count_a)),
        dma((3, chunks)), dma((3, chunks)), dma((chunks, count_a)), dma((chunks, count_a)), dma((chunks,)),
    ]


class SmallReduce:
    def __init__(self, place, sends, held, land, sems):
        self.place, self.sends, self.held, self.land = place, sends, held, land
        self.out_sem, self.in_sem = sems
        p = place
        self.devices = [p.at(core=1 - p.core), p.at(x=1 - p.x), p.at(b=1 - p.b)]

    def send(self, step):
        if step < 3:
            self.sends.send(
                self.held.at[step], self.land.at[step], self.out_sem.at[step], self.in_sem.at[step],
                self.devices[step],
            )
            return
        p = self.place
        for offset in range(1, p.count_a):
            self.sends.send(
                self.held.at[3], self.land.at[3 + offset], self.out_sem.at[3 + offset],
                self.in_sem.at[3 + offset], p.at(a=p.shard(offset)),
            )

    def receive(self, step):
        p = self.place
        if step < 3:
            arrive(self.land.at[step], self.in_sem.at[step], p.at())
            self.held[step + 1] = self.held[step] + self.land[step]
            return
        for offset in range(1, p.count_a):
            arrive(self.land.at[3 + offset], self.in_sem.at[3 + offset], p.at())
        self.land[3] = self.held[3]

    def total(self):
        p = self.place
        total = self.land[3 + lax.rem(p.a, p.count_a)]
        for a in range(1, p.count_a):
            total = total + self.land[3 + lax.rem(p.a + p.count_a - a, p.count_a)]
        return total


def halo_phase(x_ref, w_ref, b_ref, omega_ref, k_ref, kv_ref, place, head_dim):
    rows_ext, width = x_ref.shape
    low, high = slice(0, WINDOW), slice(rows_ext - WINDOW, rows_ext)
    x = jnp.concatenate([x_ref[low, :], x_ref[high, :]], 0)
    ones = block_ones(CHUNK, head_dim).astype(BF16)
    factor = head_dim ** (-0.25) / SPREAD
    row = lax.broadcasted_iota(jnp.int32, (2 * WINDOW, 1), 0)
    inside = jnp.logical_or(
        jnp.logical_and(row < WINDOW, place.seq > 0),
        jnp.logical_and(row >= WINDOW, place.seq < place.shards - 1),
    )
    for part in (1, 2):
        for chunk in range(width // CHUNK):
            cols = slice(chunk * CHUNK, (chunk + 1) * CHUNK)
            wide = slice(part * width + chunk * CHUNK, part * width + (chunk + 1) * CHUNK)
            value = (nn(x, w_ref[:, wide]) + b_ref[part][:, cols]).astype(BF16)
            if part == 1:
                k_ref[low, cols], k_ref[high, cols] = value[:WINDOW], value[WINDOW:]
                widened = value.astype(F32)
                half_norm = head_sums(widened * widened, ones) * (0.5 * head_dim ** (-0.5))
                value = jnp.exp(nn(value, omega_ref[chunk]) * factor - half_norm) * head_dim ** (-0.5)
            value = jnp.where(inside, value.astype(F32), 0.0).astype(BF16)
            kv_ref[part - 1, low, cols], kv_ref[part - 1, high, cols] = value[:WINDOW], value[WINDOW:]


def ffn_forward_shard(hidden_ref, mats, a, b, shard, bias_ref, pool, acc_ref):
    rows = hidden_ref.shape[0]
    pre = nn(hidden_ref[...], mats[0, a, b]) + bias_ref[shard, 0:1, :]
    phi = 0.5 * (1.0 + lax.erf(pre * ROOT_HALF))
    act = (pre * phi).astype(BF16)
    pool[shard, 0:rows, :] = act
    pool[shard, rows : 2 * rows, :] = (phi + pre * INV_ROOT_TAU * jnp.exp(-0.5 * pre * pre)).astype(BF16)
    acc_ref[...] += nt(act, mats[1, a, b])


def ffn_backward_shard(grad_ref, grad_turned_ref, hidden_turned_ref, mats, a, b, shard, pool, acc_ref, gbias_ref):
    rows = grad_ref.shape[0]
    grad_act = nn(grad_ref[...], mats[1, a, b])
    grad_pre = (grad_act * pool[shard, rows : 2 * rows, :].astype(F32)).astype(BF16)
    gbias_ref[shard] = jnp.broadcast_to(
        jnp.sum(grad_pre.astype(F32), 0, keepdims=True), gbias_ref.shape[1:]
    )
    acc_ref[...] += nt(grad_pre, mats[0, a, b])
    mats[1, a, b] = nn(grad_turned_ref[...], pool[shard, 0:rows, :]).astype(BF16)
    mats[0, a, b] = nn(hidden_turned_ref[...], grad_pre).astype(BF16)


def row_blocks(rows, body, size=CHUNK):
    @pl.loop(0, rows // size)
    def _(index):
        body(pl.ds(pl.multiple_of(index * size, size), size))


def hidden_phase(
    x_ref, low_ref, w_ref, b_ref, gain_ref, shift_ref, b_down_ref, normed_refs, scale_ref, hidden_ref, turned_ref, acc_ref
):
    def body(rows):
        first_sum = x_ref[rows, :].astype(F32) + nn(low_ref[rows, :], w_ref[...]) + b_ref[...].astype(F32)
        normed, inv_scale = norm_parts(first_sum)
        normed_refs[0][rows, :], normed_refs[1][rows, :], normed_refs[2][rows, :] = jnp.split(normed, 3, 1)
        scale_ref[rows, :] = jnp.broadcast_to(inv_scale, (first_sum.shape[0], scale_ref.shape[1]))
        hidden_one = normed * gain_ref[...] + shift_ref[...]
        hidden = hidden_one.astype(BF16)
        hidden_ref[rows, :] = hidden
        turned_ref[:, rows] = hidden.T
        acc_ref[rows, :] = hidden_one + b_down_ref[...].astype(F32)

    row_blocks(x_ref.shape[0], body)


def middle_phase(acc_ref, cot_ref, gain_two_ref, shift_two_ref, grad_ref, grad_turned_ref, vec_ref):
    def body(rows):
        normed_two, scale_two = norm_parts(acc_ref[rows, :])
        cot = cot_ref[rows, :].astype(F32)
        cot_ref[rows, :] = (normed_two * gain_two_ref[...] + shift_two_ref[...]).astype(BF16)
        grad_second = norm_back(cot, normed_two, scale_two, gain_two_ref[...])
        grad_ffn = grad_second.astype(BF16)
        vec_ref[0:1, :] += jnp.sum(cot * normed_two, 0, keepdims=True)
        vec_ref[1:2, :] += jnp.sum(cot, 0, keepdims=True)
        vec_ref[2:3, :] += jnp.sum(grad_ffn.astype(F32), 0, keepdims=True)
        acc_ref[rows, :] = grad_second
        grad_ref[rows, :] = grad_ffn
        grad_turned_ref[:, rows] = grad_ffn.T

    row_blocks(cot_ref.shape[0], body)


def first_back_phase(acc_ref, normed_refs, scale_ref, gain_one_ref, low_ref, vec_ref):
    def body(rows):
        grad_hidden = acc_ref[rows, :]
        normed = jnp.concatenate([ref[rows, :] for ref in normed_refs], 1)
        grad_first = norm_back(grad_hidden, normed, scale_ref[rows, 0:1], gain_one_ref[...])
        grad_low = grad_first.astype(BF16)
        acc_ref[rows, :] = grad_first
        low_ref[rows, :] = grad_low
        vec_ref[3:4, :] += jnp.sum(grad_hidden * normed, 0, keepdims=True)
        vec_ref[4:5, :] += jnp.sum(grad_hidden, 0, keepdims=True)
        vec_ref[5:6, :] += jnp.sum(grad_low.astype(F32), 0, keepdims=True)

    row_blocks(low_ref.shape[0], body)


def attn_back_phase(glow_ref, w_ref, out_ref, denom_ref, low_ref, qf_ref, dnum_ref, dden_ref, total_ref, pairs, head_dim):
    rows_all = glow_ref.shape[0]
    blocks = rows_all // WINDOW
    half = LANES // 2
    ones = block_ones(LANES, head_dim).astype(BF16)
    grad_low = glow_ref[...]
    for pair in range(pairs):
        cols = slice(pair * LANES, (pair + 1) * LANES)
        grad_attn = nt(grad_low, w_ref[cols, :])
        grad_num = (grad_attn / denom_ref[:, cols]).astype(BF16)
        grad_den = -head_sums(grad_num.astype(F32) * out_ref[:, cols], ones)
        low_ref[:, cols] = grad_num
        denom_ref[:, cols] = grad_den
        total = jnp.zeros((half, LANES), F32)
        total_den = jnp.zeros((1, LANES), F32)
        for block in range(blocks):
            rows = slice(block * WINDOW, (block + 1) * WINDOW)
            query = qf_ref[rows, cols]
            num = compact(tn(query, grad_num[rows]))
            den = jnp.sum(query.astype(F32) * grad_den[rows], 0, keepdims=True)
            dnum_ref[pair * blocks + block] = num
            dden_ref[pair * blocks + block : pair * blocks + block + 1, :] = den
            total = total + num
            total_den = total_den + den
        total_ref[pair * half : (pair + 1) * half, :] = total
        total_ref[pairs * half + pair : pairs * half + pair + 1, :] = total_den


def far_back_phase(ke_ref, ve_ref, line_ref, dnum_ref, dden_ref, past_ref, future_ref, gk_ref, gv_ref, pairs, start, stop, first_col, head_dim):
    blocks = ke_ref.shape[0] // WINDOW - 2
    half = LANES // 2

    @pl.loop(start, stop)
    def _(pair):
        ones_f32 = block_ones(LANES, head_dim)
        cols = lanes(pair)
        out = lanes(pair - first_col)
        left_coef, right_coef = far_coefs(line_ref, pair)
        state_rows = pl.ds(pl.multiple_of(pair * half, half), half)
        den_row = pl.ds(pairs * half + pair, 1)
        nums = [dnum_ref[pair * blocks + block] for block in range(blocks)]
        dens = [dden_ref[pl.ds(pair * blocks + block, 1), :] for block in range(blocks)]
        for block in range(blocks):
            num_left, den_left = future_ref[state_rows, :], future_ref[den_row, :]
            num_right, den_right = past_ref[state_rows, :], past_ref[den_row, :]
            for other in range(blocks):
                if other >= block + 2:
                    num_left, den_left = num_left + nums[other], den_left + dens[other]
                if other <= block - 2:
                    num_right, den_right = num_right + nums[other], den_right + dens[other]
            rows = slice((block + 1) * WINDOW, (block + 2) * WINDOW)
            far_k, far_v = row_grads(
                ke_ref[rows, cols],
                ve_ref[rows, cols],
                left_coef * num_left + right_coef * num_right,
                left_coef * den_left + right_coef * den_right,
                ones_f32,
            )
            gk_ref[rows, out] += far_k
            gv_ref[rows, out] += far_v


def qkv_grad_phase(
    turned_ref, w_ref, omega_ref, q_ref, k_ref, qf_ref, kf_ref, gq_ref, gk_ref, gv_ref, grads_ref, parts, small_ref,
    group, wanted, place, head_dim,
):
    width, rows_ext = turned_ref.shape
    rows_all = rows_ext - 2 * WINDOW
    own = slice(WINDOW, WINDOW + rows_all)
    ones = block_ones(CHUNK, head_dim).astype(BF16)
    factor = head_dim ** (-0.25) / SPREAD
    cols = slice(group * CHUNK, (group + 1) * CHUNK)
    omega = omega_ref[group]
    base = group * 3 * CHUNK
    block = parts.shape[2]
    for part, low_ref, feat_ref in ((0, q_ref, qf_ref), (1, k_ref, kf_ref), (2, None, None)):
        if part not in wanted:
            continue
        out = slice(part * CHUNK, (part + 1) * CHUNK)

        def body(rows):
            if part == 0:
                grad = gq_ref[rows, cols]
            else:
                grad = (gk_ref if part == 1 else gv_ref)[rows, :]
            if part < 2:
                inner_up, inner_low = halves(grad * feat_ref[rows, cols].astype(F32))
                projected = (nt(inner_up, omega) + nt(inner_low, omega)) * factor
                sums = nn(inner_up, ones) + nn(inner_low, ones)
                grad = projected - sums * head_dim ** (-0.5) * low_ref[rows, cols].astype(F32)
            if part > 0:
                row = lax.broadcasted_iota(jnp.int32, (CHUNK, 1), 0) + rows.start
                inside = jnp.logical_and(
                    jnp.logical_or(row >= WINDOW, place.seq > 0),
                    jnp.logical_or(row < rows_ext - WINDOW, place.seq < place.shards - 1),
                )
                grad = jnp.where(inside, grad, 0.0)
            low = grad.astype(BF16)
            if part == 0:
                rows = pl.ds(pl.multiple_of(rows.start + WINDOW, WINDOW), CHUNK)
            grads_ref[rows, out] = low
            small_ref[6 + group : 7 + group, out] += jnp.sum(low.astype(F32), 0, keepdims=True)

        row_blocks(rows_all if part == 0 else rows_ext, body)
        rows = own if part == 0 else slice(0, rows_ext)
        weight = nn(turned_ref[:, rows], grads_ref[rows, out]).astype(BF16)
        start = width + base + part * CHUNK
        done = 0
        while done < CHUNK:
            index, at = (start + done) // block, (start + done) % block
            size = min(CHUNK - done, block - at)
            parts[index, 0:width, at : at + size] = weight[:, done : done + size]
            done += size


def table_grads(gline_ref, bucket_ref, buckets, small_ref):
    heads = gline_ref.shape[0]
    head = lax.broadcasted_iota(jnp.int32, (heads, LANES), 0)
    lane_bucket = lax.broadcasted_iota(jnp.int32, (LANES, LINE), 0)
    total = jnp.zeros((heads, LANES), F32)
    per_row = LANES // buckets
    for place in range(per_row):
        one_hot = jnp.where(lane_bucket - place * buckets == bucket_ref[...].astype(jnp.int32), 1.0, 0.0)
        sums = lax.dot_general(
            gline_ref[...], one_hot, (((1,), (1,)), ((), ())), precision=lax.Precision.HIGHEST,
            preferred_element_type=F32,
        )
        total = total + jnp.where(head % per_row == place, sums, 0.0)
    for index in range(heads // per_row):
        small_ref[13 + index : 14 + index, 0:LANES] = jnp.sum(
            total[index * per_row : (index + 1) * per_row], 0, keepdims=True
        )


def layer_kernel(pairs, head_dim, buckets, shards, *refs):
    x_h, cot_h, up_h, down_h, w_h, codes_r, table_r, wo_h = refs[:8]
    vectors, bias_up_r, buckets_r = refs[8:15], refs[15], refs[16]
    layer_h, gtok_h, total_r, small_r, result_h, core_h, ac_h = refs[17:24]
    (x_r, q_r, k_r, qf_r, kv_r, line_r, num_r, den_r, tot_r, biases, before_r, after_r, left_r, right_r,
     lden_r, rden_r, attn_r, denom_r, low_r, scale_r, hidden_r, turned_r, cot_r, acc_r,
     mats, pool, bias_r, gbias_r, gk_r, gv_r, gline_r, cg_r, gqkv_r) = refs[24:57]
    stage_r, xl_r, yl_r, zl_r, ll_r = refs[57:62]
    ac_r, ao_r, at_r, aa_r, done_r, held_r, land_r = refs[62:69]
    sum_buffers, sum_two_buffers = refs[69:75], refs[75:81]
    sems = refs[81:]
    all_rows = pl.ds(0, q_r.shape[0])
    normed_r = (gk_r.at[0, all_rows], gk_r.at[1, all_rows], gv_r.at[0, all_rows])
    gturned_r = gqkv_r.at[:, all_rows]
    edge_r, tail_r = cot_r.at[pl.ds(0, 2 * WINDOW)], cot_r.at[pl.ds(2 * WINDOW, 2 * WINDOW)]
    w_sems, s_sems, s2_sems, rs_sems = sems[:8], sems[8:12], sems[12:16], sems[16:27]
    ar_sems, sm_sems, bias_sems = sems[27:36], sems[36:38], sems[38:40]
    h_send, h_recv, t_send, t_recv, load_sem, w_r, wo_r, omega_r, packed_r = sems[40:]
    rows, width = q_r.shape
    half = LANES // 2
    line = [packed_r.at[pl.ds(index, 1)] for index in range(packed_r.shape[0])]
    b_r, bo_r, g1_r, s1_r, bdown_r, g2_r, s2_r = line[:3], *line[3:9]
    bup_r, bucket_r = line[9].at[:, pl.ds(0, up_h.shape[1])], line[10].at[:, pl.ds(0, LINE)]
    own = pl.ds(WINDOW, rows)
    place = Place(shards)
    sends = Sends()
    seq = place.seq
    peers = [place.beside(lax.rem(seq + o, shards)) for o in range(1, shards)]
    peers += [place.at(core=1 - place.core), place.at(x=1 - place.x)]
    barrier = pltpu.get_barrier_semaphore()
    for peer in peers:
        pl.semaphore_signal(barrier, inc=1, device_id=peer, device_id_type=MESH)
    loads = [
        pltpu.make_async_copy(src, dst, load_sem.at[i])
        for i, (src, dst) in enumerate((
            (down_h, hidden_r.at[pl.ds(0, down_h.shape[0])]), (up_h, mats.at[0, place.a, place.b]),
            (x_h, x_r.at[own]), (cot_h, cot_r), (w_h, w_r), (wo_h, wo_r),
        ))
    ]
    for load in loads:
        load.start()
    gather = WeightGather(place, sends, mats, width // 4, w_sems)
    key_sums = StateSums(place, sends, sum_buffers, s_sems)
    grad_sums = StateSums(place, sends, sum_two_buffers, s2_sems)
    scatter = GradScatter(place, sends, mats, total_r, ll_r.shape[0], (core_h, stage_r, xl_r, yl_r, zl_r, ll_r), rs_sems)
    chunks = done_r.shape[0]
    reduce = AllReduce(place, sends, pool, result_h, (ac_h, ac_r, ao_r, at_r, aa_r), done_r, "bmmm", ar_sems)
    little = SmallReduce(place, sends, held_r, land_r, sm_sems)
    to_right = place.beside(jnp.minimum(seq + 1, shards - 1))
    to_left = place.beside(jnp.maximum(seq - 1, 0))
    low_edge, high_edge = pl.ds(0, WINDOW), pl.ds(rows + WINDOW, WINDOW)

    small_r[...] = jnp.zeros(small_r.shape, F32)
    acc_r[0:WINDOW, :] = jnp.zeros((WINDOW, width), F32)
    acc_r[rows + WINDOW :, :] = jnp.zeros((WINDOW, width), F32)
    at = 0
    for vector in vectors:
        for start in range(0, vector.shape[0], width):
            packed_r[at, :] = vector[start : start + width].astype(F32)
            at += 1
    packed_r[at, 0 : bias_up_r.shape[0]] = bias_up_r[...].astype(F32)
    middle = (buckets_r.shape[0] + 1) // 2
    packed_r[at + 1, 0:LINE] = buckets_r[middle - LINE // 2 : middle + LINE // 2].astype(F32)
    omega_r[...] = jnp.zeros(omega_r.shape, BF16)
    heads, head_dim = codes_r.shape[:2]
    per_chunk = CHUNK // head_dim
    for head in range(heads):
        at = slice(head % per_chunk * head_dim, (head % per_chunk + 1) * head_dim)
        omega_r[head // per_chunk, at, at] = (codes_r[head].astype(F32) - CENTER).astype(BF16)
    loads[0].wait()
    mats[1, place.a, place.b] = hidden_r[0 : down_h.shape[0], :].T
    loads[1].wait()
    loads[2].wait()
    pl.semaphore_wait(barrier, len(peers))
    sends.send(
        x_r.at[pl.ds(rows, WINDOW)], x_r.at[low_edge], h_send.at[0], h_recv.at[0], to_right, place.not_last
    )
    sends.send(
        x_r.at[pl.ds(WINDOW, WINDOW)], x_r.at[high_edge], h_send.at[1], h_recv.at[1], to_left, place.not_first
    )
    biases[seq] = jnp.broadcast_to(bup_r[...], biases.shape[1:]).astype(BF16)
    for offset in range(1, shards):
        sends.send(
            biases.at[seq], biases.at[seq], bias_sems[0].at[offset], bias_sems[1].at[offset],
            place.beside(lax.rem(seq + offset, shards)),
        )
    gather.along_a(0, (0, 1))

    @pl.when(place.is_first)
    def _():
        x_r[0:WINDOW, :] = jnp.zeros((WINDOW, width), BF16)

    @pl.when(place.is_last)
    def _():
        x_r[rows + WINDOW :, :] = jnp.zeros((WINDOW, width), BF16)

    ke_r, ve_r = kv_r.at[0], kv_r.at[1]
    loads[4].wait()
    loads[5].wait()
    qkv_phase(
        x_r.at[own], w_r, b_r, omega_r, ((1, k_r.at[own], ke_r.at[own]), (2, ve_r.at[own], None)), head_dim
    )
    tot_r[pairs * half :, :] = jnp.zeros((tot_r.shape[0] - pairs * half, LANES), F32)
    state_phase(ke_r.at[own], ve_r.at[own], num_r, den_r, tot_r, pairs)
    key_sums.start(tot_r)
    gather.across(0)
    qkv_phase(x_r.at[own], w_r, b_r, omega_r, ((0, q_r, qf_r),), head_dim)
    line_phase(bucket_r, table_r, line_r)
    arrive(x_r.at[low_edge], h_recv.at[0], place.at(), place.not_first)
    arrive(x_r.at[high_edge], h_recv.at[1], place.at(), place.not_last)
    halo_phase(x_r, w_r, b_r, omega_r, k_r, kv_r, place, head_dim)
    third = pairs // 3

    def ffn(step, column, forward):
        a = place.nearest(step) if forward else place.shard(step)
        b = 1 - place.b if column else place.b
        shard = a * place.count_b + b
        if forward:
            ffn_forward_shard(hidden_r, mats, a, b, shard, bias_r, pool, acc)
        else:
            ffn_backward_shard(hidden_r, gturned_r, hidden_turned, mats, a, b, shard, pool, acc, gbias_r)

    key_sums.along_a()
    band_forward_phase(qf_r, ke_r, ve_r, line_r, attn_r, denom_r, 0, third)
    gather.along_a(1, (0,))
    band_forward_phase(qf_r, ke_r, ve_r, line_r, attn_r, denom_r, third, 2 * third)
    gather.along_a(1, (1,))
    band_forward_phase(qf_r, ke_r, ve_r, line_r, attn_r, denom_r, 2 * third, pairs)
    gather.along_b(0, (0,))
    key_sums.along_b()
    gather.across(1)
    gather.along_b(0, (1,))
    key_sums.finish(before_r, after_r)
    gather.along_a(2, (0, 1))
    gather.across(2)
    far_forward_phase(
        qf_r, ke_r, ve_r, line_r, num_r, den_r, before_r, after_r, attn_r, low_r, denom_r, left_r, right_r, lden_r,
        rden_r, pairs, head_dim,
    )
    hidden_turned = turned_r.at[:, pl.ds(0, rows)]
    acc = acc_r.at[own]
    hidden_phase(
        x_r.at[own], low_r, wo_r, bo_r, g1_r, s1_r, bdown_r, normed_r, scale_r, hidden_r, hidden_turned, acc
    )
    for offset in range(1, shards):
        arrive(biases.at[lax.rem(seq + shards - offset, shards)], bias_sems[1].at[offset], place.at())
    for shard in range(shards):
        bias_r[shard] = biases[shard, 0:8, :].astype(F32)
    ffn(0, 0, True)
    gather.along_b(1, (0, 1))
    gather.along_x(1, 0)
    gather.along_x(0, 1)
    gather.finish(0, 1)
    ffn(0, 1, True)
    gather.along_a(3, (0, 1))
    gather.across(3)
    gather.finish(1, 0)
    ffn(1, 0, True)
    gather.along_x(1, 1)
    gather.along_b(2, (0, 1))
    gather.along_x(2, 0)
    gather.finish(1, 1)
    ffn(1, 1, True)
    gather.finish(2, 0)
    ffn(2, 0, True)
    gather.along_x(2, 1)
    gather.along_x(3, 0)
    gather.along_b(3, (0, 1))
    gather.finish(2, 1)
    ffn(2, 1, True)
    gather.finish(3, 0)
    ffn(3, 0, True)
    gather.along_x(3, 1)
    gather.finish(3, 1)
    ffn(3, 1, True)
    sends.drain()
    loads[3].wait()
    middle_phase(acc, cot_r, g2_r, s2_r, hidden_r, gturned_r, small_r)
    layer_out = pltpu.make_async_copy(cot_r, layer_h, load_sem.at[6])
    layer_out.start()
    items = [(offset, column) for offset in (2, 1, 3, 0) for column in (1, 0)]
    for index, item in enumerate(items):
        ffn(*item, False)
        scatter.start(*item)
        if index > 1:
            scatter.chip(*items[index - 2])
        if index > 0:
            scatter.fetch(*items[index - 1])
        if index == 7:
            scatter.along_x(*items[0])
    first_back_phase(acc, normed_r, scale_r, g1_r, hidden_r, small_r)
    tot_r[pairs * half :, :] = jnp.zeros((tot_r.shape[0] - pairs * half, LANES), F32)
    block = pool.shape[2]
    for index in range(width // block):
        cols = slice(index * block, (index + 1) * block)
        pool[index, 0:width, :] = tn(low_r[...], hidden_r[:, cols]).astype(BF16)
    reduce.push(0)
    scatter.chip(*items[6])
    scatter.fetch(*items[7])
    scatter.along_x(*items[1])
    attn_back_phase(hidden_r, wo_r, attn_r, denom_r, low_r, qf_r, num_r, den_r, tot_r, pairs, head_dim)
    layer_out.wait()
    grad_sums.start(tot_r)
    scatter.chip(*items[7])

    def turn(block):
        turned_r[:, block] = x_r[block, :].T

    row_blocks(rows + 2 * WINDOW, turn)
    groups = pairs * LANES // CHUNK
    in_group = CHUNK // LANES

    def band(pair):
        group = pair // in_group
        band_backward_phase(
            qf_r, ke_r, ve_r, line_r, low_r, denom_r, num_r, den_r, left_r, right_r, lden_r, rden_r, attn_r,
            gk_r.at[group % 2], gv_r.at[group % 2], gline_r, cg_r, pair, pair + 1, group * in_group, head_dim,
        )

    def far(group):
        far_back_phase(
            ke_r, ve_r, line_r, num_r, den_r, before_r, after_r, gk_r.at[group % 2], gv_r.at[group % 2], pairs,
            group * in_group, (group + 1) * in_group, group * in_group, head_dim,
        )

    def grads(group, wanted):
        qkv_grad_phase(
            turned_r, w_r, omega_r, q_r, k_r, qf_r, ke_r, attn_r, gk_r.at[group % 2], gv_r.at[group % 2], gqkv_r,
            pool, small_r, group, wanted, place, head_dim,
        )

    def tokens_part(group, wanted):
        def body(block):
            if 1 not in wanted:
                block = pl.ds(pl.multiple_of(block.start + WINDOW, WINDOW), CHUNK)
            total = acc_r[block, :]
            for part in wanted:
                cols = slice(part * CHUNK, (part + 1) * CHUNK)
                wide = slice(part * width + group * CHUNK, part * width + (group + 1) * CHUNK)
                total = total + nt(gqkv_r[block, cols], w_r[:, wide])
            acc_r[block, :] = total

        row_blocks(rows + 2 * WINDOW if 1 in wanted else rows, body)

    scatter.along_x(*items[2])
    band(0)
    grad_sums.along_a()
    band(1)
    scatter.along_x(*items[3])
    grads(0, (0,))
    tokens_part(0, (0,))
    scatter.along_b(2)
    band(2)
    grad_sums.along_b()
    reduce.stage(0, 1)
    band(3)
    grad_sums.finish(before_r, after_r)
    scatter.along_x(*items[4])
    scatter.along_b(1)
    far(0)
    grads(0, (1, 2))
    reduce.push(1)
    scatter.along_x(*items[5])
    tokens_part(0, (1, 2))
    grads(1, (0,))
    tokens_part(1, (0,))
    band(4)
    scatter.along_x(*items[6])
    reduce.stage(0, 2)
    reduce.stage(1, 1)
    band(5)
    far(1)
    grads(1, (1, 2))
    reduce.push(2)
    scatter.along_x(*items[7])
    scatter.along_b(3)
    tokens_part(1, (1, 2))
    grads(2, (0,))
    tokens_part(2, (0,))
    reduce.stage(0, 3)
    reduce.stage(2, 1)
    far(2)
    grads(2, (1, 2))
    reduce.push(3)
    scatter.along_b(0)
    table_grads(gline_r, bucket_r, buckets, small_r)
    per_row = width // gbias_r.shape[2]
    for index in range(shards // per_row):
        small_r[9 + index : 10 + index, :] = jnp.concatenate(
            [gbias_r[index * per_row + i, 0:1, :] for i in range(per_row)], 1
        )
    held_r[0] = small_r[...]
    little.send(0)
    reduce.stage(1, 2)
    reduce.stage(3, 1)
    reduce.stage(0, 4)
    tokens_part(2, (1, 2))
    edge_r[0:WINDOW, :] = acc_r[0:WINDOW, :].astype(BF16)
    edge_r[WINDOW:, :] = acc_r[rows + WINDOW :, :].astype(BF16)
    top, bottom = pl.ds(0, WINDOW), pl.ds(WINDOW, WINDOW)
    sends.send(edge_r.at[top], tail_r.at[bottom], t_send.at[0], t_recv.at[1], to_left, place.not_first)
    sends.send(edge_r.at[bottom], tail_r.at[top], t_send.at[1], t_recv.at[0], to_right, place.not_last)
    reduce.stage(2, 2)
    reduce.stage(1, 3)
    little.receive(0)
    little.send(1)
    reduce.stage(0, 5)
    scatter.along_a()
    reduce.stage(3, 2)
    reduce.stage(2, 3)
    reduce.stage(1, 4)
    reduce.stage(0, 6)
    little.receive(1)
    little.send(2)
    reduce.stage(3, 3)
    reduce.stage(2, 4)
    reduce.stage(1, 5)
    reduce.stage(3, 4)
    reduce.stage(0, 7)
    reduce.stage(2, 5)
    reduce.stage(1, 6)
    little.receive(2)
    little.send(3)
    reduce.stage(3, 5)
    arrive(tail_r.at[top], t_recv.at[0], place.at(), place.not_first)
    arrive(tail_r.at[bottom], t_recv.at[1], place.at(), place.not_last)

    @pl.when(place.not_first)
    def _():
        acc_r[WINDOW : 2 * WINDOW, :] += tail_r[0:WINDOW, :].astype(F32)

    @pl.when(place.not_last)
    def _():
        acc_r[rows : rows + WINDOW, :] += tail_r[WINDOW:, :].astype(F32)

    tokens_out = pltpu.make_async_copy(acc, gtok_h, load_sem.at[7])
    tokens_out.start()
    reduce.stage(2, 6)
    reduce.stage(3, 6)
    scatter.last_x()
    reduce.stage(1, 7)
    little.receive(3)
    small_r[...] = little.total()
    reduce.stage(2, 7)
    reduce.stage(3, 7)
    scatter.finish()
    for index in range(chunks):
        reduce.stage(index, 8)
    tokens_out.wait()
    sends.drain()


def in_parts(grouped):
    groups = grouped.shape[1] // (3 * CHUNK)
    starts = [(group * 3 + part) * CHUNK for part in range(3) for group in range(groups)]
    return jnp.concatenate([grouped[:, start : start + CHUNK].astype(F32) for start in starts], 1)


def call(body, outs, operands, scratch=(), limit=60, collective_id=None, in_place=(), out_place=()):
    return pl.pallas_call(
        body,
        out_shape=[jax.ShapeDtypeStruct(shape, dtype) for shape, dtype in outs],
        in_specs=[
            pl.BlockSpec(memory_space=pl.ANY if i in in_place else pltpu.VMEM) for i in range(len(operands))
        ],
        out_specs=[
            pl.BlockSpec(memory_space=pl.ANY if i in out_place else pltpu.VMEM) for i in range(len(outs))
        ],
        scratch_shapes=list(scratch),
        compiler_params=pltpu.CompilerParams(
            vmem_limit_bytes=limit * MIB,
            collective_id=collective_id,
            has_side_effects=collective_id is not None,
        ),
    )(*operands)


def unpack_kernel(
    result_h, total_h, tokens_h, layer_h, small_r, gw_h, gwo_h, gup_r, gdown_r, gtok_h, out_h, gb_r, gbu_r, *rest
):
    vector_rs, (table_r, result_r, total_r, wide_r, tokens_r, layer_r, in_sem, out_sem) = rest[:6], rest[6:]
    blocks, width, block = result_r.shape
    chunks = wide_r.shape[0]
    per_chunk = blocks // chunks
    loads = []
    for chunk in range(chunks):
        part = pl.ds(chunk * per_chunk, per_chunk)
        loads.append(pltpu.make_async_copy(result_h.at[part], result_r.at[part], in_sem.at[chunk]))
    load_total = pltpu.make_async_copy(total_h, total_r, in_sem.at[chunks])
    load_tokens = pltpu.make_async_copy(tokens_h, tokens_r, in_sem.at[chunks + 1])
    load_layer = pltpu.make_async_copy(layer_h, layer_r, in_sem.at[chunks + 2])
    for load in loads + [load_total, load_tokens, load_layer]:
        load.start()
    stores = []

    def store(src, dst):
        copy = pltpu.make_async_copy(src, dst, out_sem.at[len(stores)])
        copy.start()
        stores.append(copy)

    for chunk in range(chunks):
        loads[chunk].wait()
        for index in range(per_chunk):
            wide_r[chunk, :, index * block : (index + 1) * block] = result_r[chunk * per_chunk + index].astype(F32)
        if chunk == 0:
            store(wide_r.at[0], gwo_h)
            continue
        for part in range(3):
            source = wide_r.at[chunk, :, pl.ds(part * CHUNK, CHUNK)]
            store(source, gw_h.at[:, pl.ds(part * width + (chunk - 1) * CHUNK, CHUNK)])
    load_tokens.wait()
    store(tokens_r, gtok_h)
    load_layer.wait()
    store(layer_r, out_h)
    load_total.wait()
    gup_r[...] = total_r[0].astype(F32)
    gdown_r[...] = total_r[1].T.astype(F32)
    for index, ref in enumerate(vector_rs):
        ref[...] = small_r[index, :]
    for group in range(width // CHUNK):
        for part in range(3):
            start = part * width + group * CHUNK
            gb_r[start : start + CHUNK] = small_r[6 + group, part * CHUNK : (part + 1) * CHUNK]
    heads, buckets = table_r.shape
    per_row = LANES // buckets
    for head in range(heads):
        at = head % per_row * buckets
        row = 13 + head // per_row
        table_r[head : head + 1, :] = small_r[row : row + 1, at : at + buckets]
    units = gbu_r.shape[0]
    seq = lax.axis_index("seq")
    per_row = width // units
    for shard in range(lax.axis_size("seq")):
        @pl.when(seq == shard)
        def _():
            at = shard % per_row * units
            gbu_r[...] = small_r[9 + shard // per_row, at : at + units]
    for copy in stores:
        copy.wait()


def fused(
    x, cot, w_up, w_down, w_qkv, b_qkv, codes, offset_bucket, bias_table, w_out, b_out, gain_one, shift_one, b_up, b_down,
    gain_two, shift_two, pairs, head_dim,
):
    rows, width = x.shape
    units = w_up.shape[1]
    heads, buckets = bias_table.shape
    count = lax.axis_size("seq")
    count_a = count // 2
    blocks, half = rows // WINDOW, LANES // 2
    middle, quarter = width // 6, width // 4
    side = (width - middle) // 2
    groups = width // CHUNK
    chunks = 1 + groups
    columns = chunks * width // units
    wide, ext = (rows, width), (rows + 2 * WINDOW, width)
    stacked, flat = (pairs * blocks, half, LANES), (pairs * blocks, LANES)
    message = (pairs * half + 32, LANES)
    mats = (2, count_a, 2, width, units)
    dma = pltpu.SemaphoreType.DMA
    vmem = pltpu.VMEM
    part = (message[0] // 2, LANES)
    sums = [vmem(shape, BF16) for shape in (message, message, part, (count_a, *part), (2, *part), (2, *part))]
    layer, gtok, total, small, result, _, _ = call(
        functools.partial(layer_kernel, pairs, head_dim, buckets, count),
        [(wide, BF16), (wide, F32), ((2, width, units), BF16), ((16, width), F32), ((columns, width, units), BF16),
         (mats[1:], BF16), ((columns, 2 * quarter, units), BF16)],
        (x, cot, w_up, w_down, w_qkv, codes, bias_table, w_out, b_qkv, b_out, gain_one, shift_one, b_down, gain_two,
         shift_two, b_up, offset_bucket),
        [vmem(ext, BF16), vmem(wide, BF16), vmem(ext, BF16), vmem(wide, BF16), vmem((2, *ext), BF16),
         vmem((heads, LINE), F32), vmem(stacked, F32), vmem(flat, F32), vmem(message, F32),
         vmem((count, 16, units), BF16), vmem(message, F32),
         vmem(message, F32), vmem(stacked, F32), vmem(stacked, F32), vmem(flat, F32), vmem(flat, F32),
         vmem(wide, F32), vmem(wide, F32), vmem(wide, BF16), vmem((rows, LANES), F32),
         vmem(wide, BF16), vmem((width, ext[0]), BF16),
         vmem(wide, BF16), vmem(ext, F32), vmem(mats, BF16), vmem((columns, 2 * rows, units), BF16),
         vmem((count, 8, units), F32), vmem((count, 8, units), F32), vmem((2, ext[0], CHUNK), F32),
         vmem((2, ext[0], CHUNK), F32), vmem((heads, LINE), F32), vmem((2 * WINDOW, 3 * WINDOW), F32),
         vmem(ext, BF16), vmem((2, width, units), BF16), vmem((count_a, 2, side, units), BF16),
         vmem((count_a, side + middle, units), BF16), vmem((count_a - 1, side + middle, units), BF16),
         vmem((middle, units), BF16),
         vmem((2, 2 * quarter, units), BF16), vmem((columns, quarter, units), BF16),
         vmem((chunks, quarter, units), BF16), vmem((chunks, count_a - 1, quarter // count_a, units), BF16),
         vmem((chunks, quarter // count_a, units), BF16), vmem((4, 16, width), F32),
         vmem((3 + count_a, 16, width), F32)]
        + sums + sums
        + gather_sems(count_a) + sums_sems(count_a) + sums_sems(count_a) + scatter_sems(count_a)
        + reduce_sems(chunks, count_a)
        + [dma((3 + count_a,)), dma((3 + count_a,))] + [dma((count,)), dma((count,))] + [ dma((2,)), dma((2,)), dma((2,)), dma((2,)), dma((8,)),
           vmem(w_qkv.shape, BF16), vmem(w_out.shape, BF16),
           vmem((groups, CHUNK, CHUNK), BF16), vmem((16, width), F32)],
        limit=62,
        collective_id=0,
        in_place=(0, 1, 2, 3, 4, 7),
        out_place=(0, 1, 4, 5, 6),
    )
    vector = ((width,), F32)
    gw_qkv, gw_out, gup, gdown, gtok, layer, gb_qkv, grad_b_up, g2, s2, bd, g1, s1, bo, gtable = call(
        unpack_kernel,
        [((width, 3 * width), F32), ((width, width), F32), ((width, units), F32), ((units, width), F32), (wide, F32),
         (wide, BF16), ((3 * width,), F32), ((units,), F32)] + [vector] * 6 + [((heads, buckets), F32)],
        (result, total, gtok, layer, small),
        [vmem((columns, width, units), BF16), vmem((2, width, units), BF16), vmem((chunks, width, width), F32),
         vmem(wide, F32), vmem(wide, BF16), dma((chunks + 3,)), dma((3 * chunks,))],
        in_place=(0, 1, 2, 3),
        out_place=(0, 1, 4, 5),
    )
    return (
        layer[None], gtok[None], gw_qkv, gb_qkv, gw_out, bo, g1, s1, gup, grad_b_up, gdown, bd, g2, s2, gtable,
    )


def shards(
    tokens, cotangent, w_qkv, b_qkv, w_out, b_out, gain_one, shift_one, w_up, b_up, w_down, b_down,
    gain_two, shift_two, feature_codes, bias_table, offset_bucket,
):
    rows, width = tokens.shape[1:]
    heads, head_dim, feats = feature_codes.shape
    buckets = bias_table.shape[1]
    pairs = heads // 2
    blocks = rows // WINDOW
    half = LANES // 2
    hidden_units = w_up.shape[1]
    length = (offset_bucket.shape[0] + 1) // 2
    count = lax.axis_size("seq")
    x = tokens[0]
    state = (pairs * half + 8, LANES)
    stacked = (pairs * blocks, half, LANES)
    flat = (pairs * blocks, LANES)
    wide = (rows, width)

    def halo(block):
        forward = [(i, i + 1) for i in range(count - 1)]
        backward = [(target, source) for source, target in forward]
        low = lax.ppermute(block[rows - WINDOW :], "seq", forward)
        high = lax.ppermute(block[:WINDOW], "seq", backward)
        return jnp.concatenate([low, block, high], 0)

    me = lax.axis_index("seq")
    ids = jnp.arange(count)

    def prefix(message):
        every = lax.all_gather(message, "seq", axis=0)
        before = jnp.sum(jnp.where((ids < me)[:, None, None], every, 0.0), 0)
        after = jnp.sum(jnp.where((ids > me)[:, None, None], every, 0.0), 0)
        return before, after

    if lax.axis_size("row") == 4 and count == 8:
        return fused(
            x, cotangent[0], w_up, w_down, w_qkv, b_qkv, feature_codes, offset_bucket, bias_table, w_out, b_out, gain_one,
            shift_one, b_up, b_down, gain_two, shift_two, pairs, head_dim,
        )

    bucket_line = offset_bucket[length - LINE // 2 : length + LINE // 2][None]
    omega_int = (feature_codes.astype(F32) - CENTER).astype(BF16)
    group = CHUNK // head_dim
    eye = jnp.eye(group, dtype=BF16)
    omega = (
        omega_int.reshape(heads // group, group, head_dim, 1, feats)
        * eye[None, :, None, :, None]
    ).reshape(heads // group, CHUNK, CHUNK)

    def body_one(x_r, w_r, b_r, o_r, bu_r, ta_r, q_r, k_r, v_r, qf_r, kf_r, line_r, num_r, den_r, tot_r):
        parts = ((1, k_r, kf_r), (2, v_r, None), (0, q_r, qf_r))
        qkv_phase(x_r, w_r, [b_r.at[pl.ds(i, 1)] for i in range(3)], o_r, parts, head_dim)
        line_phase(bu_r, ta_r, line_r)
        state_phase(kf_r, v_r, num_r, den_r, tot_r, pairs)

    q, k, v, qf, kf, line, num, den, total = call(
        body_one,
        [(wide, BF16)] * 5
        + [((heads, LINE), F32), (stacked, F32), (flat, F32), (state, F32)],
        (x, w_qkv, b_qkv.astype(F32).reshape(3, width), omega, bucket_line, bias_table),
    )
    up_all = lax.all_gather(w_up, "seq", axis=0)
    down_all = lax.all_gather(jnp.transpose(w_down), "seq", axis=0)
    b_up_all = jnp.broadcast_to(lax.all_gather(b_up, "seq", axis=0)[:, None, :], (count, 8, hidden_units))

    ke, ve = halo(kf), halo(v)
    before, after = prefix(total)

    def body_two(*refs):
        ins, outs = refs[:12], refs[12:]
        qf_r, ke_r, ve_r, line_r, num_r, den_r, bef_r, aft_r, x_r, w_r, b_r, _ = ins
        out_r, low_r, dnm_r, l_r, r_r, ld_r, rd_r, nrm_r, sc_r = outs
        band_forward_phase(qf_r, ke_r, ve_r, line_r, out_r, dnm_r, 0, pairs)
        far_forward_phase(
            qf_r, ke_r, ve_r, line_r, num_r, den_r, bef_r, aft_r,
            out_r, low_r, dnm_r, l_r, r_r, ld_r, rd_r, pairs, head_dim,
        )
        out_phase(x_r, low_r, w_r, b_r, nrm_r, sc_r)

    attn, attn_low, denom, left, right, left_den, right_den, normed, scale = call(
        body_two,
        [(wide, F32), (wide, BF16), (wide, F32), (stacked, F32), (stacked, F32), (flat, F32),
         (flat, F32), (wide, F32), ((rows, LANES), F32)],
        (qf, ke, ve, line, num, den, before, after, x, w_out, b_out[None], gain_one[None]),
    )
    layer, first, first_low, vec, gup, gdown, gbias = call(
        ffn_phase,
        [(wide, BF16), (wide, F32), (wide, BF16), ((8, width), F32),
         ((count, width, hidden_units), BF16), ((count, width, hidden_units), BF16),
         ((count, 8, hidden_units), F32)],
        (normed, scale, gain_one[None], shift_one[None], up_all, b_up_all, down_all, b_down[None],
         gain_two[None], shift_two[None], cotangent[0]),
        (pltpu.VMEM((count, rows, hidden_units), BF16), pltpu.VMEM((count, rows, hidden_units), BF16),
         pltpu.VMEM(wide, F32)),
    )

    def reduced(part):
        return lax.psum(lax.psum_scatter(part, "seq", scatter_dimension=0), "row").astype(F32)

    grad_w_up = reduced(gup)
    grad_w_down = jnp.transpose(reduced(gdown))
    grad_b_up = reduced(gbias[:, 0])
    ext = (rows + 2 * WINDOW, width)

    def body_four(*refs):
        (gl_r, w_r, lo_r, ou_r, dn_r, qf_r, ke_r, ve_r, li_r, l_r, r_r, ld_r, rd_r, bu_r) = refs[:14]
        gw_r, gq_r, gk_r, gv_r, dnum_r, dden_r, tot_r, gt_r, gnum_r, gden_r, gline_r, cg_r = refs[14:]
        out_back_phase(
            gl_r, w_r, lo_r, ou_r, dn_r, qf_r, gnum_r, gden_r, gw_r, dnum_r, dden_r, tot_r, pairs, head_dim
        )
        band_backward_phase(
            qf_r, ke_r, ve_r, li_r, gnum_r, gden_r, dnum_r, dden_r, l_r, r_r, ld_r, rd_r,
            gq_r, gk_r, gv_r, gline_r, cg_r, 0, pairs, 0, head_dim,
        )
        gt_r[...] = table_phase(gline_r, bu_r, buckets)

    gw_out, gq, gk, gv, dnum, dden, gtotal, gtable = call(
        body_four,
        [((width, width), F32), (wide, F32), (ext, F32), (ext, F32), (stacked, F32), (flat, F32),
         (state, F32), (bias_table.shape, F32)],
        (first_low, w_out, attn_low, attn, denom, qf, ke, ve, line, left, right, left_den, right_den,
         bucket_line),
        (pltpu.VMEM(wide, BF16), pltpu.VMEM(wide, F32), pltpu.VMEM((heads, LINE), F32),
         pltpu.VMEM((2 * WINDOW, 3 * WINDOW), F32)),
    )
    past, future = prefix(gtotal)
    forward = [(i, i + 1) for i in range(count - 1)]
    backward = [(target, source) for source, target in forward]
    to_left = jnp.stack([gk[:WINDOW], gv[:WINDOW]]).astype(BF16)
    to_right = jnp.stack([gk[rows + WINDOW :], gv[rows + WINDOW :]]).astype(BF16)
    low_in = lax.ppermute(to_right, "seq", forward)
    high_in = lax.ppermute(to_left, "seq", backward)

    def body_five(*refs):
        (x_r, w_r, o_r, q_r, k_r, v_r, qf_r, kf_r, li_r, dn_r, dd_r, pa_r, fu_r, lo_r, hi_r, gq_r,
         gki_r, gvi_r, fi_r) = refs[:19]
        gt_r, gw_r, gb_r, gk_r, gv_r, turned_r = refs[19:]
        gk_r[...] = gki_r[...]
        gv_r[...] = gvi_r[...]
        gt_r[...] = fi_r[...]
        turned_r[...] = x_r[...].T
        key_back_phase(
            kf_r, v_r, li_r, dn_r, dd_r, pa_r, fu_r, lo_r, hi_r, gk_r, gv_r, pairs, 0, pairs, head_dim
        )
        for group in range(width // CHUNK):
            qkv_back_phase(
                turned_r, w_r, o_r, q_r, k_r, qf_r, kf_r, gq_r, gk_r, gv_r, gt_r, gw_r, gb_r, group, head_dim
            )

    gtok, gw_qkv, small = call(
        body_five,
        [(wide, F32), ((width, 4 * width), F32), ((16, width), F32)],
        (x, w_qkv, omega, q, k, v, qf, kf, line, dnum, dden, past, future, low_in, high_in, gq, gk, gv,
         first),
        (pltpu.VMEM(ext, F32), pltpu.VMEM(ext, F32), pltpu.VMEM((width, rows), BF16)),
    )
    gw_qkv = in_parts(gw_qkv[:, width:])
    gb_qkv = in_parts(small[6 : 6 + width // CHUNK].reshape(1, -1))
    summed = lax.psum((gw_qkv, gb_qkv[0], gw_out, vec, gtable), ("row", "seq"))
    gw_qkv, gb_qkv, gw_out, vec, gtable = summed
    return (
        layer[None], gtok[None], gw_qkv, gb_qkv, gw_out, vec[5], vec[3], vec[4], grad_w_up, grad_b_up,
        grad_w_down, vec[2], vec[0], vec[1], gtable,
    )


def solution(mesh):
    placed = (
        P("row", "seq", None), P("row", "seq", None), P(), P(), P(), P(), P(), P(), P(None, "seq"),
        P("seq"), P("seq", None), P(), P(), P(), P(), P(), P(),
    )
    return jax.shard_map(
        shards,
        mesh=mesh,
        in_specs=placed,
        out_specs=(
            P("row", "seq", None), P("row", "seq", None), P(), P(), P(), P(), P(), P(), P(None, "seq"),
            P("seq"), P("seq", None), P(), P(), P(), P(),
        ),
        check_vma=False,
    )
```

```python
import functools
import math

import jax
import jax.numpy as jnp
from jax import lax
from jax.experimental import pallas as pl
from jax.experimental.pallas import tpu as pltpu
from jax.sharding import PartitionSpec as P

WINDOW = 128
LANES = 128
LINE = 512
CHUNK = 256
EPS = 1e-06
CENTER = 7.5
SPREAD = math.sqrt(21.25)
ROOT_HALF = 0.7071067811865476
INV_ROOT_TAU = 0.3989422804014327
MIB = 1 << 20
F32 = jnp.float32
BF16 = jnp.bfloat16


def nn(a, b):
    return lax.dot_general(a, b, (((1,), (0,)), ((), ())), preferred_element_type=F32)


def nt(a, b):
    return lax.dot_general(a, b, (((1,), (1,)), ((), ())), preferred_element_type=F32)


def tn(a, b):
    return lax.dot_general(a, b, (((0,), (0,)), ((), ())), preferred_element_type=F32)


def halves(values):
    upper = values.astype(BF16)
    return upper, (values - upper.astype(F32)).astype(BF16)


def block_ones(size, head_dim):
    rows = lax.broadcasted_iota(jnp.int32, (size, size), 0) // head_dim
    cols = lax.broadcasted_iota(jnp.int32, (size, size), 1) // head_dim
    return jnp.where(rows == cols, 1.0, 0.0)


def head_sums(values, ones):
    upper, lower = halves(values)
    return nn(upper, ones) + nn(lower, ones)


def first_half(shape):
    return lax.broadcasted_iota(jnp.int32, shape, len(shape) - 1) < LANES // 2


def both_heads(pair):
    first = first_half((1, LANES))
    mask_a = jnp.where(first, 1.0, 0.0).astype(pair.dtype)
    mask_b = jnp.where(first, 0.0, 1.0).astype(pair.dtype)
    return jnp.concatenate([pair * mask_a, pair * mask_b], 0)


def per_head(stacked):
    rows = stacked.shape[0] // 2
    return jnp.where(first_half((rows, LANES)), stacked[:rows], stacked[rows:])


def compact(full):
    half = LANES // 2
    return jnp.where(first_half((half, LANES)), full[:half], full[half:])


def expand(small, ones):
    return jnp.concatenate([small, small], 0) * ones


def block_state(keys, values):
    return compact(tn(keys, values)), jnp.sum(keys.astype(F32), 0, keepdims=True)


def coef_tile(line_ref, pair):
    tiles = []
    for head in range(2):
        row = line_ref[pl.ds(2 * pair + head, 1), :]
        wide = pltpu.roll(
            jnp.broadcast_to(row, (WINDOW, LINE)), LINE - WINDOW + 1, 1, stride=1, stride_axis=0
        )
        tiles.append(wide[:, : 3 * WINDOW])
    return jnp.concatenate(tiles, 0)


def far_coefs(line_ref, pair):
    first = first_half((1, LANES))
    row_a = line_ref[pl.ds(2 * pair, 1), :]
    row_b = line_ref[pl.ds(2 * pair + 1, 1), :]
    left = jnp.where(first, row_a[:, 0:1], row_b[:, 0:1])
    right = jnp.where(first, row_a[:, LINE - 2 : LINE - 1], row_b[:, LINE - 2 : LINE - 1])
    return left, right


def unskew_sum(tile):
    rows = tile.shape[0]
    padded = jnp.concatenate([tile, jnp.zeros((rows, LINE - tile.shape[1]), F32)], 1)
    while rows > 8:
        rows = rows // 2
        padded = pltpu.roll(padded[:rows], rows, 1) + padded[rows:]
    while rows > 1:
        rows = rows // 2
        padded = pltpu.roll(padded[:rows], rows, 1) + padded[rows:]
    return padded


def lanes(pair):
    return pl.ds(pl.multiple_of(pair * LANES, LANES), LANES)


def qkv_phase(x_ref, w_ref, b_ref, omega_ref, parts, head_dim):
    width = x_ref.shape[1]
    x = x_ref[...]
    ones = block_ones(CHUNK, head_dim).astype(BF16)
    factor = head_dim ** (-0.25) / SPREAD
    for part, low_ref, feat_ref in parts:
        for chunk in range(width // CHUNK):
            cols = slice(chunk * CHUNK, (chunk + 1) * CHUNK)
            wide = slice(part * width + chunk * CHUNK, part * width + (chunk + 1) * CHUNK)
            low = (nn(x, w_ref[:, wide]) + b_ref[part][:, cols]).astype(BF16)
            low_ref[:, cols] = low
            if feat_ref is not None:
                projected = nn(low, omega_ref[chunk]) * factor
                widened = low.astype(F32)
                half_norm = head_sums(widened * widened, ones) * (0.5 * head_dim ** (-0.5))
                feat_ref[:, cols] = (
                    jnp.exp(projected - half_norm) * head_dim ** (-0.5)
                ).astype(BF16)


def line_phase(bucket_ref, table_ref, line_ref):
    buckets = table_ref.shape[1]
    one_hot = jnp.where(
        lax.broadcasted_iota(jnp.int32, (buckets, LINE), 0) == bucket_ref[...].astype(jnp.int32), 1.0, 0.0
    )
    logs = lax.dot_general(
        table_ref[...],
        one_hot,
        (((1,), (0,)), ((), ())),
        precision=lax.Precision.HIGHEST,
        preferred_element_type=F32,
    )
    line_ref[...] = jnp.exp(logs)


def state_phase(kf_ref, v_ref, num_ref, den_ref, total_ref, pairs):
    blocks = kf_ref.shape[0] // WINDOW
    half = LANES // 2

    @pl.loop(0, pairs)
    def _(pair):
        total = jnp.zeros((half, LANES), F32)
        total_den = jnp.zeros((1, LANES), F32)
        for block in range(blocks):
            rows = slice(block * WINDOW, (block + 1) * WINDOW)
            num, den = block_state(kf_ref[rows, lanes(pair)], v_ref[rows, lanes(pair)])
            num_ref[pair * blocks + block] = num
            den_ref[pl.ds(pair * blocks + block, 1), :] = den
            total = total + num
            total_den = total_den + den
        total_ref[pl.ds(pl.multiple_of(pair * half, half), half), :] = total
        total_ref[pl.ds(pairs * half + pair, 1), :] = total_den


def band_forward_phase(qf_ref, ke_ref, ve_ref, line_ref, out_ref, denom_ref, first, last):
    blocks = qf_ref.shape[0] // WINDOW

    @pl.loop(first, last)
    def _(pair):
        cols = lanes(pair)
        coef = coef_tile(line_ref, pair)
        for block in range(blocks):
            rows = slice(block * WINDOW, (block + 1) * WINDOW)
            window = slice(block * WINDOW, (block + 3) * WINDOW)
            scores = nt(both_heads(qf_ref[rows, cols]), ke_ref[window, cols])
            weights = (coef * scores).astype(BF16)
            values = ve_ref[window, cols]
            summed = nn(weights, jnp.concatenate([values, jnp.ones_like(values)], 1))
            out_ref[rows, cols] = per_head(summed[:, :LANES])
            denom_ref[rows, cols] = per_head(summed[:, LANES:])


def far_forward_phase(
    qf_ref, ke_ref, ve_ref, line_ref, num_ref, den_ref, before_ref, after_ref,
    out_ref, low_ref, denom_ref, left_ref, right_ref, left_den_ref, right_den_ref, pairs, head_dim,
):
    blocks = qf_ref.shape[0] // WINDOW
    half = LANES // 2

    @pl.loop(0, pairs)
    def _(pair):
        ones_f32 = block_ones(LANES, head_dim)
        ones = ones_f32.astype(BF16)
        cols = lanes(pair)
        left_coef, right_coef = far_coefs(line_ref, pair)
        state_rows = pl.ds(pl.multiple_of(pair * half, half), half)
        den_row = pl.ds(pairs * half + pair, 1)
        edge_low = block_state(ke_ref[:WINDOW, cols], ve_ref[:WINDOW, cols])
        edge_high = block_state(
            ke_ref[(blocks + 1) * WINDOW :, cols], ve_ref[(blocks + 1) * WINDOW :, cols]
        )
        past = (before_ref[state_rows, :], before_ref[den_row, :])
        future = (after_ref[state_rows, :], after_ref[den_row, :])

        def block_of(block):
            index = pair * blocks + block
            return num_ref[index], den_ref[pl.ds(index, 1), :]

        def add(one, two, sign=1.0):
            return tuple(a + sign * b for a, b in zip(one, two))

        lefts = [add(past, edge_low, -1.0), past]
        for block in range(2, blocks):
            lefts.append(add(lefts[-1], block_of(block - 2)))
        rights = [add(future, edge_high, -1.0), future]
        for block in range(2, blocks):
            rights.append(add(rights[-1], block_of(blocks + 1 - block)))
        rights = rights[::-1]
        for block in range(blocks):
            rows = slice(block * WINDOW, (block + 1) * WINDOW)
            index = pair * blocks + block
            query = qf_ref[rows, cols]
            left, left_den = lefts[block]
            right, right_den = rights[block]
            left_ref[index] = left
            right_ref[index] = right
            left_den_ref[pl.ds(index, 1), :] = left_den
            right_den_ref[pl.ds(index, 1), :] = right_den
            upper, lower = halves(expand(left_coef * left + right_coef * right, ones_f32))
            numer = out_ref[rows, cols] + nn(query, upper) + nn(query, lower)
            den_far = left_coef * left_den + right_coef * right_den
            denom = denom_ref[rows, cols] + head_sums(query.astype(F32) * den_far, ones)
            out = numer / denom
            out_ref[rows, cols] = out
            low_ref[rows, cols] = out.astype(BF16)
            denom_ref[rows, cols] = denom


def norm_parts(values):
    center = values - jnp.mean(values, -1, keepdims=True)
    inv_scale = lax.rsqrt(jnp.mean(center * center, -1, keepdims=True) + EPS)
    return center * inv_scale, inv_scale


def out_phase(x_ref, low_ref, w_ref, b_ref, normed_ref, scale_ref):
    first_sum = x_ref[...].astype(F32) + nn(low_ref[...], w_ref[...]) + b_ref[...].astype(F32)
    normed, inv_scale = norm_parts(first_sum)
    normed_ref[...] = normed
    scale_ref[...] = jnp.broadcast_to(inv_scale, scale_ref.shape)


def norm_back(grad_out, normed, inv_scale, gain):
    grad_normed = grad_out * gain
    centered = grad_normed - jnp.mean(grad_normed, -1, keepdims=True)
    return inv_scale * (centered - normed * jnp.mean(grad_normed * normed, -1, keepdims=True))


def ffn_phase(
    normed_ref, scale_ref, gain_one_ref, shift_one_ref, up_ref, b_up_ref, down_ref, b_down_ref,
    gain_two_ref, shift_two_ref, cot_ref, layer_ref, first_ref, low_ref, vec_ref, gup_ref, gdown_ref,
    gbias_ref, act_ref, slope_ref, acc_ref,
):
    shards = up_ref.shape[0]
    normed_one = normed_ref[...]
    hidden_one = normed_one * gain_one_ref[...] + shift_one_ref[...]
    hidden = hidden_one.astype(BF16)
    acc_ref[...] = hidden_one + b_down_ref[...].astype(F32)

    @pl.loop(0, shards)
    def _(shard):
        pre = nn(hidden, up_ref[shard]) + b_up_ref[shard, 0:1, :].astype(F32)
        phi = 0.5 * (1.0 + lax.erf(pre * ROOT_HALF))
        act = (pre * phi).astype(BF16)
        act_ref[shard] = act
        slope_ref[shard] = (phi + pre * INV_ROOT_TAU * jnp.exp(-0.5 * pre * pre)).astype(BF16)
        acc_ref[...] += nt(act, down_ref[shard])

    normed_two, scale_two = norm_parts(acc_ref[...])
    layer_ref[...] = (normed_two * gain_two_ref[...] + shift_two_ref[...]).astype(BF16)
    cot = cot_ref[...].astype(F32)
    grad_second = norm_back(cot, normed_two, scale_two, gain_two_ref[...])
    grad_ffn = grad_second.astype(BF16)
    vec_ref[0:1, :] = jnp.sum(cot * normed_two, 0, keepdims=True)
    vec_ref[1:2, :] = jnp.sum(cot, 0, keepdims=True)
    vec_ref[2:3, :] = jnp.sum(grad_ffn.astype(F32), 0, keepdims=True)
    acc_ref[...] = grad_second
    grad_turned = grad_ffn.T
    hidden_turned = hidden.T

    @pl.loop(0, shards)
    def _(shard):
        grad_act = nn(grad_ffn, down_ref[shard])
        grad_pre = (grad_act * slope_ref[shard].astype(F32)).astype(BF16)
        gdown_ref[shard] = nn(grad_turned, act_ref[shard]).astype(BF16)
        gup_ref[shard] = nn(hidden_turned, grad_pre).astype(BF16)
        gbias_ref[shard] = jnp.broadcast_to(
            jnp.sum(grad_pre.astype(F32), 0, keepdims=True), gbias_ref.shape[1:]
        )
        acc_ref[...] += nt(grad_pre, up_ref[shard])

    grad_hidden = acc_ref[...]
    grad_first = norm_back(grad_hidden, normed_one, scale_ref[:, 0:1], gain_one_ref[...])
    grad_low = grad_first.astype(BF16)
    first_ref[...] = grad_first
    low_ref[...] = grad_low
    vec_ref[3:4, :] = jnp.sum(grad_hidden * normed_one, 0, keepdims=True)
    vec_ref[4:5, :] = jnp.sum(grad_hidden, 0, keepdims=True)
    vec_ref[5:6, :] = jnp.sum(grad_low.astype(F32), 0, keepdims=True)
    vec_ref[6:8, :] = jnp.zeros((2, vec_ref.shape[1]), F32)


def out_back_phase(
    glow_ref, w_ref, low_ref, out_ref, denom_ref, qf_ref, gnum_ref, gden_ref, gw_ref, dnum_ref,
    dden_ref, total_ref, pairs, head_dim,
):
    rows_all = glow_ref.shape[0]
    blocks = rows_all // WINDOW
    half = LANES // 2
    ones = block_ones(LANES, head_dim).astype(BF16)
    grad_low = glow_ref[...]
    gw_ref[...] = tn(low_ref[...], grad_low).astype(gw_ref.dtype)
    for pair in range(pairs):
        cols = slice(pair * LANES, (pair + 1) * LANES)
        grad_attn = nt(grad_low, w_ref[cols, :])
        inverse = 1.0 / denom_ref[:, cols]
        grad_num = (grad_attn * inverse).astype(BF16)
        grad_den = -head_sums(grad_num.astype(F32) * out_ref[:, cols], ones)
        gnum_ref[:, cols] = grad_num
        gden_ref[:, cols] = grad_den
        total = jnp.zeros((half, LANES), F32)
        total_den = jnp.zeros((1, LANES), F32)
        for block in range(blocks):
            rows = slice(block * WINDOW, (block + 1) * WINDOW)
            query = qf_ref[rows, cols]
            num = compact(tn(query, grad_num[rows]))
            den = jnp.sum(query.astype(F32) * grad_den[rows], 0, keepdims=True)
            dnum_ref[pair * blocks + block] = num
            dden_ref[pair * blocks + block : pair * blocks + block + 1, :] = den
            total = total + num
            total_den = total_den + den
        total_ref[pair * half : (pair + 1) * half, :] = total
        total_ref[pairs * half + pair : pairs * half + pair + 1, :] = total_den


def row_grads(keys, values, num, den, ones_f32):
    upper, lower = halves(expand(num, ones_f32))
    grad_keys = nt(values, upper) + nt(values, lower) + den
    grad_values = nn(keys, upper) + nn(keys, lower)
    return grad_keys, grad_values


def band_backward_phase(
    qf_ref, ke_ref, ve_ref, line_ref, gnum_ref, gden_ref, dnum_ref, dden_ref, left_ref, right_ref,
    left_den_ref, right_den_ref, gq_ref, gk_ref, gv_ref, gline_ref, coef_grad_ref, start, stop, first_col, head_dim,
):
    blocks = qf_ref.shape[0] // WINDOW

    @pl.loop(start, stop)
    def _(pair):
        ones_f32 = block_ones(LANES, head_dim)
        cols = lanes(pair)
        out = lanes(pair - first_col)
        coef = coef_tile(line_ref, pair)
        left_coef, right_coef = far_coefs(line_ref, pair)
        gk_ref[:, out] = jnp.zeros((gk_ref.shape[0], LANES), F32)
        gv_ref[:, out] = jnp.zeros((gv_ref.shape[0], LANES), F32)
        coef_grad_ref[...] = jnp.zeros(coef_grad_ref.shape, F32)
        left_sum = jnp.zeros((1, LANES), F32)
        right_sum = jnp.zeros((1, LANES), F32)
        for block in range(blocks):
            rows = slice(block * WINDOW, (block + 1) * WINDOW)
            window = slice(block * WINDOW, (block + 3) * WINDOW)
            index = pair * blocks + block
            query = qf_ref[rows, cols]
            keys = ke_ref[window, cols]
            values = ve_ref[window, cols]
            grad_num = gnum_ref[rows, cols]
            grad_den = gden_ref[rows, cols]
            queries = both_heads(query)
            grads = both_heads(grad_num)
            weights = coef * nt(queries, keys)
            den_column = jnp.concatenate(
                [grad_den[:, 0:1], grad_den[:, LANES // 2 : LANES // 2 + 1]], 0
            )
            grad_weights = nt(grads, values) + den_column
            coef_grad_ref[...] += grad_weights * weights
            grad_scores = (coef * grad_weights).astype(BF16)
            gv_ref[window, out] += tn(weights.astype(BF16), grads)
            gk_ref[window, out] += tn(grad_scores, queries)
            grad_query = per_head(nn(grad_scores, keys))
            left, right = left_ref[index], right_ref[index]
            left_den = left_den_ref[pl.ds(index, 1), :]
            right_den = right_den_ref[pl.ds(index, 1), :]
            upper, lower = halves(expand(left_coef * left + right_coef * right, ones_f32))
            den_far = left_coef * left_den + right_coef * right_den
            grad_query = grad_query + nt(grad_num, upper) + nt(grad_num, lower) + grad_den * den_far
            gq_ref[rows, cols] = grad_query
            dnum = dnum_ref[index]
            dden = dden_ref[pl.ds(index, 1), :]
            left_sum = left_sum + jnp.sum(dnum * left, 0, keepdims=True) + dden * left_den
            right_sum = right_sum + jnp.sum(dnum * right, 0, keepdims=True) + dden * right_den
        for edge, block, scale in ((0, 0, left_coef), (blocks + 1, blocks - 1, right_coef)):
            rows = slice(edge * WINDOW, (edge + 1) * WINDOW)
            index = pair * blocks + block
            edge_k, edge_v = row_grads(
                ke_ref[rows, cols],
                ve_ref[rows, cols],
                scale * dnum_ref[index],
                scale * dden_ref[pl.ds(index, 1), :],
                ones_f32,
            )
            gk_ref[rows, out] -= edge_k
            gv_ref[rows, out] -= edge_v
        first = first_half((1, LANES))
        positions = lax.broadcasted_iota(jnp.int32, (1, LINE), 1)
        left_all = left_coef * left_sum
        right_all = right_coef * right_sum
        for head in range(2):
            keep = first if head == 0 else jnp.logical_not(first)
            left_one = jnp.sum(jnp.where(keep, left_all, 0.0), 1, keepdims=True)
            right_one = jnp.sum(jnp.where(keep, right_all, 0.0), 1, keepdims=True)
            line = unskew_sum(coef_grad_ref[head * WINDOW : (head + 1) * WINDOW, :])
            line = line + jnp.where(positions == 0, left_one, 0.0)
            line = line + jnp.where(positions == LINE - 2, right_one, 0.0)
            gline_ref[pl.ds(2 * pair + head, 1), :] = line


def key_back_phase(
    kf_ref, v_ref, line_ref, dnum_ref, dden_ref, past_ref, future_ref, low_in_ref, high_in_ref,
    gk_ref, gv_ref, pairs, start, stop, head_dim,
):
    blocks = kf_ref.shape[0] // WINDOW
    half = LANES // 2

    @pl.loop(start, stop)
    def _(pair):
        ones_f32 = block_ones(LANES, head_dim)
        cols = lanes(pair)
        left_coef, right_coef = far_coefs(line_ref, pair)
        state_rows = pl.ds(pl.multiple_of(pair * half, half), half)
        den_row = pl.ds(pairs * half + pair, 1)
        nums = [dnum_ref[pair * blocks + block] for block in range(blocks)]
        dens = [dden_ref[pl.ds(pair * blocks + block, 1), :] for block in range(blocks)]
        for block in range(blocks):
            num_left, den_left = future_ref[state_rows, :], future_ref[den_row, :]
            num_right, den_right = past_ref[state_rows, :], past_ref[den_row, :]
            for other in range(blocks):
                if other >= block + 2:
                    num_left, den_left = num_left + nums[other], den_left + dens[other]
                if other <= block - 2:
                    num_right, den_right = num_right + nums[other], den_right + dens[other]
            rows = slice(block * WINDOW, (block + 1) * WINDOW)
            outer = slice((block + 1) * WINDOW, (block + 2) * WINDOW)
            far_k, far_v = row_grads(
                kf_ref[rows, cols],
                v_ref[rows, cols],
                left_coef * num_left + right_coef * num_right,
                left_coef * den_left + right_coef * den_right,
                ones_f32,
            )
            if block == 0:
                far_k = far_k + low_in_ref[0, :, cols].astype(F32)
                far_v = far_v + low_in_ref[1, :, cols].astype(F32)
            if block == blocks - 1:
                far_k = far_k + high_in_ref[0, :, cols].astype(F32)
                far_v = far_v + high_in_ref[1, :, cols].astype(F32)
            gk_ref[outer, cols] += far_k
            gv_ref[outer, cols] += far_v


def qkv_back_phase(
    turned_ref, w_ref, omega_ref, q_ref, k_ref, qf_ref, kf_ref, gq_ref, gk_ref, gv_ref, gtok_ref, parts_ref,
    small_ref, group, head_dim,
):
    width, rows_all = turned_ref.shape
    own = slice(WINDOW, WINDOW + rows_all)
    ones = block_ones(CHUNK, head_dim).astype(BF16)
    factor = head_dim ** (-0.25) / SPREAD
    cols = slice(group * CHUNK, (group + 1) * CHUNK)
    omega = omega_ref[group]
    lows = []
    total = gtok_ref[...]
    for part, low_ref, feat_ref, grad in (
        (0, q_ref, qf_ref, gq_ref[:, cols]), (1, k_ref, kf_ref, gk_ref[own, cols]), (2, None, None, gv_ref[own, cols]),
    ):
        if part < 2:
            inner_up, inner_low = halves(grad * feat_ref[:, cols].astype(F32))
            projected = (nt(inner_up, omega) + nt(inner_low, omega)) * factor
            sums = nn(inner_up, ones) + nn(inner_low, ones)
            grad = projected - sums * head_dim ** (-0.5) * low_ref[:, cols].astype(F32)
        low = grad.astype(BF16)
        lows.append(low)
        total = total + nt(low, w_ref[:, part * width + group * CHUNK : part * width + (group + 1) * CHUNK])
    gtok_ref[...] = total
    joined = jnp.concatenate(lows, 1)
    small_ref[8 + group : 9 + group, :] = jnp.sum(joined.astype(F32), 0, keepdims=True)
    parts_ref[:, (group + 1) * width : (group + 2) * width] = nn(turned_ref[...], joined).astype(parts_ref.dtype)


def table_phase(gline_ref, bucket_ref, buckets):
    one_hot = jnp.where(
        lax.broadcasted_iota(jnp.int32, (buckets, LINE), 0) == bucket_ref[...].astype(jnp.int32), 1.0, 0.0
    )
    return lax.dot_general(
        gline_ref[...],
        one_hot,
        (((1,), (1,)), ((), ())),
        precision=lax.Precision.HIGHEST,
        preferred_element_type=F32,
    )


MESH = pl.DeviceIdType.MESH


def guarded(when, action):
    if when is None:
        action()
    else:
        pl.when(when)(action)


class Place:
    def __init__(self, shards):
        self.row, self.seq = lax.axis_index("row"), lax.axis_index("seq")
        self.count_b = 2
        self.count_a = shards // self.count_b
        self.shards = shards
        self.x, self.core = self.row // 2, self.row % 2
        self.a, self.b = self.seq // self.count_b, self.seq % self.count_b
        self.is_first, self.is_last = self.seq == 0, self.seq == shards - 1
        self.not_first, self.not_last = self.seq > 0, self.seq < shards - 1

    def at(self, x=None, core=None, a=None, b=None):
        x = self.x if x is None else x
        core = self.core if core is None else core
        a = self.a if a is None else a
        b = self.b if b is None else b
        return (x * 2 + core, a * self.count_b + b)

    def beside(self, seq):
        return (self.row, seq)

    def shard(self, offset):
        return lax.rem(self.a + offset, self.count_a)

    def nearest(self, step):
        orders = []
        for a in range(self.count_a):
            orders.append(sorted(range(self.count_a), key=lambda other: (abs(other - a), other)))
        index = jnp.int32(orders[0][step])
        for a in range(1, self.count_a):
            index = jnp.where(self.a == a, orders[a][step], index)
        return index


class Sends:
    def __init__(self):
        self.started = []

    def send(self, src, dst, send_sem, recv_sem, device, when=None):
        copy = pltpu.make_async_remote_copy(
            src_ref=src, dst_ref=dst, send_sem=send_sem, recv_sem=recv_sem, device_id=device,
            device_id_type=MESH,
        )
        guarded(when, copy.start)
        self.started.append((when, copy))

    def drain(self):
        for when, copy in self.started:
            guarded(when, copy.wait_send)
        self.started = []


def arrive(dst, sem, device, when=None):
    copy = pltpu.make_async_remote_copy(
        src_ref=dst, dst_ref=dst, send_sem=sem, recv_sem=sem, device_id=device, device_id_type=MESH
    )
    guarded(when, copy.wait_recv)


class WeightGather:
    def __init__(self, place, sends, mats, middle, sems):
        self.place, self.sends, self.mats, self.mid = place, sends, mats, middle
        self.z_send, self.z_recv, self.y_send, self.y_recv, self.x_send, self.x_recv, self.c_send, self.c_recv = sems
        self.side = (mats.shape[3] - middle) // 2

    def outer(self, a, b, x, core=None):
        core = self.place.core if core is None else core
        start = pl.multiple_of(x * (self.side + self.mid), 16)
        return self.mats.at[core, a, b, pl.ds(start, self.side), :]

    def both(self, a, b, core=None):
        core = self.place.core if core is None else core
        kinds = [(0, self.outer(a, b, self.place.x, core))]
        if self.mid:
            kinds.append((1, self.mats.at[core, a, b, pl.ds(self.side, self.mid), :]))
        return kinds

    def column(self, column):
        return 1 - self.place.b if column else self.place.b

    def rounds(self, step):
        p = self.place
        if step == 0:
            return [(p.a, None, (1, -1))]
        last = p.count_a - 1
        return [
            (jnp.maximum(p.a - step, 0), p.a - step >= 0, (1,)),
            (jnp.minimum(p.a + step, last), p.a + step <= last, (-1,)),
        ]

    def along_a(self, step, wanted):
        p = self.place
        for a, there, moves in self.rounds(step):
            for kind, here in self.both(a, p.b):
                if kind not in wanted:
                    continue
                if step > 0:
                    arrive(here, self.z_recv.at[kind, a], p.at(), there)
                for move in moves:
                    target = p.a + move
                    ok = target <= p.count_a - 1 if move > 0 else target >= 0
                    if there is not None:
                        ok = jnp.logical_and(ok, there)
                    self.sends.send(
                        here, here, self.z_send.at[(1 - move) // 2, kind, a], self.z_recv.at[kind, a],
                        p.at(a=jnp.clip(target, 0, p.count_a - 1)), ok,
                    )
                if step > 0:
                    self.pass_on(kind, 0, a, here, there)

    def across(self, step):
        p = self.place
        for a, there, _ in self.rounds(step):
            for kind, here in self.both(a, p.b):
                self.sends.send(
                    here, here, self.y_send.at[kind, a], self.y_recv.at[kind, a], p.at(b=1 - p.b), there
                )

    def pass_on(self, kind, column, a, here, when=None):
        p = self.place
        if kind == 0:
            self.sends.send(
                here, here, self.x_send.at[column, a], self.x_recv.at[column, a], p.at(x=1 - p.x), when
            )
        self.sends.send(
            here, here, self.c_send.at[kind, column, a], self.c_recv.at[kind, column, a], p.at(core=1 - p.core), when
        )

    def along_b(self, step, wanted):
        p = self.place
        a = p.nearest(step)
        for kind, here in self.both(a, 1 - p.b):
            if kind in wanted:
                arrive(here, self.y_recv.at[kind, a], p.at())
                self.pass_on(kind, 1, a, here)

    def along_x(self, step, column):
        p = self.place
        a = p.nearest(step)
        here = self.outer(a, self.column(column), 1 - p.x)
        arrive(here, self.x_recv.at[column, a], p.at())
        self.sends.send(
            here, here, self.c_send.at[2, column, a], self.c_recv.at[2, column, a], p.at(core=1 - p.core)
        )

    def finish(self, step, column):
        p = self.place
        a = p.nearest(step)
        other, b = 1 - p.core, self.column(column)
        for kind, here in self.both(a, b, other) + [(2, self.outer(a, b, 1 - p.x, other))]:
            arrive(here, self.c_recv.at[kind, column, a], p.at())


def gather_sems(count_a):
    dma = pltpu.SemaphoreType.DMA
    return [
        dma((2, 2, count_a)), dma((2, count_a)), dma((2, count_a)), dma((2, count_a)),
        dma((2, count_a)), dma((2, count_a)), dma((3, 2, count_a)), dma((3, 2, count_a)),
    ]


class StateSums:
    def __init__(self, place, sends, buffers, sems):
        self.place, self.sends = place, sends
        self.own, self.peer, self.pair, self.far, self.sums, self.land = buffers
        self.y_send, self.y_recv, self.z_send, self.z_recv = sems
        self.half = self.pair.shape[0]

    def rows(self, b):
        return pl.ds(pl.multiple_of(b * self.half, 16), self.half)

    def start(self, message_ref):
        p = self.place
        self.own[...] = message_ref[...].astype(BF16)
        self.sends.send(self.own, self.peer, self.y_send.at[0], self.y_recv.at[0], p.at(b=1 - p.b))

    def along_a(self):
        p = self.place
        arrive(self.peer, self.y_recv.at[0], p.at())
        mine = self.rows(p.b)
        self.pair[...] = (self.own[mine, :].astype(F32) + self.peer[mine, :].astype(F32)).astype(BF16)
        for offset in range(1, p.count_a):
            self.sends.send(
                self.pair, self.far.at[p.a], self.z_send.at[offset], self.z_recv.at[offset],
                p.at(a=p.shard(offset)),
            )

    def along_b(self):
        p = self.place
        self.far[p.a] = jnp.zeros(self.pair.shape, BF16)
        for offset in range(1, p.count_a):
            source = p.shard(p.count_a - offset)
            arrive(self.far.at[source], self.z_recv.at[offset], p.at())
        for index in range(2):
            total = jnp.zeros(self.pair.shape, F32)
            for a in range(p.count_a):
                keep = a < p.a if index == 0 else a > p.a
                total = total + jnp.where(keep, 1.0, 0.0) * self.far[a].astype(F32)
            self.sums[index] = total.astype(BF16)
        self.sends.send(self.sums, self.land, self.y_send.at[1], self.y_recv.at[1], p.at(b=1 - p.b))

    def finish(self, before_ref, after_ref):
        p = self.place
        arrive(self.land, self.y_recv.at[1], p.at())
        for index, ref in ((0, before_ref), (1, after_ref)):
            ref[self.rows(p.b), :] = self.sums[index].astype(F32)
            ref[self.rows(1 - p.b), :] = self.land[index].astype(F32)
        peer = self.peer[...].astype(F32)
        before_ref[...] += jnp.where(p.b == 1, 1.0, 0.0) * peer
        after_ref[...] += jnp.where(p.b == 0, 1.0, 0.0) * peer


def sums_sems(count_a):
    dma = pltpu.SemaphoreType.DMA
    return [dma((2,)), dma((2,)), dma((count_a,)), dma((count_a,))]


class GradScatter:
    def __init__(self, place, sends, grads, total, middle, lands, sems):
        self.place, self.sends, self.grads, self.total, self.mid = place, sends, grads, total, middle
        self.core_land, self.stage, self.x_land, self.y_land, self.z_land, self.last_land = lands
        (self.copy, self.c_send, self.c_recv, self.x_send, self.x_recv, self.y_send, self.y_recv, self.z_send,
         self.z_recv, self.l_send, self.l_recv) = sems
        self.side = (grads.shape[3] - middle) // 2

    def outer(self, x):
        return pl.ds(pl.multiple_of(x * (self.side + self.mid), 16), self.side)

    def window(self):
        return pl.ds(pl.multiple_of(self.place.x * self.side, 16), self.side + self.mid)

    def column(self, column):
        return 1 - self.place.b if column else self.place.b

    def start(self, offset, column):
        p = self.place
        item = (offset, column)
        self.sends.send(
            self.grads.at[1 - p.core, p.shard(offset), self.column(column)], self.core_land.at[item],
            self.c_send.at[item], self.c_recv.at[item], p.at(core=1 - p.core),
        )

    def add(self, ref, land):
        ref[...] = (ref[...].astype(F32) + land[...].astype(F32)).astype(BF16)

    def staged(self, offset, column):
        item = (offset, column)
        return pltpu.make_async_copy(self.core_land.at[item], self.stage.at[1 - column], self.copy.at[item])

    def fetch(self, offset, column):
        item = (offset, column)
        arrive(self.core_land.at[item], self.c_recv.at[item], self.place.at())
        self.staged(offset, column).start()

    def chip(self, offset, column):
        p = self.place
        item = (offset, column)
        self.staged(offset, column).wait()
        here = self.grads.at[p.core, p.shard(offset), self.column(column)]
        self.add(here, self.stage.at[1 - column])
        self.sends.send(
            here.at[self.outer(1 - p.x), :], self.x_land.at[item], self.x_send.at[item], self.x_recv.at[item],
            p.at(x=1 - p.x),
        )

    def along_x(self, offset, column):
        p = self.place
        item = (offset, column)
        here = self.grads.at[p.core, p.shard(offset), self.column(column)]
        arrive(self.x_land.at[item], self.x_recv.at[item], p.at())
        self.add(here.at[self.outer(p.x), :], self.x_land.at[item])
        if column:
            self.sends.send(
                here.at[self.window(), :], self.y_land.at[offset], self.y_send.at[offset], self.y_recv.at[offset],
                p.at(b=1 - p.b),
            )

    def along_b(self, offset):
        p = self.place
        a = p.shard(offset)
        arrive(self.y_land.at[offset], self.y_recv.at[offset], p.at())
        mine = self.grads.at[p.core, a, p.b, self.window(), :]
        self.add(mine, self.y_land.at[offset])
        if offset:
            self.sends.send(
                mine, self.z_land.at[offset - 1], self.z_send.at[offset], self.z_recv.at[offset], p.at(a=a)
            )

    def along_a(self):
        p = self.place
        own = self.grads.at[p.core, p.a, p.b]
        mine = own.at[self.window(), :]
        total = mine[...].astype(F32)
        for offset in range(1, p.count_a):
            arrive(self.z_land.at[offset - 1], self.z_recv.at[offset], p.at())
            total = total + self.z_land[offset - 1].astype(F32)
        mine[...] = total.astype(BF16)
        middle = pl.ds(self.side, self.mid)
        outer = self.outer(p.x)
        self.total[p.core, outer, :] = self.grads[p.core, p.a, p.b, outer, :]
        self.sends.send(
            own.at[middle, :], self.last_land, self.l_send.at[0], self.l_recv.at[0], p.at(x=1 - p.x)
        )
        here = self.total.at[p.core, outer, :]
        self.sends.send(here, here, self.l_send.at[1], self.l_recv.at[1], p.at(x=1 - p.x))

    def last_x(self):
        p = self.place
        middle = pl.ds(self.side, self.mid)
        arrive(self.last_land, self.l_recv.at[0], p.at())
        self.total[p.core, middle, :] = (
            self.grads[p.core, p.a, p.b, middle, :].astype(F32) + self.last_land[...].astype(F32)
        ).astype(BF16)
        arrive(self.total.at[p.core, self.outer(1 - p.x), :], self.l_recv.at[1], p.at())
        here = self.total.at[p.core]
        self.sends.send(here, here, self.l_send.at[2], self.l_recv.at[2], p.at(core=1 - p.core))

    def finish(self):
        arrive(self.total.at[1 - self.place.core], self.l_recv.at[2], self.place.at())


def scatter_sems(count_a):
    dma = pltpu.SemaphoreType.DMA
    return [dma((count_a, 2)) for _ in range(5)] + [dma((count_a,)) for _ in range(4)] + [dma((3,)), dma((3,))]


class AllReduce:
    def __init__(self, place, sends, parts, result, lands, done, orders, sems):
        self.place, self.sends, self.parts, self.result = place, sends, parts, result
        self.core_land, self.staged, self.one_land, self.two_land, self.a_land = lands
        self.done, self.orders = done, orders
        (self.s_send, self.s_recv, self.z_send, self.z_recv, self.g_send, self.g_recv, self.zg_send, self.zg_recv,
         self.copy) = sems
        self.half = result.shape[1] // 2
        self.quarter = self.half // 2
        self.slim = self.quarter // place.count_a

    def ways(self, index):
        p = self.place
        other_x, other_b = p.at(x=1 - p.x), p.at(b=1 - p.b)
        straight = {"x": True, "b": False}.get(self.orders[index], p.core == 0)
        one = tuple(jnp.where(straight, u, w) for u, w in zip(other_x, other_b))
        two = tuple(jnp.where(straight, w, u) for u, w in zip(other_x, other_b))
        return jnp.where(straight, p.x, p.b), jnp.where(straight, p.b, p.x), one, two

    def half_rows(self, core):
        return pl.ds(pl.multiple_of(core * self.half, self.half), self.half)

    def quarter_rows(self, one):
        start = self.place.core * self.half + one * self.quarter
        return pl.ds(pl.multiple_of(start, self.quarter), self.quarter)

    def slim_rows(self, one, a):
        start = self.place.core * self.half + one * self.quarter + a * self.slim
        return pl.ds(pl.multiple_of(start, self.slim), self.slim)

    def push(self, index):
        p = self.place
        blocks = pl.ds(2 * index, 2)
        self.sends.send(
            self.parts.at[blocks, self.half_rows(1 - p.core), :], self.core_land.at[blocks],
            self.s_send.at[0, index], self.s_recv.at[0, index], p.at(core=1 - p.core),
        )

    def add(self, ref, land):
        ref[...] = (ref[...].astype(F32) + land[...].astype(F32)).astype(BF16)

    def stage(self, index, number):
        p = self.place
        one, two, one_device, two_device = self.ways(index)
        blocks = pl.ds(2 * index, 2)
        mine, other = 2 * index + two, 2 * index + 1 - two
        parts, result = self.parts, self.result
        if number == 0:
            land = self.core_land.at[blocks]
            arrive(land, self.s_recv.at[0, index], p.at())
            pltpu.make_async_copy(land, self.staged, self.copy.at[index]).start()
        elif number == 1:
            pltpu.make_async_copy(self.core_land.at[blocks], self.staged, self.copy.at[index]).wait()
            self.add(parts.at[blocks, self.half_rows(p.core), :], self.staged)
            self.sends.send(
                parts.at[blocks, self.quarter_rows(1 - one), :], self.one_land.at[blocks],
                self.s_send.at[1, index], self.s_recv.at[1, index], one_device,
            )
        elif number == 2:
            land = self.one_land.at[blocks]
            arrive(land, self.s_recv.at[1, index], p.at())
            self.add(parts.at[blocks, self.quarter_rows(one), :], land)
            self.sends.send(
                parts.at[other, self.quarter_rows(one), :], self.two_land.at[index],
                self.s_send.at[2, index], self.s_recv.at[2, index], two_device,
            )
        elif number == 3:
            land = self.two_land.at[index]
            arrive(land, self.s_recv.at[2, index], p.at())
            self.add(parts.at[mine, self.quarter_rows(one), :], land)
            for offset in range(1, p.count_a):
                a = p.shard(offset)
                self.sends.send(
                    parts.at[mine, self.slim_rows(one, a), :], self.a_land.at[index, offset - 1],
                    self.z_send.at[index, offset], self.z_recv.at[index, offset], p.at(a=a),
                )
        elif number == 4:
            rows = self.slim_rows(one, p.a)
            total = parts[mine, rows, :].astype(F32)
            for offset in range(1, p.count_a):
                arrive(self.a_land.at[index, offset - 1], self.z_recv.at[index, offset], p.at())
                total = total + self.a_land[index, offset - 1].astype(F32)
            self.done[index] = total.astype(BF16)
            here = result.at[mine, rows, :]
            pltpu.make_async_copy(self.done.at[index], here, self.copy.at[index]).start()
            for offset in range(1, p.count_a):
                self.sends.send(
                    self.done.at[index], here, self.zg_send.at[index, offset], self.zg_recv.at[index, offset],
                    p.at(a=p.shard(offset)),
                )
        elif number == 5:
            pltpu.make_async_copy(
                self.done.at[index], result.at[mine, self.slim_rows(one, p.a), :], self.copy.at[index]
            ).wait()
            for offset in range(1, p.count_a):
                a = lax.rem(p.a + p.count_a - offset, p.count_a)
                arrive(result.at[mine, self.slim_rows(one, a), :], self.zg_recv.at[index, offset], p.at())
            here = result.at[mine, self.quarter_rows(one), :]
            self.sends.send(here, here, self.g_send.at[0, index], self.g_recv.at[0, index], two_device)
        elif number == 6:
            arrive(result.at[other, self.quarter_rows(one), :], self.g_recv.at[0, index], p.at())
            here = result.at[blocks, self.quarter_rows(one), :]
            self.sends.send(here, here, self.g_send.at[1, index], self.g_recv.at[1, index], one_device)
        elif number == 7:
            arrive(result.at[blocks, self.quarter_rows(1 - one), :], self.g_recv.at[1, index], p.at())
            here = result.at[blocks, self.half_rows(p.core), :]
            self.sends.send(here, here, self.g_send.at[2, index], self.g_recv.at[2, index], p.at(core=1 - p.core))
        elif number == 8:
            arrive(result.at[blocks, self.half_rows(1 - p.core), :], self.g_recv.at[2, index], p.at())


def reduce_sems(chunks, count_a):
    dma = pltpu.SemaphoreType.DMA
    return [
        dma((3, chunks)), dma((3, chunks)), dma((chunks, count_a)), dma((chunks, count_a)),
        dma((3, chunks)), dma((3, chunks)), dma((chunks, count_a)), dma((chunks, count_a)), dma((chunks,)),
    ]


class SmallReduce:
    def __init__(self, place, sends, held, land, sems):
        self.place, self.sends, self.held, self.land = place, sends, held, land
        self.out_sem, self.in_sem = sems
        p = place
        self.devices = [p.at(core=1 - p.core), p.at(x=1 - p.x), p.at(b=1 - p.b)]

    def send(self, step):
        if step < 3:
            self.sends.send(
                self.held.at[step], self.land.at[step], self.out_sem.at[step], self.in_sem.at[step],
                self.devices[step],
            )
            return
        p = self.place
        for offset in range(1, p.count_a):
            self.sends.send(
                self.held.at[3], self.land.at[3 + offset], self.out_sem.at[3 + offset],
                self.in_sem.at[3 + offset], p.at(a=p.shard(offset)),
            )

    def receive(self, step):
        p = self.place
        if step < 3:
            arrive(self.land.at[step], self.in_sem.at[step], p.at())
            self.held[step + 1] = self.held[step] + self.land[step]
            return
        for offset in range(1, p.count_a):
            arrive(self.land.at[3 + offset], self.in_sem.at[3 + offset], p.at())
        self.land[3] = self.held[3]

    def total(self):
        p = self.place
        total = self.land[3 + lax.rem(p.a, p.count_a)]
        for a in range(1, p.count_a):
            total = total + self.land[3 + lax.rem(p.a + p.count_a - a, p.count_a)]
        return total


def halo_phase(x_ref, w_ref, b_ref, omega_ref, k_ref, kv_ref, place, head_dim):
    rows_ext, width = x_ref.shape
    low, high = slice(0, WINDOW), slice(rows_ext - WINDOW, rows_ext)
    x = jnp.concatenate([x_ref[low, :], x_ref[high, :]], 0)
    ones = block_ones(CHUNK, head_dim).astype(BF16)
    factor = head_dim ** (-0.25) / SPREAD
    row = lax.broadcasted_iota(jnp.int32, (2 * WINDOW, 1), 0)
    inside = jnp.logical_or(
        jnp.logical_and(row < WINDOW, place.seq > 0),
        jnp.logical_and(row >= WINDOW, place.seq < place.shards - 1),
    )
    for part in (1, 2):
        for chunk in range(width // CHUNK):
            cols = slice(chunk * CHUNK, (chunk + 1) * CHUNK)
            wide = slice(part * width + chunk * CHUNK, part * width + (chunk + 1) * CHUNK)
            value = (nn(x, w_ref[:, wide]) + b_ref[part][:, cols]).astype(BF16)
            if part == 1:
                k_ref[low, cols], k_ref[high, cols] = value[:WINDOW], value[WINDOW:]
                widened = value.astype(F32)
                half_norm = head_sums(widened * widened, ones) * (0.5 * head_dim ** (-0.5))
                value = jnp.exp(nn(value, omega_ref[chunk]) * factor - half_norm) * head_dim ** (-0.5)
            value = jnp.where(inside, value.astype(F32), 0.0).astype(BF16)
            kv_ref[part - 1, low, cols], kv_ref[part - 1, high, cols] = value[:WINDOW], value[WINDOW:]


def ffn_forward_shard(hidden_ref, mats, a, b, shard, bias_ref, pool, acc_ref):
    rows = hidden_ref.shape[0]
    pre = nn(hidden_ref[...], mats[0, a, b]) + bias_ref[shard, 0:1, :]
    phi = 0.5 * (1.0 + lax.erf(pre * ROOT_HALF))
    act = (pre * phi).astype(BF16)
    pool[shard, 0:rows, :] = act
    pool[shard, rows : 2 * rows, :] = (phi + pre * INV_ROOT_TAU * jnp.exp(-0.5 * pre * pre)).astype(BF16)
    acc_ref[...] += nt(act, mats[1, a, b])


def ffn_backward_shard(grad_ref, grad_turned_ref, hidden_turned_ref, mats, a, b, shard, pool, acc_ref, gbias_ref):
    rows = grad_ref.shape[0]
    grad_act = nn(grad_ref[...], mats[1, a, b])
    grad_pre = (grad_act * pool[shard, rows : 2 * rows, :].astype(F32)).astype(BF16)
    gbias_ref[shard] = jnp.broadcast_to(
        jnp.sum(grad_pre.astype(F32), 0, keepdims=True), gbias_ref.shape[1:]
    )
    acc_ref[...] += nt(grad_pre, mats[0, a, b])
    mats[1, a, b] = nn(grad_turned_ref[...], pool[shard, 0:rows, :]).astype(BF16)
    mats[0, a, b] = nn(hidden_turned_ref[...], grad_pre).astype(BF16)


def row_blocks(rows, body, size=CHUNK):
    @pl.loop(0, rows // size)
    def _(index):
        body(pl.ds(pl.multiple_of(index * size, size), size))


def hidden_phase(
    x_ref, low_ref, w_ref, b_ref, gain_ref, shift_ref, b_down_ref, normed_refs, scale_ref, hidden_ref, turned_ref, acc_ref
):
    def body(rows):
        first_sum = x_ref[rows, :].astype(F32) + nn(low_ref[rows, :], w_ref[...]) + b_ref[...].astype(F32)
        normed, inv_scale = norm_parts(first_sum)
        normed_refs[0][rows, :], normed_refs[1][rows, :], normed_refs[2][rows, :] = jnp.split(normed, 3, 1)
        scale_ref[rows, :] = jnp.broadcast_to(inv_scale, (first_sum.shape[0], scale_ref.shape[1]))
        hidden_one = normed * gain_ref[...] + shift_ref[...]
        hidden = hidden_one.astype(BF16)
        hidden_ref[rows, :] = hidden
        turned_ref[:, rows] = hidden.T
        acc_ref[rows, :] = hidden_one + b_down_ref[...].astype(F32)

    row_blocks(x_ref.shape[0], body)


def middle_phase(acc_ref, cot_ref, gain_two_ref, shift_two_ref, grad_ref, grad_turned_ref, vec_ref):
    def body(rows):
        normed_two, scale_two = norm_parts(acc_ref[rows, :])
        cot = cot_ref[rows, :].astype(F32)
        cot_ref[rows, :] = (normed_two * gain_two_ref[...] + shift_two_ref[...]).astype(BF16)
        grad_second = norm_back(cot, normed_two, scale_two, gain_two_ref[...])
        grad_ffn = grad_second.astype(BF16)
        vec_ref[0:1, :] += jnp.sum(cot * normed_two, 0, keepdims=True)
        vec_ref[1:2, :] += jnp.sum(cot, 0, keepdims=True)
        vec_ref[2:3, :] += jnp.sum(grad_ffn.astype(F32), 0, keepdims=True)
        acc_ref[rows, :] = grad_second
        grad_ref[rows, :] = grad_ffn
        grad_turned_ref[:, rows] = grad_ffn.T

    row_blocks(cot_ref.shape[0], body)


def first_back_phase(acc_ref, normed_refs, scale_ref, gain_one_ref, low_ref, vec_ref):
    def body(rows):
        grad_hidden = acc_ref[rows, :]
        normed = jnp.concatenate([ref[rows, :] for ref in normed_refs], 1)
        grad_first = norm_back(grad_hidden, normed, scale_ref[rows, 0:1], gain_one_ref[...])
        grad_low = grad_first.astype(BF16)
        acc_ref[rows, :] = grad_first
        low_ref[rows, :] = grad_low
        vec_ref[3:4, :] += jnp.sum(grad_hidden * normed, 0, keepdims=True)
        vec_ref[4:5, :] += jnp.sum(grad_hidden, 0, keepdims=True)
        vec_ref[5:6, :] += jnp.sum(grad_low.astype(F32), 0, keepdims=True)

    row_blocks(low_ref.shape[0], body)


def attn_back_phase(glow_ref, w_ref, out_ref, denom_ref, low_ref, qf_ref, dnum_ref, dden_ref, total_ref, pairs, head_dim):
    rows_all = glow_ref.shape[0]
    blocks = rows_all // WINDOW
    half = LANES // 2
    ones = block_ones(CHUNK, head_dim).astype(BF16)
    grad_low = glow_ref[...]
    per_chunk = CHUNK // LANES
    for chunk in range(pairs // per_chunk):
        wide = slice(chunk * CHUNK, (chunk + 1) * CHUNK)
        grad_attn = nt(grad_low, w_ref[wide, :])
        grad_num = (grad_attn / denom_ref[:, wide]).astype(BF16)
        low_ref[:, wide] = grad_num
        denom_ref[:, wide] = -head_sums(grad_num.astype(F32) * out_ref[:, wide], ones)
        for pair in range(chunk * per_chunk, (chunk + 1) * per_chunk):
            cols = slice(pair * LANES, (pair + 1) * LANES)
            total = jnp.zeros((half, LANES), F32)
            total_den = jnp.zeros((1, LANES), F32)
            for block in range(blocks):
                rows = slice(block * WINDOW, (block + 1) * WINDOW)
                query = qf_ref[rows, cols]
                num = compact(tn(query, low_ref[rows, cols]))
                den = jnp.sum(query.astype(F32) * denom_ref[rows, cols], 0, keepdims=True)
                dnum_ref[pair * blocks + block] = num
                dden_ref[pair * blocks + block : pair * blocks + block + 1, :] = den
                total = total + num
                total_den = total_den + den
            total_ref[pair * half : (pair + 1) * half, :] = total
            total_ref[pairs * half + pair : pairs * half + pair + 1, :] = total_den


def far_back_phase(ke_ref, ve_ref, line_ref, dnum_ref, dden_ref, past_ref, future_ref, gk_ref, gv_ref, pairs, start, stop, first_col, head_dim):
    blocks = ke_ref.shape[0] // WINDOW - 2
    half = LANES // 2

    @pl.loop(start, stop)
    def _(pair):
        ones_f32 = block_ones(LANES, head_dim)
        cols = lanes(pair)
        out = lanes(pair - first_col)
        left_coef, right_coef = far_coefs(line_ref, pair)
        state_rows = pl.ds(pl.multiple_of(pair * half, half), half)
        den_row = pl.ds(pairs * half + pair, 1)
        nums = [dnum_ref[pair * blocks + block] for block in range(blocks)]
        dens = [dden_ref[pl.ds(pair * blocks + block, 1), :] for block in range(blocks)]
        for block in range(blocks):
            num_left, den_left = future_ref[state_rows, :], future_ref[den_row, :]
            num_right, den_right = past_ref[state_rows, :], past_ref[den_row, :]
            for other in range(blocks):
                if other >= block + 2:
                    num_left, den_left = num_left + nums[other], den_left + dens[other]
                if other <= block - 2:
                    num_right, den_right = num_right + nums[other], den_right + dens[other]
            rows = slice((block + 1) * WINDOW, (block + 2) * WINDOW)
            far_k, far_v = row_grads(
                ke_ref[rows, cols],
                ve_ref[rows, cols],
                left_coef * num_left + right_coef * num_right,
                left_coef * den_left + right_coef * den_right,
                ones_f32,
            )
            gk_ref[rows, out] += far_k
            gv_ref[rows, out] += far_v


def qkv_grad_phase(
    turned_ref, w_ref, omega_ref, q_ref, k_ref, qf_ref, kf_ref, gq_ref, gk_ref, gv_ref, grads_ref, parts, small_ref,
    group, wanted, place, head_dim,
):
    width, rows_ext = turned_ref.shape
    rows_all = rows_ext - 2 * WINDOW
    own = slice(WINDOW, WINDOW + rows_all)
    ones = block_ones(CHUNK, head_dim).astype(BF16)
    factor = head_dim ** (-0.25) / SPREAD
    cols = slice(group * CHUNK, (group + 1) * CHUNK)
    omega = omega_ref[group]
    base = group * 3 * CHUNK
    block = parts.shape[2]
    for part, low_ref, feat_ref in ((0, q_ref, qf_ref), (1, k_ref, kf_ref), (2, None, None)):
        if part not in wanted:
            continue
        out = slice(part * CHUNK, (part + 1) * CHUNK)

        def body(rows):
            if part == 0:
                grad = gq_ref[rows, cols]
            else:
                grad = (gk_ref if part == 1 else gv_ref)[rows, :]
            if part < 2:
                inner_up, inner_low = halves(grad * feat_ref[rows, cols].astype(F32))
                projected = (nt(inner_up, omega) + nt(inner_low, omega)) * factor
                sums = nn(inner_up, ones) + nn(inner_low, ones)
                grad = projected - sums * head_dim ** (-0.5) * low_ref[rows, cols].astype(F32)
            if part > 0:
                row = lax.broadcasted_iota(jnp.int32, (CHUNK, 1), 0) + rows.start
                inside = jnp.logical_and(
                    jnp.logical_or(row >= WINDOW, place.seq > 0),
                    jnp.logical_or(row < rows_ext - WINDOW, place.seq < place.shards - 1),
                )
                grad = jnp.where(inside, grad, 0.0)
            low = grad.astype(BF16)
            if part == 0:
                rows = pl.ds(pl.multiple_of(rows.start + WINDOW, WINDOW), CHUNK)
            grads_ref[rows, out] = low
            small_ref[6 + group : 7 + group, out] += jnp.sum(low.astype(F32), 0, keepdims=True)

        row_blocks(rows_all if part == 0 else rows_ext, body)
        rows = own if part == 0 else slice(0, rows_ext)
        weight = nn(turned_ref[:, rows], grads_ref[rows, out]).astype(BF16)
        start = width + base + part * CHUNK
        done = 0
        while done < CHUNK:
            index, at = (start + done) // block, (start + done) % block
            size = min(CHUNK - done, block - at)
            parts[index, 0:width, at : at + size] = weight[:, done : done + size]
            done += size


def table_grads(gline_ref, bucket_ref, buckets, small_ref):
    heads = gline_ref.shape[0]
    head = lax.broadcasted_iota(jnp.int32, (heads, LANES), 0)
    lane_bucket = lax.broadcasted_iota(jnp.int32, (LANES, LINE), 0)
    total = jnp.zeros((heads, LANES), F32)
    per_row = LANES // buckets
    for place in range(per_row):
        one_hot = jnp.where(lane_bucket - place * buckets == bucket_ref[...].astype(jnp.int32), 1.0, 0.0)
        sums = lax.dot_general(
            gline_ref[...], one_hot, (((1,), (1,)), ((), ())), precision=lax.Precision.HIGHEST,
            preferred_element_type=F32,
        )
        total = total + jnp.where(head % per_row == place, sums, 0.0)
    for index in range(heads // per_row):
        small_ref[13 + index : 14 + index, 0:LANES] = jnp.sum(
            total[index * per_row : (index + 1) * per_row], 0, keepdims=True
        )


def layer_kernel(pairs, head_dim, buckets, shards, *refs):
    x_h, cot_h, up_h, down_h, w_h, codes_r, table_r, wo_h = refs[:8]
    vectors, bias_up_r, buckets_r = refs[8:15], refs[15], refs[16]
    layer_h, gtok_h, total_r, small_r, result_h, core_h, ac_h = refs[17:24]
    (x_r, q_r, k_r, qf_r, kv_r, line_r, num_r, den_r, tot_r, biases, before_r, after_r, left_r, right_r,
     lden_r, rden_r, attn_r, denom_r, low_r, scale_r, hidden_r, turned_r, cot_r, acc_r,
     mats, pool, bias_r, gbias_r, gk_r, gv_r, gline_r, cg_r, gqkv_r) = refs[24:57]
    stage_r, xl_r, yl_r, zl_r, ll_r = refs[57:62]
    ac_r, ao_r, at_r, aa_r, done_r, held_r, land_r = refs[62:69]
    sum_buffers, sum_two_buffers = refs[69:75], refs[75:81]
    sems = refs[81:]
    all_rows = pl.ds(0, q_r.shape[0])
    normed_r = (gk_r.at[0, all_rows], gk_r.at[1, all_rows], gv_r.at[0, all_rows])
    gturned_r = gqkv_r.at[:, all_rows]
    edge_r, tail_r = cot_r.at[pl.ds(0, 2 * WINDOW)], cot_r.at[pl.ds(2 * WINDOW, 2 * WINDOW)]
    w_sems, s_sems, s2_sems, rs_sems = sems[:8], sems[8:12], sems[12:16], sems[16:27]
    ar_sems, sm_sems, bias_sems = sems[27:36], sems[36:38], sems[38:40]
    h_send, h_recv, t_send, t_recv, load_sem, w_r, wo_r, omega_r, packed_r = sems[40:]
    rows, width = q_r.shape
    half = LANES // 2
    line = [packed_r.at[pl.ds(index, 1)] for index in range(packed_r.shape[0])]
    b_r, bo_r, g1_r, s1_r, bdown_r, g2_r, s2_r = line[:3], *line[3:9]
    bup_r, bucket_r = line[9].at[:, pl.ds(0, up_h.shape[1])], line[10].at[:, pl.ds(0, LINE)]
    own = pl.ds(WINDOW, rows)
    place = Place(shards)
    sends = Sends()
    seq = place.seq
    peers = [place.beside(lax.rem(seq + o, shards)) for o in range(1, shards)]
    peers += [place.at(core=1 - place.core), place.at(x=1 - place.x)]
    barrier = pltpu.get_barrier_semaphore()
    for peer in peers:
        pl.semaphore_signal(barrier, inc=1, device_id=peer, device_id_type=MESH)
    loads = [
        pltpu.make_async_copy(src, dst, load_sem.at[i])
        for i, (src, dst) in enumerate((
            (down_h, hidden_r.at[pl.ds(0, down_h.shape[0])]), (up_h, mats.at[0, place.a, place.b]),
            (x_h, x_r.at[own]), (cot_h, cot_r), (w_h, w_r), (wo_h, wo_r),
        ))
    ]
    for load in loads:
        load.start()
    gather = WeightGather(place, sends, mats, width // 4, w_sems)
    key_sums = StateSums(place, sends, sum_buffers, s_sems)
    grad_sums = StateSums(place, sends, sum_two_buffers, s2_sems)
    scatter = GradScatter(place, sends, mats, total_r, ll_r.shape[0], (core_h, stage_r, xl_r, yl_r, zl_r, ll_r), rs_sems)
    chunks = done_r.shape[0]
    reduce = AllReduce(place, sends, pool, result_h, (ac_h, ac_r, ao_r, at_r, aa_r), done_r, "bmmm", ar_sems)
    little = SmallReduce(place, sends, held_r, land_r, sm_sems)
    to_right = place.beside(jnp.minimum(seq + 1, shards - 1))
    to_left = place.beside(jnp.maximum(seq - 1, 0))
    low_edge, high_edge = pl.ds(0, WINDOW), pl.ds(rows + WINDOW, WINDOW)

    small_r[...] = jnp.zeros(small_r.shape, F32)
    acc_r[0:WINDOW, :] = jnp.zeros((WINDOW, width), F32)
    acc_r[rows + WINDOW :, :] = jnp.zeros((WINDOW, width), F32)
    at = 0
    for vector in vectors:
        for start in range(0, vector.shape[0], width):
            packed_r[at, :] = vector[start : start + width].astype(F32)
            at += 1
    packed_r[at, 0 : bias_up_r.shape[0]] = bias_up_r[...].astype(F32)
    middle = (buckets_r.shape[0] + 1) // 2
    packed_r[at + 1, 0:LINE] = buckets_r[middle - LINE // 2 : middle + LINE // 2].astype(F32)
    omega_r[...] = jnp.zeros(omega_r.shape, BF16)
    heads, head_dim = codes_r.shape[:2]
    per_chunk = CHUNK // head_dim
    for head in range(heads):
        at = slice(head % per_chunk * head_dim, (head % per_chunk + 1) * head_dim)
        omega_r[head // per_chunk, at, at] = (codes_r[head].astype(F32) - CENTER).astype(BF16)
    loads[0].wait()
    mats[1, place.a, place.b] = hidden_r[0 : down_h.shape[0], :].T
    loads[1].wait()
    loads[2].wait()
    pl.semaphore_wait(barrier, len(peers))
    sends.send(
        x_r.at[pl.ds(rows, WINDOW)], x_r.at[low_edge], h_send.at[0], h_recv.at[0], to_right, place.not_last
    )
    sends.send(
        x_r.at[pl.ds(WINDOW, WINDOW)], x_r.at[high_edge], h_send.at[1], h_recv.at[1], to_left, place.not_first
    )
    biases[seq] = jnp.broadcast_to(bup_r[...], biases.shape[1:]).astype(BF16)
    for offset in range(1, shards):
        sends.send(
            biases.at[seq], biases.at[seq], bias_sems[0].at[offset], bias_sems[1].at[offset],
            place.beside(lax.rem(seq + offset, shards)),
        )
    gather.along_a(0, (0, 1))

    @pl.when(place.is_first)
    def _():
        x_r[0:WINDOW, :] = jnp.zeros((WINDOW, width), BF16)

    @pl.when(place.is_last)
    def _():
        x_r[rows + WINDOW :, :] = jnp.zeros((WINDOW, width), BF16)

    ke_r, ve_r = kv_r.at[0], kv_r.at[1]
    loads[4].wait()
    loads[5].wait()
    qkv_phase(
        x_r.at[own], w_r, b_r, omega_r, ((1, k_r.at[own], ke_r.at[own]), (2, ve_r.at[own], None)), head_dim
    )
    tot_r[pairs * half :, :] = jnp.zeros((tot_r.shape[0] - pairs * half, LANES), F32)
    state_phase(ke_r.at[own], ve_r.at[own], num_r, den_r, tot_r, pairs)
    key_sums.start(tot_r)
    gather.across(0)
    qkv_phase(x_r.at[own], w_r, b_r, omega_r, ((0, q_r, qf_r),), head_dim)
    line_phase(bucket_r, table_r, line_r)
    arrive(x_r.at[low_edge], h_recv.at[0], place.at(), place.not_first)
    arrive(x_r.at[high_edge], h_recv.at[1], place.at(), place.not_last)
    halo_phase(x_r, w_r, b_r, omega_r, k_r, kv_r, place, head_dim)
    third = pairs // 3

    def ffn(step, column, forward):
        a = place.nearest(step) if forward else place.shard(step)
        b = 1 - place.b if column else place.b
        shard = a * place.count_b + b
        if forward:
            ffn_forward_shard(hidden_r, mats, a, b, shard, bias_r, pool, acc)
        else:
            ffn_backward_shard(hidden_r, gturned_r, hidden_turned, mats, a, b, shard, pool, acc, gbias_r)

    key_sums.along_a()
    band_forward_phase(qf_r, ke_r, ve_r, line_r, attn_r, denom_r, 0, third)
    gather.along_a(1, (0,))
    band_forward_phase(qf_r, ke_r, ve_r, line_r, attn_r, denom_r, third, 2 * third)
    gather.along_a(1, (1,))
    band_forward_phase(qf_r, ke_r, ve_r, line_r, attn_r, denom_r, 2 * third, pairs)
    gather.along_b(0, (0,))
    key_sums.along_b()
    gather.across(1)
    gather.along_b(0, (1,))
    key_sums.finish(before_r, after_r)
    gather.along_a(2, (0, 1))
    gather.across(2)
    far_forward_phase(
        qf_r, ke_r, ve_r, line_r, num_r, den_r, before_r, after_r, attn_r, low_r, denom_r, left_r, right_r, lden_r,
        rden_r, pairs, head_dim,
    )
    hidden_turned = turned_r.at[:, pl.ds(0, rows)]
    acc = acc_r.at[own]
    hidden_phase(
        x_r.at[own], low_r, wo_r, bo_r, g1_r, s1_r, bdown_r, normed_r, scale_r, hidden_r, hidden_turned, acc
    )
    for offset in range(1, shards):
        arrive(biases.at[lax.rem(seq + shards - offset, shards)], bias_sems[1].at[offset], place.at())
    for shard in range(shards):
        bias_r[shard] = biases[shard, 0:8, :].astype(F32)
    ffn(0, 0, True)
    gather.along_b(1, (0, 1))
    gather.along_x(1, 0)
    gather.along_x(0, 1)
    gather.finish(0, 1)
    ffn(0, 1, True)
    gather.along_a(3, (0, 1))
    gather.across(3)
    gather.finish(1, 0)
    ffn(1, 0, True)
    gather.along_x(1, 1)
    gather.along_b(2, (0, 1))
    gather.along_x(2, 0)
    gather.finish(1, 1)
    ffn(1, 1, True)
    gather.finish(2, 0)
    ffn(2, 0, True)
    gather.along_x(2, 1)
    gather.along_x(3, 0)
    gather.along_b(3, (0, 1))
    gather.finish(2, 1)
    ffn(2, 1, True)
    gather.finish(3, 0)
    ffn(3, 0, True)
    gather.along_x(3, 1)
    gather.finish(3, 1)
    ffn(3, 1, True)
    sends.drain()
    loads[3].wait()
    middle_phase(acc, cot_r, g2_r, s2_r, hidden_r, gturned_r, small_r)
    layer_out = pltpu.make_async_copy(cot_r, layer_h, load_sem.at[6])
    layer_out.start()
    items = [(offset, column) for offset in (2, 1, 3, 0) for column in (1, 0)]
    for index, item in enumerate(items):
        ffn(*item, False)
        scatter.start(*item)
        if index > 1:
            scatter.chip(*items[index - 2])
        if index > 0:
            scatter.fetch(*items[index - 1])
        if index == 7:
            scatter.along_x(*items[0])
    first_back_phase(acc, normed_r, scale_r, g1_r, hidden_r, small_r)
    tot_r[pairs * half :, :] = jnp.zeros((tot_r.shape[0] - pairs * half, LANES), F32)
    block = pool.shape[2]
    for index in range(width // block):
        cols = slice(index * block, (index + 1) * block)
        pool[index, 0:width, :] = tn(low_r[...], hidden_r[:, cols]).astype(BF16)
    reduce.push(0)
    scatter.chip(*items[6])
    scatter.fetch(*items[7])
    scatter.along_x(*items[1])
    attn_back_phase(hidden_r, wo_r, attn_r, denom_r, low_r, qf_r, num_r, den_r, tot_r, pairs, head_dim)
    layer_out.wait()
    grad_sums.start(tot_r)
    scatter.chip(*items[7])

    def turn(block):
        turned_r[:, block] = x_r[block, :].T

    row_blocks(rows + 2 * WINDOW, turn)
    groups = pairs * LANES // CHUNK
    in_group = CHUNK // LANES

    kept = [gqkv_r, x_r, gqkv_r]

    def band(pair):
        group = pair // in_group
        band_backward_phase(
            qf_r, ke_r, ve_r, line_r, low_r, denom_r, num_r, den_r, left_r, right_r, lden_r, rden_r, attn_r,
            gk_r.at[group % 2], gv_r.at[group % 2], gline_r, cg_r, pair, pair + 1, group * in_group, head_dim,
        )

    def far(group):
        far_back_phase(
            ke_r, ve_r, line_r, num_r, den_r, before_r, after_r, gk_r.at[group % 2], gv_r.at[group % 2], pairs,
            group * in_group, (group + 1) * in_group, group * in_group, head_dim,
        )

    def grads(group, wanted):
        qkv_grad_phase(
            turned_r, w_r, omega_r, q_r, k_r, qf_r, ke_r, attn_r, gk_r.at[group % 2], gv_r.at[group % 2], kept[group],
            pool, small_r, group, wanted, place, head_dim,
        )

    def tokens_part(group, wanted):
        def body(block):
            if 1 not in wanted:
                block = pl.ds(pl.multiple_of(block.start + WINDOW, WINDOW), CHUNK)
            total = acc_r[block, :]
            for part in wanted:
                cols = slice(part * CHUNK, (part + 1) * CHUNK)
                wide = slice(part * width + group * CHUNK, part * width + (group + 1) * CHUNK)
                total = total + nt(kept[group][block, cols], w_r[:, wide])
            acc_r[block, :] = total

        row_blocks(rows + 2 * WINDOW if 1 in wanted else rows, body)

    scatter.along_x(*items[2])
    band(0)
    grad_sums.along_a()
    band(1)
    scatter.along_x(*items[3])
    grads(0, (0,))
    tokens_part(0, (0,))
    scatter.along_b(2)
    reduce.stage(0, 0)
    band(2)
    grad_sums.along_b()
    reduce.stage(0, 1)
    band(3)
    grad_sums.finish(before_r, after_r)
    scatter.along_x(*items[4])
    scatter.along_b(1)
    far(0)
    grads(0, (1, 2))
    reduce.push(1)
    scatter.along_x(*items[5])
    tokens_part(0, (1, 2))
    grads(1, (0,))
    reduce.stage(1, 0)
    band(4)
    scatter.along_x(*items[6])
    reduce.stage(0, 2)
    reduce.stage(1, 1)
    band(5)
    far(1)
    grads(1, (1, 2))
    reduce.push(2)
    scatter.along_x(*items[7])
    scatter.along_b(3)
    grads(2, (0,))
    reduce.stage(2, 0)
    reduce.stage(0, 3)
    reduce.stage(2, 1)
    far(2)
    grads(2, (1, 2))
    reduce.push(3)
    scatter.along_b(0)
    table_grads(gline_r, bucket_r, buckets, small_r)
    per_row = width // gbias_r.shape[2]
    for index in range(shards // per_row):
        small_r[9 + index : 10 + index, :] = jnp.concatenate(
            [gbias_r[index * per_row + i, 0:1, :] for i in range(per_row)], 1
        )
    held_r[0] = small_r[...]
    little.send(0)
    reduce.stage(1, 2)
    reduce.stage(3, 0)
    reduce.stage(0, 4)
    tokens_part(1, (0,))
    tokens_part(1, (1, 2))
    reduce.stage(3, 1)
    tokens_part(2, (0,))
    tokens_part(2, (1, 2))
    edge_r[0:WINDOW, :] = acc_r[0:WINDOW, :].astype(BF16)
    edge_r[WINDOW:, :] = acc_r[rows + WINDOW :, :].astype(BF16)
    top, bottom = pl.ds(0, WINDOW), pl.ds(WINDOW, WINDOW)
    sends.send(edge_r.at[top], tail_r.at[bottom], t_send.at[0], t_recv.at[1], to_left, place.not_first)
    sends.send(edge_r.at[bottom], tail_r.at[top], t_send.at[1], t_recv.at[0], to_right, place.not_last)
    reduce.stage(2, 2)
    reduce.stage(1, 3)
    little.receive(0)
    little.send(1)
    reduce.stage(0, 5)
    scatter.along_a()
    reduce.stage(3, 2)
    reduce.stage(2, 3)
    reduce.stage(1, 4)
    reduce.stage(0, 6)
    little.receive(1)
    little.send(2)
    reduce.stage(3, 3)
    reduce.stage(2, 4)
    reduce.stage(1, 5)
    reduce.stage(3, 4)
    reduce.stage(0, 7)
    reduce.stage(2, 5)
    reduce.stage(1, 6)
    little.receive(2)
    little.send(3)
    reduce.stage(3, 5)
    arrive(tail_r.at[top], t_recv.at[0], place.at(), place.not_first)
    arrive(tail_r.at[bottom], t_recv.at[1], place.at(), place.not_last)

    @pl.when(place.not_first)
    def _():
        acc_r[WINDOW : 2 * WINDOW, :] += tail_r[0:WINDOW, :].astype(F32)

    @pl.when(place.not_last)
    def _():
        acc_r[rows : rows + WINDOW, :] += tail_r[WINDOW:, :].astype(F32)

    tokens_out = pltpu.make_async_copy(acc, gtok_h, load_sem.at[7])
    tokens_out.start()
    reduce.stage(2, 6)
    reduce.stage(3, 6)
    scatter.last_x()
    reduce.stage(1, 7)
    little.receive(3)
    small_r[...] = little.total()
    reduce.stage(2, 7)
    reduce.stage(3, 7)
    scatter.finish()
    for index in range(chunks):
        reduce.stage(index, 8)
    tokens_out.wait()
    sends.drain()


def in_parts(grouped):
    groups = grouped.shape[1] // (3 * CHUNK)
    starts = [(group * 3 + part) * CHUNK for part in range(3) for group in range(groups)]
    return jnp.concatenate([grouped[:, start : start + CHUNK].astype(F32) for start in starts], 1)


def call(body, outs, operands, scratch=(), limit=60, collective_id=None, in_place=(), out_place=()):
    return pl.pallas_call(
        body,
        out_shape=[jax.ShapeDtypeStruct(shape, dtype) for shape, dtype in outs],
        in_specs=[
            pl.BlockSpec(memory_space=pl.ANY if i in in_place else pltpu.VMEM) for i in range(len(operands))
        ],
        out_specs=[
            pl.BlockSpec(memory_space=pl.ANY if i in out_place else pltpu.VMEM) for i in range(len(outs))
        ],
        scratch_shapes=list(scratch),
        compiler_params=pltpu.CompilerParams(
            vmem_limit_bytes=limit * MIB,
            collective_id=collective_id,
            has_side_effects=collective_id is not None,
        ),
    )(*operands)


def unpack_kernel(
    result_h, total_h, tokens_h, layer_h, small_r, gw_h, gwo_h, gup_r, gdown_r, gtok_h, out_h, gb_r, gbu_r, *rest
):
    vector_rs, (table_r, result_r, total_r, wide_r, tokens_r, layer_r, in_sem, out_sem) = rest[:6], rest[6:]
    blocks, width, block = result_r.shape
    chunks = wide_r.shape[0]
    per_chunk = blocks // chunks
    loads = []
    for chunk in range(chunks):
        part = pl.ds(chunk * per_chunk, per_chunk)
        loads.append(pltpu.make_async_copy(result_h.at[part], result_r.at[part], in_sem.at[chunk]))
    load_total = pltpu.make_async_copy(total_h, total_r, in_sem.at[chunks])
    load_tokens = pltpu.make_async_copy(tokens_h, tokens_r, in_sem.at[chunks + 1])
    load_layer = pltpu.make_async_copy(layer_h, layer_r, in_sem.at[chunks + 2])
    for load in loads + [load_total, load_tokens, load_layer]:
        load.start()
    stores = []

    def store(src, dst):
        copy = pltpu.make_async_copy(src, dst, out_sem.at[len(stores)])
        copy.start()
        stores.append(copy)

    for chunk in range(chunks):
        loads[chunk].wait()
        for index in range(per_chunk):
            wide_r[chunk, :, index * block : (index + 1) * block] = result_r[chunk * per_chunk + index].astype(F32)
        if chunk == 0:
            store(wide_r.at[0], gwo_h)
            continue
        for part in range(3):
            source = wide_r.at[chunk, :, pl.ds(part * CHUNK, CHUNK)]
            store(source, gw_h.at[:, pl.ds(part * width + (chunk - 1) * CHUNK, CHUNK)])
    load_tokens.wait()
    store(tokens_r, gtok_h)
    load_layer.wait()
    store(layer_r, out_h)
    load_total.wait()
    gup_r[...] = total_r[0].astype(F32)
    gdown_r[...] = total_r[1].T.astype(F32)
    for index, ref in enumerate(vector_rs):
        ref[...] = small_r[index, :]
    for group in range(width // CHUNK):
        for part in range(3):
            start = part * width + group * CHUNK
            gb_r[start : start + CHUNK] = small_r[6 + group, part * CHUNK : (part + 1) * CHUNK]
    heads, buckets = table_r.shape
    per_row = LANES // buckets
    for head in range(heads):
        at = head % per_row * buckets
        row = 13 + head // per_row
        table_r[head : head + 1, :] = small_r[row : row + 1, at : at + buckets]
    units = gbu_r.shape[0]
    seq = lax.axis_index("seq")
    per_row = width // units
    for shard in range(lax.axis_size("seq")):
        @pl.when(seq == shard)
        def _():
            at = shard % per_row * units
            gbu_r[...] = small_r[9 + shard // per_row, at : at + units]
    for copy in stores:
        copy.wait()


def fused(
    x, cot, w_up, w_down, w_qkv, b_qkv, codes, offset_bucket, bias_table, w_out, b_out, gain_one, shift_one, b_up, b_down,
    gain_two, shift_two, pairs, head_dim,
):
    rows, width = x.shape
    units = w_up.shape[1]
    heads, buckets = bias_table.shape
    count = lax.axis_size("seq")
    count_a = count // 2
    blocks, half = rows // WINDOW, LANES // 2
    middle, quarter = width // 6, width // 4
    side = (width - middle) // 2
    groups = width // CHUNK
    chunks = 1 + groups
    columns = chunks * width // units
    wide, ext = (rows, width), (rows + 2 * WINDOW, width)
    stacked, flat = (pairs * blocks, half, LANES), (pairs * blocks, LANES)
    message = (pairs * half + 32, LANES)
    mats = (2, count_a, 2, width, units)
    dma = pltpu.SemaphoreType.DMA
    vmem = pltpu.VMEM
    part = (message[0] // 2, LANES)
    sums = [vmem(shape, BF16) for shape in (message, message, part, (count_a, *part), (2, *part), (2, *part))]
    layer, gtok, total, small, result, _, _ = call(
        functools.partial(layer_kernel, pairs, head_dim, buckets, count),
        [(wide, BF16), (wide, F32), ((2, width, units), BF16), ((16, width), F32), ((columns, width, units), BF16),
         (mats[1:], BF16), ((columns, 2 * quarter, units), BF16)],
        (x, cot, w_up, w_down, w_qkv, codes, bias_table, w_out, b_qkv, b_out, gain_one, shift_one, b_down, gain_two,
         shift_two, b_up, offset_bucket),
        [vmem(ext, BF16), vmem(wide, BF16), vmem(ext, BF16), vmem(wide, BF16), vmem((2, *ext), BF16),
         vmem((heads, LINE), F32), vmem(stacked, F32), vmem(flat, F32), vmem(message, F32),
         vmem((count, 16, units), BF16), vmem(message, F32),
         vmem(message, F32), vmem(stacked, F32), vmem(stacked, F32), vmem(flat, F32), vmem(flat, F32),
         vmem(wide, F32), vmem(wide, F32), vmem(wide, BF16), vmem((rows, LANES), F32),
         vmem(wide, BF16), vmem((width, ext[0]), BF16),
         vmem(wide, BF16), vmem(ext, F32), vmem(mats, BF16), vmem((columns, 2 * rows, units), BF16),
         vmem((count, 8, units), F32), vmem((count, 8, units), F32), vmem((2, ext[0], CHUNK), F32),
         vmem((2, ext[0], CHUNK), F32), vmem((heads, LINE), F32), vmem((2 * WINDOW, 3 * WINDOW), F32),
         vmem(ext, BF16), vmem((2, width, units), BF16), vmem((count_a, 2, side, units), BF16),
         vmem((count_a, side + middle, units), BF16), vmem((count_a - 1, side + middle, units), BF16),
         vmem((middle, units), BF16),
         vmem((2, 2 * quarter, units), BF16), vmem((columns, quarter, units), BF16),
         vmem((chunks, quarter, units), BF16), vmem((chunks, count_a - 1, quarter // count_a, units), BF16),
         vmem((chunks, quarter // count_a, units), BF16), vmem((4, 16, width), F32),
         vmem((3 + count_a, 16, width), F32)]
        + sums + sums
        + gather_sems(count_a) + sums_sems(count_a) + sums_sems(count_a) + scatter_sems(count_a)
        + reduce_sems(chunks, count_a)
        + [dma((3 + count_a,)), dma((3 + count_a,))] + [dma((count,)), dma((count,))] + [ dma((2,)), dma((2,)), dma((2,)), dma((2,)), dma((8,)),
           vmem(w_qkv.shape, BF16), vmem(w_out.shape, BF16),
           vmem((groups, CHUNK, CHUNK), BF16), vmem((16, width), F32)],
        limit=62,
        collective_id=0,
        in_place=(0, 1, 2, 3, 4, 7),
        out_place=(0, 1, 4, 5, 6),
    )
    vector = ((width,), F32)
    gw_qkv, gw_out, gup, gdown, gtok, layer, gb_qkv, grad_b_up, g2, s2, bd, g1, s1, bo, gtable = call(
        unpack_kernel,
        [((width, 3 * width), F32), ((width, width), F32), ((width, units), F32), ((units, width), F32), (wide, F32),
         (wide, BF16), ((3 * width,), F32), ((units,), F32)] + [vector] * 6 + [((heads, buckets), F32)],
        (result, total, gtok, layer, small),
        [vmem((columns, width, units), BF16), vmem((2, width, units), BF16), vmem((chunks, width, width), F32),
         vmem(wide, F32), vmem(wide, BF16), dma((chunks + 3,)), dma((3 * chunks,))],
        in_place=(0, 1, 2, 3),
        out_place=(0, 1, 4, 5),
    )
    return (
        layer[None], gtok[None], gw_qkv, gb_qkv, gw_out, bo, g1, s1, gup, grad_b_up, gdown, bd, g2, s2, gtable,
    )


def shards(
    tokens, cotangent, w_qkv, b_qkv, w_out, b_out, gain_one, shift_one, w_up, b_up, w_down, b_down,
    gain_two, shift_two, feature_codes, bias_table, offset_bucket,
):
    rows, width = tokens.shape[1:]
    heads, head_dim, feats = feature_codes.shape
    buckets = bias_table.shape[1]
    pairs = heads // 2
    blocks = rows // WINDOW
    half = LANES // 2
    hidden_units = w_up.shape[1]
    length = (offset_bucket.shape[0] + 1) // 2
    count = lax.axis_size("seq")
    x = tokens[0]
    state = (pairs * half + 8, LANES)
    stacked = (pairs * blocks, half, LANES)
    flat = (pairs * blocks, LANES)
    wide = (rows, width)

    def halo(block):
        forward = [(i, i + 1) for i in range(count - 1)]
        backward = [(target, source) for source, target in forward]
        low = lax.ppermute(block[rows - WINDOW :], "seq", forward)
        high = lax.ppermute(block[:WINDOW], "seq", backward)
        return jnp.concatenate([low, block, high], 0)

    me = lax.axis_index("seq")
    ids = jnp.arange(count)

    def prefix(message):
        every = lax.all_gather(message, "seq", axis=0)
        before = jnp.sum(jnp.where((ids < me)[:, None, None], every, 0.0), 0)
        after = jnp.sum(jnp.where((ids > me)[:, None, None], every, 0.0), 0)
        return before, after

    if lax.axis_size("row") == 4 and count == 8:
        return fused(
            x, cotangent[0], w_up, w_down, w_qkv, b_qkv, feature_codes, offset_bucket, bias_table, w_out, b_out, gain_one,
            shift_one, b_up, b_down, gain_two, shift_two, pairs, head_dim,
        )

    bucket_line = offset_bucket[length - LINE // 2 : length + LINE // 2][None]
    omega_int = (feature_codes.astype(F32) - CENTER).astype(BF16)
    group = CHUNK // head_dim
    eye = jnp.eye(group, dtype=BF16)
    omega = (
        omega_int.reshape(heads // group, group, head_dim, 1, feats)
        * eye[None, :, None, :, None]
    ).reshape(heads // group, CHUNK, CHUNK)

    def body_one(x_r, w_r, b_r, o_r, bu_r, ta_r, q_r, k_r, v_r, qf_r, kf_r, line_r, num_r, den_r, tot_r):
        parts = ((1, k_r, kf_r), (2, v_r, None), (0, q_r, qf_r))
        qkv_phase(x_r, w_r, [b_r.at[pl.ds(i, 1)] for i in range(3)], o_r, parts, head_dim)
        line_phase(bu_r, ta_r, line_r)
        state_phase(kf_r, v_r, num_r, den_r, tot_r, pairs)

    q, k, v, qf, kf, line, num, den, total = call(
        body_one,
        [(wide, BF16)] * 5
        + [((heads, LINE), F32), (stacked, F32), (flat, F32), (state, F32)],
        (x, w_qkv, b_qkv.astype(F32).reshape(3, width), omega, bucket_line, bias_table),
    )
    up_all = lax.all_gather(w_up, "seq", axis=0)
    down_all = lax.all_gather(jnp.transpose(w_down), "seq", axis=0)
    b_up_all = jnp.broadcast_to(lax.all_gather(b_up, "seq", axis=0)[:, None, :], (count, 8, hidden_units))

    ke, ve = halo(kf), halo(v)
    before, after = prefix(total)

    def body_two(*refs):
        ins, outs = refs[:12], refs[12:]
        qf_r, ke_r, ve_r, line_r, num_r, den_r, bef_r, aft_r, x_r, w_r, b_r, _ = ins
        out_r, low_r, dnm_r, l_r, r_r, ld_r, rd_r, nrm_r, sc_r = outs
        band_forward_phase(qf_r, ke_r, ve_r, line_r, out_r, dnm_r, 0, pairs)
        far_forward_phase(
            qf_r, ke_r, ve_r, line_r, num_r, den_r, bef_r, aft_r,
            out_r, low_r, dnm_r, l_r, r_r, ld_r, rd_r, pairs, head_dim,
        )
        out_phase(x_r, low_r, w_r, b_r, nrm_r, sc_r)

    attn, attn_low, denom, left, right, left_den, right_den, normed, scale = call(
        body_two,
        [(wide, F32), (wide, BF16), (wide, F32), (stacked, F32), (stacked, F32), (flat, F32),
         (flat, F32), (wide, F32), ((rows, LANES), F32)],
        (qf, ke, ve, line, num, den, before, after, x, w_out, b_out[None], gain_one[None]),
    )
    layer, first, first_low, vec, gup, gdown, gbias = call(
        ffn_phase,
        [(wide, BF16), (wide, F32), (wide, BF16), ((8, width), F32),
         ((count, width, hidden_units), BF16), ((count, width, hidden_units), BF16),
         ((count, 8, hidden_units), F32)],
        (normed, scale, gain_one[None], shift_one[None], up_all, b_up_all, down_all, b_down[None],
         gain_two[None], shift_two[None], cotangent[0]),
        (pltpu.VMEM((count, rows, hidden_units), BF16), pltpu.VMEM((count, rows, hidden_units), BF16),
         pltpu.VMEM(wide, F32)),
    )

    def reduced(part):
        return lax.psum(lax.psum_scatter(part, "seq", scatter_dimension=0), "row").astype(F32)

    grad_w_up = reduced(gup)
    grad_w_down = jnp.transpose(reduced(gdown))
    grad_b_up = reduced(gbias[:, 0])
    ext = (rows + 2 * WINDOW, width)

    def body_four(*refs):
        (gl_r, w_r, lo_r, ou_r, dn_r, qf_r, ke_r, ve_r, li_r, l_r, r_r, ld_r, rd_r, bu_r) = refs[:14]
        gw_r, gq_r, gk_r, gv_r, dnum_r, dden_r, tot_r, gt_r, gnum_r, gden_r, gline_r, cg_r = refs[14:]
        out_back_phase(
            gl_r, w_r, lo_r, ou_r, dn_r, qf_r, gnum_r, gden_r, gw_r, dnum_r, dden_r, tot_r, pairs, head_dim
        )
        band_backward_phase(
            qf_r, ke_r, ve_r, li_r, gnum_r, gden_r, dnum_r, dden_r, l_r, r_r, ld_r, rd_r,
            gq_r, gk_r, gv_r, gline_r, cg_r, 0, pairs, 0, head_dim,
        )
        gt_r[...] = table_phase(gline_r, bu_r, buckets)

    gw_out, gq, gk, gv, dnum, dden, gtotal, gtable = call(
        body_four,
        [((width, width), F32), (wide, F32), (ext, F32), (ext, F32), (stacked, F32), (flat, F32),
         (state, F32), (bias_table.shape, F32)],
        (first_low, w_out, attn_low, attn, denom, qf, ke, ve, line, left, right, left_den, right_den,
         bucket_line),
        (pltpu.VMEM(wide, BF16), pltpu.VMEM(wide, F32), pltpu.VMEM((heads, LINE), F32),
         pltpu.VMEM((2 * WINDOW, 3 * WINDOW), F32)),
    )
    past, future = prefix(gtotal)
    forward = [(i, i + 1) for i in range(count - 1)]
    backward = [(target, source) for source, target in forward]
    to_left = jnp.stack([gk[:WINDOW], gv[:WINDOW]]).astype(BF16)
    to_right = jnp.stack([gk[rows + WINDOW :], gv[rows + WINDOW :]]).astype(BF16)
    low_in = lax.ppermute(to_right, "seq", forward)
    high_in = lax.ppermute(to_left, "seq", backward)

    def body_five(*refs):
        (x_r, w_r, o_r, q_r, k_r, v_r, qf_r, kf_r, li_r, dn_r, dd_r, pa_r, fu_r, lo_r, hi_r, gq_r,
         gki_r, gvi_r, fi_r) = refs[:19]
        gt_r, gw_r, gb_r, gk_r, gv_r, turned_r = refs[19:]
        gk_r[...] = gki_r[...]
        gv_r[...] = gvi_r[...]
        gt_r[...] = fi_r[...]
        turned_r[...] = x_r[...].T
        key_back_phase(
            kf_r, v_r, li_r, dn_r, dd_r, pa_r, fu_r, lo_r, hi_r, gk_r, gv_r, pairs, 0, pairs, head_dim
        )
        for group in range(width // CHUNK):
            qkv_back_phase(
                turned_r, w_r, o_r, q_r, k_r, qf_r, kf_r, gq_r, gk_r, gv_r, gt_r, gw_r, gb_r, group, head_dim
            )

    gtok, gw_qkv, small = call(
        body_five,
        [(wide, F32), ((width, 4 * width), F32), ((16, width), F32)],
        (x, w_qkv, omega, q, k, v, qf, kf, line, dnum, dden, past, future, low_in, high_in, gq, gk, gv,
         first),
        (pltpu.VMEM(ext, F32), pltpu.VMEM(ext, F32), pltpu.VMEM((width, rows), BF16)),
    )
    gw_qkv = in_parts(gw_qkv[:, width:])
    gb_qkv = in_parts(small[6 : 6 + width // CHUNK].reshape(1, -1))
    summed = lax.psum((gw_qkv, gb_qkv[0], gw_out, vec, gtable), ("row", "seq"))
    gw_qkv, gb_qkv, gw_out, vec, gtable = summed
    return (
        layer[None], gtok[None], gw_qkv, gb_qkv, gw_out, vec[5], vec[3], vec[4], grad_w_up, grad_b_up,
        grad_w_down, vec[2], vec[0], vec[1], gtable,
    )


def solution(mesh):
    placed = (
        P("row", "seq", None), P("row", "seq", None), P(), P(), P(), P(), P(), P(), P(None, "seq"),
        P("seq"), P("seq", None), P(), P(), P(), P(), P(), P(),
    )
    return jax.shard_map(
        shards,
        mesh=mesh,
        in_specs=placed,
        out_specs=(
            P("row", "seq", None), P("row", "seq", None), P(), P(), P(), P(), P(), P(), P(None, "seq"),
            P("seq"), P("seq", None), P(), P(), P(), P(),
        ),
        check_vma=False,
    )
```

```python
import functools
import math

import jax
import jax.numpy as jnp
from jax import lax
from jax.experimental import pallas as pl
from jax.experimental.pallas import tpu as pltpu
from jax.sharding import PartitionSpec as P

WINDOW = 128
LANES = 128
LINE = 512
CHUNK = 256
EPS = 1e-06
CENTER = 7.5
SPREAD = math.sqrt(21.25)
ROOT_HALF = 0.7071067811865476
INV_ROOT_TAU = 0.3989422804014327
MIB = 1 << 20
F32 = jnp.float32
BF16 = jnp.bfloat16


def nn(a, b):
    return lax.dot_general(a, b, (((1,), (0,)), ((), ())), preferred_element_type=F32)


def nt(a, b):
    return lax.dot_general(a, b, (((1,), (1,)), ((), ())), preferred_element_type=F32)


def tn(a, b):
    return lax.dot_general(a, b, (((0,), (0,)), ((), ())), preferred_element_type=F32)


def halves(values):
    upper = values.astype(BF16)
    return upper, (values - upper.astype(F32)).astype(BF16)


def block_ones(size, head_dim):
    rows = lax.broadcasted_iota(jnp.int32, (size, size), 0) // head_dim
    cols = lax.broadcasted_iota(jnp.int32, (size, size), 1) // head_dim
    return jnp.where(rows == cols, 1.0, 0.0)


def head_sums(values, ones):
    upper, lower = halves(values)
    return nn(upper, ones) + nn(lower, ones)


def first_half(shape):
    return lax.broadcasted_iota(jnp.int32, shape, len(shape) - 1) < LANES // 2


def both_heads(pair):
    first = first_half((1, LANES))
    mask_a = jnp.where(first, 1.0, 0.0).astype(pair.dtype)
    mask_b = jnp.where(first, 0.0, 1.0).astype(pair.dtype)
    return jnp.concatenate([pair * mask_a, pair * mask_b], 0)


def per_head(stacked):
    rows = stacked.shape[0] // 2
    return jnp.where(first_half((rows, LANES)), stacked[:rows], stacked[rows:])


def compact(full):
    half = LANES // 2
    return jnp.where(first_half((half, LANES)), full[:half], full[half:])


def expand(small, ones):
    return jnp.concatenate([small, small], 0) * ones


def block_state(keys, values):
    return compact(tn(keys, values)), jnp.sum(keys.astype(F32), 0, keepdims=True)


def coef_tile(line_ref, pair):
    tiles = []
    for head in range(2):
        row = line_ref[pl.ds(2 * pair + head, 1), :]
        wide = pltpu.roll(
            jnp.broadcast_to(row, (WINDOW, LINE)), LINE - WINDOW + 1, 1, stride=1, stride_axis=0
        )
        tiles.append(wide[:, : 3 * WINDOW])
    return jnp.concatenate(tiles, 0)


def far_coefs(line_ref, pair):
    first = first_half((1, LANES))
    row_a = line_ref[pl.ds(2 * pair, 1), :]
    row_b = line_ref[pl.ds(2 * pair + 1, 1), :]
    left = jnp.where(first, row_a[:, 0:1], row_b[:, 0:1])
    right = jnp.where(first, row_a[:, LINE - 2 : LINE - 1], row_b[:, LINE - 2 : LINE - 1])
    return left, right


def unskew_sum(tile):
    rows = tile.shape[0]
    padded = jnp.concatenate([tile, jnp.zeros((rows, LINE - tile.shape[1]), F32)], 1)
    while rows > 8:
        rows = rows // 2
        padded = pltpu.roll(padded[:rows], rows, 1) + padded[rows:]
    while rows > 1:
        rows = rows // 2
        padded = pltpu.roll(padded[:rows], rows, 1) + padded[rows:]
    return padded


def lanes(pair):
    return pl.ds(pl.multiple_of(pair * LANES, LANES), LANES)


def qkv_phase(x_ref, w_ref, b_ref, omega_ref, parts, head_dim):
    width = x_ref.shape[1]
    x = x_ref[...]
    ones = block_ones(CHUNK, head_dim).astype(BF16)
    factor = head_dim ** (-0.25) / SPREAD
    for part, low_ref, feat_ref in parts:
        for chunk in range(width // CHUNK):
            cols = slice(chunk * CHUNK, (chunk + 1) * CHUNK)
            wide = slice(part * width + chunk * CHUNK, part * width + (chunk + 1) * CHUNK)
            low = (nn(x, w_ref[:, wide]) + b_ref[part][:, cols]).astype(BF16)
            low_ref[:, cols] = low
            if feat_ref is not None:
                projected = nn(low, omega_ref[chunk]) * factor
                widened = low.astype(F32)
                half_norm = head_sums(widened * widened, ones) * (0.5 * head_dim ** (-0.5))
                feat_ref[:, cols] = (
                    jnp.exp(projected - half_norm) * head_dim ** (-0.5)
                ).astype(BF16)


def line_phase(bucket_ref, table_ref, line_ref):
    buckets = table_ref.shape[1]
    one_hot = jnp.where(
        lax.broadcasted_iota(jnp.int32, (buckets, LINE), 0) == bucket_ref[...].astype(jnp.int32), 1.0, 0.0
    )
    logs = lax.dot_general(
        table_ref[...],
        one_hot,
        (((1,), (0,)), ((), ())),
        precision=lax.Precision.HIGHEST,
        preferred_element_type=F32,
    )
    line_ref[...] = jnp.exp(logs)


def state_phase(kf_ref, v_ref, num_ref, den_ref, total_ref, pairs):
    blocks = kf_ref.shape[0] // WINDOW
    half = LANES // 2

    @pl.loop(0, pairs)
    def _(pair):
        total = jnp.zeros((half, LANES), F32)
        total_den = jnp.zeros((1, LANES), F32)
        for block in range(blocks):
            rows = slice(block * WINDOW, (block + 1) * WINDOW)
            num, den = block_state(kf_ref[rows, lanes(pair)], v_ref[rows, lanes(pair)])
            num_ref[pair * blocks + block] = num
            den_ref[pl.ds(pair * blocks + block, 1), :] = den
            total = total + num
            total_den = total_den + den
        total_ref[pl.ds(pl.multiple_of(pair * half, half), half), :] = total
        total_ref[pl.ds(pairs * half + pair, 1), :] = total_den


def band_forward_phase(qf_ref, ke_ref, ve_ref, line_ref, out_ref, denom_ref, first, last):
    blocks = qf_ref.shape[0] // WINDOW

    @pl.loop(first, last)
    def _(pair):
        cols = lanes(pair)
        coef = coef_tile(line_ref, pair)
        for block in range(blocks):
            rows = slice(block * WINDOW, (block + 1) * WINDOW)
            window = slice(block * WINDOW, (block + 3) * WINDOW)
            scores = nt(both_heads(qf_ref[rows, cols]), ke_ref[window, cols])
            weights = (coef * scores).astype(BF16)
            values = ve_ref[window, cols]
            summed = nn(weights, jnp.concatenate([values, jnp.ones_like(values)], 1))
            out_ref[rows, cols] = per_head(summed[:, :LANES])
            denom_ref[rows, cols] = per_head(summed[:, LANES:])


def far_forward_phase(
    qf_ref, ke_ref, ve_ref, line_ref, num_ref, den_ref, before_ref, after_ref,
    out_ref, low_ref, denom_ref, left_ref, right_ref, left_den_ref, right_den_ref, pairs, head_dim,
):
    blocks = qf_ref.shape[0] // WINDOW
    half = LANES // 2

    @pl.loop(0, pairs)
    def _(pair):
        ones_f32 = block_ones(LANES, head_dim)
        ones = ones_f32.astype(BF16)
        cols = lanes(pair)
        left_coef, right_coef = far_coefs(line_ref, pair)
        state_rows = pl.ds(pl.multiple_of(pair * half, half), half)
        den_row = pl.ds(pairs * half + pair, 1)
        edge_low = block_state(ke_ref[:WINDOW, cols], ve_ref[:WINDOW, cols])
        edge_high = block_state(
            ke_ref[(blocks + 1) * WINDOW :, cols], ve_ref[(blocks + 1) * WINDOW :, cols]
        )
        past = (before_ref[state_rows, :], before_ref[den_row, :])
        future = (after_ref[state_rows, :], after_ref[den_row, :])

        def block_of(block):
            index = pair * blocks + block
            return num_ref[index], den_ref[pl.ds(index, 1), :]

        def add(one, two, sign=1.0):
            return tuple(a + sign * b for a, b in zip(one, two))

        lefts = [add(past, edge_low, -1.0), past]
        for block in range(2, blocks):
            lefts.append(add(lefts[-1], block_of(block - 2)))
        rights = [add(future, edge_high, -1.0), future]
        for block in range(2, blocks):
            rights.append(add(rights[-1], block_of(blocks + 1 - block)))
        rights = rights[::-1]
        for block in range(blocks):
            rows = slice(block * WINDOW, (block + 1) * WINDOW)
            index = pair * blocks + block
            query = qf_ref[rows, cols]
            left, left_den = lefts[block]
            right, right_den = rights[block]
            left_ref[index] = left
            right_ref[index] = right
            left_den_ref[pl.ds(index, 1), :] = left_den
            right_den_ref[pl.ds(index, 1), :] = right_den
            upper, lower = halves(expand(left_coef * left + right_coef * right, ones_f32))
            numer = out_ref[rows, cols] + nn(query, upper) + nn(query, lower)
            den_far = left_coef * left_den + right_coef * right_den
            denom = denom_ref[rows, cols] + head_sums(query.astype(F32) * den_far, ones)
            out = numer / denom
            out_ref[rows, cols] = out
            low_ref[rows, cols] = out.astype(BF16)
            denom_ref[rows, cols] = denom


def norm_parts(values):
    center = values - jnp.mean(values, -1, keepdims=True)
    inv_scale = lax.rsqrt(jnp.mean(center * center, -1, keepdims=True) + EPS)
    return center * inv_scale, inv_scale


def out_phase(x_ref, low_ref, w_ref, b_ref, normed_ref, scale_ref):
    first_sum = x_ref[...].astype(F32) + nn(low_ref[...], w_ref[...]) + b_ref[...].astype(F32)
    normed, inv_scale = norm_parts(first_sum)
    normed_ref[...] = normed
    scale_ref[...] = jnp.broadcast_to(inv_scale, scale_ref.shape)


def norm_back(grad_out, normed, inv_scale, gain):
    grad_normed = grad_out * gain
    centered = grad_normed - jnp.mean(grad_normed, -1, keepdims=True)
    return inv_scale * (centered - normed * jnp.mean(grad_normed * normed, -1, keepdims=True))


def ffn_phase(
    normed_ref, scale_ref, gain_one_ref, shift_one_ref, up_ref, b_up_ref, down_ref, b_down_ref,
    gain_two_ref, shift_two_ref, cot_ref, layer_ref, first_ref, low_ref, vec_ref, gup_ref, gdown_ref,
    gbias_ref, act_ref, slope_ref, acc_ref,
):
    shards = up_ref.shape[0]
    normed_one = normed_ref[...]
    hidden_one = normed_one * gain_one_ref[...] + shift_one_ref[...]
    hidden = hidden_one.astype(BF16)
    acc_ref[...] = hidden_one + b_down_ref[...].astype(F32)

    @pl.loop(0, shards)
    def _(shard):
        pre = nn(hidden, up_ref[shard]) + b_up_ref[shard, 0:1, :].astype(F32)
        phi = 0.5 * (1.0 + lax.erf(pre * ROOT_HALF))
        act = (pre * phi).astype(BF16)
        act_ref[shard] = act
        slope_ref[shard] = (phi + pre * INV_ROOT_TAU * jnp.exp(-0.5 * pre * pre)).astype(BF16)
        acc_ref[...] += nt(act, down_ref[shard])

    normed_two, scale_two = norm_parts(acc_ref[...])
    layer_ref[...] = (normed_two * gain_two_ref[...] + shift_two_ref[...]).astype(BF16)
    cot = cot_ref[...].astype(F32)
    grad_second = norm_back(cot, normed_two, scale_two, gain_two_ref[...])
    grad_ffn = grad_second.astype(BF16)
    vec_ref[0:1, :] = jnp.sum(cot * normed_two, 0, keepdims=True)
    vec_ref[1:2, :] = jnp.sum(cot, 0, keepdims=True)
    vec_ref[2:3, :] = jnp.sum(grad_ffn.astype(F32), 0, keepdims=True)
    acc_ref[...] = grad_second
    grad_turned = grad_ffn.T
    hidden_turned = hidden.T

    @pl.loop(0, shards)
    def _(shard):
        grad_act = nn(grad_ffn, down_ref[shard])
        grad_pre = (grad_act * slope_ref[shard].astype(F32)).astype(BF16)
        gdown_ref[shard] = nn(grad_turned, act_ref[shard]).astype(BF16)
        gup_ref[shard] = nn(hidden_turned, grad_pre).astype(BF16)
        gbias_ref[shard] = jnp.broadcast_to(
            jnp.sum(grad_pre.astype(F32), 0, keepdims=True), gbias_ref.shape[1:]
        )
        acc_ref[...] += nt(grad_pre, up_ref[shard])

    grad_hidden = acc_ref[...]
    grad_first = norm_back(grad_hidden, normed_one, scale_ref[:, 0:1], gain_one_ref[...])
    grad_low = grad_first.astype(BF16)
    first_ref[...] = grad_first
    low_ref[...] = grad_low
    vec_ref[3:4, :] = jnp.sum(grad_hidden * normed_one, 0, keepdims=True)
    vec_ref[4:5, :] = jnp.sum(grad_hidden, 0, keepdims=True)
    vec_ref[5:6, :] = jnp.sum(grad_low.astype(F32), 0, keepdims=True)
    vec_ref[6:8, :] = jnp.zeros((2, vec_ref.shape[1]), F32)


def out_back_phase(
    glow_ref, w_ref, low_ref, out_ref, denom_ref, qf_ref, gnum_ref, gden_ref, gw_ref, dnum_ref,
    dden_ref, total_ref, pairs, head_dim,
):
    rows_all = glow_ref.shape[0]
    blocks = rows_all // WINDOW
    half = LANES // 2
    ones = block_ones(LANES, head_dim).astype(BF16)
    grad_low = glow_ref[...]
    gw_ref[...] = tn(low_ref[...], grad_low).astype(gw_ref.dtype)
    for pair in range(pairs):
        cols = slice(pair * LANES, (pair + 1) * LANES)
        grad_attn = nt(grad_low, w_ref[cols, :])
        inverse = 1.0 / denom_ref[:, cols]
        grad_num = (grad_attn * inverse).astype(BF16)
        grad_den = -head_sums(grad_num.astype(F32) * out_ref[:, cols], ones)
        gnum_ref[:, cols] = grad_num
        gden_ref[:, cols] = grad_den
        total = jnp.zeros((half, LANES), F32)
        total_den = jnp.zeros((1, LANES), F32)
        for block in range(blocks):
            rows = slice(block * WINDOW, (block + 1) * WINDOW)
            query = qf_ref[rows, cols]
            num = compact(tn(query, grad_num[rows]))
            den = jnp.sum(query.astype(F32) * grad_den[rows], 0, keepdims=True)
            dnum_ref[pair * blocks + block] = num
            dden_ref[pair * blocks + block : pair * blocks + block + 1, :] = den
            total = total + num
            total_den = total_den + den
        total_ref[pair * half : (pair + 1) * half, :] = total
        total_ref[pairs * half + pair : pairs * half + pair + 1, :] = total_den


def row_grads(keys, values, num, den, ones_f32):
    upper, lower = halves(expand(num, ones_f32))
    grad_keys = nt(values, upper) + nt(values, lower) + den
    grad_values = nn(keys, upper) + nn(keys, lower)
    return grad_keys, grad_values


def band_backward_phase(
    qf_ref, ke_ref, ve_ref, line_ref, gnum_ref, gden_ref, dnum_ref, dden_ref, left_ref, right_ref,
    left_den_ref, right_den_ref, gq_ref, gk_ref, gv_ref, gline_ref, coef_grad_ref, start, stop, first_col, head_dim,
):
    blocks = qf_ref.shape[0] // WINDOW

    @pl.loop(start, stop)
    def _(pair):
        ones_f32 = block_ones(LANES, head_dim)
        cols = lanes(pair)
        out = lanes(pair - first_col)
        coef = coef_tile(line_ref, pair)
        left_coef, right_coef = far_coefs(line_ref, pair)
        gk_ref[:, out] = jnp.zeros((gk_ref.shape[0], LANES), F32)
        gv_ref[:, out] = jnp.zeros((gv_ref.shape[0], LANES), F32)
        coef_grad_ref[...] = jnp.zeros(coef_grad_ref.shape, F32)
        left_sum = jnp.zeros((1, LANES), F32)
        right_sum = jnp.zeros((1, LANES), F32)
        for block in range(blocks):
            rows = slice(block * WINDOW, (block + 1) * WINDOW)
            window = slice(block * WINDOW, (block + 3) * WINDOW)
            index = pair * blocks + block
            query = qf_ref[rows, cols]
            keys = ke_ref[window, cols]
            values = ve_ref[window, cols]
            grad_num = gnum_ref[rows, cols]
            grad_den = gden_ref[rows, cols]
            queries = both_heads(query)
            grads = both_heads(grad_num)
            weights = coef * nt(queries, keys)
            den_column = jnp.concatenate(
                [grad_den[:, 0:1], grad_den[:, LANES // 2 : LANES // 2 + 1]], 0
            )
            grad_weights = nt(grads, values) + den_column
            coef_grad_ref[...] += grad_weights * weights
            grad_scores = (coef * grad_weights).astype(BF16)
            gv_ref[window, out] += tn(weights.astype(BF16), grads)
            gk_ref[window, out] += tn(grad_scores, queries)
            grad_query = per_head(nn(grad_scores, keys))
            left, right = left_ref[index], right_ref[index]
            left_den = left_den_ref[pl.ds(index, 1), :]
            right_den = right_den_ref[pl.ds(index, 1), :]
            upper, lower = halves(expand(left_coef * left + right_coef * right, ones_f32))
            den_far = left_coef * left_den + right_coef * right_den
            grad_query = grad_query + nt(grad_num, upper) + nt(grad_num, lower) + grad_den * den_far
            gq_ref[rows, cols] = grad_query
            dnum = dnum_ref[index]
            dden = dden_ref[pl.ds(index, 1), :]
            left_sum = left_sum + jnp.sum(dnum * left, 0, keepdims=True) + dden * left_den
            right_sum = right_sum + jnp.sum(dnum * right, 0, keepdims=True) + dden * right_den
        for edge, block, scale in ((0, 0, left_coef), (blocks + 1, blocks - 1, right_coef)):
            rows = slice(edge * WINDOW, (edge + 1) * WINDOW)
            index = pair * blocks + block
            edge_k, edge_v = row_grads(
                ke_ref[rows, cols],
                ve_ref[rows, cols],
                scale * dnum_ref[index],
                scale * dden_ref[pl.ds(index, 1), :],
                ones_f32,
            )
            gk_ref[rows, out] -= edge_k
            gv_ref[rows, out] -= edge_v
        first = first_half((1, LANES))
        positions = lax.broadcasted_iota(jnp.int32, (1, LINE), 1)
        left_all = left_coef * left_sum
        right_all = right_coef * right_sum
        for head in range(2):
            keep = first if head == 0 else jnp.logical_not(first)
            left_one = jnp.sum(jnp.where(keep, left_all, 0.0), 1, keepdims=True)
            right_one = jnp.sum(jnp.where(keep, right_all, 0.0), 1, keepdims=True)
            line = unskew_sum(coef_grad_ref[head * WINDOW : (head + 1) * WINDOW, :])
            line = line + jnp.where(positions == 0, left_one, 0.0)
            line = line + jnp.where(positions == LINE - 2, right_one, 0.0)
            gline_ref[pl.ds(2 * pair + head, 1), :] = line


def key_back_phase(
    kf_ref, v_ref, line_ref, dnum_ref, dden_ref, past_ref, future_ref, low_in_ref, high_in_ref,
    gk_ref, gv_ref, pairs, start, stop, head_dim,
):
    blocks = kf_ref.shape[0] // WINDOW
    half = LANES // 2

    @pl.loop(start, stop)
    def _(pair):
        ones_f32 = block_ones(LANES, head_dim)
        cols = lanes(pair)
        left_coef, right_coef = far_coefs(line_ref, pair)
        state_rows = pl.ds(pl.multiple_of(pair * half, half), half)
        den_row = pl.ds(pairs * half + pair, 1)
        nums = [dnum_ref[pair * blocks + block] for block in range(blocks)]
        dens = [dden_ref[pl.ds(pair * blocks + block, 1), :] for block in range(blocks)]
        for block in range(blocks):
            num_left, den_left = future_ref[state_rows, :], future_ref[den_row, :]
            num_right, den_right = past_ref[state_rows, :], past_ref[den_row, :]
            for other in range(blocks):
                if other >= block + 2:
                    num_left, den_left = num_left + nums[other], den_left + dens[other]
                if other <= block - 2:
                    num_right, den_right = num_right + nums[other], den_right + dens[other]
            rows = slice(block * WINDOW, (block + 1) * WINDOW)
            outer = slice((block + 1) * WINDOW, (block + 2) * WINDOW)
            far_k, far_v = row_grads(
                kf_ref[rows, cols],
                v_ref[rows, cols],
                left_coef * num_left + right_coef * num_right,
                left_coef * den_left + right_coef * den_right,
                ones_f32,
            )
            if block == 0:
                far_k = far_k + low_in_ref[0, :, cols].astype(F32)
                far_v = far_v + low_in_ref[1, :, cols].astype(F32)
            if block == blocks - 1:
                far_k = far_k + high_in_ref[0, :, cols].astype(F32)
                far_v = far_v + high_in_ref[1, :, cols].astype(F32)
            gk_ref[outer, cols] += far_k
            gv_ref[outer, cols] += far_v


def qkv_back_phase(
    turned_ref, w_ref, omega_ref, q_ref, k_ref, qf_ref, kf_ref, gq_ref, gk_ref, gv_ref, gtok_ref, parts_ref,
    small_ref, group, head_dim,
):
    width, rows_all = turned_ref.shape
    own = slice(WINDOW, WINDOW + rows_all)
    ones = block_ones(CHUNK, head_dim).astype(BF16)
    factor = head_dim ** (-0.25) / SPREAD
    cols = slice(group * CHUNK, (group + 1) * CHUNK)
    omega = omega_ref[group]
    lows = []
    total = gtok_ref[...]
    for part, low_ref, feat_ref, grad in (
        (0, q_ref, qf_ref, gq_ref[:, cols]), (1, k_ref, kf_ref, gk_ref[own, cols]), (2, None, None, gv_ref[own, cols]),
    ):
        if part < 2:
            inner_up, inner_low = halves(grad * feat_ref[:, cols].astype(F32))
            projected = (nt(inner_up, omega) + nt(inner_low, omega)) * factor
            sums = nn(inner_up, ones) + nn(inner_low, ones)
            grad = projected - sums * head_dim ** (-0.5) * low_ref[:, cols].astype(F32)
        low = grad.astype(BF16)
        lows.append(low)
        total = total + nt(low, w_ref[:, part * width + group * CHUNK : part * width + (group + 1) * CHUNK])
    gtok_ref[...] = total
    joined = jnp.concatenate(lows, 1)
    small_ref[8 + group : 9 + group, :] = jnp.sum(joined.astype(F32), 0, keepdims=True)
    parts_ref[:, (group + 1) * width : (group + 2) * width] = nn(turned_ref[...], joined).astype(parts_ref.dtype)


def table_phase(gline_ref, bucket_ref, buckets):
    one_hot = jnp.where(
        lax.broadcasted_iota(jnp.int32, (buckets, LINE), 0) == bucket_ref[...].astype(jnp.int32), 1.0, 0.0
    )
    return lax.dot_general(
        gline_ref[...],
        one_hot,
        (((1,), (1,)), ((), ())),
        precision=lax.Precision.HIGHEST,
        preferred_element_type=F32,
    )


MESH = pl.DeviceIdType.MESH


def guarded(when, action):
    if when is None:
        action()
    else:
        pl.when(when)(action)


class Place:
    def __init__(self, shards):
        self.row, self.seq = lax.axis_index("row"), lax.axis_index("seq")
        self.count_b = 2
        self.count_a = shards // self.count_b
        self.shards = shards
        self.x, self.core = self.row // 2, self.row % 2
        self.a, self.b = self.seq // self.count_b, self.seq % self.count_b
        self.is_first, self.is_last = self.seq == 0, self.seq == shards - 1
        self.not_first, self.not_last = self.seq > 0, self.seq < shards - 1

    def at(self, x=None, core=None, a=None, b=None):
        x = self.x if x is None else x
        core = self.core if core is None else core
        a = self.a if a is None else a
        b = self.b if b is None else b
        return (x * 2 + core, a * self.count_b + b)

    def beside(self, seq):
        return (self.row, seq)

    def shard(self, offset):
        return lax.rem(self.a + offset, self.count_a)

    def nearest(self, step):
        orders = []
        for a in range(self.count_a):
            orders.append(sorted(range(self.count_a), key=lambda other: (abs(other - a), other)))
        index = jnp.int32(orders[0][step])
        for a in range(1, self.count_a):
            index = jnp.where(self.a == a, orders[a][step], index)
        return index


class Sends:
    def __init__(self):
        self.started = []

    def send(self, src, dst, send_sem, recv_sem, device, when=None):
        copy = pltpu.make_async_remote_copy(
            src_ref=src, dst_ref=dst, send_sem=send_sem, recv_sem=recv_sem, device_id=device,
            device_id_type=MESH,
        )
        guarded(when, copy.start)
        self.started.append((when, copy))

    def drain(self):
        for when, copy in self.started:
            guarded(when, copy.wait_send)
        self.started = []


def arrive(dst, sem, device, when=None):
    copy = pltpu.make_async_remote_copy(
        src_ref=dst, dst_ref=dst, send_sem=sem, recv_sem=sem, device_id=device, device_id_type=MESH
    )
    guarded(when, copy.wait_recv)


class WeightGather:
    def __init__(self, place, sends, mats, middle, sems):
        self.place, self.sends, self.mats, self.mid = place, sends, mats, middle
        self.z_send, self.z_recv, self.y_send, self.y_recv, self.x_send, self.x_recv, self.c_send, self.c_recv = sems
        self.side = (mats.shape[3] - middle) // 2

    def outer(self, a, b, x, core=None):
        core = self.place.core if core is None else core
        start = pl.multiple_of(x * (self.side + self.mid), 16)
        return self.mats.at[core, a, b, pl.ds(start, self.side), :]

    def both(self, a, b, core=None):
        core = self.place.core if core is None else core
        kinds = [(0, self.outer(a, b, self.place.x, core))]
        if self.mid:
            kinds.append((1, self.mats.at[core, a, b, pl.ds(self.side, self.mid), :]))
        return kinds

    def column(self, column):
        return 1 - self.place.b if column else self.place.b

    def rounds(self, step):
        p = self.place
        if step == 0:
            return [(p.a, None, (1, -1))]
        last = p.count_a - 1
        return [
            (jnp.maximum(p.a - step, 0), p.a - step >= 0, (1,)),
            (jnp.minimum(p.a + step, last), p.a + step <= last, (-1,)),
        ]

    def along_a(self, step, wanted):
        p = self.place
        for a, there, moves in self.rounds(step):
            for kind, here in self.both(a, p.b):
                if kind not in wanted:
                    continue
                if step > 0:
                    arrive(here, self.z_recv.at[kind, a], p.at(), there)
                for move in moves:
                    target = p.a + move
                    ok = target <= p.count_a - 1 if move > 0 else target >= 0
                    if there is not None:
                        ok = jnp.logical_and(ok, there)
                    self.sends.send(
                        here, here, self.z_send.at[(1 - move) // 2, kind, a], self.z_recv.at[kind, a],
                        p.at(a=jnp.clip(target, 0, p.count_a - 1)), ok,
                    )
                if step > 0:
                    self.pass_on(kind, 0, a, here, there)

    def across(self, step):
        p = self.place
        for a, there, _ in self.rounds(step):
            for kind, here in self.both(a, p.b):
                self.sends.send(
                    here, here, self.y_send.at[kind, a], self.y_recv.at[kind, a], p.at(b=1 - p.b), there
                )

    def pass_on(self, kind, column, a, here, when=None):
        p = self.place
        if kind == 0:
            self.sends.send(
                here, here, self.x_send.at[column, a], self.x_recv.at[column, a], p.at(x=1 - p.x), when
            )
        self.sends.send(
            here, here, self.c_send.at[kind, column, a], self.c_recv.at[kind, column, a], p.at(core=1 - p.core), when
        )

    def along_b(self, step, wanted):
        p = self.place
        a = p.nearest(step)
        for kind, here in self.both(a, 1 - p.b):
            if kind in wanted:
                arrive(here, self.y_recv.at[kind, a], p.at())
                self.pass_on(kind, 1, a, here)

    def along_x(self, step, column):
        p = self.place
        a = p.nearest(step)
        here = self.outer(a, self.column(column), 1 - p.x)
        arrive(here, self.x_recv.at[column, a], p.at())
        self.sends.send(
            here, here, self.c_send.at[2, column, a], self.c_recv.at[2, column, a], p.at(core=1 - p.core)
        )

    def finish(self, step, column):
        p = self.place
        a = p.nearest(step)
        other, b = 1 - p.core, self.column(column)
        for kind, here in self.both(a, b, other) + [(2, self.outer(a, b, 1 - p.x, other))]:
            arrive(here, self.c_recv.at[kind, column, a], p.at())


def gather_sems(count_a):
    dma = pltpu.SemaphoreType.DMA
    return [
        dma((2, 2, count_a)), dma((2, count_a)), dma((2, count_a)), dma((2, count_a)),
        dma((2, count_a)), dma((2, count_a)), dma((3, 2, count_a)), dma((3, 2, count_a)),
    ]


class StateSums:
    def __init__(self, place, sends, buffers, sems):
        self.place, self.sends = place, sends
        self.own, self.peer, self.pair, self.far, self.sums, self.land = buffers
        self.y_send, self.y_recv, self.z_send, self.z_recv = sems
        self.half = self.pair.shape[0]

    def rows(self, b):
        return pl.ds(pl.multiple_of(b * self.half, 16), self.half)

    def start(self, message_ref):
        p = self.place
        self.own[...] = message_ref[...]
        self.sends.send(self.own, self.peer, self.y_send.at[0], self.y_recv.at[0], p.at(b=1 - p.b))

    def along_a(self):
        p = self.place
        arrive(self.peer, self.y_recv.at[0], p.at())
        mine = self.rows(p.b)
        self.pair[...] = (self.own[mine, :] + self.peer[mine, :])
        for offset in range(1, p.count_a):
            self.sends.send(
                self.pair, self.far.at[p.a], self.z_send.at[offset], self.z_recv.at[offset],
                p.at(a=p.shard(offset)),
            )

    def along_b(self):
        p = self.place
        self.far[p.a] = jnp.zeros(self.pair.shape, F32)
        for offset in range(1, p.count_a):
            source = p.shard(p.count_a - offset)
            arrive(self.far.at[source], self.z_recv.at[offset], p.at())
        for index in range(2):
            total = jnp.zeros(self.pair.shape, F32)
            for a in range(p.count_a):
                keep = a < p.a if index == 0 else a > p.a
                total = total + jnp.where(keep, 1.0, 0.0) * self.far[a]
            self.sums[index] = total
        self.sends.send(self.sums, self.land, self.y_send.at[1], self.y_recv.at[1], p.at(b=1 - p.b))

    def finish(self, before_ref, after_ref):
        p = self.place
        arrive(self.land, self.y_recv.at[1], p.at())
        for index, ref in ((0, before_ref), (1, after_ref)):
            ref[self.rows(p.b), :] = self.sums[index]
            ref[self.rows(1 - p.b), :] = self.land[index]
        peer = self.peer[...]
        before_ref[...] += jnp.where(p.b == 1, 1.0, 0.0) * peer
        after_ref[...] += jnp.where(p.b == 0, 1.0, 0.0) * peer


def sums_sems(count_a):
    dma = pltpu.SemaphoreType.DMA
    return [dma((2,)), dma((2,)), dma((count_a,)), dma((count_a,))]


class GradScatter:
    def __init__(self, place, sends, grads, total, middle, lands, sems):
        self.place, self.sends, self.grads, self.total, self.mid = place, sends, grads, total, middle
        self.core_land, self.stage, self.x_land, self.y_land, self.z_land, self.last_land = lands
        (self.copy, self.c_send, self.c_recv, self.x_send, self.x_recv, self.y_send, self.y_recv, self.z_send,
         self.z_recv, self.l_send, self.l_recv) = sems
        self.side = (grads.shape[3] - middle) // 2

    def outer(self, x):
        return pl.ds(pl.multiple_of(x * (self.side + self.mid), 16), self.side)

    def window(self):
        return pl.ds(pl.multiple_of(self.place.x * self.side, 16), self.side + self.mid)

    def column(self, column):
        return 1 - self.place.b if column else self.place.b

    def start(self, offset, column):
        p = self.place
        item = (offset, column)
        self.sends.send(
            self.grads.at[1 - p.core, p.shard(offset), self.column(column)], self.core_land.at[item],
            self.c_send.at[item], self.c_recv.at[item], p.at(core=1 - p.core),
        )

    def add(self, ref, land):
        ref[...] = (ref[...].astype(F32) + land[...].astype(F32)).astype(BF16)

    def staged(self, offset, column):
        item = (offset, column)
        return pltpu.make_async_copy(self.core_land.at[item], self.stage.at[1 - column], self.copy.at[item])

    def fetch(self, offset, column):
        item = (offset, column)
        arrive(self.core_land.at[item], self.c_recv.at[item], self.place.at())
        self.staged(offset, column).start()

    def chip(self, offset, column):
        p = self.place
        item = (offset, column)
        self.staged(offset, column).wait()
        here = self.grads.at[p.core, p.shard(offset), self.column(column)]
        self.add(here, self.stage.at[1 - column])
        self.sends.send(
            here.at[self.outer(1 - p.x), :], self.x_land.at[item], self.x_send.at[item], self.x_recv.at[item],
            p.at(x=1 - p.x),
        )

    def along_x(self, offset, column):
        p = self.place
        item = (offset, column)
        here = self.grads.at[p.core, p.shard(offset), self.column(column)]
        arrive(self.x_land.at[item], self.x_recv.at[item], p.at())
        self.add(here.at[self.outer(p.x), :], self.x_land.at[item])
        if column:
            self.sends.send(
                here.at[self.window(), :], self.y_land.at[offset], self.y_send.at[offset], self.y_recv.at[offset],
                p.at(b=1 - p.b),
            )

    def along_b(self, offset):
        p = self.place
        a = p.shard(offset)
        arrive(self.y_land.at[offset], self.y_recv.at[offset], p.at())
        mine = self.grads.at[p.core, a, p.b, self.window(), :]
        self.add(mine, self.y_land.at[offset])
        if offset:
            self.sends.send(
                mine, self.z_land.at[offset - 1], self.z_send.at[offset], self.z_recv.at[offset], p.at(a=a)
            )

    def along_a(self):
        p = self.place
        own = self.grads.at[p.core, p.a, p.b]
        mine = own.at[self.window(), :]
        total = mine[...].astype(F32)
        for offset in range(1, p.count_a):
            arrive(self.z_land.at[offset - 1], self.z_recv.at[offset], p.at())
            total = total + self.z_land[offset - 1].astype(F32)
        mine[...] = total.astype(BF16)
        middle = pl.ds(self.side, self.mid)
        outer = self.outer(p.x)
        self.total[p.core, outer, :] = self.grads[p.core, p.a, p.b, outer, :]
        self.sends.send(
            own.at[middle, :], self.last_land, self.l_send.at[0], self.l_recv.at[0], p.at(x=1 - p.x)
        )
        here = self.total.at[p.core, outer, :]
        self.sends.send(here, here, self.l_send.at[1], self.l_recv.at[1], p.at(x=1 - p.x))

    def last_x(self):
        p = self.place
        middle = pl.ds(self.side, self.mid)
        arrive(self.last_land, self.l_recv.at[0], p.at())
        self.total[p.core, middle, :] = (
            self.grads[p.core, p.a, p.b, middle, :].astype(F32) + self.last_land[...].astype(F32)
        ).astype(BF16)
        arrive(self.total.at[p.core, self.outer(1 - p.x), :], self.l_recv.at[1], p.at())
        here = self.total.at[p.core]
        self.sends.send(here, here, self.l_send.at[2], self.l_recv.at[2], p.at(core=1 - p.core))

    def finish(self):
        arrive(self.total.at[1 - self.place.core], self.l_recv.at[2], self.place.at())


def scatter_sems(count_a):
    dma = pltpu.SemaphoreType.DMA
    return [dma((count_a, 2)) for _ in range(5)] + [dma((count_a,)) for _ in range(4)] + [dma((3,)), dma((3,))]


class AllReduce:
    def __init__(self, place, sends, parts, result, lands, done, orders, sems):
        self.place, self.sends, self.parts, self.result = place, sends, parts, result
        self.core_land, self.staged, self.one_land, self.two_land, self.a_land = lands
        self.done, self.orders = done, orders
        (self.s_send, self.s_recv, self.z_send, self.z_recv, self.g_send, self.g_recv, self.zg_send, self.zg_recv,
         self.copy) = sems
        self.half = result.shape[1] // 2
        self.quarter = self.half // 2
        self.slim = self.quarter // place.count_a

    def ways(self, index):
        p = self.place
        other_x, other_b = p.at(x=1 - p.x), p.at(b=1 - p.b)
        straight = {"x": True, "b": False}.get(self.orders[index], p.core == 0)
        one = tuple(jnp.where(straight, u, w) for u, w in zip(other_x, other_b))
        two = tuple(jnp.where(straight, w, u) for u, w in zip(other_x, other_b))
        return jnp.where(straight, p.x, p.b), jnp.where(straight, p.b, p.x), one, two

    def half_rows(self, core):
        return pl.ds(pl.multiple_of(core * self.half, self.half), self.half)

    def quarter_rows(self, one):
        start = self.place.core * self.half + one * self.quarter
        return pl.ds(pl.multiple_of(start, self.quarter), self.quarter)

    def slim_rows(self, one, a):
        start = self.place.core * self.half + one * self.quarter + a * self.slim
        return pl.ds(pl.multiple_of(start, self.slim), self.slim)

    def push(self, index):
        p = self.place
        blocks = pl.ds(2 * index, 2)
        self.sends.send(
            self.parts.at[blocks, self.half_rows(1 - p.core), :], self.core_land.at[blocks],
            self.s_send.at[0, index], self.s_recv.at[0, index], p.at(core=1 - p.core),
        )

    def add(self, ref, land):
        ref[...] = (ref[...].astype(F32) + land[...].astype(F32)).astype(BF16)

    def stage(self, index, number):
        p = self.place
        one, two, one_device, two_device = self.ways(index)
        blocks = pl.ds(2 * index, 2)
        mine, other = 2 * index + two, 2 * index + 1 - two
        parts, result = self.parts, self.result
        if number == 0:
            land = self.core_land.at[blocks]
            arrive(land, self.s_recv.at[0, index], p.at())
            pltpu.make_async_copy(land, self.staged, self.copy.at[index]).start()
        elif number == 1:
            pltpu.make_async_copy(self.core_land.at[blocks], self.staged, self.copy.at[index]).wait()
            self.add(parts.at[blocks, self.half_rows(p.core), :], self.staged)
            self.sends.send(
                parts.at[blocks, self.quarter_rows(1 - one), :], self.one_land.at[blocks],
                self.s_send.at[1, index], self.s_recv.at[1, index], one_device,
            )
        elif number == 2:
            land = self.one_land.at[blocks]
            arrive(land, self.s_recv.at[1, index], p.at())
            self.add(parts.at[blocks, self.quarter_rows(one), :], land)
            self.sends.send(
                parts.at[other, self.quarter_rows(one), :], self.two_land.at[index],
                self.s_send.at[2, index], self.s_recv.at[2, index], two_device,
            )
        elif number == 3:
            land = self.two_land.at[index]
            arrive(land, self.s_recv.at[2, index], p.at())
            self.add(parts.at[mine, self.quarter_rows(one), :], land)
            for offset in range(1, p.count_a):
                a = p.shard(offset)
                self.sends.send(
                    parts.at[mine, self.slim_rows(one, a), :], self.a_land.at[index, offset - 1],
                    self.z_send.at[index, offset], self.z_recv.at[index, offset], p.at(a=a),
                )
        elif number == 4:
            rows = self.slim_rows(one, p.a)
            total = parts[mine, rows, :].astype(F32)
            for offset in range(1, p.count_a):
                arrive(self.a_land.at[index, offset - 1], self.z_recv.at[index, offset], p.at())
                total = total + self.a_land[index, offset - 1].astype(F32)
            self.done[index] = total.astype(BF16)
            here = result.at[mine, rows, :]
            pltpu.make_async_copy(self.done.at[index], here, self.copy.at[index]).start()
            for offset in range(1, p.count_a):
                self.sends.send(
                    self.done.at[index], here, self.zg_send.at[index, offset], self.zg_recv.at[index, offset],
                    p.at(a=p.shard(offset)),
                )
        elif number == 5:
            pltpu.make_async_copy(
                self.done.at[index], result.at[mine, self.slim_rows(one, p.a), :], self.copy.at[index]
            ).wait()
            for offset in range(1, p.count_a):
                a = lax.rem(p.a + p.count_a - offset, p.count_a)
                arrive(result.at[mine, self.slim_rows(one, a), :], self.zg_recv.at[index, offset], p.at())
            here = result.at[mine, self.quarter_rows(one), :]
            self.sends.send(here, here, self.g_send.at[0, index], self.g_recv.at[0, index], two_device)
        elif number == 6:
            arrive(result.at[other, self.quarter_rows(one), :], self.g_recv.at[0, index], p.at())
            here = result.at[blocks, self.quarter_rows(one), :]
            self.sends.send(here, here, self.g_send.at[1, index], self.g_recv.at[1, index], one_device)
        elif number == 7:
            arrive(result.at[blocks, self.quarter_rows(1 - one), :], self.g_recv.at[1, index], p.at())
            here = result.at[blocks, self.half_rows(p.core), :]
            self.sends.send(here, here, self.g_send.at[2, index], self.g_recv.at[2, index], p.at(core=1 - p.core))
        elif number == 8:
            arrive(result.at[blocks, self.half_rows(1 - p.core), :], self.g_recv.at[2, index], p.at())


def reduce_sems(chunks, count_a):
    dma = pltpu.SemaphoreType.DMA
    return [
        dma((3, chunks)), dma((3, chunks)), dma((chunks, count_a)), dma((chunks, count_a)),
        dma((3, chunks)), dma((3, chunks)), dma((chunks, count_a)), dma((chunks, count_a)), dma((chunks,)),
    ]


class SmallReduce:
    def __init__(self, place, sends, held, land, sems):
        self.place, self.sends, self.held, self.land = place, sends, held, land
        self.out_sem, self.in_sem = sems
        p = place
        self.devices = [p.at(core=1 - p.core), p.at(x=1 - p.x), p.at(b=1 - p.b)]

    def send(self, step):
        if step < 3:
            self.sends.send(
                self.held.at[step], self.land.at[step], self.out_sem.at[step], self.in_sem.at[step],
                self.devices[step],
            )
            return
        p = self.place
        for offset in range(1, p.count_a):
            self.sends.send(
                self.held.at[3], self.land.at[3 + offset], self.out_sem.at[3 + offset],
                self.in_sem.at[3 + offset], p.at(a=p.shard(offset)),
            )

    def receive(self, step):
        p = self.place
        if step < 3:
            arrive(self.land.at[step], self.in_sem.at[step], p.at())
            self.held[step + 1] = self.held[step] + self.land[step]
            return
        for offset in range(1, p.count_a):
            arrive(self.land.at[3 + offset], self.in_sem.at[3 + offset], p.at())
        self.land[3] = self.held[3]

    def total(self):
        p = self.place
        total = self.land[3 + lax.rem(p.a, p.count_a)]
        for a in range(1, p.count_a):
            total = total + self.land[3 + lax.rem(p.a + p.count_a - a, p.count_a)]
        return total


def halo_phase(x_ref, w_ref, b_ref, omega_ref, k_ref, kv_ref, place, head_dim):
    rows_ext, width = x_ref.shape
    low, high = slice(0, WINDOW), slice(rows_ext - WINDOW, rows_ext)
    x = jnp.concatenate([x_ref[low, :], x_ref[high, :]], 0)
    ones = block_ones(CHUNK, head_dim).astype(BF16)
    factor = head_dim ** (-0.25) / SPREAD
    row = lax.broadcasted_iota(jnp.int32, (2 * WINDOW, 1), 0)
    inside = jnp.logical_or(
        jnp.logical_and(row < WINDOW, place.seq > 0),
        jnp.logical_and(row >= WINDOW, place.seq < place.shards - 1),
    )
    for part in (1, 2):
        for chunk in range(width // CHUNK):
            cols = slice(chunk * CHUNK, (chunk + 1) * CHUNK)
            wide = slice(part * width + chunk * CHUNK, part * width + (chunk + 1) * CHUNK)
            value = (nn(x, w_ref[:, wide]) + b_ref[part][:, cols]).astype(BF16)
            if part == 1:
                k_ref[low, cols], k_ref[high, cols] = value[:WINDOW], value[WINDOW:]
                widened = value.astype(F32)
                half_norm = head_sums(widened * widened, ones) * (0.5 * head_dim ** (-0.5))
                value = jnp.exp(nn(value, omega_ref[chunk]) * factor - half_norm) * head_dim ** (-0.5)
            value = jnp.where(inside, value.astype(F32), 0.0).astype(BF16)
            kv_ref[part - 1, low, cols], kv_ref[part - 1, high, cols] = value[:WINDOW], value[WINDOW:]


def ffn_forward_shard(hidden_ref, mats, a, b, shard, bias_ref, pool, acc_ref):
    rows = hidden_ref.shape[0]
    pre = nn(hidden_ref[...], mats[0, a, b]) + bias_ref[shard, 0:1, :]
    phi = 0.5 * (1.0 + lax.erf(pre * ROOT_HALF))
    act = (pre * phi).astype(BF16)
    pool[shard, 0:rows, :] = act
    pool[shard, rows : 2 * rows, :] = (phi + pre * INV_ROOT_TAU * jnp.exp(-0.5 * pre * pre)).astype(BF16)
    acc_ref[...] += nt(act, mats[1, a, b])


def ffn_backward_shard(grad_ref, grad_turned_ref, hidden_turned_ref, mats, a, b, shard, pool, acc_ref, gbias_ref):
    rows = grad_ref.shape[0]
    grad_act = nn(grad_ref[...], mats[1, a, b])
    grad_pre = (grad_act * pool[shard, rows : 2 * rows, :].astype(F32)).astype(BF16)
    gbias_ref[shard] = jnp.broadcast_to(
        jnp.sum(grad_pre.astype(F32), 0, keepdims=True), gbias_ref.shape[1:]
    )
    acc_ref[...] += nt(grad_pre, mats[0, a, b])
    mats[1, a, b] = nn(grad_turned_ref[...], pool[shard, 0:rows, :]).astype(BF16)
    mats[0, a, b] = nn(hidden_turned_ref[...], grad_pre).astype(BF16)


def row_blocks(rows, body, size=CHUNK):
    @pl.loop(0, rows // size)
    def _(index):
        body(pl.ds(pl.multiple_of(index * size, size), size))


def hidden_phase(
    x_ref, low_ref, w_ref, b_ref, gain_ref, shift_ref, b_down_ref, normed_refs, scale_ref, hidden_ref, turned_ref, acc_ref
):
    def body(rows):
        first_sum = x_ref[rows, :].astype(F32) + nn(low_ref[rows, :], w_ref[...]) + b_ref[...].astype(F32)
        normed, inv_scale = norm_parts(first_sum)
        normed_refs[0][rows, :], normed_refs[1][rows, :], normed_refs[2][rows, :] = jnp.split(normed, 3, 1)
        scale_ref[rows, :] = jnp.broadcast_to(inv_scale, (first_sum.shape[0], scale_ref.shape[1]))
        hidden_one = normed * gain_ref[...] + shift_ref[...]
        hidden = hidden_one.astype(BF16)
        hidden_ref[rows, :] = hidden
        turned_ref[:, rows] = hidden.T
        acc_ref[rows, :] = hidden_one + b_down_ref[...].astype(F32)

    row_blocks(x_ref.shape[0], body)


def middle_phase(acc_ref, cot_ref, gain_two_ref, shift_two_ref, grad_ref, grad_turned_ref, vec_ref):
    def body(rows):
        normed_two, scale_two = norm_parts(acc_ref[rows, :])
        cot = cot_ref[rows, :].astype(F32)
        cot_ref[rows, :] = (normed_two * gain_two_ref[...] + shift_two_ref[...]).astype(BF16)
        grad_second = norm_back(cot, normed_two, scale_two, gain_two_ref[...])
        grad_ffn = grad_second.astype(BF16)
        vec_ref[0:1, :] += jnp.sum(cot * normed_two, 0, keepdims=True)
        vec_ref[1:2, :] += jnp.sum(cot, 0, keepdims=True)
        vec_ref[2:3, :] += jnp.sum(grad_ffn.astype(F32), 0, keepdims=True)
        acc_ref[rows, :] = grad_second
        grad_ref[rows, :] = grad_ffn
        grad_turned_ref[:, rows] = grad_ffn.T

    row_blocks(cot_ref.shape[0], body)


def first_back_phase(acc_ref, normed_refs, scale_ref, gain_one_ref, low_ref, vec_ref):
    def body(rows):
        grad_hidden = acc_ref[rows, :]
        normed = jnp.concatenate([ref[rows, :] for ref in normed_refs], 1)
        grad_first = norm_back(grad_hidden, normed, scale_ref[rows, 0:1], gain_one_ref[...])
        grad_low = grad_first.astype(BF16)
        acc_ref[rows, :] = grad_first
        low_ref[rows, :] = grad_low
        vec_ref[3:4, :] += jnp.sum(grad_hidden * normed, 0, keepdims=True)
        vec_ref[4:5, :] += jnp.sum(grad_hidden, 0, keepdims=True)
        vec_ref[5:6, :] += jnp.sum(grad_low.astype(F32), 0, keepdims=True)

    row_blocks(low_ref.shape[0], body)


def attn_back_phase(glow_ref, w_ref, out_ref, denom_ref, low_ref, qf_ref, dnum_ref, dden_ref, total_ref, pairs, head_dim):
    rows_all = glow_ref.shape[0]
    blocks = rows_all // WINDOW
    half = LANES // 2
    ones = block_ones(CHUNK, head_dim).astype(BF16)
    grad_low = glow_ref[...]
    per_chunk = CHUNK // LANES
    for chunk in range(pairs // per_chunk):
        wide = slice(chunk * CHUNK, (chunk + 1) * CHUNK)
        grad_attn = nt(grad_low, w_ref[wide, :])
        grad_num = (grad_attn / denom_ref[:, wide]).astype(BF16)
        low_ref[:, wide] = grad_num
        denom_ref[:, wide] = -head_sums(grad_num.astype(F32) * out_ref[:, wide], ones)
        for pair in range(chunk * per_chunk, (chunk + 1) * per_chunk):
            cols = slice(pair * LANES, (pair + 1) * LANES)
            total = jnp.zeros((half, LANES), F32)
            total_den = jnp.zeros((1, LANES), F32)
            for block in range(blocks):
                rows = slice(block * WINDOW, (block + 1) * WINDOW)
                query = qf_ref[rows, cols]
                num = compact(tn(query, low_ref[rows, cols]))
                den = jnp.sum(query.astype(F32) * denom_ref[rows, cols], 0, keepdims=True)
                dnum_ref[pair * blocks + block] = num
                dden_ref[pair * blocks + block : pair * blocks + block + 1, :] = den
                total = total + num
                total_den = total_den + den
            total_ref[pair * half : (pair + 1) * half, :] = total
            total_ref[pairs * half + pair : pairs * half + pair + 1, :] = total_den


def far_back_phase(ke_ref, ve_ref, line_ref, dnum_ref, dden_ref, past_ref, future_ref, gk_ref, gv_ref, pairs, start, stop, first_col, head_dim):
    blocks = ke_ref.shape[0] // WINDOW - 2
    half = LANES // 2

    @pl.loop(start, stop)
    def _(pair):
        ones_f32 = block_ones(LANES, head_dim)
        cols = lanes(pair)
        out = lanes(pair - first_col)
        left_coef, right_coef = far_coefs(line_ref, pair)
        state_rows = pl.ds(pl.multiple_of(pair * half, half), half)
        den_row = pl.ds(pairs * half + pair, 1)
        nums = [dnum_ref[pair * blocks + block] for block in range(blocks)]
        dens = [dden_ref[pl.ds(pair * blocks + block, 1), :] for block in range(blocks)]
        for block in range(blocks):
            num_left, den_left = future_ref[state_rows, :], future_ref[den_row, :]
            num_right, den_right = past_ref[state_rows, :], past_ref[den_row, :]
            for other in range(blocks):
                if other >= block + 2:
                    num_left, den_left = num_left + nums[other], den_left + dens[other]
                if other <= block - 2:
                    num_right, den_right = num_right + nums[other], den_right + dens[other]
            rows = slice((block + 1) * WINDOW, (block + 2) * WINDOW)
            far_k, far_v = row_grads(
                ke_ref[rows, cols],
                ve_ref[rows, cols],
                left_coef * num_left + right_coef * num_right,
                left_coef * den_left + right_coef * den_right,
                ones_f32,
            )
            gk_ref[rows, out] += far_k
            gv_ref[rows, out] += far_v


def qkv_grad_phase(
    turned_ref, w_ref, omega_ref, q_ref, k_ref, qf_ref, kf_ref, gq_ref, gk_ref, gv_ref, grads_ref, parts, small_ref,
    group, wanted, place, head_dim,
):
    width, rows_ext = turned_ref.shape
    rows_all = rows_ext - 2 * WINDOW
    own = slice(WINDOW, WINDOW + rows_all)
    ones = block_ones(CHUNK, head_dim).astype(BF16)
    factor = head_dim ** (-0.25) / SPREAD
    cols = slice(group * CHUNK, (group + 1) * CHUNK)
    omega = omega_ref[group]
    base = group * 3 * CHUNK
    block = parts.shape[2]
    for part, low_ref, feat_ref in ((0, q_ref, qf_ref), (1, k_ref, kf_ref), (2, None, None)):
        if part not in wanted:
            continue
        out = slice(part * CHUNK, (part + 1) * CHUNK)

        def body(rows):
            if part == 0:
                grad = gq_ref[rows, cols]
            else:
                grad = (gk_ref if part == 1 else gv_ref)[rows, :]
            if part < 2:
                inner_up, inner_low = halves(grad * feat_ref[rows, cols].astype(F32))
                projected = (nt(inner_up, omega) + nt(inner_low, omega)) * factor
                sums = nn(inner_up, ones) + nn(inner_low, ones)
                grad = projected - sums * head_dim ** (-0.5) * low_ref[rows, cols].astype(F32)
            if part > 0:
                row = lax.broadcasted_iota(jnp.int32, (CHUNK, 1), 0) + rows.start
                inside = jnp.logical_and(
                    jnp.logical_or(row >= WINDOW, place.seq > 0),
                    jnp.logical_or(row < rows_ext - WINDOW, place.seq < place.shards - 1),
                )
                grad = jnp.where(inside, grad, 0.0)
            low = grad.astype(BF16)
            if part == 0:
                rows = pl.ds(pl.multiple_of(rows.start + WINDOW, WINDOW), CHUNK)
            grads_ref[rows, out] = low
            small_ref[6 + group : 7 + group, out] += jnp.sum(low.astype(F32), 0, keepdims=True)

        row_blocks(rows_all if part == 0 else rows_ext, body)
        rows = own if part == 0 else slice(0, rows_ext)
        weight = nn(turned_ref[:, rows], grads_ref[rows, out]).astype(BF16)
        start = width + base + part * CHUNK
        done = 0
        while done < CHUNK:
            index, at = (start + done) // block, (start + done) % block
            size = min(CHUNK - done, block - at)
            parts[index, 0:width, at : at + size] = weight[:, done : done + size]
            done += size


def table_grads(gline_ref, bucket_ref, buckets, small_ref):
    heads = gline_ref.shape[0]
    head = lax.broadcasted_iota(jnp.int32, (heads, LANES), 0)
    lane_bucket = lax.broadcasted_iota(jnp.int32, (LANES, LINE), 0)
    total = jnp.zeros((heads, LANES), F32)
    per_row = LANES // buckets
    for place in range(per_row):
        one_hot = jnp.where(lane_bucket - place * buckets == bucket_ref[...].astype(jnp.int32), 1.0, 0.0)
        sums = lax.dot_general(
            gline_ref[...], one_hot, (((1,), (1,)), ((), ())), precision=lax.Precision.HIGHEST,
            preferred_element_type=F32,
        )
        total = total + jnp.where(head % per_row == place, sums, 0.0)
    for index in range(heads // per_row):
        small_ref[13 + index : 14 + index, 0:LANES] = jnp.sum(
            total[index * per_row : (index + 1) * per_row], 0, keepdims=True
        )


def layer_kernel(pairs, head_dim, buckets, shards, *refs):
    x_h, cot_h, up_h, down_h, w_h, codes_r, table_r, wo_h = refs[:8]
    vectors, bias_up_r, buckets_r = refs[8:15], refs[15], refs[16]
    layer_h, gtok_h, total_r, small_r, result_h, core_h, ac_h = refs[17:24]
    (x_r, q_r, k_r, qf_r, kv_r, line_r, num_r, den_r, tot_r, biases, before_r, after_r, left_r, right_r,
     lden_r, rden_r, attn_r, denom_r, low_r, scale_r, hidden_r, turned_r, cot_r, acc_r,
     mats, pool, bias_r, gbias_r, gk_r, gv_r, gline_r, cg_r, gqkv_r) = refs[24:57]
    stage_r, xl_r, yl_r, zl_r, ll_r = refs[57:62]
    ac_r, ao_r, at_r, aa_r, done_r, held_r, land_r = refs[62:69]
    sum_buffers, sum_two_buffers = refs[69:75], refs[75:81]
    sems = refs[81:]
    all_rows = pl.ds(0, q_r.shape[0])
    normed_r = (gk_r.at[0, all_rows], gk_r.at[1, all_rows], gv_r.at[0, all_rows])
    gturned_r = gqkv_r.at[:, all_rows]
    edge_r, tail_r = cot_r.at[pl.ds(0, 2 * WINDOW)], cot_r.at[pl.ds(2 * WINDOW, 2 * WINDOW)]
    w_sems, s_sems, s2_sems, rs_sems = sems[:8], sems[8:12], sems[12:16], sems[16:27]
    ar_sems, sm_sems, bias_sems = sems[27:36], sems[36:38], sems[38:40]
    h_send, h_recv, t_send, t_recv, load_sem, w_r, wo_r, omega_r, packed_r = sems[40:]
    rows, width = q_r.shape
    half = LANES // 2
    line = [packed_r.at[pl.ds(index, 1)] for index in range(packed_r.shape[0])]
    b_r, bo_r, g1_r, s1_r, bdown_r, g2_r, s2_r = line[:3], *line[3:9]
    bup_r, bucket_r = line[9].at[:, pl.ds(0, up_h.shape[1])], line[10].at[:, pl.ds(0, LINE)]
    own = pl.ds(WINDOW, rows)
    place = Place(shards)
    sends = Sends()
    seq = place.seq
    peers = [place.beside(lax.rem(seq + o, shards)) for o in range(1, shards)]
    peers += [place.at(core=1 - place.core), place.at(x=1 - place.x)]
    barrier = pltpu.get_barrier_semaphore()
    for peer in peers:
        pl.semaphore_signal(barrier, inc=1, device_id=peer, device_id_type=MESH)
    loads = [
        pltpu.make_async_copy(src, dst, load_sem.at[i])
        for i, (src, dst) in enumerate((
            (down_h, hidden_r.at[pl.ds(0, down_h.shape[0])]), (up_h, mats.at[0, place.a, place.b]),
            (x_h, x_r.at[own]), (cot_h, cot_r), (w_h, w_r), (wo_h, wo_r),
        ))
    ]
    for load in loads:
        load.start()
    gather = WeightGather(place, sends, mats, width // 4, w_sems)
    key_sums = StateSums(place, sends, sum_buffers, s_sems)
    grad_sums = StateSums(place, sends, sum_two_buffers, s2_sems)
    scatter = GradScatter(place, sends, mats, total_r, ll_r.shape[0], (core_h, stage_r, xl_r, yl_r, zl_r, ll_r), rs_sems)
    chunks = done_r.shape[0]
    reduce = AllReduce(place, sends, pool, result_h, (ac_h, ac_r, ao_r, at_r, aa_r), done_r, "bmmm", ar_sems)
    little = SmallReduce(place, sends, held_r, land_r, sm_sems)
    to_right = place.beside(jnp.minimum(seq + 1, shards - 1))
    to_left = place.beside(jnp.maximum(seq - 1, 0))
    low_edge, high_edge = pl.ds(0, WINDOW), pl.ds(rows + WINDOW, WINDOW)

    small_r[...] = jnp.zeros(small_r.shape, F32)
    acc_r[0:WINDOW, :] = jnp.zeros((WINDOW, width), F32)
    acc_r[rows + WINDOW :, :] = jnp.zeros((WINDOW, width), F32)
    at = 0
    for vector in vectors:
        for start in range(0, vector.shape[0], width):
            packed_r[at, :] = vector[start : start + width].astype(F32)
            at += 1
    packed_r[at, 0 : bias_up_r.shape[0]] = bias_up_r[...].astype(F32)
    middle = (buckets_r.shape[0] + 1) // 2
    packed_r[at + 1, 0:LINE] = buckets_r[middle - LINE // 2 : middle + LINE // 2].astype(F32)
    omega_r[...] = jnp.zeros(omega_r.shape, BF16)
    heads, head_dim = codes_r.shape[:2]
    per_chunk = CHUNK // head_dim
    for head in range(heads):
        at = slice(head % per_chunk * head_dim, (head % per_chunk + 1) * head_dim)
        omega_r[head // per_chunk, at, at] = (codes_r[head].astype(F32) - CENTER).astype(BF16)
    loads[0].wait()
    mats[1, place.a, place.b] = hidden_r[0 : down_h.shape[0], :].T
    loads[1].wait()
    loads[2].wait()
    pl.semaphore_wait(barrier, len(peers))
    sends.send(
        x_r.at[pl.ds(rows, WINDOW)], x_r.at[low_edge], h_send.at[0], h_recv.at[0], to_right, place.not_last
    )
    sends.send(
        x_r.at[pl.ds(WINDOW, WINDOW)], x_r.at[high_edge], h_send.at[1], h_recv.at[1], to_left, place.not_first
    )
    biases[seq] = jnp.broadcast_to(bup_r[...], biases.shape[1:]).astype(BF16)
    for offset in range(1, shards):
        sends.send(
            biases.at[seq], biases.at[seq], bias_sems[0].at[offset], bias_sems[1].at[offset],
            place.beside(lax.rem(seq + offset, shards)),
        )
    gather.along_a(0, (0, 1))

    @pl.when(place.is_first)
    def _():
        x_r[0:WINDOW, :] = jnp.zeros((WINDOW, width), BF16)

    @pl.when(place.is_last)
    def _():
        x_r[rows + WINDOW :, :] = jnp.zeros((WINDOW, width), BF16)

    ke_r, ve_r = kv_r.at[0], kv_r.at[1]
    loads[4].wait()
    loads[5].wait()
    qkv_phase(
        x_r.at[own], w_r, b_r, omega_r, ((1, k_r.at[own], ke_r.at[own]), (2, ve_r.at[own], None)), head_dim
    )
    tot_r[pairs * half :, :] = jnp.zeros((tot_r.shape[0] - pairs * half, LANES), F32)
    state_phase(ke_r.at[own], ve_r.at[own], num_r, den_r, tot_r, pairs)
    key_sums.start(tot_r)
    gather.across(0)
    qkv_phase(x_r.at[own], w_r, b_r, omega_r, ((0, q_r, qf_r),), head_dim)
    line_phase(bucket_r, table_r, line_r)
    arrive(x_r.at[low_edge], h_recv.at[0], place.at(), place.not_first)
    arrive(x_r.at[high_edge], h_recv.at[1], place.at(), place.not_last)
    halo_phase(x_r, w_r, b_r, omega_r, k_r, kv_r, place, head_dim)
    third = pairs // 3

    def ffn(step, column, forward):
        a = place.nearest(step) if forward else place.shard(step)
        b = 1 - place.b if column else place.b
        shard = a * place.count_b + b
        if forward:
            ffn_forward_shard(hidden_r, mats, a, b, shard, bias_r, pool, acc)
        else:
            ffn_backward_shard(hidden_r, gturned_r, hidden_turned, mats, a, b, shard, pool, acc, gbias_r)

    key_sums.along_a()
    band_forward_phase(qf_r, ke_r, ve_r, line_r, attn_r, denom_r, 0, third)
    gather.along_a(1, (0,))
    band_forward_phase(qf_r, ke_r, ve_r, line_r, attn_r, denom_r, third, 2 * third)
    gather.along_a(1, (1,))
    band_forward_phase(qf_r, ke_r, ve_r, line_r, attn_r, denom_r, 2 * third, pairs)
    gather.along_b(0, (0,))
    key_sums.along_b()
    gather.across(1)
    gather.along_b(0, (1,))
    key_sums.finish(before_r, after_r)
    gather.along_a(2, (0, 1))
    gather.across(2)
    far_forward_phase(
        qf_r, ke_r, ve_r, line_r, num_r, den_r, before_r, after_r, attn_r, low_r, denom_r, left_r, right_r, lden_r,
        rden_r, pairs, head_dim,
    )
    hidden_turned = turned_r.at[:, pl.ds(0, rows)]
    acc = acc_r.at[own]
    hidden_phase(
        x_r.at[own], low_r, wo_r, bo_r, g1_r, s1_r, bdown_r, normed_r, scale_r, hidden_r, hidden_turned, acc
    )
    for offset in range(1, shards):
        arrive(biases.at[lax.rem(seq + shards - offset, shards)], bias_sems[1].at[offset], place.at())
    for shard in range(shards):
        bias_r[shard] = biases[shard, 0:8, :].astype(F32)
    ffn(0, 0, True)
    gather.along_b(1, (0, 1))
    gather.along_x(1, 0)
    gather.along_x(0, 1)
    gather.finish(0, 1)
    ffn(0, 1, True)
    gather.along_a(3, (0, 1))
    gather.across(3)
    gather.finish(1, 0)
    ffn(1, 0, True)
    gather.along_x(1, 1)
    gather.along_b(2, (0, 1))
    gather.along_x(2, 0)
    gather.finish(1, 1)
    ffn(1, 1, True)
    gather.finish(2, 0)
    ffn(2, 0, True)
    gather.along_x(2, 1)
    gather.along_x(3, 0)
    gather.along_b(3, (0, 1))
    gather.finish(2, 1)
    ffn(2, 1, True)
    gather.finish(3, 0)
    ffn(3, 0, True)
    gather.along_x(3, 1)
    gather.finish(3, 1)
    ffn(3, 1, True)
    sends.drain()
    loads[3].wait()
    middle_phase(acc, cot_r, g2_r, s2_r, hidden_r, gturned_r, small_r)
    layer_out = pltpu.make_async_copy(cot_r, layer_h, load_sem.at[6])
    layer_out.start()
    items = [(offset, column) for offset in (2, 1, 3, 0) for column in (1, 0)]
    for index, item in enumerate(items):
        ffn(*item, False)
        scatter.start(*item)
        if index > 1:
            scatter.chip(*items[index - 2])
        if index > 0:
            scatter.fetch(*items[index - 1])
        if index == 7:
            scatter.along_x(*items[0])
    first_back_phase(acc, normed_r, scale_r, g1_r, hidden_r, small_r)
    tot_r[pairs * half :, :] = jnp.zeros((tot_r.shape[0] - pairs * half, LANES), F32)
    block = pool.shape[2]
    for index in range(width // block):
        cols = slice(index * block, (index + 1) * block)
        pool[index, 0:width, :] = tn(low_r[...], hidden_r[:, cols]).astype(BF16)
    reduce.push(0)
    scatter.chip(*items[6])
    scatter.fetch(*items[7])
    scatter.along_x(*items[1])
    attn_back_phase(hidden_r, wo_r, attn_r, denom_r, low_r, qf_r, num_r, den_r, tot_r, pairs, head_dim)
    layer_out.wait()
    grad_sums.start(tot_r)
    scatter.chip(*items[7])

    def turn(block):
        turned_r[:, block] = x_r[block, :].T

    row_blocks(rows + 2 * WINDOW, turn)
    groups = pairs * LANES // CHUNK
    in_group = CHUNK // LANES

    kept = [gqkv_r, x_r, gqkv_r]

    def band(pair):
        group = pair // in_group
        band_backward_phase(
            qf_r, ke_r, ve_r, line_r, low_r, denom_r, num_r, den_r, left_r, right_r, lden_r, rden_r, attn_r,
            gk_r.at[group % 2], gv_r.at[group % 2], gline_r, cg_r, pair, pair + 1, group * in_group, head_dim,
        )

    def far(group):
        far_back_phase(
            ke_r, ve_r, line_r, num_r, den_r, before_r, after_r, gk_r.at[group % 2], gv_r.at[group % 2], pairs,
            group * in_group, (group + 1) * in_group, group * in_group, head_dim,
        )

    def grads(group, wanted):
        qkv_grad_phase(
            turned_r, w_r, omega_r, q_r, k_r, qf_r, ke_r, attn_r, gk_r.at[group % 2], gv_r.at[group % 2], kept[group],
            pool, small_r, group, wanted, place, head_dim,
        )

    def tokens_part(group, wanted):
        def body(block):
            if 1 not in wanted:
                block = pl.ds(pl.multiple_of(block.start + WINDOW, WINDOW), CHUNK)
            total = acc_r[block, :]
            for part in wanted:
                cols = slice(part * CHUNK, (part + 1) * CHUNK)
                wide = slice(part * width + group * CHUNK, part * width + (group + 1) * CHUNK)
                total = total + nt(kept[group][block, cols], w_r[:, wide])
            acc_r[block, :] = total

        row_blocks(rows + 2 * WINDOW if 1 in wanted else rows, body)

    scatter.along_x(*items[2])
    band(0)
    grad_sums.along_a()
    band(1)
    scatter.along_x(*items[3])
    grads(0, (0,))
    tokens_part(0, (0,))
    scatter.along_b(2)
    reduce.stage(0, 0)
    band(2)
    grad_sums.along_b()
    reduce.stage(0, 1)
    band(3)
    grad_sums.finish(before_r, after_r)
    scatter.along_x(*items[4])
    scatter.along_b(1)
    far(0)
    grads(0, (1, 2))
    reduce.push(1)
    scatter.along_x(*items[5])
    tokens_part(0, (1, 2))
    grads(1, (0,))
    reduce.stage(1, 0)
    band(4)
    scatter.along_x(*items[6])
    reduce.stage(0, 2)
    reduce.stage(1, 1)
    band(5)
    far(1)
    grads(1, (1, 2))
    reduce.push(2)
    scatter.along_x(*items[7])
    scatter.along_b(3)
    grads(2, (0,))
    reduce.stage(2, 0)
    reduce.stage(0, 3)
    reduce.stage(2, 1)
    far(2)
    grads(2, (1, 2))
    reduce.push(3)
    scatter.along_b(0)
    table_grads(gline_r, bucket_r, buckets, small_r)
    per_row = width // gbias_r.shape[2]
    for index in range(shards // per_row):
        small_r[9 + index : 10 + index, :] = jnp.concatenate(
            [gbias_r[index * per_row + i, 0:1, :] for i in range(per_row)], 1
        )
    held_r[0] = small_r[...]
    little.send(0)
    reduce.stage(1, 2)
    reduce.stage(3, 0)
    reduce.stage(0, 4)
    tokens_part(1, (0,))
    tokens_part(1, (1, 2))
    reduce.stage(3, 1)
    tokens_part(2, (0,))
    tokens_part(2, (1, 2))
    edge_r[0:WINDOW, :] = acc_r[0:WINDOW, :].astype(BF16)
    edge_r[WINDOW:, :] = acc_r[rows + WINDOW :, :].astype(BF16)
    top, bottom = pl.ds(0, WINDOW), pl.ds(WINDOW, WINDOW)
    sends.send(edge_r.at[top], tail_r.at[bottom], t_send.at[0], t_recv.at[1], to_left, place.not_first)
    sends.send(edge_r.at[bottom], tail_r.at[top], t_send.at[1], t_recv.at[0], to_right, place.not_last)
    reduce.stage(2, 2)
    reduce.stage(1, 3)
    little.receive(0)
    little.send(1)
    reduce.stage(0, 5)
    scatter.along_a()
    reduce.stage(3, 2)
    reduce.stage(2, 3)
    reduce.stage(1, 4)
    reduce.stage(0, 6)
    little.receive(1)
    little.send(2)
    reduce.stage(3, 3)
    reduce.stage(2, 4)
    reduce.stage(1, 5)
    reduce.stage(3, 4)
    reduce.stage(0, 7)
    reduce.stage(2, 5)
    reduce.stage(1, 6)
    little.receive(2)
    little.send(3)
    reduce.stage(3, 5)
    arrive(tail_r.at[top], t_recv.at[0], place.at(), place.not_first)
    arrive(tail_r.at[bottom], t_recv.at[1], place.at(), place.not_last)

    @pl.when(place.not_first)
    def _():
        acc_r[WINDOW : 2 * WINDOW, :] += tail_r[0:WINDOW, :].astype(F32)

    @pl.when(place.not_last)
    def _():
        acc_r[rows : rows + WINDOW, :] += tail_r[WINDOW:, :].astype(F32)

    tokens_out = pltpu.make_async_copy(acc, gtok_h, load_sem.at[7])
    tokens_out.start()
    reduce.stage(2, 6)
    reduce.stage(3, 6)
    scatter.last_x()
    reduce.stage(1, 7)
    little.receive(3)
    small_r[...] = little.total()
    reduce.stage(2, 7)
    reduce.stage(3, 7)
    scatter.finish()
    for index in range(chunks):
        reduce.stage(index, 8)
    tokens_out.wait()
    sends.drain()


def in_parts(grouped):
    groups = grouped.shape[1] // (3 * CHUNK)
    starts = [(group * 3 + part) * CHUNK for part in range(3) for group in range(groups)]
    return jnp.concatenate([grouped[:, start : start + CHUNK].astype(F32) for start in starts], 1)


def call(body, outs, operands, scratch=(), limit=60, collective_id=None, in_place=(), out_place=()):
    return pl.pallas_call(
        body,
        out_shape=[jax.ShapeDtypeStruct(shape, dtype) for shape, dtype in outs],
        in_specs=[
            pl.BlockSpec(memory_space=pl.ANY if i in in_place else pltpu.VMEM) for i in range(len(operands))
        ],
        out_specs=[
            pl.BlockSpec(memory_space=pl.ANY if i in out_place else pltpu.VMEM) for i in range(len(outs))
        ],
        scratch_shapes=list(scratch),
        compiler_params=pltpu.CompilerParams(
            vmem_limit_bytes=limit * MIB,
            collective_id=collective_id,
            has_side_effects=collective_id is not None,
        ),
    )(*operands)


def unpack_kernel(
    result_h, total_h, tokens_h, layer_h, small_r, gw_h, gwo_h, gup_r, gdown_r, gtok_h, out_h, gb_r, gbu_r, *rest
):
    vector_rs, (table_r, result_r, total_r, wide_r, tokens_r, layer_r, in_sem, out_sem) = rest[:6], rest[6:]
    blocks, width, block = result_r.shape
    chunks = wide_r.shape[0]
    per_chunk = blocks // chunks
    loads = []
    for chunk in range(chunks):
        part = pl.ds(chunk * per_chunk, per_chunk)
        loads.append(pltpu.make_async_copy(result_h.at[part], result_r.at[part], in_sem.at[chunk]))
    load_total = pltpu.make_async_copy(total_h, total_r, in_sem.at[chunks])
    load_tokens = pltpu.make_async_copy(tokens_h, tokens_r, in_sem.at[chunks + 1])
    load_layer = pltpu.make_async_copy(layer_h, layer_r, in_sem.at[chunks + 2])
    for load in loads + [load_total, load_tokens, load_layer]:
        load.start()
    stores = []

    def store(src, dst):
        copy = pltpu.make_async_copy(src, dst, out_sem.at[len(stores)])
        copy.start()
        stores.append(copy)

    for chunk in range(chunks):
        loads[chunk].wait()
        for index in range(per_chunk):
            wide_r[chunk, :, index * block : (index + 1) * block] = result_r[chunk * per_chunk + index].astype(F32)
        if chunk == 0:
            store(wide_r.at[0], gwo_h)
            continue
        for part in range(3):
            source = wide_r.at[chunk, :, pl.ds(part * CHUNK, CHUNK)]
            store(source, gw_h.at[:, pl.ds(part * width + (chunk - 1) * CHUNK, CHUNK)])
    load_tokens.wait()
    store(tokens_r, gtok_h)
    load_layer.wait()
    store(layer_r, out_h)
    load_total.wait()
    gup_r[...] = total_r[0].astype(F32)
    gdown_r[...] = total_r[1].T.astype(F32)
    for index, ref in enumerate(vector_rs):
        ref[...] = small_r[index, :]
    for group in range(width // CHUNK):
        for part in range(3):
            start = part * width + group * CHUNK
            gb_r[start : start + CHUNK] = small_r[6 + group, part * CHUNK : (part + 1) * CHUNK]
    heads, buckets = table_r.shape
    per_row = LANES // buckets
    for head in range(heads):
        at = head % per_row * buckets
        row = 13 + head // per_row
        table_r[head : head + 1, :] = small_r[row : row + 1, at : at + buckets]
    units = gbu_r.shape[0]
    seq = lax.axis_index("seq")
    per_row = width // units
    for shard in range(lax.axis_size("seq")):
        @pl.when(seq == shard)
        def _():
            at = shard % per_row * units
            gbu_r[...] = small_r[9 + shard // per_row, at : at + units]
    for copy in stores:
        copy.wait()


def fused(
    x, cot, w_up, w_down, w_qkv, b_qkv, codes, offset_bucket, bias_table, w_out, b_out, gain_one, shift_one, b_up, b_down,
    gain_two, shift_two, pairs, head_dim,
):
    rows, width = x.shape
    units = w_up.shape[1]
    heads, buckets = bias_table.shape
    count = lax.axis_size("seq")
    count_a = count // 2
    blocks, half = rows // WINDOW, LANES // 2
    middle, quarter = width // 6, width // 4
    side = (width - middle) // 2
    groups = width // CHUNK
    chunks = 1 + groups
    columns = chunks * width // units
    wide, ext = (rows, width), (rows + 2 * WINDOW, width)
    stacked, flat = (pairs * blocks, half, LANES), (pairs * blocks, LANES)
    message = (pairs * half + 32, LANES)
    mats = (2, count_a, 2, width, units)
    dma = pltpu.SemaphoreType.DMA
    vmem = pltpu.VMEM
    part = (message[0] // 2, LANES)
    sums = [vmem(shape, F32) for shape in (message, message, part, (count_a, *part), (2, *part), (2, *part))]
    layer, gtok, total, small, result, _, _ = call(
        functools.partial(layer_kernel, pairs, head_dim, buckets, count),
        [(wide, BF16), (wide, F32), ((2, width, units), BF16), ((16, width), F32), ((columns, width, units), BF16),
         (mats[1:], BF16), ((columns, 2 * quarter, units), BF16)],
        (x, cot, w_up, w_down, w_qkv, codes, bias_table, w_out, b_qkv, b_out, gain_one, shift_one, b_down, gain_two,
         shift_two, b_up, offset_bucket),
        [vmem(ext, BF16), vmem(wide, BF16), vmem(ext, BF16), vmem(wide, BF16), vmem((2, *ext), BF16),
         vmem((heads, LINE), F32), vmem(stacked, F32), vmem(flat, F32), vmem(message, F32),
         vmem((count, 16, units), BF16), vmem(message, F32),
         vmem(message, F32), vmem(stacked, F32), vmem(stacked, F32), vmem(flat, F32), vmem(flat, F32),
         vmem(wide, F32), vmem(wide, F32), vmem(wide, BF16), vmem((rows, LANES), F32),
         vmem(wide, BF16), vmem((width, ext[0]), BF16),
         vmem(wide, BF16), vmem(ext, F32), vmem(mats, BF16), vmem((columns, 2 * rows, units), BF16),
         vmem((count, 8, units), F32), vmem((count, 8, units), F32), vmem((2, ext[0], CHUNK), F32),
         vmem((2, ext[0], CHUNK), F32), vmem((heads, LINE), F32), vmem((2 * WINDOW, 3 * WINDOW), F32),
         vmem(ext, BF16), vmem((2, width, units), BF16), vmem((count_a, 2, side, units), BF16),
         vmem((count_a, side + middle, units), BF16), vmem((count_a - 1, side + middle, units), BF16),
         vmem((middle, units), BF16),
         vmem((2, 2 * quarter, units), BF16), vmem((columns, quarter, units), BF16),
         vmem((chunks, quarter, units), BF16), vmem((chunks, count_a - 1, quarter // count_a, units), BF16),
         vmem((chunks, quarter // count_a, units), BF16), vmem((4, 16, width), F32),
         vmem((3 + count_a, 16, width), F32)]
        + sums + sums
        + gather_sems(count_a) + sums_sems(count_a) + sums_sems(count_a) + scatter_sems(count_a)
        + reduce_sems(chunks, count_a)
        + [dma((3 + count_a,)), dma((3 + count_a,))] + [dma((count,)), dma((count,))] + [ dma((2,)), dma((2,)), dma((2,)), dma((2,)), dma((8,)),
           vmem(w_qkv.shape, BF16), vmem(w_out.shape, BF16),
           vmem((groups, CHUNK, CHUNK), BF16), vmem((16, width), F32)],
        limit=62,
        collective_id=0,
        in_place=(0, 1, 2, 3, 4, 7),
        out_place=(0, 1, 4, 5, 6),
    )
    vector = ((width,), F32)
    gw_qkv, gw_out, gup, gdown, gtok, layer, gb_qkv, grad_b_up, g2, s2, bd, g1, s1, bo, gtable = call(
        unpack_kernel,
        [((width, 3 * width), F32), ((width, width), F32), ((width, units), F32), ((units, width), F32), (wide, F32),
         (wide, BF16), ((3 * width,), F32), ((units,), F32)] + [vector] * 6 + [((heads, buckets), F32)],
        (result, total, gtok, layer, small),
        [vmem((columns, width, units), BF16), vmem((2, width, units), BF16), vmem((chunks, width, width), F32),
         vmem(wide, F32), vmem(wide, BF16), dma((chunks + 3,)), dma((3 * chunks,))],
        in_place=(0, 1, 2, 3),
        out_place=(0, 1, 4, 5),
    )
    return (
        layer[None], gtok[None], gw_qkv, gb_qkv, gw_out, bo, g1, s1, gup, grad_b_up, gdown, bd, g2, s2, gtable,
    )


def shards(
    tokens, cotangent, w_qkv, b_qkv, w_out, b_out, gain_one, shift_one, w_up, b_up, w_down, b_down,
    gain_two, shift_two, feature_codes, bias_table, offset_bucket,
):
    rows, width = tokens.shape[1:]
    heads, head_dim, feats = feature_codes.shape
    buckets = bias_table.shape[1]
    pairs = heads // 2
    blocks = rows // WINDOW
    half = LANES // 2
    hidden_units = w_up.shape[1]
    length = (offset_bucket.shape[0] + 1) // 2
    count = lax.axis_size("seq")
    x = tokens[0]
    state = (pairs * half + 8, LANES)
    stacked = (pairs * blocks, half, LANES)
    flat = (pairs * blocks, LANES)
    wide = (rows, width)

    def halo(block):
        forward = [(i, i + 1) for i in range(count - 1)]
        backward = [(target, source) for source, target in forward]
        low = lax.ppermute(block[rows - WINDOW :], "seq", forward)
        high = lax.ppermute(block[:WINDOW], "seq", backward)
        return jnp.concatenate([low, block, high], 0)

    me = lax.axis_index("seq")
    ids = jnp.arange(count)

    def prefix(message):
        every = lax.all_gather(message, "seq", axis=0)
        before = jnp.sum(jnp.where((ids < me)[:, None, None], every, 0.0), 0)
        after = jnp.sum(jnp.where((ids > me)[:, None, None], every, 0.0), 0)
        return before, after

    if lax.axis_size("row") == 4 and count == 8:
        return fused(
            x, cotangent[0], w_up, w_down, w_qkv, b_qkv, feature_codes, offset_bucket, bias_table, w_out, b_out, gain_one,
            shift_one, b_up, b_down, gain_two, shift_two, pairs, head_dim,
        )

    bucket_line = offset_bucket[length - LINE // 2 : length + LINE // 2][None]
    omega_int = (feature_codes.astype(F32) - CENTER).astype(BF16)
    group = CHUNK // head_dim
    eye = jnp.eye(group, dtype=BF16)
    omega = (
        omega_int.reshape(heads // group, group, head_dim, 1, feats)
        * eye[None, :, None, :, None]
    ).reshape(heads // group, CHUNK, CHUNK)

    def body_one(x_r, w_r, b_r, o_r, bu_r, ta_r, q_r, k_r, v_r, qf_r, kf_r, line_r, num_r, den_r, tot_r):
        parts = ((1, k_r, kf_r), (2, v_r, None), (0, q_r, qf_r))
        qkv_phase(x_r, w_r, [b_r.at[pl.ds(i, 1)] for i in range(3)], o_r, parts, head_dim)
        line_phase(bu_r, ta_r, line_r)
        state_phase(kf_r, v_r, num_r, den_r, tot_r, pairs)

    q, k, v, qf, kf, line, num, den, total = call(
        body_one,
        [(wide, BF16)] * 5
        + [((heads, LINE), F32), (stacked, F32), (flat, F32), (state, F32)],
        (x, w_qkv, b_qkv.astype(F32).reshape(3, width), omega, bucket_line, bias_table),
    )
    up_all = lax.all_gather(w_up, "seq", axis=0)
    down_all = lax.all_gather(jnp.transpose(w_down), "seq", axis=0)
    b_up_all = jnp.broadcast_to(lax.all_gather(b_up, "seq", axis=0)[:, None, :], (count, 8, hidden_units))

    ke, ve = halo(kf), halo(v)
    before, after = prefix(total)

    def body_two(*refs):
        ins, outs = refs[:12], refs[12:]
        qf_r, ke_r, ve_r, line_r, num_r, den_r, bef_r, aft_r, x_r, w_r, b_r, _ = ins
        out_r, low_r, dnm_r, l_r, r_r, ld_r, rd_r, nrm_r, sc_r = outs
        band_forward_phase(qf_r, ke_r, ve_r, line_r, out_r, dnm_r, 0, pairs)
        far_forward_phase(
            qf_r, ke_r, ve_r, line_r, num_r, den_r, bef_r, aft_r,
            out_r, low_r, dnm_r, l_r, r_r, ld_r, rd_r, pairs, head_dim,
        )
        out_phase(x_r, low_r, w_r, b_r, nrm_r, sc_r)

    attn, attn_low, denom, left, right, left_den, right_den, normed, scale = call(
        body_two,
        [(wide, F32), (wide, BF16), (wide, F32), (stacked, F32), (stacked, F32), (flat, F32),
         (flat, F32), (wide, F32), ((rows, LANES), F32)],
        (qf, ke, ve, line, num, den, before, after, x, w_out, b_out[None], gain_one[None]),
    )
    layer, first, first_low, vec, gup, gdown, gbias = call(
        ffn_phase,
        [(wide, BF16), (wide, F32), (wide, BF16), ((8, width), F32),
         ((count, width, hidden_units), BF16), ((count, width, hidden_units), BF16),
         ((count, 8, hidden_units), F32)],
        (normed, scale, gain_one[None], shift_one[None], up_all, b_up_all, down_all, b_down[None],
         gain_two[None], shift_two[None], cotangent[0]),
        (pltpu.VMEM((count, rows, hidden_units), BF16), pltpu.VMEM((count, rows, hidden_units), BF16),
         pltpu.VMEM(wide, F32)),
    )

    def reduced(part):
        return lax.psum(lax.psum_scatter(part, "seq", scatter_dimension=0), "row").astype(F32)

    grad_w_up = reduced(gup)
    grad_w_down = jnp.transpose(reduced(gdown))
    grad_b_up = reduced(gbias[:, 0])
    ext = (rows + 2 * WINDOW, width)

    def body_four(*refs):
        (gl_r, w_r, lo_r, ou_r, dn_r, qf_r, ke_r, ve_r, li_r, l_r, r_r, ld_r, rd_r, bu_r) = refs[:14]
        gw_r, gq_r, gk_r, gv_r, dnum_r, dden_r, tot_r, gt_r, gnum_r, gden_r, gline_r, cg_r = refs[14:]
        out_back_phase(
            gl_r, w_r, lo_r, ou_r, dn_r, qf_r, gnum_r, gden_r, gw_r, dnum_r, dden_r, tot_r, pairs, head_dim
        )
        band_backward_phase(
            qf_r, ke_r, ve_r, li_r, gnum_r, gden_r, dnum_r, dden_r, l_r, r_r, ld_r, rd_r,
            gq_r, gk_r, gv_r, gline_r, cg_r, 0, pairs, 0, head_dim,
        )
        gt_r[...] = table_phase(gline_r, bu_r, buckets)

    gw_out, gq, gk, gv, dnum, dden, gtotal, gtable = call(
        body_four,
        [((width, width), F32), (wide, F32), (ext, F32), (ext, F32), (stacked, F32), (flat, F32),
         (state, F32), (bias_table.shape, F32)],
        (first_low, w_out, attn_low, attn, denom, qf, ke, ve, line, left, right, left_den, right_den,
         bucket_line),
        (pltpu.VMEM(wide, BF16), pltpu.VMEM(wide, F32), pltpu.VMEM((heads, LINE), F32),
         pltpu.VMEM((2 * WINDOW, 3 * WINDOW), F32)),
    )
    past, future = prefix(gtotal)
    forward = [(i, i + 1) for i in range(count - 1)]
    backward = [(target, source) for source, target in forward]
    to_left = jnp.stack([gk[:WINDOW], gv[:WINDOW]]).astype(BF16)
    to_right = jnp.stack([gk[rows + WINDOW :], gv[rows + WINDOW :]]).astype(BF16)
    low_in = lax.ppermute(to_right, "seq", forward)
    high_in = lax.ppermute(to_left, "seq", backward)

    def body_five(*refs):
        (x_r, w_r, o_r, q_r, k_r, v_r, qf_r, kf_r, li_r, dn_r, dd_r, pa_r, fu_r, lo_r, hi_r, gq_r,
         gki_r, gvi_r, fi_r) = refs[:19]
        gt_r, gw_r, gb_r, gk_r, gv_r, turned_r = refs[19:]
        gk_r[...] = gki_r[...]
        gv_r[...] = gvi_r[...]
        gt_r[...] = fi_r[...]
        turned_r[...] = x_r[...].T
        key_back_phase(
            kf_r, v_r, li_r, dn_r, dd_r, pa_r, fu_r, lo_r, hi_r, gk_r, gv_r, pairs, 0, pairs, head_dim
        )
        for group in range(width // CHUNK):
            qkv_back_phase(
                turned_r, w_r, o_r, q_r, k_r, qf_r, kf_r, gq_r, gk_r, gv_r, gt_r, gw_r, gb_r, group, head_dim
            )

    gtok, gw_qkv, small = call(
        body_five,
        [(wide, F32), ((width, 4 * width), F32), ((16, width), F32)],
        (x, w_qkv, omega, q, k, v, qf, kf, line, dnum, dden, past, future, low_in, high_in, gq, gk, gv,
         first),
        (pltpu.VMEM(ext, F32), pltpu.VMEM(ext, F32), pltpu.VMEM((width, rows), BF16)),
    )
    gw_qkv = in_parts(gw_qkv[:, width:])
    gb_qkv = in_parts(small[6 : 6 + width // CHUNK].reshape(1, -1))
    summed = lax.psum((gw_qkv, gb_qkv[0], gw_out, vec, gtable), ("row", "seq"))
    gw_qkv, gb_qkv, gw_out, vec, gtable = summed
    return (
        layer[None], gtok[None], gw_qkv, gb_qkv, gw_out, vec[5], vec[3], vec[4], grad_w_up, grad_b_up,
        grad_w_down, vec[2], vec[0], vec[1], gtable,
    )


def solution(mesh):
    placed = (
        P("row", "seq", None), P("row", "seq", None), P(), P(), P(), P(), P(), P(), P(None, "seq"),
        P("seq"), P("seq", None), P(), P(), P(), P(), P(), P(),
    )
    return jax.shard_map(
        shards,
        mesh=mesh,
        in_specs=placed,
        out_specs=(
            P("row", "seq", None), P("row", "seq", None), P(), P(), P(), P(), P(), P(), P(None, "seq"),
            P("seq"), P("seq", None), P(), P(), P(), P(),
        ),
        check_vma=False,
    )
```
